32 devices in a mesh: ctx: 8 (over y, x, core), fsdp: 4 (over z).
Axes of the slice: x: 2, y: 2, z: 4, core: 2. Of those that a mesh axis runs over, the one named last changes fastest.
Arguments:
- hidden_in: bfloat16 [4, 1024, 2048], P('fsdp', 'ctx'), may hold values from -6 to 6
- cotangent: bfloat16 [4, 1024, 2048], P('fsdp', 'ctx'), may hold values from -6 to 6
- teacher: bfloat16 [4, 1024, 2048], P('fsdp', 'ctx'), may hold values from -6 to 6
- valid_mask: int32 [4, 1024], P('fsdp', 'ctx'), may hold values 0 or 1
- doc_starts: int32 [4, 8], P('fsdp'), may hold values from 0 to 1023, as said below
- attn_gain: bfloat16 [2048], P('fsdp'), may hold values from 0.5 to 1.5
- w_query: bfloat16 [2048, 2048], P('fsdp'), may hold values from -0.125 to 0.125
- w_key: bfloat16 [2048, 1024], P('fsdp'), may hold values from -0.125 to 0.125
- value_weight: bfloat16 [2048, 1024], P('fsdp'), may hold values from -0.125 to 0.125
- w_output: bfloat16 [2048, 2048], P('fsdp'), may hold values from -1 to 1
- mlp_gain: bfloat16 [2048], P('fsdp'), may hold values from 0.5 to 1.5
- w_gate: bfloat16 [2048, 8192], P('fsdp'), may hold values from -0.125 to 0.125
- w_up: bfloat16 [2048, 8192], P('fsdp'), may hold values from -0.125 to 0.125
- w_down: bfloat16 [8192, 2048], P('fsdp'), may hold values from -0.0625 to 0.0625
Outputs:
- loss: float32 [], replicated
- output: bfloat16 [4, 1024, 2048], P('fsdp', 'ctx')
- grad_input: bfloat16 [4, 1024, 2048], P('fsdp', 'ctx')
- grad_attn_gain: float32 [2048], P(('ctx', 'fsdp'))
- grad_query: float32 [2048, 2048], P(('ctx', 'fsdp'))
- grad_key: float32 [2048, 1024], P(('ctx', 'fsdp'))
- grad_value: float32 [2048, 1024], P(('ctx', 'fsdp'))
- grad_out_proj: float32 [2048, 2048], P(('ctx', 'fsdp'))
- grad_mlp_gain: float32 [2048], P(('ctx', 'fsdp'))
- grad_gate: float32 [2048, 8192], P(('ctx', 'fsdp'))
- grad_up: float32 [2048, 8192], P(('ctx', 'fsdp'))
- grad_down: float32 [8192, 2048], P(('ctx', 'fsdp'))
The draws below stay inside these ranges and needn't reach their ends.
Inputs may be any that keep to these rules, and one draw needn't show every extreme that they name: `doc_starts`: each row begins with 0 and rises strictly, and its last start is 1023; a place belongs to the document with the last start at or before it.
All inputs are finite; a program needn't handle non-finite values. No bound on the sum of `valid_mask` on one device may be relied on, other than what follows from the above.
Results may differ from the reference program's by a relative error of at most 0.015.
Values may be sent and summed in bfloat16 or wider, within the bound.
A program may use at most 640 MiB of HBM per device.

```python
import math
import jax
import jax.numpy as jnp
from jax import lax

D = 2048
QUERY_HEADS = 16
KEY_VALUE_HEADS = 8
HEAD_SIZE = 128
FF = 8192
TOK_DEV = 128
DOCS = 8
SPAN = 64
PACKED_TOKENS = 1024
STREAMS = 4
QW = 2048
KW = 1024
N_CTX = 8


def draw_doc_starts(key, part):
    key = jax.random.fold_in(key, 7)

    def one_stream(sub):
        first_key, rest_key = jax.random.split(sub)
        lowest = (PACKED_TOKENS // TOK_DEV + 1) * SPAN
        first = jax.random.randint(first_key, (), lowest, PACKED_TOKENS - DOCS + 2)
        weights = jax.random.randint(rest_key, (DOCS - 1,), 1, 64)
        spare = PACKED_TOKENS - first - (DOCS - 1)
        lengths = 1 + spare * weights // jnp.sum(weights)
        offsets = jnp.concatenate([jnp.zeros((1,), jnp.int32), jnp.cumsum(lengths[:-1]).astype(jnp.int32)])
        starts = jnp.concatenate([jnp.zeros((1,), jnp.int32), (first + offsets).astype(jnp.int32)])
        return starts.at[DOCS - 1].set(PACKED_TOKENS - 1).astype(jnp.int32)
    return jax.vmap(one_stream)(jax.random.split(key, STREAMS))


def place_ends(values, stream_key, smallest, largest):
    longest = values.shape.index(max(values.shape))
    spots = []
    for shift in (0, 1):
        where = [jax.random.randint(jax.random.fold_in(stream_key, axis), (), 0, length) for axis, length in enumerate(values.shape)]
        where[longest] = (where[longest] + shift) % values.shape[longest]
        spots.append(tuple(where))
    return values.at[spots[0]].set(smallest).at[spots[1]].set(largest)


def block_scale(key, extent, cuts, low, largest):
    factor_of, own = 1.0, jax.random.fold_in(key, 6)
    for dim, blocks in cuts:
        steps = jnp.exp(jax.random.uniform(jax.random.fold_in(own, dim), (blocks,), jnp.float32, low / len(cuts), largest / len(cuts)))
        factor_of = factor_of * jnp.repeat(steps, extent[dim] // blocks).reshape([-1 if axis == dim else 1 for axis in range(len(extent))])
    return factor_of


def bell_draw(own_key, extent, spread, limit, cuts=(), kind=jnp.bfloat16):
    array = jax.random.normal(own_key, extent, jnp.float32) * spread
    if len(cuts) > 0:
        array = block_scale(own_key, extent, cuts, -0.22, 0.18) * array
    return jnp.clip(array, min=-limit, max=limit).astype(kind)


def setup_inputs(seed: int = 0) -> dict:
    key_of = jax.random.split(jax.random.key(seed), 15)
    return {
        "hidden_in": bell_draw(key_of[0], (STREAMS, PACKED_TOKENS, D), 1.0, 6.0, ((0, 4), (1, 8))),
        "cotangent": bell_draw(key_of[1], (STREAMS, PACKED_TOKENS, D), 1.0, 6.0, ((0, 4), (1, 8))),
        "teacher": bell_draw(key_of[2], (STREAMS, PACKED_TOKENS, D), 1.0, 6.0, ((0, 4), (1, 8))),
        "valid_mask": place_ends((jax.random.randint(key_of[3], (STREAMS, PACKED_TOKENS), 0, 4) < 3).astype(jnp.int32), jax.random.fold_in(key_of[3], 1), 0, 1),
        "doc_starts": draw_doc_starts(jax.random.fold_in(key_of[14], 71), 0),
        "attn_gain": jnp.clip(1.0 + 0.1 * jax.random.normal(key_of[5], (D,), jnp.float32), 0.5, 1.5).astype(jnp.bfloat16),
        "w_query": bell_draw(key_of[6], (D, QW), D ** -0.5, 0.125, ((0, 4),)),
        "w_key": bell_draw(key_of[7], (D, KW), D ** -0.5, 0.125, ((0, 4),)),
        "value_weight": bell_draw(key_of[8], (D, KW), D ** -0.5, 0.125, ((0, 4),)),
        "w_output": bell_draw(key_of[9], (QW, D), (QW // 64) ** -0.5, 1.0, ((0, 4),)),
        "mlp_gain": jnp.clip(1.0 + 0.1 * jax.random.normal(key_of[10], (D,), jnp.float32), 0.5, 1.5).astype(jnp.bfloat16),
        "w_gate": bell_draw(key_of[11], (D, FF), D ** -0.5, 0.125, ((0, 4),)),
        "w_up": bell_draw(key_of[12], (D, FF), D ** -0.5, 0.125, ((0, 4),)),
        "w_down": bell_draw(key_of[13], (FF, D), FF ** -0.5, 0.0625, ((0, 4),)),
    }


EPS = 1e-05
ROPE_BASE = 1000000.0
NEG = -1e+30

@jax.custom_vjp
def low(v):
    return lax.optimization_barrier(v.astype(jnp.bfloat16)).astype(jnp.float32)

@jax.custom_vjp
def low_back(v):
    return v

def low_keep(v):
    return (low(v), None)

def low_pass(kept, grad):
    return (grad,)

def back_keep(v):
    return (v, None)

def back_low(kept, grad):
    return (low(grad),)
low.defvjp(low_keep, low_pass)
low_back.defvjp(back_keep, back_low)

def places(starts):
    rowid = jnp.arange(PACKED_TOKENS, dtype=jnp.int32)
    device = rowid // TOK_DEV
    within = rowid % TOK_DEV
    span_id = jnp.where(within < SPAN, device, 2 * N_CTX - 1 - device)
    place = (span_id * SPAN + within % SPAN).astype(jnp.int32)
    before = starts[None, :] <= place[:, None]
    segment = lax.optimization_barrier(jnp.sum(before.astype(jnp.int32), axis=1)) - 1
    first = lax.optimization_barrier(jnp.max(jnp.where(before, starts[None, :], 0), axis=1))
    return (place, segment.astype(jnp.int32), (place - first).astype(jnp.int32))

def matrix_product(left, right):
    return jnp.dot(left, right, precision=lax.Precision.HIGHEST)

def rotary_embed(values, token_offset, sign):
    half = HEAD_SIZE // 2
    freq = ROPE_BASE ** (-(jnp.arange(half, dtype=jnp.float32) * 2.0 / HEAD_SIZE))
    angle = token_offset.astype(jnp.float32)[:, None] * freq[None, :]
    cosine = jnp.cos(angle)[:, None, :]
    sine = sign * jnp.sin(angle)[:, None, :]
    first = values[..., :half]
    second = values[..., half:]
    return jnp.concatenate([first * cosine - second * sine, second * cosine + first * sine], axis=-1)

def rms_norm_scale(values):
    return lax.rsqrt(lax.optimization_barrier(jnp.mean(values * values, axis=-1, keepdims=True)) + EPS)

def one_stream(layer_input, place, segment, token_offset, weights):
    first_norm_scale, w_query, w_key, value_weight, w_output, second_norm_scale, w_gate, w_up, w_down = weights
    first_normalized_input = layer_input * rms_norm_scale(layer_input)
    first_normed = low(first_normalized_input * first_norm_scale)
    qproj = low_back(matrix_product(first_normed, w_query))
    key_projected = low_back(matrix_product(first_normed, w_key))
    value_rows = low(low_back(matrix_product(first_normed, value_weight))).reshape(PACKED_TOKENS, KEY_VALUE_HEADS, HEAD_SIZE)
    query_rows = low(rotary_embed(qproj.reshape(PACKED_TOKENS, QUERY_HEADS, HEAD_SIZE), token_offset, 1.0))
    key_rows = low(rotary_embed(key_projected.reshape(PACKED_TOKENS, KEY_VALUE_HEADS, HEAD_SIZE), token_offset, 1.0))
    block_rows = math.gcd(PACKED_TOKENS, 512)
    blocks = PACKED_TOKENS // block_rows

    def attend(parts):
        query_block_rows, place_block, segment_block = parts
        grouped_queries = query_block_rows.reshape(block_rows, KEY_VALUE_HEADS, QUERY_HEADS // KEY_VALUE_HEADS, HEAD_SIZE)
        attention_scores = jnp.einsum('pcmb,vcb->cmpv', grouped_queries, key_rows, precision=lax.Precision.HIGHEST) * HEAD_SIZE ** (-0.5)
        attention_scores = low_back(attention_scores)
        allowed = (segment_block[:, None] == segment[None, :]) & (place[None, :] <= place_block[:, None])
        attention_scores = jnp.where(allowed[None, None], attention_scores, NEG)
        top = lax.optimization_barrier(jnp.max(attention_scores, axis=-1, keepdims=True))
        lse = top + jnp.log(lax.optimization_barrier(jnp.sum(jnp.exp(attention_scores - top), axis=-1, keepdims=True)))
        attention_probabilities = jnp.exp(attention_scores - lse)
        mixed_heads = jnp.einsum('uknp,puo->nuko', low(attention_probabilities), value_rows, precision=lax.Precision.HIGHEST)
        return mixed_heads.reshape(block_rows, QW)
    attn = lax.map(jax.checkpoint(attend), (query_rows.reshape(blocks, block_rows, QUERY_HEADS, HEAD_SIZE), place.reshape(blocks, block_rows), segment.reshape(blocks, block_rows)))
    attn = low(low_back(attn.reshape(PACKED_TOKENS, QW)))
    residual_state = layer_input + low_back(matrix_product(attn, w_output))
    second_normalized_input = residual_state * rms_norm_scale(residual_state)
    second_normed = low(second_normalized_input * second_norm_scale)
    gate = low_back(matrix_product(second_normed, w_gate))
    up = low_back(matrix_product(second_normed, w_up))
    act = low(jax.nn.silu(gate) * up)
    return residual_state + low_back(matrix_product(act, w_down))

def reference(hidden_in, cotangent, teacher, valid_mask, doc_starts, attn_gain, w_query, w_key, value_weight, w_output, mlp_gain, w_gate, w_up, w_down):
    layer_input = hidden_in.astype(jnp.float32)
    cot = cotangent.astype(jnp.float32)
    target = teacher.astype(jnp.float32)
    maskf = valid_mask.astype(jnp.float32)
    count = jnp.sum(maskf)
    place, segment, token_offset = jax.vmap(places)(doc_starts)
    weights = tuple((w.astype(jnp.float32) for w in (attn_gain, w_query, w_key, value_weight, w_output, mlp_gain, w_gate, w_up, w_down)))

    def objective(values, params):

        def step(carry, parts):
            stream_in, stream_place, stream_segment, stream_offset = parts
            return (carry, one_stream(stream_in, stream_place, stream_segment, stream_offset, params))
        _, outs = lax.scan(step, jnp.zeros((), jnp.float32), (values, place, segment, token_offset))
        diff = outs - target
        loss = jnp.sum(maskf * lax.optimization_barrier(jnp.mean(diff * diff, axis=-1))) / count
        return (jnp.sum(outs * cot) + loss, (outs, loss))
    total, backward, aux = jax.vjp(objective, layer_input, weights, has_aux=True)
    outs, loss = aux
    grad_x, grad_w = backward(jnp.ones_like(total))
    return (loss, outs.astype(jnp.bfloat16), grad_x.astype(jnp.bfloat16), grad_w[0], grad_w[1], grad_w[2], grad_w[3], grad_w[4], grad_w[5], grad_w[6], grad_w[7], grad_w[8])
```

```python
import functools

import jax
import jax.numpy as jnp
from jax import lax
from jax.experimental import pallas as pl
from jax.experimental.pallas import tpu as pltpu
from jax.sharding import PartitionSpec as P

QUERY_HEADS = 16
KEY_VALUE_HEADS = 8
HEAD_SIZE = 128
FF = 8192


EPS = 1e-05
ROPE_BASE = 1000000.0
NEG = -1e30
CONTRACT_ROWS = (((0,), (0,)), ((), ()))
CONTRACT_COLS = (((1,), (1,)), ((), ()))


def stream_places(rows, local_token_count, devices, starts):
    span = local_token_count // 2
    rowid = jnp.arange(rows, dtype=jnp.int32)
    device = rowid // local_token_count
    within = rowid % local_token_count
    span_id = jnp.where(within < span, device, 2 * devices - 1 - device)
    place = span_id * span + within % span
    before = starts[None, :] <= place[:, None]
    segment = jnp.sum(before.astype(jnp.int32), axis=1) - 1
    first = jnp.max(jnp.where(before, starts[None, :], 0), axis=1)
    return (place, segment, place - first)


def rotary_embed(values, token_offset, sign):
    half = HEAD_SIZE // 2
    freq = ROPE_BASE ** (-(jnp.arange(half, dtype=jnp.float32) * 2.0 / HEAD_SIZE))
    angle = token_offset.astype(jnp.float32)[:, None] * freq[None, :]
    cosine = jnp.cos(angle)[:, None, :]
    sine = sign * jnp.sin(angle)[:, None, :]
    first = values[..., :half]
    second = values[..., half:]
    return jnp.concatenate(
        [first * cosine - second * sine, second * cosine + first * sine], axis=-1
    )


def rms_norm_scale(values):
    return lax.rsqrt(jnp.mean(values * values, axis=-1, keepdims=True) + EPS)


def head_scores(query_rows, key_rows, allowed):
    attention_scores = jnp.einsum(
        "trd,sd->rts", query_rows, key_rows, preferred_element_type=jnp.float32
    ) * HEAD_SIZE ** (-0.5)
    return jnp.where(allowed[None], attention_scores, NEG)


def per_device(
    hidden_in,
    cotangent,
    teacher,
    valid_mask,
    doc_starts,
    attn_gain,
    w_query,
    w_key,
    value_weight,
    w_output,
    mlp_gain,
    w_gate,
    w_up,
    w_down,
):
    local_token_count = hidden_in.shape[1]
    width = hidden_in.shape[2]
    devices = lax.axis_size("ctx")
    index = lax.axis_index("ctx")
    packed_stream_rows = local_token_count * devices
    query_group = QUERY_HEADS // KEY_VALUE_HEADS
    place, segment, token_offset = stream_places(
        packed_stream_rows, local_token_count, devices, doc_starts[0]
    )
    own_start = index * local_token_count
    my_place = lax.dynamic_slice_in_dim(place, own_start, local_token_count)
    my_segment = lax.dynamic_slice_in_dim(segment, own_start, local_token_count)
    local_stream_offset = lax.dynamic_slice_in_dim(token_offset, own_start, local_token_count)
    allowed = (my_segment[:, None] == segment[None, :]) & (place[None, :] <= my_place[:, None])
    layer_input = hidden_in[0].astype(jnp.float32)
    attn_whole = (
        lax.all_gather(attn_gain, "fsdp", axis=0, tiled=True),
        lax.all_gather(w_query, "fsdp", axis=0, tiled=True),
        lax.all_gather(w_key, "fsdp", axis=0, tiled=True),
        lax.all_gather(value_weight, "fsdp", axis=0, tiled=True),
        lax.all_gather(w_output, "fsdp", axis=0, tiled=True),
    )
    first_norm_scale = attn_whole[0].astype(jnp.float32)
    first_inverse_norm = rms_norm_scale(layer_input)
    first_normalized_input = layer_input * first_inverse_norm
    first_normed = (first_normalized_input * first_norm_scale).astype(jnp.bfloat16)
    qproj = jnp.dot(first_normed, attn_whole[1], preferred_element_type=jnp.float32)
    key_projected = jnp.dot(first_normed, attn_whole[2], preferred_element_type=jnp.float32)
    vproj = jnp.dot(first_normed, attn_whole[3], preferred_element_type=jnp.float32).astype(
        jnp.bfloat16
    )
    query_rows = rotary_embed(
        qproj.reshape(local_token_count, QUERY_HEADS, HEAD_SIZE), local_stream_offset, 1.0
    ).astype(jnp.bfloat16)
    key_rows = (
        rotary_embed(
            key_projected.reshape(local_token_count, KEY_VALUE_HEADS, HEAD_SIZE),
            local_stream_offset,
            1.0,
        )
        .reshape(local_token_count, KEY_VALUE_HEADS * HEAD_SIZE)
        .astype(jnp.bfloat16)
    )
    every_key_row, every_value_row = (
        lax.all_gather(key_rows, "ctx", axis=0, tiled=True),
        lax.all_gather(vproj, "ctx", axis=0, tiled=True),
    )
    key_head_rows = every_key_row.reshape(packed_stream_rows, KEY_VALUE_HEADS, HEAD_SIZE).transpose(
        1, 0, 2
    )
    value_head_rows = every_value_row.reshape(
        packed_stream_rows, KEY_VALUE_HEADS, HEAD_SIZE
    ).transpose(1, 0, 2)
    query_head_rows = query_rows.reshape(
        local_token_count, KEY_VALUE_HEADS, query_group, HEAD_SIZE
    ).transpose(1, 0, 2, 3)

    def attend_head(parts):
        head_query, head_key, head_val = parts
        attention_scores = head_scores(head_query, head_key, allowed)
        top = jnp.max(attention_scores, axis=-1, keepdims=True)
        lse = top + jnp.log(jnp.sum(jnp.exp(attention_scores - top), axis=-1, keepdims=True))
        attention_probabilities = jnp.exp(attention_scores - lse)
        mixed_heads = jnp.einsum(
            "rts,sd->trd",
            attention_probabilities.astype(jnp.bfloat16),
            head_val,
            preferred_element_type=jnp.float32,
        )
        return (mixed_heads, lse)

    mixed_heads, lse = lax.map(attend_head, (query_head_rows, key_head_rows, value_head_rows))
    attn = (
        mixed_heads.transpose(1, 0, 2, 3)
        .reshape(local_token_count, QUERY_HEADS * HEAD_SIZE)
        .astype(jnp.bfloat16)
    )
    residual_state = layer_input + jnp.dot(attn, attn_whole[4], preferred_element_type=jnp.float32)
    mlp_whole = (
        lax.all_gather(mlp_gain, "fsdp", axis=0, tiled=True),
        lax.all_gather(w_gate, "fsdp", axis=0, tiled=True),
        lax.all_gather(w_up, "fsdp", axis=0, tiled=True),
        lax.all_gather(w_down, "fsdp", axis=0, tiled=True),
    )
    second_norm_scale = mlp_whole[0].astype(jnp.float32)
    second_inverse_norm = rms_norm_scale(residual_state)
    second_normalized_input = residual_state * second_inverse_norm
    second_normed = (second_normalized_input * second_norm_scale).astype(jnp.bfloat16)
    gate = jnp.dot(second_normed, mlp_whole[1], preferred_element_type=jnp.float32)
    up_val = jnp.dot(second_normed, mlp_whole[2], preferred_element_type=jnp.float32)
    sigma = jax.nn.sigmoid(gate)
    act = (gate * sigma * up_val).astype(jnp.bfloat16)
    outf = residual_state + jnp.dot(act, mlp_whole[3], preferred_element_type=jnp.float32)
    maskf = valid_mask[0].astype(jnp.float32)
    diff = outf - teacher[0].astype(jnp.float32)
    count_here = jnp.sum(maskf)
    error_here = jnp.sum(maskf * jnp.mean(diff * diff, axis=-1))
    count, error_total = lax.psum((count_here, error_here), ("ctx", "fsdp"))
    loss = error_total / count
    output_gradient = cotangent[0].astype(jnp.float32) + maskf[:, None] * diff * (
        2.0 / (count * width)
    )
    g_mo = output_gradient.astype(jnp.bfloat16)
    mlp_back = (
        lax.all_gather(mlp_gain, "fsdp", axis=0, tiled=True),
        lax.all_gather(w_gate, "fsdp", axis=0, tiled=True),
        lax.all_gather(w_up, "fsdp", axis=0, tiled=True),
        lax.all_gather(w_down, "fsdp", axis=0, tiled=True),
    )
    g_act = lax.dot_general(g_mo, mlp_back[3], CONTRACT_COLS, preferred_element_type=jnp.float32)
    g_gate = (g_act * up_val * sigma * (1.0 + gate * (1.0 - sigma))).astype(jnp.bfloat16)
    g_up = (g_act * gate * sigma).astype(jnp.bfloat16)
    gate_up_gradient = jnp.concatenate([g_gate, g_up], axis=1)
    second_norm_gradient = lax.dot_general(
        g_gate, mlp_back[1], CONTRACT_COLS, preferred_element_type=jnp.float32
    )
    second_norm_gradient = second_norm_gradient + lax.dot_general(
        g_up, mlp_back[2], CONTRACT_COLS, preferred_element_type=jnp.float32
    )
    second_hat_gradient = second_norm_gradient * second_norm_scale
    residual_gradient = output_gradient + second_inverse_norm * (
        second_hat_gradient
        - second_normalized_input
        * jnp.mean(second_hat_gradient * second_normalized_input, axis=-1, keepdims=True)
    )
    mlp_share = lax.psum_scatter(
        lax.dot_general(
            second_normed, gate_up_gradient, CONTRACT_ROWS, preferred_element_type=jnp.float32
        ),
        ("ctx", "fsdp"),
        scatter_dimension=0,
        tiled=True,
    )
    down_share = lax.psum_scatter(
        lax.dot_general(act, g_mo, CONTRACT_ROWS, preferred_element_type=jnp.float32),
        ("ctx", "fsdp"),
        scatter_dimension=0,
        tiled=True,
    )
    g_branch = residual_gradient.astype(jnp.bfloat16)
    attn_back = (
        lax.all_gather(attn_gain, "fsdp", axis=0, tiled=True),
        lax.all_gather(w_query, "fsdp", axis=0, tiled=True),
        lax.all_gather(w_key, "fsdp", axis=0, tiled=True),
        lax.all_gather(value_weight, "fsdp", axis=0, tiled=True),
        lax.all_gather(w_output, "fsdp", axis=0, tiled=True),
    )
    attention_gradient = lax.dot_general(
        g_branch, attn_back[4], CONTRACT_COLS, preferred_element_type=jnp.float32
    ).astype(jnp.bfloat16)
    heads_gradient = attention_gradient.reshape(
        local_token_count, KEY_VALUE_HEADS, query_group, HEAD_SIZE
    ).transpose(1, 0, 2, 3)

    def attend_back(parts):
        head_query, head_key, head_val, head_lse, head_grad = parts
        attention_probabilities = jnp.exp(head_scores(head_query, head_key, allowed) - head_lse)
        g_probs = jnp.einsum("trd,sd->rts", head_grad, head_val, preferred_element_type=jnp.float32)
        delta = jnp.sum(attention_probabilities * g_probs, axis=-1, keepdims=True)
        g_scores = (attention_probabilities * (g_probs - delta)).astype(jnp.bfloat16)
        g_query = jnp.einsum(
            "rts,sd->trd", g_scores, head_key, preferred_element_type=jnp.float32
        ) * HEAD_SIZE ** (-0.5)
        key_gradient = jnp.einsum(
            "rts,trd->sd", g_scores, head_query, preferred_element_type=jnp.float32
        ) * HEAD_SIZE ** (-0.5)
        value_gradient = jnp.einsum(
            "rts,trd->sd",
            attention_probabilities.astype(jnp.bfloat16),
            head_grad,
            preferred_element_type=jnp.float32,
        )
        return (g_query, key_gradient, value_gradient)

    g_query, key_gradient, value_gradient = lax.map(
        attend_back, (query_head_rows, key_head_rows, value_head_rows, lse, heads_gradient)
    )
    key_gradient_terms = key_gradient.transpose(1, 0, 2).reshape(
        packed_stream_rows, KEY_VALUE_HEADS * HEAD_SIZE
    )
    value_gradient_terms = value_gradient.transpose(1, 0, 2).reshape(
        packed_stream_rows, KEY_VALUE_HEADS * HEAD_SIZE
    )
    key_rows_gradient, g_vals = (
        lax.psum_scatter(
            key_gradient_terms.astype(jnp.bfloat16), "ctx", scatter_dimension=0, tiled=True
        ).astype(jnp.float32),
        lax.psum_scatter(
            value_gradient_terms.astype(jnp.bfloat16), "ctx", scatter_dimension=0, tiled=True
        ).astype(jnp.float32),
    )
    g_qproj = (
        rotary_embed(
            g_query.transpose(1, 0, 2, 3).reshape(local_token_count, QUERY_HEADS, HEAD_SIZE),
            local_stream_offset,
            -1.0,
        )
        .reshape(local_token_count, QUERY_HEADS * HEAD_SIZE)
        .astype(jnp.bfloat16)
    )
    g_kproj = (
        rotary_embed(
            key_rows_gradient.reshape(local_token_count, KEY_VALUE_HEADS, HEAD_SIZE),
            local_stream_offset,
            -1.0,
        )
        .reshape(local_token_count, KEY_VALUE_HEADS * HEAD_SIZE)
        .astype(jnp.bfloat16)
    )
    g_vproj = g_vals.astype(jnp.bfloat16)
    first_norm_gradient = lax.dot_general(
        g_qproj, attn_back[1], CONTRACT_COLS, preferred_element_type=jnp.float32
    )
    first_norm_gradient = first_norm_gradient + lax.dot_general(
        g_kproj, attn_back[2], CONTRACT_COLS, preferred_element_type=jnp.float32
    )
    first_norm_gradient = first_norm_gradient + lax.dot_general(
        g_vproj, attn_back[3], CONTRACT_COLS, preferred_element_type=jnp.float32
    )
    first_hat_gradient = first_norm_gradient * first_norm_scale
    g_input = residual_gradient + first_inverse_norm * (
        first_hat_gradient
        - first_normalized_input
        * jnp.mean(first_hat_gradient * first_normalized_input, axis=-1, keepdims=True)
    )
    key_value_proj_gradient = jnp.concatenate([g_kproj, g_vproj], axis=1)
    query_term = lax.dot_general(
        first_normed, g_qproj, CONTRACT_ROWS, preferred_element_type=jnp.float32
    )
    key_value_term = lax.dot_general(
        first_normed, key_value_proj_gradient, CONTRACT_ROWS, preferred_element_type=jnp.float32
    )
    output_term = lax.dot_general(attn, g_branch, CONTRACT_ROWS, preferred_element_type=jnp.float32)
    scale_gradient_terms = jnp.stack(
        [
            jnp.sum(first_norm_gradient * first_normalized_input, axis=0),
            jnp.sum(second_norm_gradient * second_normalized_input, axis=0),
        ]
    )
    query_share, key_value_share, output_share, gain_share = (
        lax.psum_scatter(query_term, ("ctx", "fsdp"), scatter_dimension=0, tiled=True),
        lax.psum_scatter(key_value_term, ("ctx", "fsdp"), scatter_dimension=0, tiled=True),
        lax.psum_scatter(output_term, ("ctx", "fsdp"), scatter_dimension=0, tiled=True),
        lax.psum_scatter(scale_gradient_terms, ("ctx", "fsdp"), scatter_dimension=1, tiled=True),
    )
    key_value_columns = KEY_VALUE_HEADS * HEAD_SIZE
    return (
        loss,
        outf.astype(jnp.bfloat16)[None],
        g_input.astype(jnp.bfloat16)[None],
        gain_share[0],
        query_share,
        key_value_share[:, :key_value_columns],
        key_value_share[:, key_value_columns:],
        output_share,
        gain_share[1],
        mlp_share[:, :FF],
        mlp_share[:, FF:],
        down_share,
    )


MESH = pl.DeviceIdType.MESH
F32 = jnp.float32
BF16 = jnp.bfloat16
NZ = 4


def place_on_plane():
    c = lax.axis_index("ctx")
    z = lax.axis_index("fsdp")
    sib = c + 1 - 2 * lax.rem(c, 2)
    xn = c + 2 - 4 * lax.rem(c // 2, 2)
    yn = c + 4 - 8 * (c // 4)
    diag = xn + yn - c
    return c, z, sib, xn, yn, diag


def meet(devices):
    barrier = pltpu.get_barrier_semaphore()
    for d in devices:
        pl.semaphore_signal(barrier, inc=1, device_id=d, device_id_type=MESH)
    pl.semaphore_wait(barrier, len(devices))


def remote(src, dst, send, recv, device):
    return pltpu.make_async_remote_copy(
        src_ref=src, dst_ref=dst, send_sem=send, recv_sem=recv, device_id=device, device_id_type=MESH
    )


class Plane:
    def __init__(self, here, slot, send, recv, half):
        self.c, self.z, self.sib, self.xn, self.yn, self.diag = here
        self.slot, self.send, self.recv, self.half = slot, send, recv, half

    def copy(self, kind, src, dst, to):
        return remote(src, dst, self.send.at[kind], self.recv.at[kind], (to, self.z))

    def first(self, src):
        mine = self.slot(self.c)
        return [self.copy(0, src, mine, self.xn), self.copy(1, src, mine, self.yn), self.copy(2, src, mine, self.sib)]

    def arrive(self):
        s = self.slot
        return [self.copy(0, s(self.xn), s(self.xn), self.xn), self.copy(1, s(self.yn), s(self.yn), self.yn)]

    def second(self):
        h = self.half
        s = self.slot
        ybot = s(self.yn).at[pl.ds(0, h)]
        xtop = s(self.xn).at[pl.ds(h, h)]
        return (
            [self.copy(4, xtop, xtop, self.yn), self.copy(5, s(self.xn), s(self.xn), self.sib)],
            [self.copy(3, ybot, ybot, self.xn), self.copy(6, s(self.yn), s(self.yn), self.sib)],
        )

    def diagonal(self):
        h = self.half
        lo, hi = self.slot(self.diag).at[pl.ds(0, h)], self.slot(self.diag).at[pl.ds(h, h)]
        return [self.copy(3, lo, lo, self.xn), self.copy(4, hi, hi, self.yn)]

    def third(self):
        d = self.slot(self.diag)
        return self.copy(7, d, d, self.sib)

    def across(self):
        s = self.slot
        return [self.copy(k, s(j), s(j), self.sib) for k, j in ((2, self.sib), (5, self.xn + self.sib - self.c), (6, self.yn + self.sib - self.c), (7, self.diag + self.sib - self.c))]


def gather_kernel(whole, x_ref, st_ref, o_ref, so_ref, local, zsend, zrecv, send, recv, ssend, srecv):
    here = place_on_plane()
    c, z, sib, xn, yn, diag = here
    rows = x_ref.shape[0]
    flat = c * NZ + z
    if whole:
        everyone = []
        for s in range(1, 32):
            other = lax.rem(flat + s, 32)
            everyone.append((other // NZ, lax.rem(other, NZ)))
        meet(everyone)
    else:
        meet([(sib, z), (xn, z), (yn, z)])

    def lane(zz, row):
        slot = (lambda j: o_ref.at[zz, j]) if whole else (lambda j: o_ref.at[j])
        return Plane(here, slot, send.at[row], recv.at[row], rows // 2)

    mine = o_ref.at[z, c] if whole else o_ref.at[c]
    keep = pltpu.make_async_copy(x_ref, mine, local.at[0])
    keep.start()
    own = lane(z, 0)

    def up(s, src, zz):
        return remote(src, o_ref.at[zz, c], zsend.at[0, s], zrecv.at[0, s], (c, z + 1))

    def down(s, src, zz):
        return remote(src, o_ref.at[zz, c], zsend.at[1, s], zrecv.at[1, s], (c, z - 1))

    if whole:
        @pl.when(z < NZ - 1)
        def _():
            up(0, x_ref, z).start()

        @pl.when(z > 0)
        def _():
            down(0, x_ref, z).start()
    for cp in own.first(x_ref):
        cp.start()
    if whole:
        keep_s = pltpu.make_async_copy(st_ref, so_ref.at[flat], local.at[1])
        keep_s.start()
        stat = [remote(st_ref, so_ref.at[flat], ssend.at[s], srecv.at[s], d) for s, d in enumerate(everyone)]
        for cp in stat:
            cp.start()

    def spread(p, src):
        for cp in p.first(src):
            cp.start()

    def onward(p):
        ax, ay = p.arrive()
        sx, sy = p.second()
        ax.wait_recv()
        for cp in sx:
            cp.start()
        ay.wait_recv()
        for cp in sy:
            cp.start()

    def finish(p, src):
        for cp in p.diagonal():
            cp.wait_recv()
        p.third().start()
        for cp in p.across():
            cp.wait_recv()
        for cp in p.first(src) + p.second()[0] + p.second()[1] + [p.third()]:
            cp.wait_send()

    steps = [(1, False), (1, True), (2, False), (2, True), (3, False), (3, True)] if whole else []
    conds = {}
    for s, above in steps:
        zz = z + s if above else z - s
        conds[(s, above)] = (zz < NZ) if above else (zz >= 0)

    for s in range(1, NZ if whole else 1):
        for above in (False, True):
            zz = z + s if above else z - s

            @pl.when(conds[(s, above)])
            def _(zz=zz, s=s, above=above):
                blk = o_ref.at[zz, c]
                if above:
                    down(s - 1, blk, zz).wait_recv()

                    @pl.when(z > 0)
                    def _():
                        down(s, blk, zz).start()
                else:
                    up(s - 1, blk, zz).wait_recv()

                    @pl.when(z < NZ - 1)
                    def _():
                        up(s, blk, zz).start()
                spread(lane(zz, s + (3 if above else 0)), blk)
        if s == 1:
            onward(own)
        else:
            for above in (False, True):
                zz = z + s - 1 if above else z - s + 1

                @pl.when(conds[(s - 1, above)])
                def _(zz=zz, s=s, above=above):
                    onward(lane(zz, s - 1 + (3 if above else 0)))
    if not whole:
        onward(own)
    else:
        for above in (False, True):
            zz = z + 3 if above else z - 3

            @pl.when(conds[(3, above)])
            def _(zz=zz, above=above):
                onward(lane(zz, 3 + (3 if above else 0)))
    finish(own, x_ref)
    for s, above in steps:
        zz = z + s if above else z - s

        @pl.when(conds[(s, above)])
        def _(zz=zz, s=s, above=above):
            finish(lane(zz, s + (3 if above else 0)), o_ref.at[zz, c])
            if above:
                @pl.when(z > 0)
                def _():
                    down(s, o_ref.at[zz, c], zz).wait_send()
            else:
                @pl.when(z < NZ - 1)
                def _():
                    up(s, o_ref.at[zz, c], zz).wait_send()
    keep.wait()
    if whole:
        @pl.when(z < NZ - 1)
        def _():
            up(0, x_ref, z).wait_send()

        @pl.when(z > 0)
        def _():
            down(0, x_ref, z).wait_send()
        keep_s.wait()
        for cp in stat:
            cp.wait()


def gather(x, stats, whole, cid):
    rows, width = x.shape
    shape = ((NZ,) if whole else ()) + (8, rows, width)
    any_ = pl.BlockSpec(memory_space=pl.ANY)
    dma = pltpu.SemaphoreType.DMA
    return pl.pallas_call(
        functools.partial(gather_kernel, whole),
        out_shape=(jax.ShapeDtypeStruct(shape, x.dtype), jax.ShapeDtypeStruct((32, 8, 128), F32)),
        in_specs=[any_, any_],
        out_specs=(any_, any_),
        scratch_shapes=[dma((2,)), dma((2, 4)), dma((2, 4)), dma((7, 8)), dma((7, 8)), dma((31,)), dma((31,))],
        compiler_params=pltpu.CompilerParams(collective_id=cid, has_side_effects=True),
        name="gather_all" if whole else "gather_plane",
    )(x, stats)


def add_rows(dst, parts, chunk=16):
    n = dst.shape[0] // chunk

    def body(i, _):
        at = pl.ds(pl.multiple_of(i * chunk, chunk), chunk)
        total = parts[0][at, :].astype(F32)
        for p in parts[1:]:
            total = total + p[at, :].astype(F32)
        dst[at, :] = total.astype(dst.dtype)
        return 0

    lax.fori_loop(0, n, body, 0)


def scatter_kernel(whole, p_ref, o_ref, acc, sibr, xh, yh, xf, yf, zr, own32, lsem, bsend, brecv, hsend, hrecv, fsend, frecv, zsend, zrecv):
    here = place_on_plane()
    c, z, sib, xn, yn, diag = here
    k = lax.rem(c, 2)
    rows = o_ref.shape[0]
    h = rows // 2
    steps = NZ if whole else 1
    order = (2, 1, 3, 0) if whole else (0,)
    planes = [lax.rem(z + s, NZ) for s in order]
    heads = [diag, xn, yn, c]

    def part(i, j):
        return p_ref.at[planes[i], j] if whole else p_ref.at[j]

    devices = [(sib, z), (xn, z), (yn, z)]
    if whole:
        devices += [(c, lax.rem(z + s, NZ)) for s in (1, 2, 3)]
    meet(devices)

    def local(i, b):
        return pltpu.make_async_copy(part(i, heads[b]), acc.at[i, b], lsem.at[i, b])

    def cross(i, b):
        other = heads[b] + sib - c
        return remote(part(i, other), sibr.at[i, b], bsend.at[i, b], brecv.at[i, b], (sib, z))

    def half_x(i):
        return remote(acc.at[i, 0, pl.ds(0, h)], xh.at[i], hsend.at[i, 0], hrecv.at[i, 0], (xn, z))

    def half_y(i):
        return remote(acc.at[i, 0, pl.ds(h, h)], yh.at[i], hsend.at[i, 1], hrecv.at[i, 1], (yn, z))

    def full_x(i):
        return remote(acc.at[i, 1], xf.at[i], fsend.at[i, 0], frecv.at[i, 0], (xn, z))

    def full_y(i):
        return remote(acc.at[i, 2], yf.at[i], fsend.at[i, 1], frecv.at[i, 1], (yn, z))

    def to_plane(i):
        return remote(acc.at[i, 3], zr.at[i], zsend.at[i], zrecv.at[i], (c, planes[i]))

    for b in range(4):
        for i in range(steps):
            cross(i, b).start()
            local(i, b).start()
    for i in range(steps):
        local(i, 0).wait()
        cross(i, 0).wait_recv()
        add_rows(acc.at[i, 0], [acc.at[i, 0], sibr.at[i, 0]])
        half_x(i).start()
        half_y(i).start()

    def close(i):
        local(i, 3).wait()
        cross(i, 3).wait_recv()
        full_x(i).wait_recv()
        full_y(i).wait_recv()
        parts = [acc.at[i, 3], sibr.at[i, 3], xf.at[i], yf.at[i]]
        if whole and order[i] == 0:
            for j in range(steps - 1):
                to_plane(j).wait_recv()
            add_rows(o_ref, parts + [zr.at[j] for j in range(steps - 1)])
        elif whole:
            add_rows(acc.at[i, 3], parts)
            to_plane(i).start()
        else:
            add_rows(o_ref, parts)

    for i in range(steps):
        local(i, 1).wait()
        cross(i, 1).wait_recv()
        local(i, 2).wait()
        cross(i, 2).wait_recv()
        half_y(i).wait_recv()
        add_rows(acc.at[i, 1, pl.ds(0, h)], [acc.at[i, 1, pl.ds(0, h)], sibr.at[i, 1, pl.ds(0, h)]])
        add_rows(acc.at[i, 1, pl.ds(h, h)], [acc.at[i, 1, pl.ds(h, h)], sibr.at[i, 1, pl.ds(h, h)], yh.at[i]])
        full_x(i).start()
        half_x(i).wait_recv()
        add_rows(acc.at[i, 2, pl.ds(0, h)], [acc.at[i, 2, pl.ds(0, h)], sibr.at[i, 2, pl.ds(0, h)], xh.at[i]])
        add_rows(acc.at[i, 2, pl.ds(h, h)], [acc.at[i, 2, pl.ds(h, h)], sibr.at[i, 2, pl.ds(h, h)]])
        full_y(i).start()
        if i > 0:
            close(i - 1)
    close(steps - 1)
    for i in range(steps):
        for b in range(4):
            cross(i, b).wait_send()
        for cp in (half_x(i), half_y(i), full_x(i), full_y(i)):
            cp.wait_send()
        if whole and order[i] != 0:
            to_plane(i).wait_send()


def scatter(p, whole, cid):
    rows, width = p.shape[-2:]
    n = NZ if whole else 1
    dma = pltpu.SemaphoreType.DMA
    v = pltpu.VMEM
    return pl.pallas_call(
        functools.partial(scatter_kernel, whole),
        out_shape=jax.ShapeDtypeStruct((rows, width), F32),
        in_specs=[pl.BlockSpec(memory_space=pl.ANY)],
        out_specs=pl.BlockSpec(memory_space=pltpu.VMEM),
        scratch_shapes=[
            v((n, 4, rows, width), BF16), v((n, 4, rows, width), BF16),
            v((n, rows // 2, width), BF16), v((n, rows // 2, width), BF16),
            v((n, rows, width), BF16), v((n, rows, width), BF16), v((3, rows, width), BF16), v((8, 128), F32),
            dma((n, 4)), dma((n, 4)), dma((n, 4)), dma((n, 2)), dma((n, 2)), dma((n, 2)), dma((n, 2)), dma((4,)), dma((4,)),
        ],
        compiler_params=pltpu.CompilerParams(collective_id=cid, has_side_effects=True, vmem_limit_bytes=56 << 20),
        name="scatter_all" if whole else "scatter_plane",
    )(p)


def open_kernel(x_ref, g_ref, wq_ref, wk_ref, wv_ref, o_ref, w_ref, go_ref, normed, local, wsend, wrecv, gsend, grecv, send, recv):
    here = place_on_plane()
    c, z, sib, xn, yn, diag = here
    rows, width = x_ref.shape
    others = [lax.rem(z + s, NZ) for s in (1, 2, 3)]
    meet([(sib, z), (xn, z), (yn, z)] + [(c, t) for t in others])
    go_ref[z] = g_ref[...]
    gains = [remote(g_ref, go_ref.at[z], gsend.at[s], grecv.at[s], (c, t)) for s, t in enumerate(others)]
    for cp in gains:
        cp.start()

    def columns(i):
        ref, lo, n = ((wq_ref, 0, 256), (wk_ref, 256, 128), (wv_ref, 384, 128))[i]
        src = ref.at[:, pl.ds(pl.multiple_of(c * n, n), n)]
        return src, w_ref.at[z, :, pl.ds(lo, n)]

    keeps, weights = [], []
    for i in range(3):
        src, dst = columns(i)
        keeps.append(pltpu.make_async_copy(src, dst, local.at[i]))
        for s, t in enumerate(others):
            weights.append(remote(src, dst, wsend.at[s, i], wrecv.at[s, i], (c, t)))
    for cp in weights + keeps:
        cp.start()
    x = x_ref[...].astype(F32)
    scaled = x * lax.rsqrt(jnp.mean(x * x, axis=-1, keepdims=True) + EPS)
    for cp in gains:
        cp.wait()
    piece = width // NZ
    for zz in range(NZ):
        normed[:, zz * piece : (zz + 1) * piece] = (
            scaled[:, zz * piece : (zz + 1) * piece] * go_ref[zz, 0:1, :]
        ).astype(BF16)
    plane = Plane(here, lambda j: o_ref.at[j], send, recv, rows // 2)
    for cp in plane.first(normed):
        cp.start()
    keep = pltpu.make_async_copy(normed, o_ref.at[c], local.at[3])
    keep.start()
    plane_rest(plane, normed)
    for cp in weights:
        cp.wait()
    for cp in keeps + [keep]:
        cp.wait()


def plane_rest(plane, src):
    for arrived, sends in zip(plane.arrive(), plane.second()):
        arrived.wait_recv()
        for cp in sends:
            cp.start()
    for cp in plane.diagonal():
        cp.wait_recv()
    plane.third().start()
    for cp in plane.across():
        cp.wait_recv()
    for cp in plane.first(src) + plane.second()[0] + plane.second()[1] + [plane.third()]:
        cp.wait_send()


def open_layer(x, gains, w_query, w_key, value_weight):
    rows, width = x.shape
    any_ = pl.BlockSpec(memory_space=pl.ANY)
    vmem = pl.BlockSpec(memory_space=pltpu.VMEM)
    dma = pltpu.SemaphoreType.DMA
    depth = w_query.shape[0]
    return pl.pallas_call(
        open_kernel,
        out_shape=(
            jax.ShapeDtypeStruct((8, rows, width), BF16),
            jax.ShapeDtypeStruct((NZ, depth, 512), BF16),
            jax.ShapeDtypeStruct((NZ,) + gains.shape, F32),
        ),
        in_specs=[vmem, vmem, any_, any_, any_],
        out_specs=(any_, any_, vmem),
        scratch_shapes=[
            pltpu.VMEM((rows, width), BF16), dma((4,)), dma((3, 3)), dma((3, 3)), dma((3,)), dma((3,)), dma((8,)), dma((8,)),
        ],
        compiler_params=pltpu.CompilerParams(collective_id=4, has_side_effects=True, vmem_limit_bytes=32 << 20),
        name="open_layer",
    )(x, gains, w_query, w_key, value_weight)


def after(value, *others):
    return lax.optimization_barrier((value,) + others)[0]


def tile_of(value):
    return jnp.full((8, 128), value, F32)


def heads_and_columns(
    hidden_in,
    cotangent,
    teacher,
    valid_mask,
    doc_starts,
    attn_gain,
    w_query,
    w_key,
    value_weight,
    w_output,
    mlp_gain,
    w_gate,
    w_up,
    w_down,
):
    rows, width = hidden_in.shape[1:]
    c = lax.axis_index("ctx")
    z = lax.axis_index("fsdp")
    devices = lax.axis_size("ctx")
    tokens = rows * devices
    group = QUERY_HEADS // KEY_VALUE_HEADS
    qcols = group * HEAD_SIZE
    ffcols = FF // (devices * NZ)
    scale = HEAD_SIZE ** (-0.5)

    layer_input = hidden_in[0].astype(F32)
    gains = jnp.concatenate(
        [attn_gain.astype(F32)[None], mlp_gain.astype(F32)[None], jnp.zeros((6, attn_gain.shape[0]), F32)]
    )
    normed_all, w_qkv, gains_all = open_layer(hidden_in[0], gains, w_query, w_key, value_weight)
    attn_scale = gains_all[:, 0, :].reshape(1, width)
    mlp_scale = gains_all[:, 1, :].reshape(1, width)
    normed_all = normed_all.reshape(tokens, width)
    w_qkv = w_qkv.reshape(width, 2 * qcols)

    out_cols = lax.dynamic_slice_in_dim(w_output, c * qcols, qcols, axis=1)
    out_cols = lax.all_gather(after(out_cols, w_qkv), "fsdp", axis=0, tiled=True)
    out_rows = lax.all_to_all(out_cols.reshape(devices, qcols, qcols), "ctx", 0, 0, tiled=True)
    out_rows = out_rows.transpose(1, 0, 2).reshape(qcols, width)
    depth = w_gate.shape[0]

    def for_planes(w):
        return lax.dynamic_slice_in_dim(w.reshape(depth, NZ, devices, ffcols), c, 1, axis=2)[:, :, 0, :]

    mlp_cols = jnp.concatenate([for_planes(w_gate), for_planes(w_up)], axis=-1).transpose(1, 0, 2)
    w_mlp = lax.all_to_all(after(mlp_cols, w_qkv), "fsdp", 0, 0, tiled=True).reshape(width, 2 * ffcols)
    down_rows = lax.dynamic_slice_in_dim(w_down, c * ffcols, ffcols, axis=0)

    place, segment, offset = stream_places(tokens, rows, devices, doc_starts[0])
    allowed = (segment[:, None] == segment[None, :]) & (place[None, :] <= place[:, None])
    qkv = jnp.dot(normed_all, w_qkv, preferred_element_type=F32)
    q = rotary_embed(qkv[:, :qcols].reshape(tokens, group, HEAD_SIZE), offset, 1.0).astype(BF16)
    k = rotary_embed(qkv[:, qcols : qcols + HEAD_SIZE].reshape(tokens, 1, HEAD_SIZE), offset, 1.0)[:, 0].astype(BF16)
    v = qkv[:, qcols + HEAD_SIZE :].astype(BF16)
    scores = head_scores(q, k, allowed)
    top = jnp.max(scores, axis=-1, keepdims=True)
    lse = top + jnp.log(jnp.sum(jnp.exp(scores - top), axis=-1, keepdims=True))
    probs = jnp.exp(scores - lse)
    probs_low = probs.astype(BF16)
    attn = jnp.einsum("rts,sd->trd", probs_low, v, preferred_element_type=F32).reshape(tokens, qcols).astype(BF16)
    branch = jnp.dot(attn, out_rows, preferred_element_type=F32).astype(BF16)
    residual = layer_input + scatter(branch.reshape(devices, rows, width), False, 3)

    r2 = rms_norm_scale(residual)
    hat2 = residual * r2
    normed2 = (hat2 * mlp_scale).astype(BF16)
    maskf = valid_mask[0].astype(F32)
    normed2_all, counts = gather(normed2, tile_of(jnp.sum(maskf)), True, 0)
    count = jnp.sum(counts[:, 0, 0])
    every = NZ * tokens
    normed2_all = normed2_all.reshape(every, width)
    gate_up = jnp.dot(normed2_all, w_mlp, preferred_element_type=F32)
    gate, up = gate_up[:, :ffcols], gate_up[:, ffcols:]
    sigma = jax.nn.sigmoid(gate)
    act = (gate * sigma * up).astype(BF16)
    down = jnp.dot(act, down_rows, preferred_element_type=F32).astype(BF16)
    outf = residual + scatter(down.reshape(NZ, devices, rows, width), True, 2)

    diff = outf - teacher[0].astype(F32)
    error_here = jnp.sum(maskf * jnp.mean(diff * diff, axis=-1))
    g_out = cotangent[0].astype(F32) + maskf[:, None] * diff * (2.0 / (count * width))
    g_mo_all, errors = gather(g_out.astype(BF16), tile_of(error_here), True, 0)
    loss = jnp.sum(errors[:, 0, 0]) / count
    g_mo_all = g_mo_all.reshape(every, width)
    g_act = lax.dot_general(g_mo_all, down_rows, CONTRACT_COLS, preferred_element_type=F32)
    g_gate = (g_act * up * sigma * (1.0 + gate * (1.0 - sigma))).astype(BF16)
    g_up = (g_act * gate * sigma).astype(BF16)
    g_gate_up = jnp.concatenate([g_gate, g_up], axis=1)
    g_norm2 = lax.dot_general(g_gate_up, w_mlp, CONTRACT_COLS, preferred_element_type=F32).astype(BF16)
    g_norm2 = scatter(g_norm2.reshape(NZ, devices, rows, width), True, 2)
    mlp_grads = lax.dot_general(normed2_all, g_gate_up, CONTRACT_ROWS, preferred_element_type=F32).astype(BF16)
    down_grads = lax.dot_general(act, g_mo_all, CONTRACT_ROWS, preferred_element_type=F32).astype(BF16)

    g_hat2 = g_norm2 * mlp_scale
    g_residual = g_out + r2 * (g_hat2 - hat2 * jnp.mean(g_hat2 * hat2, axis=-1, keepdims=True))
    g_branch_all, _ = gather(g_residual.astype(BF16), tile_of(0.0), False, 1)
    g_branch_all = g_branch_all.reshape(tokens, width)
    g_attn = lax.dot_general(g_branch_all, out_rows, CONTRACT_COLS, preferred_element_type=F32).astype(BF16)
    out_grads = lax.dot_general(attn, g_branch_all, CONTRACT_ROWS, preferred_element_type=F32).astype(BF16)
    g_heads = g_attn.reshape(tokens, group, HEAD_SIZE)
    g_probs = jnp.einsum("trd,sd->rts", g_heads, v, preferred_element_type=F32)
    delta = jnp.sum(probs * g_probs, axis=-1, keepdims=True)
    g_scores = (probs * (g_probs - delta)).astype(BF16)
    g_q = jnp.einsum("rts,sd->trd", g_scores, k, preferred_element_type=F32) * scale
    g_k = jnp.einsum("rts,trd->sd", g_scores, q, preferred_element_type=F32) * scale
    g_v = jnp.einsum("rts,trd->sd", probs_low, g_heads, preferred_element_type=F32)
    g_q = rotary_embed(g_q, offset, -1.0).reshape(tokens, qcols)
    g_k = rotary_embed(g_k[:, None], offset, -1.0)[:, 0]
    g_qkv = jnp.concatenate([g_q, g_k, g_v], axis=1).astype(BF16)
    g_norm1 = lax.dot_general(g_qkv, w_qkv, CONTRACT_COLS, preferred_element_type=F32).astype(BF16)
    g_norm1 = scatter(g_norm1.reshape(devices, rows, width), False, 3)
    qkv_grads = lax.dot_general(normed_all, g_qkv, CONTRACT_ROWS, preferred_element_type=F32).astype(BF16)

    r1 = rms_norm_scale(layer_input)
    hat1 = layer_input * r1
    g_hat1 = g_norm1 * attn_scale
    g_input = g_residual + r1 * (g_hat1 - hat1 * jnp.mean(g_hat1 * hat1, axis=-1, keepdims=True))

    both = ("ctx", "fsdp")
    parts = devices * NZ

    def exchange(value, axes, n):
        value = value.reshape(n, value.shape[0] // n, value.shape[1])
        return lax.all_to_all(value, axes, 0, 0, tiled=True)

    share = width // parts
    got = exchange(mlp_grads, both, parts).astype(F32).reshape(devices, NZ, share, 2, ffcols)
    got = got.transpose(3, 2, 1, 0, 4).reshape(2, share, FF)
    got_qkv = jnp.sum(exchange(qkv_grads, both, parts).astype(F32).reshape(devices, NZ, share, 2 * qcols), axis=1)
    got_qkv = got_qkv.transpose(1, 0, 2)
    got_out = jnp.sum(exchange(out_grads, "fsdp", NZ).astype(F32), axis=0)
    owner = [(j % devices * NZ + j // devices, j) for j in range(parts)]
    got_down = lax.ppermute(down_grads, both, owner).astype(F32)
    gain_terms = jnp.stack([jnp.sum(g_norm1 * hat1, axis=0), jnp.sum(g_norm2 * hat2, axis=0)])
    gain_terms = gain_terms.reshape(2, parts, share).transpose(1, 0, 2).reshape(parts, 1, 2 * share)
    got_gains = jnp.sum(lax.all_to_all(gain_terms, both, 0, 0, tiled=True), axis=(0, 1))
    return (
        loss,
        outf.astype(BF16)[None],
        g_input.astype(BF16)[None],
        got_gains[:share],
        got_qkv[:, :, :qcols].reshape(share, QUERY_HEADS * HEAD_SIZE),
        got_qkv[:, :, qcols : qcols + HEAD_SIZE].reshape(share, KEY_VALUE_HEADS * HEAD_SIZE),
        got_qkv[:, :, qcols + HEAD_SIZE :].reshape(share, KEY_VALUE_HEADS * HEAD_SIZE),
        got_out,
        got_gains[share:],
        got[0],
        got[1],
        got_down,
    )


def solution(mesh):
    small = dict(mesh.shape) == {"ctx": KEY_VALUE_HEADS, "fsdp": NZ}
    in_specs = (
        P("fsdp", "ctx", None),
        P("fsdp", "ctx", None),
        P("fsdp", "ctx", None),
        P("fsdp", "ctx"),
        P("fsdp", None),
        P("fsdp"),
        P("fsdp", None),
        P("fsdp", None),
        P("fsdp", None),
        P("fsdp", None),
        P("fsdp"),
        P("fsdp", None),
        P("fsdp", None),
        P("fsdp", None),
    )
    out_specs = (
        P(),
        P("fsdp", "ctx", None),
        P("fsdp", "ctx", None),
        P(("ctx", "fsdp")),
        P(("ctx", "fsdp"), None),
        P(("ctx", "fsdp"), None),
        P(("ctx", "fsdp"), None),
        P(("ctx", "fsdp"), None),
        P(("ctx", "fsdp")),
        P(("ctx", "fsdp"), None),
        P(("ctx", "fsdp"), None),
        P(("ctx", "fsdp"), None),
    )
    return jax.shard_map(
        heads_and_columns if small else per_device, mesh=mesh, in_specs=in_specs, out_specs=out_specs, check_vma=False
    )
```

```python
import functools

import jax
import jax.numpy as jnp
from jax import lax
from jax.experimental import pallas as pl
from jax.experimental.pallas import tpu as pltpu
from jax.sharding import PartitionSpec as P

QUERY_HEADS = 16
KEY_VALUE_HEADS = 8
HEAD_SIZE = 128
FF = 8192


EPS = 1e-05
ROPE_BASE = 1000000.0
NEG = -1e30
CONTRACT_ROWS = (((0,), (0,)), ((), ()))
CONTRACT_COLS = (((1,), (1,)), ((), ()))


def stream_places(rows, local_token_count, devices, starts):
    span = local_token_count // 2
    rowid = jnp.arange(rows, dtype=jnp.int32)
    device = rowid // local_token_count
    within = rowid % local_token_count
    span_id = jnp.where(within < span, device, 2 * devices - 1 - device)
    place = span_id * span + within % span
    before = starts[None, :] <= place[:, None]
    segment = jnp.sum(before.astype(jnp.int32), axis=1) - 1
    first = jnp.max(jnp.where(before, starts[None, :], 0), axis=1)
    return (place, segment, place - first)


def rotary_embed(values, token_offset, sign):
    half = HEAD_SIZE // 2
    freq = ROPE_BASE ** (-(jnp.arange(half, dtype=jnp.float32) * 2.0 / HEAD_SIZE))
    angle = token_offset.astype(jnp.float32)[:, None] * freq[None, :]
    cosine = jnp.cos(angle)[:, None, :]
    sine = sign * jnp.sin(angle)[:, None, :]
    first = values[..., :half]
    second = values[..., half:]
    return jnp.concatenate(
        [first * cosine - second * sine, second * cosine + first * sine], axis=-1
    )


def rms_norm_scale(values):
    return lax.rsqrt(jnp.mean(values * values, axis=-1, keepdims=True) + EPS)


def head_scores(query_rows, key_rows, allowed):
    attention_scores = jnp.einsum(
        "trd,sd->rts", query_rows, key_rows, preferred_element_type=jnp.float32
    ) * HEAD_SIZE ** (-0.5)
    return jnp.where(allowed[None], attention_scores, NEG)


def per_device(
    hidden_in,
    cotangent,
    teacher,
    valid_mask,
    doc_starts,
    attn_gain,
    w_query,
    w_key,
    value_weight,
    w_output,
    mlp_gain,
    w_gate,
    w_up,
    w_down,
):
    local_token_count = hidden_in.shape[1]
    width = hidden_in.shape[2]
    devices = lax.axis_size("ctx")
    index = lax.axis_index("ctx")
    packed_stream_rows = local_token_count * devices
    query_group = QUERY_HEADS // KEY_VALUE_HEADS
    place, segment, token_offset = stream_places(
        packed_stream_rows, local_token_count, devices, doc_starts[0]
    )
    own_start = index * local_token_count
    my_place = lax.dynamic_slice_in_dim(place, own_start, local_token_count)
    my_segment = lax.dynamic_slice_in_dim(segment, own_start, local_token_count)
    local_stream_offset = lax.dynamic_slice_in_dim(token_offset, own_start, local_token_count)
    allowed = (my_segment[:, None] == segment[None, :]) & (place[None, :] <= my_place[:, None])
    layer_input = hidden_in[0].astype(jnp.float32)
    attn_whole = (
        lax.all_gather(attn_gain, "fsdp", axis=0, tiled=True),
        lax.all_gather(w_query, "fsdp", axis=0, tiled=True),
        lax.all_gather(w_key, "fsdp", axis=0, tiled=True),
        lax.all_gather(value_weight, "fsdp", axis=0, tiled=True),
        lax.all_gather(w_output, "fsdp", axis=0, tiled=True),
    )
    first_norm_scale = attn_whole[0].astype(jnp.float32)
    first_inverse_norm = rms_norm_scale(layer_input)
    first_normalized_input = layer_input * first_inverse_norm
    first_normed = (first_normalized_input * first_norm_scale).astype(jnp.bfloat16)
    qproj = jnp.dot(first_normed, attn_whole[1], preferred_element_type=jnp.float32)
    key_projected = jnp.dot(first_normed, attn_whole[2], preferred_element_type=jnp.float32)
    vproj = jnp.dot(first_normed, attn_whole[3], preferred_element_type=jnp.float32).astype(
        jnp.bfloat16
    )
    query_rows = rotary_embed(
        qproj.reshape(local_token_count, QUERY_HEADS, HEAD_SIZE), local_stream_offset, 1.0
    ).astype(jnp.bfloat16)
    key_rows = (
        rotary_embed(
            key_projected.reshape(local_token_count, KEY_VALUE_HEADS, HEAD_SIZE),
            local_stream_offset,
            1.0,
        )
        .reshape(local_token_count, KEY_VALUE_HEADS * HEAD_SIZE)
        .astype(jnp.bfloat16)
    )
    every_key_row, every_value_row = (
        lax.all_gather(key_rows, "ctx", axis=0, tiled=True),
        lax.all_gather(vproj, "ctx", axis=0, tiled=True),
    )
    key_head_rows = every_key_row.reshape(packed_stream_rows, KEY_VALUE_HEADS, HEAD_SIZE).transpose(
        1, 0, 2
    )
    value_head_rows = every_value_row.reshape(
        packed_stream_rows, KEY_VALUE_HEADS, HEAD_SIZE
    ).transpose(1, 0, 2)
    query_head_rows = query_rows.reshape(
        local_token_count, KEY_VALUE_HEADS, query_group, HEAD_SIZE
    ).transpose(1, 0, 2, 3)

    def attend_head(parts):
        head_query, head_key, head_val = parts
        attention_scores = head_scores(head_query, head_key, allowed)
        top = jnp.max(attention_scores, axis=-1, keepdims=True)
        lse = top + jnp.log(jnp.sum(jnp.exp(attention_scores - top), axis=-1, keepdims=True))
        attention_probabilities = jnp.exp(attention_scores - lse)
        mixed_heads = jnp.einsum(
            "rts,sd->trd",
            attention_probabilities.astype(jnp.bfloat16),
            head_val,
            preferred_element_type=jnp.float32,
        )
        return (mixed_heads, lse)

    mixed_heads, lse = lax.map(attend_head, (query_head_rows, key_head_rows, value_head_rows))
    attn = (
        mixed_heads.transpose(1, 0, 2, 3)
        .reshape(local_token_count, QUERY_HEADS * HEAD_SIZE)
        .astype(jnp.bfloat16)
    )
    residual_state = layer_input + jnp.dot(attn, attn_whole[4], preferred_element_type=jnp.float32)
    mlp_whole = (
        lax.all_gather(mlp_gain, "fsdp", axis=0, tiled=True),
        lax.all_gather(w_gate, "fsdp", axis=0, tiled=True),
        lax.all_gather(w_up, "fsdp", axis=0, tiled=True),
        lax.all_gather(w_down, "fsdp", axis=0, tiled=True),
    )
    second_norm_scale = mlp_whole[0].astype(jnp.float32)
    second_inverse_norm = rms_norm_scale(residual_state)
    second_normalized_input = residual_state * second_inverse_norm
    second_normed = (second_normalized_input * second_norm_scale).astype(jnp.bfloat16)
    gate = jnp.dot(second_normed, mlp_whole[1], preferred_element_type=jnp.float32)
    up_val = jnp.dot(second_normed, mlp_whole[2], preferred_element_type=jnp.float32)
    sigma = jax.nn.sigmoid(gate)
    act = (gate * sigma * up_val).astype(jnp.bfloat16)
    outf = residual_state + jnp.dot(act, mlp_whole[3], preferred_element_type=jnp.float32)
    maskf = valid_mask[0].astype(jnp.float32)
    diff = outf - teacher[0].astype(jnp.float32)
    count_here = jnp.sum(maskf)
    error_here = jnp.sum(maskf * jnp.mean(diff * diff, axis=-1))
    count, error_total = lax.psum((count_here, error_here), ("ctx", "fsdp"))
    loss = error_total / count
    output_gradient = cotangent[0].astype(jnp.float32) + maskf[:, None] * diff * (
        2.0 / (count * width)
    )
    g_mo = output_gradient.astype(jnp.bfloat16)
    mlp_back = (
        lax.all_gather(mlp_gain, "fsdp", axis=0, tiled=True),
        lax.all_gather(w_gate, "fsdp", axis=0, tiled=True),
        lax.all_gather(w_up, "fsdp", axis=0, tiled=True),
        lax.all_gather(w_down, "fsdp", axis=0, tiled=True),
    )
    g_act = lax.dot_general(g_mo, mlp_back[3], CONTRACT_COLS, preferred_element_type=jnp.float32)
    g_gate = (g_act * up_val * sigma * (1.0 + gate * (1.0 - sigma))).astype(jnp.bfloat16)
    g_up = (g_act * gate * sigma).astype(jnp.bfloat16)
    gate_up_gradient = jnp.concatenate([g_gate, g_up], axis=1)
    second_norm_gradient = lax.dot_general(
        g_gate, mlp_back[1], CONTRACT_COLS, preferred_element_type=jnp.float32
    )
    second_norm_gradient = second_norm_gradient + lax.dot_general(
        g_up, mlp_back[2], CONTRACT_COLS, preferred_element_type=jnp.float32
    )
    second_hat_gradient = second_norm_gradient * second_norm_scale
    residual_gradient = output_gradient + second_inverse_norm * (
        second_hat_gradient
        - second_normalized_input
        * jnp.mean(second_hat_gradient * second_normalized_input, axis=-1, keepdims=True)
    )
    mlp_share = lax.psum_scatter(
        lax.dot_general(
            second_normed, gate_up_gradient, CONTRACT_ROWS, preferred_element_type=jnp.float32
        ),
        ("ctx", "fsdp"),
        scatter_dimension=0,
        tiled=True,
    )
    down_share = lax.psum_scatter(
        lax.dot_general(act, g_mo, CONTRACT_ROWS, preferred_element_type=jnp.float32),
        ("ctx", "fsdp"),
        scatter_dimension=0,
        tiled=True,
    )
    g_branch = residual_gradient.astype(jnp.bfloat16)
    attn_back = (
        lax.all_gather(attn_gain, "fsdp", axis=0, tiled=True),
        lax.all_gather(w_query, "fsdp", axis=0, tiled=True),
        lax.all_gather(w_key, "fsdp", axis=0, tiled=True),
        lax.all_gather(value_weight, "fsdp", axis=0, tiled=True),
        lax.all_gather(w_output, "fsdp", axis=0, tiled=True),
    )
    attention_gradient = lax.dot_general(
        g_branch, attn_back[4], CONTRACT_COLS, preferred_element_type=jnp.float32
    ).astype(jnp.bfloat16)
    heads_gradient = attention_gradient.reshape(
        local_token_count, KEY_VALUE_HEADS, query_group, HEAD_SIZE
    ).transpose(1, 0, 2, 3)

    def attend_back(parts):
        head_query, head_key, head_val, head_lse, head_grad = parts
        attention_probabilities = jnp.exp(head_scores(head_query, head_key, allowed) - head_lse)
        g_probs = jnp.einsum("trd,sd->rts", head_grad, head_val, preferred_element_type=jnp.float32)
        delta = jnp.sum(attention_probabilities * g_probs, axis=-1, keepdims=True)
        g_scores = (attention_probabilities * (g_probs - delta)).astype(jnp.bfloat16)
        g_query = jnp.einsum(
            "rts,sd->trd", g_scores, head_key, preferred_element_type=jnp.float32
        ) * HEAD_SIZE ** (-0.5)
        key_gradient = jnp.einsum(
            "rts,trd->sd", g_scores, head_query, preferred_element_type=jnp.float32
        ) * HEAD_SIZE ** (-0.5)
        value_gradient = jnp.einsum(
            "rts,trd->sd",
            attention_probabilities.astype(jnp.bfloat16),
            head_grad,
            preferred_element_type=jnp.float32,
        )
        return (g_query, key_gradient, value_gradient)

    g_query, key_gradient, value_gradient = lax.map(
        attend_back, (query_head_rows, key_head_rows, value_head_rows, lse, heads_gradient)
    )
    key_gradient_terms = key_gradient.transpose(1, 0, 2).reshape(
        packed_stream_rows, KEY_VALUE_HEADS * HEAD_SIZE
    )
    value_gradient_terms = value_gradient.transpose(1, 0, 2).reshape(
        packed_stream_rows, KEY_VALUE_HEADS * HEAD_SIZE
    )
    key_rows_gradient, g_vals = (
        lax.psum_scatter(
            key_gradient_terms.astype(jnp.bfloat16), "ctx", scatter_dimension=0, tiled=True
        ).astype(jnp.float32),
        lax.psum_scatter(
            value_gradient_terms.astype(jnp.bfloat16), "ctx", scatter_dimension=0, tiled=True
        ).astype(jnp.float32),
    )
    g_qproj = (
        rotary_embed(
            g_query.transpose(1, 0, 2, 3).reshape(local_token_count, QUERY_HEADS, HEAD_SIZE),
            local_stream_offset,
            -1.0,
        )
        .reshape(local_token_count, QUERY_HEADS * HEAD_SIZE)
        .astype(jnp.bfloat16)
    )
    g_kproj = (
        rotary_embed(
            key_rows_gradient.reshape(local_token_count, KEY_VALUE_HEADS, HEAD_SIZE),
            local_stream_offset,
            -1.0,
        )
        .reshape(local_token_count, KEY_VALUE_HEADS * HEAD_SIZE)
        .astype(jnp.bfloat16)
    )
    g_vproj = g_vals.astype(jnp.bfloat16)
    first_norm_gradient = lax.dot_general(
        g_qproj, attn_back[1], CONTRACT_COLS, preferred_element_type=jnp.float32
    )
    first_norm_gradient = first_norm_gradient + lax.dot_general(
        g_kproj, attn_back[2], CONTRACT_COLS, preferred_element_type=jnp.float32
    )
    first_norm_gradient = first_norm_gradient + lax.dot_general(
        g_vproj, attn_back[3], CONTRACT_COLS, preferred_element_type=jnp.float32
    )
    first_hat_gradient = first_norm_gradient * first_norm_scale
    g_input = residual_gradient + first_inverse_norm * (
        first_hat_gradient
        - first_normalized_input
        * jnp.mean(first_hat_gradient * first_normalized_input, axis=-1, keepdims=True)
    )
    key_value_proj_gradient = jnp.concatenate([g_kproj, g_vproj], axis=1)
    query_term = lax.dot_general(
        first_normed, g_qproj, CONTRACT_ROWS, preferred_element_type=jnp.float32
    )
    key_value_term = lax.dot_general(
        first_normed, key_value_proj_gradient, CONTRACT_ROWS, preferred_element_type=jnp.float32
    )
    output_term = lax.dot_general(attn, g_branch, CONTRACT_ROWS, preferred_element_type=jnp.float32)
    scale_gradient_terms = jnp.stack(
        [
            jnp.sum(first_norm_gradient * first_normalized_input, axis=0),
            jnp.sum(second_norm_gradient * second_normalized_input, axis=0),
        ]
    )
    query_share, key_value_share, output_share, gain_share = (
        lax.psum_scatter(query_term, ("ctx", "fsdp"), scatter_dimension=0, tiled=True),
        lax.psum_scatter(key_value_term, ("ctx", "fsdp"), scatter_dimension=0, tiled=True),
        lax.psum_scatter(output_term, ("ctx", "fsdp"), scatter_dimension=0, tiled=True),
        lax.psum_scatter(scale_gradient_terms, ("ctx", "fsdp"), scatter_dimension=1, tiled=True),
    )
    key_value_columns = KEY_VALUE_HEADS * HEAD_SIZE
    return (
        loss,
        outf.astype(jnp.bfloat16)[None],
        g_input.astype(jnp.bfloat16)[None],
        gain_share[0],
        query_share,
        key_value_share[:, :key_value_columns],
        key_value_share[:, key_value_columns:],
        output_share,
        gain_share[1],
        mlp_share[:, :FF],
        mlp_share[:, FF:],
        down_share,
    )


MESH = pl.DeviceIdType.MESH
F32 = jnp.float32
BF16 = jnp.bfloat16
NZ = 4


def place_on_plane():
    c = lax.axis_index("ctx")
    z = lax.axis_index("fsdp")
    sib = c + 1 - 2 * lax.rem(c, 2)
    xn = c + 2 - 4 * lax.rem(c // 2, 2)
    yn = c + 4 - 8 * (c // 4)
    diag = xn + yn - c
    return c, z, sib, xn, yn, diag


def meet(devices):
    barrier = pltpu.get_barrier_semaphore()
    for d in devices:
        pl.semaphore_signal(barrier, inc=1, device_id=d, device_id_type=MESH)
    pl.semaphore_wait(barrier, len(devices))


def remote(src, dst, send, recv, device):
    return pltpu.make_async_remote_copy(
        src_ref=src, dst_ref=dst, send_sem=send, recv_sem=recv, device_id=device, device_id_type=MESH
    )


def takes(micros):
    return pl.CostEstimate(flops=0, bytes_accessed=micros * 3_500_000, transcendentals=0)


class Plane:
    def __init__(self, here, slot, send, recv, half):
        self.c, self.z, self.sib, self.xn, self.yn, self.diag = here
        self.slot, self.send, self.recv, self.half = slot, send, recv, half

    def copy(self, kind, src, dst, to):
        return remote(src, dst, self.send.at[kind], self.recv.at[kind], (to, self.z))

    def first(self, src):
        mine = self.slot(self.c)
        return [self.copy(0, src, mine, self.xn), self.copy(1, src, mine, self.yn), self.copy(2, src, mine, self.sib)]

    def arrive(self):
        s = self.slot
        return [self.copy(0, s(self.xn), s(self.xn), self.xn), self.copy(1, s(self.yn), s(self.yn), self.yn)]

    def second(self):
        h = self.half
        s = self.slot
        ybot = s(self.yn).at[pl.ds(0, h)]
        xtop = s(self.xn).at[pl.ds(h, h)]
        return (
            [self.copy(4, xtop, xtop, self.yn), self.copy(5, s(self.xn), s(self.xn), self.sib)],
            [self.copy(3, ybot, ybot, self.xn), self.copy(6, s(self.yn), s(self.yn), self.sib)],
        )

    def diagonal(self):
        h = self.half
        lo, hi = self.slot(self.diag).at[pl.ds(0, h)], self.slot(self.diag).at[pl.ds(h, h)]
        return [self.copy(3, lo, lo, self.xn), self.copy(4, hi, hi, self.yn)]

    def third(self):
        d = self.slot(self.diag)
        return self.copy(7, d, d, self.sib)

    def across(self):
        s = self.slot
        return [self.copy(k, s(j), s(j), self.sib) for k, j in ((2, self.sib), (5, self.xn + self.sib - self.c), (6, self.yn + self.sib - self.c), (7, self.diag + self.sib - self.c))]


def gather_kernel(whole, x_ref, st_ref, o_ref, so_ref, local, zsend, zrecv, send, recv, ssend, srecv):
    here = place_on_plane()
    c, z, sib, xn, yn, diag = here
    rows = x_ref.shape[0]
    flat = c * NZ + z
    if whole:
        everyone = []
        for s in range(1, 32):
            other = lax.rem(flat + s, 32)
            everyone.append((other // NZ, lax.rem(other, NZ)))
        meet(everyone)
    else:
        meet([(sib, z), (xn, z), (yn, z)])

    def lane(zz, row):
        slot = (lambda j: o_ref.at[zz, j]) if whole else (lambda j: o_ref.at[j])
        return Plane(here, slot, send.at[row], recv.at[row], rows // 2)

    mine = o_ref.at[z, c] if whole else o_ref.at[c]
    keep = pltpu.make_async_copy(x_ref, mine, local.at[0])
    keep.start()
    own = lane(z, 0)

    def up(s, src, zz):
        return remote(src, o_ref.at[zz, c], zsend.at[0, s], zrecv.at[0, s], (c, z + 1))

    def down(s, src, zz):
        return remote(src, o_ref.at[zz, c], zsend.at[1, s], zrecv.at[1, s], (c, z - 1))

    if whole:
        @pl.when(z < NZ - 1)
        def _():
            up(0, x_ref, z).start()

        @pl.when(z > 0)
        def _():
            down(0, x_ref, z).start()
    for cp in own.first(x_ref):
        cp.start()
    if whole:
        keep_s = pltpu.make_async_copy(st_ref, so_ref.at[flat], local.at[1])
        keep_s.start()
        stat = [remote(st_ref, so_ref.at[flat], ssend.at[s], srecv.at[s], d) for s, d in enumerate(everyone)]
        for cp in stat:
            cp.start()

    def spread(p, src):
        for cp in p.first(src):
            cp.start()

    def onward(p):
        ax, ay = p.arrive()
        sx, sy = p.second()
        ax.wait_recv()
        for cp in sx:
            cp.start()
        ay.wait_recv()
        for cp in sy:
            cp.start()

    def finish(p, src):
        for cp in p.diagonal():
            cp.wait_recv()
        p.third().start()
        for cp in p.across():
            cp.wait_recv()
        for cp in p.first(src) + p.second()[0] + p.second()[1] + [p.third()]:
            cp.wait_send()

    steps = [(1, False), (1, True), (2, False), (2, True), (3, False), (3, True)] if whole else []
    conds = {}
    for s, above in steps:
        zz = z + s if above else z - s
        conds[(s, above)] = (zz < NZ) if above else (zz >= 0)

    for s in range(1, NZ if whole else 1):
        for above in (False, True):
            zz = z + s if above else z - s

            @pl.when(conds[(s, above)])
            def _(zz=zz, s=s, above=above):
                blk = o_ref.at[zz, c]
                if above:
                    down(s - 1, blk, zz).wait_recv()

                    @pl.when(z > 0)
                    def _():
                        down(s, blk, zz).start()
                else:
                    up(s - 1, blk, zz).wait_recv()

                    @pl.when(z < NZ - 1)
                    def _():
                        up(s, blk, zz).start()
                spread(lane(zz, s + (3 if above else 0)), blk)
        if s == 1:
            onward(own)
        else:
            for above in (False, True):
                zz = z + s - 1 if above else z - s + 1

                @pl.when(conds[(s - 1, above)])
                def _(zz=zz, s=s, above=above):
                    onward(lane(zz, s - 1 + (3 if above else 0)))
    if not whole:
        onward(own)
    else:
        for above in (False, True):
            zz = z + 3 if above else z - 3

            @pl.when(conds[(3, above)])
            def _(zz=zz, above=above):
                onward(lane(zz, 3 + (3 if above else 0)))
    finish(own, x_ref)
    for s, above in steps:
        zz = z + s if above else z - s

        @pl.when(conds[(s, above)])
        def _(zz=zz, s=s, above=above):
            finish(lane(zz, s + (3 if above else 0)), o_ref.at[zz, c])
            if above:
                @pl.when(z > 0)
                def _():
                    down(s, o_ref.at[zz, c], zz).wait_send()
            else:
                @pl.when(z < NZ - 1)
                def _():
                    up(s, o_ref.at[zz, c], zz).wait_send()
    keep.wait()
    if whole:
        @pl.when(z < NZ - 1)
        def _():
            up(0, x_ref, z).wait_send()

        @pl.when(z > 0)
        def _():
            down(0, x_ref, z).wait_send()
        keep_s.wait()
        for cp in stat:
            cp.wait()


def gather(x, stats, whole, cid):
    rows, width = x.shape
    shape = ((NZ,) if whole else ()) + (8, rows, width)
    any_ = pl.BlockSpec(memory_space=pl.ANY)
    dma = pltpu.SemaphoreType.DMA
    return pl.pallas_call(
        functools.partial(gather_kernel, whole),
        out_shape=(jax.ShapeDtypeStruct(shape, x.dtype), jax.ShapeDtypeStruct((32, 8, 128), F32)),
        in_specs=[any_, any_],
        out_specs=(any_, any_),
        scratch_shapes=[dma((2,)), dma((2, 4)), dma((2, 4)), dma((7, 8)), dma((7, 8)), dma((31,)), dma((31,))],
        compiler_params=pltpu.CompilerParams(collective_id=cid, has_side_effects=True),
        cost_estimate=takes(80 if whole else 25),
        name="gather_all" if whole else "gather_plane",
    )(x, stats)


def add_rows(dst, parts, chunk=16):
    n = dst.shape[0] // chunk

    def body(i, _):
        at = pl.ds(pl.multiple_of(i * chunk, chunk), chunk)
        total = parts[0][at, :].astype(F32)
        for p in parts[1:]:
            total = total + p[at, :].astype(F32)
        dst[at, :] = total.astype(dst.dtype)
        return 0

    lax.fori_loop(0, n, body, 0)


def scatter_kernel(whole, p_ref, o_ref, acc, sibr, xh, yh, xf, yf, zr, own32, lsem, bsend, brecv, hsend, hrecv, fsend, frecv, zsend, zrecv):
    here = place_on_plane()
    c, z, sib, xn, yn, diag = here
    k = lax.rem(c, 2)
    rows = o_ref.shape[0]
    h = rows // 2
    steps = NZ if whole else 1
    order = (2, 1, 3, 0) if whole else (0,)
    planes = [lax.rem(z + s, NZ) for s in order]
    heads = [diag, xn, yn, c]

    def part(i, j):
        return p_ref.at[planes[i], j] if whole else p_ref.at[j]

    devices = [(sib, z), (xn, z), (yn, z)]
    if whole:
        devices += [(c, lax.rem(z + s, NZ)) for s in (1, 2, 3)]
    meet(devices)

    def local(i, b):
        return pltpu.make_async_copy(part(i, heads[b]), acc.at[i, b], lsem.at[i, b])

    def cross(i, b):
        other = heads[b] + sib - c
        return remote(part(i, other), sibr.at[i, b], bsend.at[i, b], brecv.at[i, b], (sib, z))

    def half_x(i):
        return remote(acc.at[i, 0, pl.ds(0, h)], xh.at[i], hsend.at[i, 0], hrecv.at[i, 0], (xn, z))

    def half_y(i):
        return remote(acc.at[i, 0, pl.ds(h, h)], yh.at[i], hsend.at[i, 1], hrecv.at[i, 1], (yn, z))

    def full_x(i):
        return remote(acc.at[i, 1], xf.at[i], fsend.at[i, 0], frecv.at[i, 0], (xn, z))

    def full_y(i):
        return remote(acc.at[i, 2], yf.at[i], fsend.at[i, 1], frecv.at[i, 1], (yn, z))

    def to_plane(i):
        return remote(acc.at[i, 3], zr.at[i], zsend.at[i], zrecv.at[i], (c, planes[i]))

    for b in range(4):
        for i in range(steps):
            cross(i, b).start()
            local(i, b).start()
    for i in range(steps):
        local(i, 0).wait()
        cross(i, 0).wait_recv()
        add_rows(acc.at[i, 0], [acc.at[i, 0], sibr.at[i, 0]])
        half_x(i).start()
        half_y(i).start()

    def close(i):
        local(i, 3).wait()
        cross(i, 3).wait_recv()
        full_x(i).wait_recv()
        full_y(i).wait_recv()
        parts = [acc.at[i, 3], sibr.at[i, 3], xf.at[i], yf.at[i]]
        if whole and order[i] == 0:
            for j in range(steps - 1):
                to_plane(j).wait_recv()
            add_rows(o_ref, parts + [zr.at[j] for j in range(steps - 1)])
        elif whole:
            add_rows(acc.at[i, 3], parts)
            to_plane(i).start()
        else:
            add_rows(o_ref, parts)

    for i in range(steps):
        local(i, 1).wait()
        cross(i, 1).wait_recv()
        local(i, 2).wait()
        cross(i, 2).wait_recv()
        half_y(i).wait_recv()
        add_rows(acc.at[i, 1, pl.ds(0, h)], [acc.at[i, 1, pl.ds(0, h)], sibr.at[i, 1, pl.ds(0, h)]])
        add_rows(acc.at[i, 1, pl.ds(h, h)], [acc.at[i, 1, pl.ds(h, h)], sibr.at[i, 1, pl.ds(h, h)], yh.at[i]])
        full_x(i).start()
        half_x(i).wait_recv()
        add_rows(acc.at[i, 2, pl.ds(0, h)], [acc.at[i, 2, pl.ds(0, h)], sibr.at[i, 2, pl.ds(0, h)], xh.at[i]])
        add_rows(acc.at[i, 2, pl.ds(h, h)], [acc.at[i, 2, pl.ds(h, h)], sibr.at[i, 2, pl.ds(h, h)]])
        full_y(i).start()
        if i > 0:
            close(i - 1)
    close(steps - 1)
    for i in range(steps):
        for b in range(4):
            cross(i, b).wait_send()
        for cp in (half_x(i), half_y(i), full_x(i), full_y(i)):
            cp.wait_send()
        if whole and order[i] != 0:
            to_plane(i).wait_send()


def scatter(p, whole, cid):
    rows, width = p.shape[-2:]
    n = NZ if whole else 1
    dma = pltpu.SemaphoreType.DMA
    v = pltpu.VMEM
    return pl.pallas_call(
        functools.partial(scatter_kernel, whole),
        out_shape=jax.ShapeDtypeStruct((rows, width), F32),
        in_specs=[pl.BlockSpec(memory_space=pl.ANY)],
        out_specs=pl.BlockSpec(memory_space=pltpu.VMEM),
        scratch_shapes=[
            v((n, 4, rows, width), BF16), v((n, 4, rows, width), BF16),
            v((n, rows // 2, width), BF16), v((n, rows // 2, width), BF16),
            v((n, rows, width), BF16), v((n, rows, width), BF16), v((3, rows, width), BF16), v((8, 128), F32),
            dma((n, 4)), dma((n, 4)), dma((n, 4)), dma((n, 2)), dma((n, 2)), dma((n, 2)), dma((n, 2)), dma((4,)), dma((4,)),
        ],
        compiler_params=pltpu.CompilerParams(collective_id=cid, has_side_effects=True, vmem_limit_bytes=56 << 20),
        cost_estimate=takes(90 if whole else 25),
        name="scatter_all" if whole else "scatter_plane",
    )(p)


def plane_order(z):
    pick = jnp.where
    return [z, pick(z == 0, 1, z - 1), pick(z == 3, 1, pick(z == 2, 3, 2)), pick(z < 2, 3, 0)]


def chip_at(c, b):
    x, y = lax.rem(c // 2, 2), c // 4
    xb, yb = lax.rem(b, 2), b // 2
    return (x + xb - 2 * x * xb) + 2 * (y + yb - 2 * y * yb)


class Gather:
    def __init__(self, here, x_ref, o_ref, keep, zsend, zrecv, send, recv):
        self.here, self.x, self.o = here, x_ref, o_ref
        self.c, self.z = here[0], here[1]
        self.order = plane_order(self.z)
        self.zsend, self.zrecv = zsend, zrecv
        self.planes = [
            Plane(here, functools.partial(lambda zz, j: o_ref.at[zz, j], zz), send.at[zz], recv.at[zz], x_ref.shape[0] // 2)
            for zz in self.order
        ]
        self.keep = pltpu.make_async_copy(x_ref, o_ref.at[self.z, self.c], keep)

    def hop(self, up, t):
        zz = self.order[t]
        src = self.x if t == 0 else self.o.at[zz, self.c]
        row = 0 if up else 1
        return remote(
            src, self.o.at[zz, self.c], self.zsend.at[row, zz], self.zrecv.at[zz], (self.c, self.z + (1 if up else -1))
        )

    def hops(self, t, act):
        zz, z = self.order[t], self.z

        @pl.when((zz <= z) & (z < NZ - 1))
        def _():
            act(self.hop(True, t))

        @pl.when((zz >= z) & (z > 0))
        def _():
            act(self.hop(False, t))

    def spread(self, t):
        if t > 0:
            self.hop(True, t).wait_recv()
        self.hops(t, lambda cp: cp.start())
        for cp in self.planes[t].first(self.source(t)):
            cp.start()

    def source(self, t):
        return self.x if t == 0 else self.o.at[self.order[t], self.c]

    def onward(self, t):
        p = self.planes[t]
        for arrived, sends in zip(p.arrive(), p.second()):
            arrived.wait_recv()
            for cp in sends:
                cp.start()

    def close(self, t):
        p = self.planes[t]
        for cp in p.diagonal():
            cp.wait_recv()
        p.third().start()
        for cp in p.across():
            cp.wait_recv()
        if t == 0:
            self.keep.wait()

    def end(self):
        for t, p in enumerate(self.planes):
            for cp in p.first(self.source(t)) + p.second()[0] + p.second()[1] + [p.third()]:
                cp.wait_send()
            self.hops(t, lambda cp: cp.wait_send())


class Scatter:
    def __init__(self, here, order, part, sibr, xh, yh, xf, yf, zr, bsend, brecv, hsend, hrecv, fsend, frecv, zsend, zrecv):
        self.c, self.z, self.sib, self.xn, self.yn, self.diag = here
        self.k = lax.rem(self.c, 2)
        self.order = order
        self.part, self.sibr, self.xh, self.yh, self.xf, self.yf, self.zr = part, sibr, xh, yh, xf, yf, zr
        self.sems = (bsend, brecv, hsend, hrecv, fsend, frecv, zsend, zrecv)
        self.h = part.shape[3] // 2

    def mine(self, t, b):
        return self.part.at[t, b, self.k]

    def cross(self, t, b):
        send, recv = self.sems[0:2]
        return remote(self.part.at[t, b, 1 - self.k], self.sibr.at[t, b], send.at[t, b], recv.at[t, b], (self.sib, self.z))

    def halves(self, t):
        send, recv = self.sems[2:4]
        src = self.mine(t, 3)
        return (
            remote(src.at[pl.ds(0, self.h)], self.xh.at[t], send.at[t, 0], recv.at[t, 0], (self.xn, self.z)),
            remote(src.at[pl.ds(self.h, self.h)], self.yh.at[t], send.at[t, 1], recv.at[t, 1], (self.yn, self.z)),
        )

    def fulls(self, t):
        send, recv = self.sems[4:6]
        return (
            remote(self.mine(t, 1), self.xf.at[t], send.at[t, 0], recv.at[t, 0], (self.xn, self.z)),
            remote(self.mine(t, 2), self.yf.at[t], send.at[t, 1], recv.at[t, 1], (self.yn, self.z)),
        )

    def hop(self, t):
        send, recv = self.sems[6:8]
        return remote(self.mine(t, 0), self.zr.at[self.z], send.at[t], recv.at[self.z], (self.c, self.order[t]))

    def came(self, t):
        send, recv = self.sems[6:8]
        zz = self.order[t]
        return remote(self.zr.at[zz], self.zr.at[zz], send.at[t], recv.at[zz], (self.c, zz))

    def one(self, t):
        self.cross(t, 3).wait_recv()
        add_rows(self.mine(t, 3), [self.mine(t, 3), self.sibr.at[t, 3]])
        for cp in self.halves(t):
            cp.start()

    def two(self, t):
        h = self.h
        top, low = pl.ds(0, h), pl.ds(h, h)
        hx, hy = self.halves(t)
        fx, fy = self.fulls(t)
        self.cross(t, 1).wait_recv()
        m, s = self.mine(t, 1), self.sibr.at[t, 1]
        add_rows(m.at[top], [m.at[top], s.at[top]])
        hy.wait_recv()
        add_rows(m.at[low], [m.at[low], s.at[low], self.yh.at[t]])
        fx.start()
        self.cross(t, 2).wait_recv()
        m, s = self.mine(t, 2), self.sibr.at[t, 2]
        add_rows(m.at[low], [m.at[low], s.at[low]])
        hx.wait_recv()
        add_rows(m.at[top], [m.at[top], s.at[top], self.xh.at[t]])
        fy.start()

    def three(self, t, o_ref):
        self.cross(t, 0).wait_recv()
        for cp in self.fulls(t):
            cp.wait_recv()
        parts = [self.mine(t, 0), self.sibr.at[t, 0], self.xf.at[t], self.yf.at[t]]
        if t == 0:
            add_rows(o_ref, parts)
        else:
            add_rows(self.mine(t, 0), parts)
            self.hop(t).start()

    def end(self, o_ref):
        n = len(self.order)
        for t in range(1, n):
            self.came(t).wait_recv()
        if n > 1:
            add_rows(o_ref, [o_ref] + [self.zr.at[self.order[t]] for t in range(1, n)])
        for t in range(n):
            for b in range(4):
                self.cross(t, b).wait_send()
            for cp in self.halves(t) + self.fulls(t):
                cp.wait_send()
            if t > 0:
                self.hop(t).wait_send()


def scatter_scratch(n, rows, width):
    v, dma = pltpu.VMEM, pltpu.SemaphoreType.DMA
    return [
        v((n, 4, 2, rows, width), BF16), v((n, 4, rows, width), BF16),
        v((n, rows // 2, width), BF16), v((n, rows // 2, width), BF16),
        v((n, rows, width), BF16), v((n, rows, width), BF16), v((NZ, rows, width), BF16),
        dma((n, 4)), dma((n, 4)), dma((n, 2)), dma((n, 2)), dma((n, 2)), dma((n, 2)), dma((NZ,)), dma((NZ,)),
    ]


def everyone_else(c, z):
    flat = c * NZ + z
    others = [lax.rem(flat + s, 32) for s in range(1, 32)]
    return flat, [(o // NZ, lax.rem(o, NZ)) for o in others]


def feed_kernel(
    x_ref, st_ref, w_ref, d_ref, o_ref, all_ref, so_ref, gu_ref, xs, gs, xsem, gsem, keep, zsend, zrecv, send, recv, ssend, srecv, *scat
):
    here = place_on_plane()
    c, z = here[0], here[1]
    flat, everyone = everyone_else(c, z)
    meet(everyone)
    gather_ = Gather(here, x_ref, all_ref, keep.at[0], zsend, zrecv, send, recv)
    order = gather_.order
    sums = Scatter(here, order, *scat)
    ff = d_ref.shape[0]
    gather_.keep.start()
    gather_.spread(0)
    keep_s = pltpu.make_async_copy(st_ref, so_ref.at[flat], keep.at[1])
    keep_s.start()
    stat = [remote(st_ref, so_ref.at[flat], ssend.at[s], srecv.at[s], d) for s, d in enumerate(everyone)]
    for cp in stat:
        cp.start()

    def load(t, b):
        src = all_ref.at[order[t], pl.ds(2 * chip_at(c, b), 2)]
        return pltpu.make_async_copy(src, xs.at[b], xsem.at[b])

    def store(t, b):
        return pltpu.make_async_copy(gs.at[b], gu_ref.at[order[t], chip_at(c, b)], gsem.at[b])

    def work(t):
        for b in range(4):
            load(t, b).start()

        def body(b, _):
            load(t, b).wait()
            if t > 0:
                store(t - 1, b).wait()
            x = xs[b].reshape(-1, xs.shape[-1])
            gu = jnp.dot(x, w_ref[...], preferred_element_type=F32)
            gs[b] = gu
            store(t, b).start()
            gate, up = gu[:, :ff], gu[:, ff:]
            act = (gate * jax.nn.sigmoid(gate) * up).astype(BF16)
            p = jnp.dot(act, d_ref[...], preferred_element_type=F32).astype(BF16)
            sums.part[t, b] = p.reshape(sums.part.shape[2:])
            sums.cross(t, b).start()
            return 0

        lax.fori_loop(0, 4, body, 0)

    fused_steps(gather_, sums, work, o_ref)
    for b in range(4):
        store(3, b).wait()
    keep_s.wait()
    for cp in stat:
        cp.wait()


def fused_steps(gather_, sums, work, o_ref):
    gather_.spread(1)
    gather_.onward(0)
    gather_.spread(2)
    gather_.close(0)
    work(0)
    gather_.onward(1)
    gather_.spread(3)
    sums.one(0)
    gather_.close(1)
    work(1)
    gather_.onward(2)
    sums.two(0)
    sums.one(1)
    gather_.close(2)
    work(2)
    gather_.onward(3)
    sums.two(1)
    sums.one(2)
    sums.three(0, o_ref)
    gather_.close(3)
    work(3)
    sums.one(3)
    sums.two(2)
    sums.three(1, o_ref)
    sums.two(3)
    sums.three(2, o_ref)
    sums.three(3, o_ref)
    sums.end(o_ref)
    gather_.end()


def gather_sems():
    dma = pltpu.SemaphoreType.DMA
    return [dma((2,)), dma((2, 4)), dma((4,)), dma((4, 8)), dma((4, 8)), dma((31,)), dma((31,))]


def feed_forward(x, stats, w, d):
    rows, width = x.shape
    cols = w.shape[1]
    any_ = pl.BlockSpec(memory_space=pl.ANY)
    vmem = pl.BlockSpec(memory_space=pltpu.VMEM)
    dma = pltpu.SemaphoreType.DMA
    return pl.pallas_call(
        feed_kernel,
        out_shape=(
            jax.ShapeDtypeStruct((rows, width), F32),
            jax.ShapeDtypeStruct((NZ, 8, rows, width), BF16),
            jax.ShapeDtypeStruct((32, 8, 128), F32),
            jax.ShapeDtypeStruct((NZ, 4, 2 * rows, cols), F32),
        ),
        in_specs=[vmem, any_, vmem, vmem],
        out_specs=(vmem, any_, any_, any_),
        scratch_shapes=[
            pltpu.VMEM((4, 2, rows, width), BF16), pltpu.VMEM((4, 2 * rows, cols), F32), dma((4,)), dma((4,)),
        ] + gather_sems() + scatter_scratch(NZ, rows, width),
        compiler_params=pltpu.CompilerParams(collective_id=5, has_side_effects=True, vmem_limit_bytes=60 << 20),
        cost_estimate=takes(150),
        name="feed_forward",
    )(x, stats, w, d)


ROWS_AT_ONCE = 256


def turn(u, cosine, sine):
    return u * cosine + pltpu.roll(u, HEAD_SIZE // 2, 1) * sine


def block_probs(q, k, first, place, keys_place):
    scores = lax.dot_general(q, k, CONTRACT_COLS, preferred_element_type=F32) * HEAD_SIZE ** (-0.5)
    allowed = (keys_place >= first) & (keys_place <= place)
    scores = jnp.where(allowed, scores, NEG)
    raised = jnp.exp(scores - jnp.max(scores, axis=-1, keepdims=True))
    return raised / jnp.sum(raised, axis=-1, keepdims=True)


def exchange_loop(c, z, act):
    flat = c * NZ + z

    def body(s, _):
        to, frm = lax.rem(flat + s, 32), lax.rem(flat + 32 - s, 32)
        act(s, to // NZ, lax.rem(to, NZ), frm // NZ, lax.rem(frm, NZ))
        return 0

    lax.fori_loop(1, 32, body, 0)


def back_kernel(
    g_ref, q_ref, k_ref, v_ref, attn_ref, cos_ref, sin_ref, first_ref, place_ref, keys_ref, wqkv_ref, wout_ref, norm_ref,
    gate_ref, up_ref, down_ref,
    o_ref, mlp_o, down_o, qkv_o, out_o,
    gb, ga, gqkv, gk, gv, outg, qkvg, normed, msend, mrecv, qsend, qrecv, osend, orecv, lsem, psend, precv, *scat
):
    here = place_on_plane()
    c, z, sib, xn, yn, diag = here
    flat, everyone = everyone_else(c, z)
    meet(everyone)
    rows, width = g_ref.shape
    tokens = 8 * rows
    plane = Plane(here, lambda j: gb.at[j], psend, precv, rows // 2)
    sums = Scatter(here, [z], *scat)
    for cp in plane.first(g_ref):
        cp.start()
    fetch = pltpu.make_async_copy(norm_ref, normed, lsem.at[0])
    fetch.start()
    gb[c] = g_ref[...]
    share = width // 32
    col = z * 8 + c

    def mlp_copy(i, s, tc, tz):
        src = (gate_ref, up_ref)[i].at[pl.ds(pl.multiple_of((tc * NZ + tz) * share, share), share)]
        dst = mlp_o.at[i, :, pl.ds(pl.multiple_of(col * gate_ref.shape[1], gate_ref.shape[1]), gate_ref.shape[1])]
        return src, dst

    def mlp_sends(act):
        def one(s, tc, tz, fc, fz):
            for i in range(2):
                src, dst = mlp_copy(i, s, tc, tz)
                act(remote(src, dst, msend.at[i, s], mrecv.at[i, s], (tc, tz)))

        exchange_loop(c, z, one)

    keeps = []
    for i in range(2):
        src, dst = mlp_copy(i, 0, c, z)
        keeps.append(pltpu.make_async_copy(src, dst, lsem.at[1 + i]))
    owner = ((col // NZ), lax.rem(col, NZ))
    down_send = remote(down_ref, down_o, msend.at[0, 0], mrecv.at[0, 0], owner)
    down_keep = pltpu.make_async_copy(down_ref, down_o, lsem.at[3])

    for arrived, sends in zip(plane.arrive(), plane.second()):
        arrived.wait_recv()
        for cp in sends:
            cp.start()
    for cp in plane.diagonal():
        cp.wait_recv()
    plane.third().start()
    mlp_sends(lambda cp: cp.start())
    for cp in keeps:
        cp.start()

    @pl.when(col != flat)
    def _():
        down_send.start()

    @pl.when(col == flat)
    def _():
        down_keep.start()

    for cp in plane.across():
        cp.wait_recv()

    def heads(i, _):
        at = pl.ds(pl.multiple_of(i * ROWS_AT_ONCE, ROWS_AT_ONCE), ROWS_AT_ONCE)
        g = gb[pl.ds(i * 2, 2)].reshape(ROWS_AT_ONCE, width)
        ga[at, :] = lax.dot_general(g, wout_ref[...], CONTRACT_COLS, preferred_element_type=F32).astype(BF16)
        return 0

    lax.fori_loop(0, tokens // ROWS_AT_ONCE, heads, 0)
    gk[...] = jnp.zeros_like(gk)
    gv[...] = jnp.zeros_like(gv)

    def attend(i, _):
        at = pl.ds(pl.multiple_of(i * ROWS_AT_ONCE, ROWS_AT_ONCE), ROWS_AT_ONCE)
        k, v = k_ref[...], v_ref[...]
        cosine, sine = cos_ref[at, :], sin_ref[at, :]
        first, place, keys = first_ref[at, :], place_ref[at, :], keys_ref[...]
        for h in range(QUERY_HEADS // KEY_VALUE_HEADS):
            lanes = slice(h * HEAD_SIZE, (h + 1) * HEAD_SIZE)
            q, g = q_ref[at, lanes], ga[at, lanes]
            probs = block_probs(q, k, first, place, keys)
            g_probs = lax.dot_general(g, v, CONTRACT_COLS, preferred_element_type=F32)
            delta = jnp.sum(probs * g_probs, axis=-1, keepdims=True)
            g_scores = (probs * (g_probs - delta)).astype(BF16)
            g_q = jnp.dot(g_scores, k, preferred_element_type=F32) * HEAD_SIZE ** (-0.5)
            gqkv[at, lanes] = turn(g_q, cosine, -sine).astype(BF16)
            gk[...] += lax.dot_general(g_scores, q, CONTRACT_ROWS, preferred_element_type=F32)
            gv[...] += lax.dot_general(probs.astype(BF16), g, CONTRACT_ROWS, preferred_element_type=F32)
        return 0

    lax.fori_loop(0, tokens // ROWS_AT_ONCE, attend, 0)
    qcols = q_ref.shape[1]
    g_k = gk[...] * HEAD_SIZE ** (-0.5)
    gqkv[:, qcols : qcols + HEAD_SIZE] = turn(g_k, cos_ref[...], -sin_ref[...]).astype(BF16)
    gqkv[:, qcols + HEAD_SIZE :] = gv[...].astype(BF16)

    fetch.wait()
    piece = 512

    def project(i, _):
        at = pl.ds(pl.multiple_of(i * piece, piece), piece)
        qkvg[at, :] = lax.dot_general(normed[:, at], gqkv[...], CONTRACT_ROWS, preferred_element_type=F32).astype(BF16)
        return 0

    lax.fori_loop(0, width // piece, project, 0)
    cols = qkvg.shape[1]

    def qkv_copy(tc, tz):
        src = qkvg.at[pl.ds(pl.multiple_of((tc * NZ + tz) * share, share), share)]
        return src, qkv_o.at[z, :, pl.ds(pl.multiple_of(c * cols, cols), cols)]

    def qkv_sends(act):
        def one(s, tc, tz, fc, fz):
            src, dst = qkv_copy(tc, tz)
            act(remote(src, dst, qsend.at[s], qrecv.at[s], (tc, tz)))

        exchange_loop(c, z, one)

    qkv_sends(lambda cp: cp.start())
    src, dst = qkv_copy(c, z)
    keep_q = pltpu.make_async_copy(src, dst, lsem.at[4])
    keep_q.start()

    for b in (3, 1, 2, 0):
        chip = chip_at(c, b)
        at = pl.ds(pl.multiple_of(chip * ROWS_AT_ONCE, ROWS_AT_ONCE), ROWS_AT_ONCE)
        p = lax.dot_general(gqkv[at, :], wqkv_ref[...], CONTRACT_COLS, preferred_element_type=F32).astype(BF16)
        sums.part[0, b] = p.reshape(2, rows, width)
        sums.cross(0, b).start()
    sums.one(0)

    def outs(i, _):
        at = pl.ds(pl.multiple_of(i * piece, piece), piece)
        g = gb[:, :, at].reshape(tokens, piece)
        outg[:, at] = lax.dot_general(attn_ref[...], g, CONTRACT_ROWS, preferred_element_type=F32).astype(BF16)
        return 0

    lax.fori_loop(0, width // piece, outs, 0)
    out_sends = []
    for s in (1, 2, 3):
        to = lax.rem(z + s, NZ)
        src = outg.at[pl.ds(pl.multiple_of(to * share, share), share)]
        out_sends.append(remote(src, out_o.at[z], osend.at[s], orecv.at[s], (c, to)))
    for cp in out_sends:
        cp.start()
    keep_o = pltpu.make_async_copy(outg.at[pl.ds(pl.multiple_of(z * share, share), share)], out_o.at[z], lsem.at[5])
    keep_o.start()
    sums.two(0)
    sums.three(0, o_ref)
    sums.end(o_ref)
    for cp in plane.first(g_ref) + plane.second()[0] + plane.second()[1] + [plane.third()]:
        cp.wait_send()
    mlp_sends(lambda cp: cp.wait())

    @pl.when(col != flat)
    def _():
        down_send.wait()

    @pl.when(col == flat)
    def _():
        down_keep.wait()

    for cp in out_sends:
        cp.wait()
    qkv_sends(lambda cp: cp.wait())
    for cp in keeps + [keep_q, keep_o]:
        cp.wait()


def attention_back(g, q, k, v, attn, cosine, sine, first, place, keys, w_qkv, w_out, normed, gate_g, up_g, down_g):
    rows, width = g.shape
    tokens = q.shape[0]
    any_ = pl.BlockSpec(memory_space=pl.ANY)
    vmem = pl.BlockSpec(memory_space=pltpu.VMEM)
    dma, buf = pltpu.SemaphoreType.DMA, pltpu.VMEM
    share = width // 32
    cols = w_qkv.shape[1]
    return pl.pallas_call(
        back_kernel,
        out_shape=(
            jax.ShapeDtypeStruct((rows, width), F32),
            jax.ShapeDtypeStruct((2, share, 32 * gate_g.shape[1]), BF16),
            jax.ShapeDtypeStruct(down_g.shape, BF16),
            jax.ShapeDtypeStruct((NZ, share, 8 * cols), BF16),
            jax.ShapeDtypeStruct((NZ, share, width), BF16),
        ),
        in_specs=[vmem] * 12 + [any_] * 4,
        out_specs=(vmem,) + (any_,) * 4,
        scratch_shapes=[
            buf((8, rows, width), BF16), buf(q.shape, BF16), buf((tokens, cols), BF16), buf(k.shape, F32), buf(v.shape, F32),
            buf(w_out.shape, BF16), buf((width, cols), BF16), buf(normed.shape, BF16),
            dma((2, 32)), dma((2, 32)), dma((32,)), dma((32,)), dma((4,)), dma((4,)), dma((6,)), dma((8,)), dma((8,)),
        ] + scatter_scratch(1, rows, width),
        compiler_params=pltpu.CompilerParams(collective_id=6, has_side_effects=True, vmem_limit_bytes=60 << 20),
        cost_estimate=takes(110),
        name="attention_back",
    )(g, q, k, v, attn, cosine, sine, first, place, keys, w_qkv, w_out, normed, gate_g, up_g, down_g)


def open_kernel(x_ref, g_ref, wq_ref, wk_ref, wv_ref, o_ref, w_ref, go_ref, normed, local, wsend, wrecv, gsend, grecv, send, recv):
    here = place_on_plane()
    c, z, sib, xn, yn, diag = here
    rows, width = x_ref.shape
    others = [lax.rem(z + s, NZ) for s in (1, 2, 3)]
    meet([(sib, z), (xn, z), (yn, z)] + [(c, t) for t in others])
    go_ref[z] = g_ref[...]
    gains = [remote(g_ref, go_ref.at[z], gsend.at[s], grecv.at[s], (c, t)) for s, t in enumerate(others)]
    for cp in gains:
        cp.start()

    def columns(i):
        ref, lo, n = ((wq_ref, 0, 256), (wk_ref, 256, 128), (wv_ref, 384, 128))[i]
        src = ref.at[:, pl.ds(pl.multiple_of(c * n, n), n)]
        return src, w_ref.at[z, :, pl.ds(lo, n)]

    keeps, weights = [], []
    for i in range(3):
        src, dst = columns(i)
        keeps.append(pltpu.make_async_copy(src, dst, local.at[i]))
        for s, t in enumerate(others):
            weights.append(remote(src, dst, wsend.at[s, i], wrecv.at[s, i], (c, t)))
    for cp in weights + keeps:
        cp.start()
    x = x_ref[...].astype(F32)
    scaled = x * lax.rsqrt(jnp.mean(x * x, axis=-1, keepdims=True) + EPS)
    for cp in gains:
        cp.wait()
    piece = width // NZ
    for zz in range(NZ):
        normed[:, zz * piece : (zz + 1) * piece] = (
            scaled[:, zz * piece : (zz + 1) * piece] * go_ref[zz, 0:1, :]
        ).astype(BF16)
    plane = Plane(here, lambda j: o_ref.at[j], send, recv, rows // 2)
    for cp in plane.first(normed):
        cp.start()
    keep = pltpu.make_async_copy(normed, o_ref.at[c], local.at[3])
    keep.start()
    plane_rest(plane, normed)
    for cp in weights:
        cp.wait()
    for cp in keeps + [keep]:
        cp.wait()


def plane_rest(plane, src):
    for arrived, sends in zip(plane.arrive(), plane.second()):
        arrived.wait_recv()
        for cp in sends:
            cp.start()
    for cp in plane.diagonal():
        cp.wait_recv()
    plane.third().start()
    for cp in plane.across():
        cp.wait_recv()
    for cp in plane.first(src) + plane.second()[0] + plane.second()[1] + [plane.third()]:
        cp.wait_send()


def open_layer(x, gains, w_query, w_key, value_weight):
    rows, width = x.shape
    any_ = pl.BlockSpec(memory_space=pl.ANY)
    vmem = pl.BlockSpec(memory_space=pltpu.VMEM)
    dma = pltpu.SemaphoreType.DMA
    depth = w_query.shape[0]
    return pl.pallas_call(
        open_kernel,
        out_shape=(
            jax.ShapeDtypeStruct((8, rows, width), BF16),
            jax.ShapeDtypeStruct((NZ, depth, 512), BF16),
            jax.ShapeDtypeStruct((NZ,) + gains.shape, F32),
        ),
        in_specs=[vmem, vmem, any_, any_, any_],
        out_specs=(any_, any_, vmem),
        scratch_shapes=[
            pltpu.VMEM((rows, width), BF16), dma((4,)), dma((3, 3)), dma((3, 3)), dma((3,)), dma((3,)), dma((8,)), dma((8,)),
        ],
        compiler_params=pltpu.CompilerParams(collective_id=4, has_side_effects=True, vmem_limit_bytes=32 << 20),
        cost_estimate=takes(50),
        name="open_layer",
    )(x, gains, w_query, w_key, value_weight)


def after(value, *others):
    return lax.optimization_barrier((value,) + others)[0]


def tile_of(value):
    return jnp.full((8, 128), value, F32)


def heads_and_columns(
    hidden_in,
    cotangent,
    teacher,
    valid_mask,
    doc_starts,
    attn_gain,
    w_query,
    w_key,
    value_weight,
    w_output,
    mlp_gain,
    w_gate,
    w_up,
    w_down,
):
    rows, width = hidden_in.shape[1:]
    c = lax.axis_index("ctx")
    z = lax.axis_index("fsdp")
    devices = lax.axis_size("ctx")
    tokens = rows * devices
    group = QUERY_HEADS // KEY_VALUE_HEADS
    qcols = group * HEAD_SIZE
    ffcols = FF // (devices * NZ)
    scale = HEAD_SIZE ** (-0.5)

    layer_input = hidden_in[0].astype(F32)
    gains = jnp.concatenate(
        [attn_gain.astype(F32)[None], mlp_gain.astype(F32)[None], jnp.zeros((6, attn_gain.shape[0]), F32)]
    )
    normed_all, w_qkv, gains_all = open_layer(hidden_in[0], gains, w_query, w_key, value_weight)
    attn_scale = gains_all[:, 0, :].reshape(1, width)
    mlp_scale = gains_all[:, 1, :].reshape(1, width)
    normed_all = normed_all.reshape(tokens, width)
    w_qkv = w_qkv.reshape(width, 2 * qcols)

    out_cols = lax.dynamic_slice_in_dim(w_output, c * qcols, qcols, axis=1)
    out_cols = lax.all_gather(after(out_cols, w_qkv), "fsdp", axis=0, tiled=True)
    out_rows = lax.all_to_all(out_cols.reshape(devices, qcols, qcols), "ctx", 0, 0, tiled=True)
    out_rows = out_rows.transpose(1, 0, 2).reshape(qcols, width)
    mlp_cols = jnp.stack(
        [
            jnp.concatenate(
                [lax.dynamic_slice_in_dim(w, (zz * devices + c) * ffcols, ffcols, axis=1) for w in (w_gate, w_up)], axis=1
            )
            for zz in range(NZ)
        ]
    )
    w_mlp = lax.all_to_all(after(mlp_cols, w_qkv), "fsdp", 0, 0, tiled=True).reshape(width, 2 * ffcols)
    down_rows = lax.dynamic_slice_in_dim(w_down, c * ffcols, ffcols, axis=0)

    place, segment, offset = stream_places(tokens, rows, devices, doc_starts[0])
    allowed = (segment[:, None] == segment[None, :]) & (place[None, :] <= place[:, None])
    freq = ROPE_BASE ** (-(jnp.arange(HEAD_SIZE // 2, dtype=F32) * 2.0 / HEAD_SIZE))
    angle = offset.astype(F32)[:, None] * freq[None, :]
    cosine = jnp.concatenate([jnp.cos(angle)] * 2, axis=1)
    sine = jnp.concatenate([-jnp.sin(angle), jnp.sin(angle)], axis=1)
    columns = ((place - offset)[:, None], place[:, None], place[None, :])
    qkv = jnp.dot(normed_all, w_qkv, preferred_element_type=F32)
    q = rotary_embed(qkv[:, :qcols].reshape(tokens, group, HEAD_SIZE), offset, 1.0).astype(BF16)
    k = rotary_embed(qkv[:, qcols : qcols + HEAD_SIZE].reshape(tokens, 1, HEAD_SIZE), offset, 1.0)[:, 0].astype(BF16)
    v = qkv[:, qcols + HEAD_SIZE :].astype(BF16)
    scores = head_scores(q, k, allowed)
    top = jnp.max(scores, axis=-1, keepdims=True)
    lse = top + jnp.log(jnp.sum(jnp.exp(scores - top), axis=-1, keepdims=True))
    probs = jnp.exp(scores - lse)
    probs_low = probs.astype(BF16)
    attn = jnp.einsum("rts,sd->trd", probs_low, v, preferred_element_type=F32).reshape(tokens, qcols).astype(BF16)
    branch = jnp.dot(attn, out_rows, preferred_element_type=F32).astype(BF16)
    residual = layer_input + scatter(branch.reshape(devices, rows, width), False, 3)

    r2 = rms_norm_scale(residual)
    hat2 = residual * r2
    normed2 = (hat2 * mlp_scale).astype(BF16)
    maskf = valid_mask[0].astype(F32)
    normed2_all, counts = gather(normed2, tile_of(jnp.sum(maskf)), True, 0)
    count = jnp.sum(counts[:, 0, 0])
    every = NZ * tokens
    normed2_all = normed2_all.reshape(every, width)
    gate_up = jnp.dot(normed2_all, w_mlp, preferred_element_type=F32)
    gate, up = gate_up[:, :ffcols], gate_up[:, ffcols:]
    sigma = jax.nn.sigmoid(gate)
    act = (gate * sigma * up).astype(BF16)
    down = jnp.dot(act, down_rows, preferred_element_type=F32).astype(BF16)
    outf = residual + scatter(down.reshape(NZ, devices, rows, width), True, 2)

    diff = outf - teacher[0].astype(F32)
    error_here = jnp.sum(maskf * jnp.mean(diff * diff, axis=-1))
    g_out = cotangent[0].astype(F32) + maskf[:, None] * diff * (2.0 / (count * width))
    g_mo_all, errors = gather(g_out.astype(BF16), tile_of(error_here), True, 0)
    loss = jnp.sum(errors[:, 0, 0]) / count
    g_mo_all = g_mo_all.reshape(every, width)
    g_act = lax.dot_general(g_mo_all, down_rows, CONTRACT_COLS, preferred_element_type=F32)
    g_gate = (g_act * up * sigma * (1.0 + gate * (1.0 - sigma))).astype(BF16)
    g_up = (g_act * gate * sigma).astype(BF16)
    g_gate_up = jnp.concatenate([g_gate, g_up], axis=1)
    g_norm2 = lax.dot_general(g_gate_up, w_mlp, CONTRACT_COLS, preferred_element_type=F32).astype(BF16)
    g_norm2 = scatter(g_norm2.reshape(NZ, devices, rows, width), True, 2)
    gate_grads = lax.dot_general(normed2_all, g_gate, CONTRACT_ROWS, preferred_element_type=F32).astype(BF16)
    up_grads = lax.dot_general(normed2_all, g_up, CONTRACT_ROWS, preferred_element_type=F32).astype(BF16)
    down_grads = lax.dot_general(act, g_mo_all, CONTRACT_ROWS, preferred_element_type=F32).astype(BF16)

    g_hat2 = g_norm2 * mlp_scale
    g_residual = g_out + r2 * (g_hat2 - hat2 * jnp.mean(g_hat2 * hat2, axis=-1, keepdims=True))
    g_norm1, got, got_down, got_qkv, got_out = attention_back(
        g_residual.astype(BF16), q.reshape(tokens, qcols), k, v, attn, cosine, sine, *columns, w_qkv, out_rows, normed_all,
        gate_grads, up_grads, down_grads,
    )

    r1 = rms_norm_scale(layer_input)
    hat1 = layer_input * r1
    g_hat1 = g_norm1 * attn_scale
    g_input = g_residual + r1 * (g_hat1 - hat1 * jnp.mean(g_hat1 * hat1, axis=-1, keepdims=True))

    both = ("ctx", "fsdp")
    parts = devices * NZ

    share = width // parts
    got = got.astype(F32)
    got_qkv = jnp.sum(got_qkv.astype(F32), axis=0).reshape(share, devices, 2 * qcols)
    got_out = jnp.sum(got_out.astype(F32), axis=0)
    got_down = got_down.astype(F32)
    gain_terms = jnp.stack([jnp.sum(g_norm1 * hat1, axis=0), jnp.sum(g_norm2 * hat2, axis=0)])
    gain_terms = gain_terms.reshape(2, parts, share).transpose(1, 0, 2).reshape(parts, 1, 2 * share)
    got_gains = jnp.sum(lax.all_to_all(gain_terms, both, 0, 0, tiled=True), axis=(0, 1))
    return (
        loss,
        outf.astype(BF16)[None],
        g_input.astype(BF16)[None],
        got_gains[:share],
        got_qkv[:, :, :qcols].reshape(share, QUERY_HEADS * HEAD_SIZE),
        got_qkv[:, :, qcols : qcols + HEAD_SIZE].reshape(share, KEY_VALUE_HEADS * HEAD_SIZE),
        got_qkv[:, :, qcols + HEAD_SIZE :].reshape(share, KEY_VALUE_HEADS * HEAD_SIZE),
        got_out,
        got_gains[share:],
        got[0],
        got[1],
        got_down,
    )


def solution(mesh):
    small = dict(mesh.shape) == {"ctx": KEY_VALUE_HEADS, "fsdp": NZ}
    in_specs = (
        P("fsdp", "ctx", None),
        P("fsdp", "ctx", None),
        P("fsdp", "ctx", None),
        P("fsdp", "ctx"),
        P("fsdp", None),
        P("fsdp"),
        P("fsdp", None),
        P("fsdp", None),
        P("fsdp", None),
        P("fsdp", None),
        P("fsdp"),
        P("fsdp", None),
        P("fsdp", None),
        P("fsdp", None),
    )
    out_specs = (
        P(),
        P("fsdp", "ctx", None),
        P("fsdp", "ctx", None),
        P(("ctx", "fsdp")),
        P(("ctx", "fsdp"), None),
        P(("ctx", "fsdp"), None),
        P(("ctx", "fsdp"), None),
        P(("ctx", "fsdp"), None),
        P(("ctx", "fsdp")),
        P(("ctx", "fsdp"), None),
        P(("ctx", "fsdp"), None),
        P(("ctx", "fsdp"), None),
    )
    return jax.shard_map(
        heads_and_columns if small else per_device, mesh=mesh, in_specs=in_specs, out_specs=out_specs, check_vma=False
    )
```

```python
import functools

import jax
import jax.numpy as jnp
from jax import lax
from jax.experimental import pallas as pl
from jax.experimental.pallas import tpu as pltpu
from jax.sharding import PartitionSpec as P

QUERY_HEADS = 16
KEY_VALUE_HEADS = 8
HEAD_SIZE = 128
FF = 8192


EPS = 1e-05
ROPE_BASE = 1000000.0
NEG = -1e30
CONTRACT_ROWS = (((0,), (0,)), ((), ()))
CONTRACT_COLS = (((1,), (1,)), ((), ()))


def stream_places(rows, local_token_count, devices, starts):
    span = local_token_count // 2
    rowid = jnp.arange(rows, dtype=jnp.int32)
    device = rowid // local_token_count
    within = rowid % local_token_count
    span_id = jnp.where(within < span, device, 2 * devices - 1 - device)
    place = span_id * span + within % span
    before = starts[None, :] <= place[:, None]
    segment = jnp.sum(before.astype(jnp.int32), axis=1) - 1
    first = jnp.max(jnp.where(before, starts[None, :], 0), axis=1)
    return (place, segment, place - first)


def rotary_embed(values, token_offset, sign):
    half = HEAD_SIZE // 2
    freq = ROPE_BASE ** (-(jnp.arange(half, dtype=jnp.float32) * 2.0 / HEAD_SIZE))
    angle = token_offset.astype(jnp.float32)[:, None] * freq[None, :]
    cosine = jnp.cos(angle)[:, None, :]
    sine = sign * jnp.sin(angle)[:, None, :]
    first = values[..., :half]
    second = values[..., half:]
    return jnp.concatenate(
        [first * cosine - second * sine, second * cosine + first * sine], axis=-1
    )


def rms_norm_scale(values):
    return lax.rsqrt(jnp.mean(values * values, axis=-1, keepdims=True) + EPS)


def head_scores(query_rows, key_rows, allowed):
    attention_scores = jnp.einsum(
        "trd,sd->rts", query_rows, key_rows, preferred_element_type=jnp.float32
    ) * HEAD_SIZE ** (-0.5)
    return jnp.where(allowed[None], attention_scores, NEG)


def per_device(
    hidden_in,
    cotangent,
    teacher,
    valid_mask,
    doc_starts,
    attn_gain,
    w_query,
    w_key,
    value_weight,
    w_output,
    mlp_gain,
    w_gate,
    w_up,
    w_down,
):
    local_token_count = hidden_in.shape[1]
    width = hidden_in.shape[2]
    devices = lax.axis_size("ctx")
    index = lax.axis_index("ctx")
    packed_stream_rows = local_token_count * devices
    query_group = QUERY_HEADS // KEY_VALUE_HEADS
    place, segment, token_offset = stream_places(
        packed_stream_rows, local_token_count, devices, doc_starts[0]
    )
    own_start = index * local_token_count
    my_place = lax.dynamic_slice_in_dim(place, own_start, local_token_count)
    my_segment = lax.dynamic_slice_in_dim(segment, own_start, local_token_count)
    local_stream_offset = lax.dynamic_slice_in_dim(token_offset, own_start, local_token_count)
    allowed = (my_segment[:, None] == segment[None, :]) & (place[None, :] <= my_place[:, None])
    layer_input = hidden_in[0].astype(jnp.float32)
    attn_whole = (
        lax.all_gather(attn_gain, "fsdp", axis=0, tiled=True),
        lax.all_gather(w_query, "fsdp", axis=0, tiled=True),
        lax.all_gather(w_key, "fsdp", axis=0, tiled=True),
        lax.all_gather(value_weight, "fsdp", axis=0, tiled=True),
        lax.all_gather(w_output, "fsdp", axis=0, tiled=True),
    )
    first_norm_scale = attn_whole[0].astype(jnp.float32)
    first_inverse_norm = rms_norm_scale(layer_input)
    first_normalized_input = layer_input * first_inverse_norm
    first_normed = (first_normalized_input * first_norm_scale).astype(jnp.bfloat16)
    qproj = jnp.dot(first_normed, attn_whole[1], preferred_element_type=jnp.float32)
    key_projected = jnp.dot(first_normed, attn_whole[2], preferred_element_type=jnp.float32)
    vproj = jnp.dot(first_normed, attn_whole[3], preferred_element_type=jnp.float32).astype(
        jnp.bfloat16
    )
    query_rows = rotary_embed(
        qproj.reshape(local_token_count, QUERY_HEADS, HEAD_SIZE), local_stream_offset, 1.0
    ).astype(jnp.bfloat16)
    key_rows = (
        rotary_embed(
            key_projected.reshape(local_token_count, KEY_VALUE_HEADS, HEAD_SIZE),
            local_stream_offset,
            1.0,
        )
        .reshape(local_token_count, KEY_VALUE_HEADS * HEAD_SIZE)
        .astype(jnp.bfloat16)
    )
    every_key_row, every_value_row = (
        lax.all_gather(key_rows, "ctx", axis=0, tiled=True),
        lax.all_gather(vproj, "ctx", axis=0, tiled=True),
    )
    key_head_rows = every_key_row.reshape(packed_stream_rows, KEY_VALUE_HEADS, HEAD_SIZE).transpose(
        1, 0, 2
    )
    value_head_rows = every_value_row.reshape(
        packed_stream_rows, KEY_VALUE_HEADS, HEAD_SIZE
    ).transpose(1, 0, 2)
    query_head_rows = query_rows.reshape(
        local_token_count, KEY_VALUE_HEADS, query_group, HEAD_SIZE
    ).transpose(1, 0, 2, 3)

    def attend_head(parts):
        head_query, head_key, head_val = parts
        attention_scores = head_scores(head_query, head_key, allowed)
        top = jnp.max(attention_scores, axis=-1, keepdims=True)
        lse = top + jnp.log(jnp.sum(jnp.exp(attention_scores - top), axis=-1, keepdims=True))
        attention_probabilities = jnp.exp(attention_scores - lse)
        mixed_heads = jnp.einsum(
            "rts,sd->trd",
            attention_probabilities.astype(jnp.bfloat16),
            head_val,
            preferred_element_type=jnp.float32,
        )
        return (mixed_heads, lse)

    mixed_heads, lse = lax.map(attend_head, (query_head_rows, key_head_rows, value_head_rows))
    attn = (
        mixed_heads.transpose(1, 0, 2, 3)
        .reshape(local_token_count, QUERY_HEADS * HEAD_SIZE)
        .astype(jnp.bfloat16)
    )
    residual_state = layer_input + jnp.dot(attn, attn_whole[4], preferred_element_type=jnp.float32)
    mlp_whole = (
        lax.all_gather(mlp_gain, "fsdp", axis=0, tiled=True),
        lax.all_gather(w_gate, "fsdp", axis=0, tiled=True),
        lax.all_gather(w_up, "fsdp", axis=0, tiled=True),
        lax.all_gather(w_down, "fsdp", axis=0, tiled=True),
    )
    second_norm_scale = mlp_whole[0].astype(jnp.float32)
    second_inverse_norm = rms_norm_scale(residual_state)
    second_normalized_input = residual_state * second_inverse_norm
    second_normed = (second_normalized_input * second_norm_scale).astype(jnp.bfloat16)
    gate = jnp.dot(second_normed, mlp_whole[1], preferred_element_type=jnp.float32)
    up_val = jnp.dot(second_normed, mlp_whole[2], preferred_element_type=jnp.float32)
    sigma = jax.nn.sigmoid(gate)
    act = (gate * sigma * up_val).astype(jnp.bfloat16)
    outf = residual_state + jnp.dot(act, mlp_whole[3], preferred_element_type=jnp.float32)
    maskf = valid_mask[0].astype(jnp.float32)
    diff = outf - teacher[0].astype(jnp.float32)
    count_here = jnp.sum(maskf)
    error_here = jnp.sum(maskf * jnp.mean(diff * diff, axis=-1))
    count, error_total = lax.psum((count_here, error_here), ("ctx", "fsdp"))
    loss = error_total / count
    output_gradient = cotangent[0].astype(jnp.float32) + maskf[:, None] * diff * (
        2.0 / (count * width)
    )
    g_mo = output_gradient.astype(jnp.bfloat16)
    mlp_back = (
        lax.all_gather(mlp_gain, "fsdp", axis=0, tiled=True),
        lax.all_gather(w_gate, "fsdp", axis=0, tiled=True),
        lax.all_gather(w_up, "fsdp", axis=0, tiled=True),
        lax.all_gather(w_down, "fsdp", axis=0, tiled=True),
    )
    g_act = lax.dot_general(g_mo, mlp_back[3], CONTRACT_COLS, preferred_element_type=jnp.float32)
    g_gate = (g_act * up_val * sigma * (1.0 + gate * (1.0 - sigma))).astype(jnp.bfloat16)
    g_up = (g_act * gate * sigma).astype(jnp.bfloat16)
    gate_up_gradient = jnp.concatenate([g_gate, g_up], axis=1)
    second_norm_gradient = lax.dot_general(
        g_gate, mlp_back[1], CONTRACT_COLS, preferred_element_type=jnp.float32
    )
    second_norm_gradient = second_norm_gradient + lax.dot_general(
        g_up, mlp_back[2], CONTRACT_COLS, preferred_element_type=jnp.float32
    )
    second_hat_gradient = second_norm_gradient * second_norm_scale
    residual_gradient = output_gradient + second_inverse_norm * (
        second_hat_gradient
        - second_normalized_input
        * jnp.mean(second_hat_gradient * second_normalized_input, axis=-1, keepdims=True)
    )
    mlp_share = lax.psum_scatter(
        lax.dot_general(
            second_normed, gate_up_gradient, CONTRACT_ROWS, preferred_element_type=jnp.float32
        ),
        ("ctx", "fsdp"),
        scatter_dimension=0,
        tiled=True,
    )
    down_share = lax.psum_scatter(
        lax.dot_general(act, g_mo, CONTRACT_ROWS, preferred_element_type=jnp.float32),
        ("ctx", "fsdp"),
        scatter_dimension=0,
        tiled=True,
    )
    g_branch = residual_gradient.astype(jnp.bfloat16)
    attn_back = (
        lax.all_gather(attn_gain, "fsdp", axis=0, tiled=True),
        lax.all_gather(w_query, "fsdp", axis=0, tiled=True),
        lax.all_gather(w_key, "fsdp", axis=0, tiled=True),
        lax.all_gather(value_weight, "fsdp", axis=0, tiled=True),
        lax.all_gather(w_output, "fsdp", axis=0, tiled=True),
    )
    attention_gradient = lax.dot_general(
        g_branch, attn_back[4], CONTRACT_COLS, preferred_element_type=jnp.float32
    ).astype(jnp.bfloat16)
    heads_gradient = attention_gradient.reshape(
        local_token_count, KEY_VALUE_HEADS, query_group, HEAD_SIZE
    ).transpose(1, 0, 2, 3)

    def attend_back(parts):
        head_query, head_key, head_val, head_lse, head_grad = parts
        attention_probabilities = jnp.exp(head_scores(head_query, head_key, allowed) - head_lse)
        g_probs = jnp.einsum("trd,sd->rts", head_grad, head_val, preferred_element_type=jnp.float32)
        delta = jnp.sum(attention_probabilities * g_probs, axis=-1, keepdims=True)
        g_scores = (attention_probabilities * (g_probs - delta)).astype(jnp.bfloat16)
        g_query = jnp.einsum(
            "rts,sd->trd", g_scores, head_key, preferred_element_type=jnp.float32
        ) * HEAD_SIZE ** (-0.5)
        key_gradient = jnp.einsum(
            "rts,trd->sd", g_scores, head_query, preferred_element_type=jnp.float32
        ) * HEAD_SIZE ** (-0.5)
        value_gradient = jnp.einsum(
            "rts,trd->sd",
            attention_probabilities.astype(jnp.bfloat16),
            head_grad,
            preferred_element_type=jnp.float32,
        )
        return (g_query, key_gradient, value_gradient)

    g_query, key_gradient, value_gradient = lax.map(
        attend_back, (query_head_rows, key_head_rows, value_head_rows, lse, heads_gradient)
    )
    key_gradient_terms = key_gradient.transpose(1, 0, 2).reshape(
        packed_stream_rows, KEY_VALUE_HEADS * HEAD_SIZE
    )
    value_gradient_terms = value_gradient.transpose(1, 0, 2).reshape(
        packed_stream_rows, KEY_VALUE_HEADS * HEAD_SIZE
    )
    key_rows_gradient, g_vals = (
        lax.psum_scatter(
            key_gradient_terms.astype(jnp.bfloat16), "ctx", scatter_dimension=0, tiled=True
        ).astype(jnp.float32),
        lax.psum_scatter(
            value_gradient_terms.astype(jnp.bfloat16), "ctx", scatter_dimension=0, tiled=True
        ).astype(jnp.float32),
    )
    g_qproj = (
        rotary_embed(
            g_query.transpose(1, 0, 2, 3).reshape(local_token_count, QUERY_HEADS, HEAD_SIZE),
            local_stream_offset,
            -1.0,
        )
        .reshape(local_token_count, QUERY_HEADS * HEAD_SIZE)
        .astype(jnp.bfloat16)
    )
    g_kproj = (
        rotary_embed(
            key_rows_gradient.reshape(local_token_count, KEY_VALUE_HEADS, HEAD_SIZE),
            local_stream_offset,
            -1.0,
        )
        .reshape(local_token_count, KEY_VALUE_HEADS * HEAD_SIZE)
        .astype(jnp.bfloat16)
    )
    g_vproj = g_vals.astype(jnp.bfloat16)
    first_norm_gradient = lax.dot_general(
        g_qproj, attn_back[1], CONTRACT_COLS, preferred_element_type=jnp.float32
    )
    first_norm_gradient = first_norm_gradient + lax.dot_general(
        g_kproj, attn_back[2], CONTRACT_COLS, preferred_element_type=jnp.float32
    )
    first_norm_gradient = first_norm_gradient + lax.dot_general(
        g_vproj, attn_back[3], CONTRACT_COLS, preferred_element_type=jnp.float32
    )
    first_hat_gradient = first_norm_gradient * first_norm_scale
    g_input = residual_gradient + first_inverse_norm * (
        first_hat_gradient
        - first_normalized_input
        * jnp.mean(first_hat_gradient * first_normalized_input, axis=-1, keepdims=True)
    )
    key_value_proj_gradient = jnp.concatenate([g_kproj, g_vproj], axis=1)
    query_term = lax.dot_general(
        first_normed, g_qproj, CONTRACT_ROWS, preferred_element_type=jnp.float32
    )
    key_value_term = lax.dot_general(
        first_normed, key_value_proj_gradient, CONTRACT_ROWS, preferred_element_type=jnp.float32
    )
    output_term = lax.dot_general(attn, g_branch, CONTRACT_ROWS, preferred_element_type=jnp.float32)
    scale_gradient_terms = jnp.stack(
        [
            jnp.sum(first_norm_gradient * first_normalized_input, axis=0),
            jnp.sum(second_norm_gradient * second_normalized_input, axis=0),
        ]
    )
    query_share, key_value_share, output_share, gain_share = (
        lax.psum_scatter(query_term, ("ctx", "fsdp"), scatter_dimension=0, tiled=True),
        lax.psum_scatter(key_value_term, ("ctx", "fsdp"), scatter_dimension=0, tiled=True),
        lax.psum_scatter(output_term, ("ctx", "fsdp"), scatter_dimension=0, tiled=True),
        lax.psum_scatter(scale_gradient_terms, ("ctx", "fsdp"), scatter_dimension=1, tiled=True),
    )
    key_value_columns = KEY_VALUE_HEADS * HEAD_SIZE
    return (
        loss,
        outf.astype(jnp.bfloat16)[None],
        g_input.astype(jnp.bfloat16)[None],
        gain_share[0],
        query_share,
        key_value_share[:, :key_value_columns],
        key_value_share[:, key_value_columns:],
        output_share,
        gain_share[1],
        mlp_share[:, :FF],
        mlp_share[:, FF:],
        down_share,
    )


MESH = pl.DeviceIdType.MESH
F32 = jnp.float32
BF16 = jnp.bfloat16
NZ = 4


def place_on_plane():
    c = lax.axis_index("ctx")
    z = lax.axis_index("fsdp")
    sib = c + 1 - 2 * lax.rem(c, 2)
    xn = c + 2 - 4 * lax.rem(c // 2, 2)
    yn = c + 4 - 8 * (c // 4)
    diag = xn + yn - c
    return c, z, sib, xn, yn, diag


def meet(devices):
    barrier = pltpu.get_barrier_semaphore()
    for d in devices:
        pl.semaphore_signal(barrier, inc=1, device_id=d, device_id_type=MESH)
    pl.semaphore_wait(barrier, len(devices))


def remote(src, dst, send, recv, device):
    return pltpu.make_async_remote_copy(
        src_ref=src, dst_ref=dst, send_sem=send, recv_sem=recv, device_id=device, device_id_type=MESH
    )


def takes(micros):
    return pl.CostEstimate(flops=0, bytes_accessed=micros * 3_500_000, transcendentals=0)


class Plane:
    def __init__(self, here, slot, send, recv, half):
        self.c, self.z, self.sib, self.xn, self.yn, self.diag = here
        self.slot, self.send, self.recv, self.half = slot, send, recv, half

    def copy(self, kind, src, dst, to):
        return remote(src, dst, self.send.at[kind], self.recv.at[kind], (to, self.z))

    def first(self, src):
        mine = self.slot(self.c)
        return [self.copy(0, src, mine, self.xn), self.copy(1, src, mine, self.yn), self.copy(2, src, mine, self.sib)]

    def arrive(self):
        s = self.slot
        return [self.copy(0, s(self.xn), s(self.xn), self.xn), self.copy(1, s(self.yn), s(self.yn), self.yn)]

    def second(self):
        h = self.half
        s = self.slot
        ybot = s(self.yn).at[pl.ds(0, h)]
        xtop = s(self.xn).at[pl.ds(h, h)]
        return (
            [self.copy(4, xtop, xtop, self.yn), self.copy(5, s(self.xn), s(self.xn), self.sib)],
            [self.copy(3, ybot, ybot, self.xn), self.copy(6, s(self.yn), s(self.yn), self.sib)],
        )

    def diagonal(self):
        h = self.half
        lo, hi = self.slot(self.diag).at[pl.ds(0, h)], self.slot(self.diag).at[pl.ds(h, h)]
        return [self.copy(3, lo, lo, self.xn), self.copy(4, hi, hi, self.yn)]

    def third(self):
        d = self.slot(self.diag)
        return self.copy(7, d, d, self.sib)

    def across(self):
        s = self.slot
        return [self.copy(k, s(j), s(j), self.sib) for k, j in ((2, self.sib), (5, self.xn + self.sib - self.c), (6, self.yn + self.sib - self.c), (7, self.diag + self.sib - self.c))]


def add_rows(dst, parts, chunk=16):
    n = dst.shape[0] // chunk

    def body(i, _):
        at = pl.ds(pl.multiple_of(i * chunk, chunk), chunk)
        total = parts[0][at, :].astype(F32)
        for p in parts[1:]:
            total = total + p[at, :].astype(F32)
        dst[at, :] = total.astype(dst.dtype)
        return 0

    lax.fori_loop(0, n, body, 0)


def plane_order(z):
    pick = jnp.where
    return [z, pick(z == 0, 1, z - 1), pick(z == 3, 1, pick(z == 2, 3, 2)), pick(z < 2, 3, 0)]


def chip_at(c, b):
    x, y = lax.rem(c // 2, 2), c // 4
    xb, yb = lax.rem(b, 2), b // 2
    return (x + xb - 2 * x * xb) + 2 * (y + yb - 2 * y * yb)


class Gather:
    def __init__(self, here, x_ref, o_ref, keep, zsend, zrecv, send, recv):
        self.here, self.x, self.o = here, x_ref, o_ref
        self.c, self.z = here[0], here[1]
        self.order = plane_order(self.z)
        self.zsend, self.zrecv = zsend, zrecv
        self.planes = [
            Plane(here, functools.partial(lambda zz, j: o_ref.at[zz, j], zz), send.at[zz], recv.at[zz], x_ref.shape[0] // 2)
            for zz in self.order
        ]
        self.keep = pltpu.make_async_copy(x_ref, o_ref.at[self.z, self.c], keep)

    def hop(self, up, t):
        zz = self.order[t]
        src = self.x if t == 0 else self.o.at[zz, self.c]
        row = 0 if up else 1
        return remote(
            src, self.o.at[zz, self.c], self.zsend.at[row, zz], self.zrecv.at[zz], (self.c, self.z + (1 if up else -1))
        )

    def hops(self, t, act):
        zz, z = self.order[t], self.z

        @pl.when((zz <= z) & (z < NZ - 1))
        def _():
            act(self.hop(True, t))

        @pl.when((zz >= z) & (z > 0))
        def _():
            act(self.hop(False, t))

    def spread(self, t):
        if t > 0:
            self.hop(True, t).wait_recv()
        self.hops(t, lambda cp: cp.start())
        for cp in self.planes[t].first(self.source(t)):
            cp.start()

    def source(self, t):
        return self.x if t == 0 else self.o.at[self.order[t], self.c]

    def onward(self, t):
        p = self.planes[t]
        for arrived, sends in zip(p.arrive(), p.second()):
            arrived.wait_recv()
            for cp in sends:
                cp.start()

    def close(self, t):
        p = self.planes[t]
        for cp in p.diagonal():
            cp.wait_recv()
        p.third().start()
        for cp in p.across():
            cp.wait_recv()
        if t == 0:
            self.keep.wait()

    def end(self):
        for t, p in enumerate(self.planes):
            for cp in p.first(self.source(t)) + p.second()[0] + p.second()[1] + [p.third()]:
                cp.wait_send()
            self.hops(t, lambda cp: cp.wait_send())


class Scatter:
    def __init__(self, here, order, part, sibr, xh, yh, xf, yf, zr, bsend, brecv, hsend, hrecv, fsend, frecv, zsend, zrecv):
        self.c, self.z, self.sib, self.xn, self.yn, self.diag = here
        self.k = lax.rem(self.c, 2)
        self.order = order
        self.part, self.sibr, self.xh, self.yh, self.xf, self.yf, self.zr = part, sibr, xh, yh, xf, yf, zr
        self.sems = (bsend, brecv, hsend, hrecv, fsend, frecv, zsend, zrecv)
        self.h = part.shape[3] // 2

    def mine(self, t, b):
        return self.part.at[t, b, self.k]

    def cross(self, t, b):
        send, recv = self.sems[0:2]
        return remote(self.part.at[t, b, 1 - self.k], self.sibr.at[t, b], send.at[t, b], recv.at[t, b], (self.sib, self.z))

    def halves(self, t):
        send, recv = self.sems[2:4]
        src = self.mine(t, 3)
        return (
            remote(src.at[pl.ds(0, self.h)], self.xh.at[t], send.at[t, 0], recv.at[t, 0], (self.xn, self.z)),
            remote(src.at[pl.ds(self.h, self.h)], self.yh.at[t], send.at[t, 1], recv.at[t, 1], (self.yn, self.z)),
        )

    def fulls(self, t):
        send, recv = self.sems[4:6]
        return (
            remote(self.mine(t, 1), self.xf.at[t], send.at[t, 0], recv.at[t, 0], (self.xn, self.z)),
            remote(self.mine(t, 2), self.yf.at[t], send.at[t, 1], recv.at[t, 1], (self.yn, self.z)),
        )

    def hop(self, t):
        send, recv = self.sems[6:8]
        return remote(self.mine(t, 0), self.zr.at[self.z], send.at[t], recv.at[self.z], (self.c, self.order[t]))

    def came(self, t):
        send, recv = self.sems[6:8]
        zz = self.order[t]
        return remote(self.zr.at[zz], self.zr.at[zz], send.at[t], recv.at[zz], (self.c, zz))

    def one(self, t):
        self.cross(t, 3).wait_recv()
        add_rows(self.mine(t, 3), [self.mine(t, 3), self.sibr.at[t, 3]])
        for cp in self.halves(t):
            cp.start()

    def two(self, t):
        h = self.h
        top, low = pl.ds(0, h), pl.ds(h, h)
        hx, hy = self.halves(t)
        fx, fy = self.fulls(t)
        self.cross(t, 1).wait_recv()
        m, s = self.mine(t, 1), self.sibr.at[t, 1]
        add_rows(m.at[top], [m.at[top], s.at[top]])
        hy.wait_recv()
        add_rows(m.at[low], [m.at[low], s.at[low], self.yh.at[t]])
        fx.start()
        self.cross(t, 2).wait_recv()
        m, s = self.mine(t, 2), self.sibr.at[t, 2]
        add_rows(m.at[low], [m.at[low], s.at[low]])
        hx.wait_recv()
        add_rows(m.at[top], [m.at[top], s.at[top], self.xh.at[t]])
        fy.start()

    def three(self, t, o_ref):
        self.cross(t, 0).wait_recv()
        for cp in self.fulls(t):
            cp.wait_recv()
        parts = [self.mine(t, 0), self.sibr.at[t, 0], self.xf.at[t], self.yf.at[t]]
        if t == 0:
            add_rows(o_ref, parts)
        else:
            add_rows(self.mine(t, 0), parts)
            self.hop(t).start()

    def end(self, o_ref):
        n = len(self.order)
        for t in range(1, n):
            self.came(t).wait_recv()
        if n > 1:
            add_rows(o_ref, [o_ref] + [self.zr.at[self.order[t]] for t in range(1, n)])
        for t in range(n):
            for b in range(4):
                self.cross(t, b).wait_send()
            for cp in self.halves(t) + self.fulls(t):
                cp.wait_send()
            if t > 0:
                self.hop(t).wait_send()


def scatter_scratch(n, rows, width):
    v, dma = pltpu.VMEM, pltpu.SemaphoreType.DMA
    return [
        v((n, 4, 2, rows, width), BF16), v((n, 4, rows, width), BF16),
        v((n, rows // 2, width), BF16), v((n, rows // 2, width), BF16),
        v((n, rows, width), BF16), v((n, rows, width), BF16), v((NZ, rows, width), BF16),
        dma((n, 4)), dma((n, 4)), dma((n, 2)), dma((n, 2)), dma((n, 2)), dma((n, 2)), dma((NZ,)), dma((NZ,)),
    ]


def everyone_else(c, z):
    flat = c * NZ + z
    others = [lax.rem(flat + s, 32) for s in range(1, 32)]
    return flat, [(o // NZ, lax.rem(o, NZ)) for o in others]


def feed_kernel(
    x_ref, st_ref, wg_ref, wu_ref, d_ref, o_ref, all_ref, so_ref, gu_ref, w_ref,
    xs, gs, xsem, gsem, wsend, wrecv, wkeep, keep, zsend, zrecv, send, recv, ssend, srecv, *scat
):
    here = place_on_plane()
    c, z = here[0], here[1]
    flat, everyone = everyone_else(c, z)
    meet(everyone)
    gather_ = Gather(here, x_ref, all_ref, keep.at[0], zsend, zrecv, send, recv)
    order = gather_.order
    sums = Scatter(here, order, *scat)
    ff = d_ref.shape[0]
    gather_.keep.start()
    gather_.spread(0)
    keep_s = pltpu.make_async_copy(st_ref, so_ref.at[flat], keep.at[1])
    keep_s.start()
    stat = [remote(st_ref, so_ref.at[flat], ssend.at[s], srecv.at[s], d) for s, d in enumerate(everyone)]
    for cp in stat:
        cp.start()

    def load(t, b):
        src = all_ref.at[order[t], pl.ds(2 * chip_at(c, b), 2)]
        return pltpu.make_async_copy(src, xs.at[b], xsem.at[b])

    def store(t, b):
        return pltpu.make_async_copy(gs.at[b], gu_ref.at[order[t], chip_at(c, b)], gsem.at[b])

    def work(t):
        for b in range(4):
            load(t, b).start()

        def body(b, _):
            load(t, b).wait()
            if t != 1:
                store(1, b).wait()
            x = xs[b].reshape(-1, xs.shape[-1])
            gu = jnp.dot(x, w_ref[...].reshape(x.shape[1], -1), preferred_element_type=F32)
            gs[b] = gu
            store(t, b).start()
            gate, up = gu[:, :ff], gu[:, ff:]
            act = (gate * jax.nn.sigmoid(gate) * up).astype(BF16)
            p = jnp.dot(act, d_ref[...], preferred_element_type=F32).astype(BF16)
            sums.part[t, b] = p.reshape(sums.part.shape[2:])
            sums.cross(t, b).start()
            return 0

        lax.fori_loop(0, 4, body, 0)

    weights, weight_keeps = [], []
    for i, ref in enumerate((wg_ref, wu_ref)):
        for hop in range(NZ):
            to = lax.rem(z + hop, NZ)
            src = ref.at[:, pl.ds(pl.multiple_of((c * NZ + to) * ff, ff), ff)]
            dst = w_ref.at[z, :, pl.ds(i * ff, ff)]
            if hop == 0:
                weight_keeps.append(pltpu.make_async_copy(src, dst, wkeep.at[i]))
            else:
                weights.append(remote(src, dst, wsend.at[i, hop], wrecv.at[i, hop], (c, to)))

    def early():
        for cp in weight_keeps + weights:
            cp.start()

    def ready():
        for cp in weight_keeps + weights:
            cp.wait()

    fused_steps(gather_, sums, work, o_ref, early=early, ready=ready)
    for b in range(4):
        store(0, b).wait()
    keep_s.wait()
    for cp in stat:
        cp.wait()


def fused_steps(gather_, sums, work, o_ref, more=lambda t: None, early=lambda: None, ready=lambda: None):
    gather_.spread(1)
    gather_.onward(0)
    early()
    gather_.spread(2)
    gather_.onward(1)
    gather_.spread(3)
    gather_.onward(2)
    ready()
    gather_.close(1)
    work(1)
    gather_.onward(3)
    sums.one(1)
    more(1)
    gather_.close(2)
    work(2)
    sums.two(1)
    sums.one(2)
    more(2)
    gather_.close(3)
    work(3)
    sums.two(2)
    sums.one(3)
    sums.three(1, o_ref)
    more(3)
    sums.two(3)
    sums.three(2, o_ref)
    gather_.close(0)
    work(0)
    sums.one(0)
    sums.three(3, o_ref)
    sums.two(0)
    more(0)
    sums.three(0, o_ref)
    sums.end(o_ref)
    gather_.end()


def gather_sems():
    dma = pltpu.SemaphoreType.DMA
    return [dma((2,)), dma((2, 4)), dma((4,)), dma((4, 8)), dma((4, 8)), dma((31,)), dma((31,))]


def feed_forward(x, stats, w_gate, w_up, d):
    rows, width = x.shape
    depth, cols = w_gate.shape[0], 2 * d.shape[0]
    any_ = pl.BlockSpec(memory_space=pl.ANY)
    vmem = pl.BlockSpec(memory_space=pltpu.VMEM)
    dma = pltpu.SemaphoreType.DMA
    return pl.pallas_call(
        feed_kernel,
        out_shape=(
            jax.ShapeDtypeStruct((rows, width), F32),
            jax.ShapeDtypeStruct((NZ, 8, rows, width), BF16),
            jax.ShapeDtypeStruct((32, 8, 128), F32),
            jax.ShapeDtypeStruct((NZ, 4, 2 * rows, cols), F32),
            jax.ShapeDtypeStruct((NZ, depth, cols), BF16),
        ),
        in_specs=[vmem, any_, any_, any_, vmem],
        out_specs=(vmem, any_, any_, any_, vmem),
        scratch_shapes=[
            pltpu.VMEM((4, 2, rows, width), BF16), pltpu.VMEM((4, 2 * rows, cols), F32), dma((4,)), dma((4,)),
            dma((2, 4)), dma((2, 4)), dma((2,)),
        ] + gather_sems() + scatter_scratch(NZ, rows, width),
        compiler_params=pltpu.CompilerParams(collective_id=5, has_side_effects=True, vmem_limit_bytes=60 << 20),
        cost_estimate=takes(180),
        name="feed_forward",
    )(x, stats, w_gate, w_up, d)


def feed_back_kernel(
    x_ref, st_ref, w_ref, d_ref, n_ref, gu_ref, o_ref, all_ref, so_ref, gate_o, up_o, down_o,
    xs, ns, gs, gg, acts, total, xsem, nsem, gsem, keep, zsend, zrecv, send, recv, ssend, srecv, *scat
):
    here = place_on_plane()
    c, z = here[0], here[1]
    flat, everyone = everyone_else(c, z)
    meet(everyone)
    gather_ = Gather(here, x_ref, all_ref, keep.at[0], zsend, zrecv, send, recv)
    order = gather_.order
    sums = Scatter(here, order, *scat)
    ff = d_ref.shape[0]
    tokens = 8 * x_ref.shape[0]
    gather_.keep.start()
    gather_.spread(0)
    keep_s = pltpu.make_async_copy(st_ref, so_ref.at[flat], keep.at[1])
    keep_s.start()
    stat = [remote(st_ref, so_ref.at[flat], ssend.at[s], srecv.at[s], d) for s, d in enumerate(everyone)]
    for cp in stat:
        cp.start()

    def loads(t, b):
        chip = chip_at(c, b)
        pair = pl.ds(2 * chip, 2)
        return (
            pltpu.make_async_copy(gu_ref.at[order[t], chip], gs.at[b], gsem.at[b]),
            pltpu.make_async_copy(all_ref.at[order[t], pair], xs.at[b], xsem.at[b]),
            pltpu.make_async_copy(n_ref.at[order[t], pair], ns.at[b], nsem.at[b]),
        )

    def work(t):
        for b in range(4):
            for cp in loads(t, b):
                cp.start()

        def body(b, _):
            stored, tokens_in, _ = loads(t, b)
            stored.wait()
            tokens_in.wait()
            g = xs[b].reshape(-1, xs.shape[-1])
            g_act = lax.dot_general(g, d_ref[...], CONTRACT_COLS, preferred_element_type=F32)
            gate, up = gs[b, :, :ff], gs[b, :, ff:]
            sg = jax.nn.sigmoid(gate)
            acts[b] = (gate * sg * up).astype(BF16)
            gg[b, :, :ff] = (g_act * up * sg * (1.0 + gate * (1.0 - sg))).astype(BF16)
            gg[b, :, ff:] = (g_act * gate * sg).astype(BF16)
            p = lax.dot_general(gg[b], w_ref[...].reshape(o_ref.shape[1], -1), CONTRACT_COLS, preferred_element_type=F32).astype(BF16)
            sums.part[t, b] = p.reshape(sums.part.shape[2:])
            sums.cross(t, b).start()
            return 0

        lax.fori_loop(0, 4, body, 0)

    piece = 512

    def more(t):
        for b in range(4):
            loads(t, b)[2].wait()

        def body(i, _):
            at = pl.ds(pl.multiple_of(i * piece, piece), piece)
            n = ns[:, :, :, at].reshape(tokens, piece)
            w_term = lax.dot_general(n, gg[...].reshape(tokens, -1), CONTRACT_ROWS, preferred_element_type=F32)
            g = xs[:, :, :, at].reshape(tokens, piece)
            d_term = lax.dot_general(acts[...].reshape(tokens, -1), g, CONTRACT_ROWS, preferred_element_type=F32)
            if t != 1:
                w_term = w_term + total[at, :]
                d_term = d_term + down_o[:, at]
            down_o[:, at] = d_term
            if t != 0:
                total[at, :] = w_term
            else:
                gate_o[at, :] = w_term[:, :ff].astype(BF16)
                up_o[at, :] = w_term[:, ff:].astype(BF16)
            return 0

        lax.fori_loop(0, o_ref.shape[1] // piece, body, 0)

    fused_steps(gather_, sums, work, o_ref, more)
    keep_s.wait()
    for cp in stat:
        cp.wait()


def feed_back(x, stats, w, d, normed, gate_up):
    rows, width = x.shape
    cols = w.shape[2]
    ff = d.shape[0]
    any_ = pl.BlockSpec(memory_space=pl.ANY)
    vmem = pl.BlockSpec(memory_space=pltpu.VMEM)
    dma, buf = pltpu.SemaphoreType.DMA, pltpu.VMEM
    return pl.pallas_call(
        feed_back_kernel,
        out_shape=(
            jax.ShapeDtypeStruct((rows, width), F32),
            jax.ShapeDtypeStruct((NZ, 8, rows, width), BF16),
            jax.ShapeDtypeStruct((32, 8, 128), F32),
            jax.ShapeDtypeStruct((width, ff), BF16),
            jax.ShapeDtypeStruct((width, ff), BF16),
            jax.ShapeDtypeStruct((ff, width), F32),
        ),
        in_specs=[vmem, any_, vmem, vmem, any_, any_],
        out_specs=(vmem, any_, any_, vmem, vmem, vmem),
        scratch_shapes=[
            buf((4, 2, rows, width), BF16), buf((4, 2, rows, width), BF16), buf((4, 2 * rows, cols), F32),
            buf((4, 2 * rows, cols), BF16), buf((4, 2 * rows, ff), BF16), buf((width, cols), F32),
            dma((4,)), dma((4,)), dma((4,)),
        ] + gather_sems() + scatter_scratch(NZ, rows, width),
        compiler_params=pltpu.CompilerParams(collective_id=7, has_side_effects=True, vmem_limit_bytes=63 << 20),
        cost_estimate=takes(180),
        name="feed_back",
    )(x, stats, w, d, normed, gate_up)


ROWS_AT_ONCE = 256


def turn(u, cosine, sine):
    return u * cosine + pltpu.roll(u, HEAD_SIZE // 2, 1) * sine


def block_probs(q, k, first, place, keys_place):
    scores = lax.dot_general(q, k, CONTRACT_COLS, preferred_element_type=F32) * HEAD_SIZE ** (-0.5)
    allowed = (keys_place >= first) & (keys_place <= place)
    scores = jnp.where(allowed, scores, NEG)
    raised = jnp.exp(scores - jnp.max(scores, axis=-1, keepdims=True))
    return raised / jnp.sum(raised, axis=-1, keepdims=True)


def exchange_loop(c, z, act):
    flat = c * NZ + z

    def body(s, _):
        to, frm = lax.rem(flat + s, 32), lax.rem(flat + 32 - s, 32)
        act(s, to // NZ, lax.rem(to, NZ), frm // NZ, lax.rem(frm, NZ))
        return 0

    lax.fori_loop(1, 32, body, 0)


def back_kernel(
    g_ref, q_ref, k_ref, v_ref, attn_ref, cos_ref, sin_ref, first_ref, place_ref, keys_ref, wqkv_ref, wout_ref, norm_ref,
    gate_ref, up_ref,
    o_ref, mlp_o, qkv_o, out_o,
    gb, ga, gqkv, gk, gv, outg, qkvg, normed, msend, mrecv, qsend, qrecv, osend, orecv, lsem, psend, precv, *scat
):
    here = place_on_plane()
    c, z, sib, xn, yn, diag = here
    flat, everyone = everyone_else(c, z)
    meet(everyone)
    rows, width = g_ref.shape
    tokens = 8 * rows
    plane = Plane(here, lambda j: gb.at[j], psend, precv, rows // 2)
    sums = Scatter(here, [z], *scat)
    for cp in plane.first(g_ref):
        cp.start()
    fetch = pltpu.make_async_copy(norm_ref, normed, lsem.at[0])
    fetch.start()
    gb[c] = g_ref[...]
    share = width // 32

    def mlp_copy(i, s, tc, tz):
        src = (gate_ref, up_ref)[i].at[pl.ds(pl.multiple_of((tc * NZ + tz) * share, share), share)]
        dst = mlp_o.at[i, :, pl.ds(pl.multiple_of(flat * gate_ref.shape[1], gate_ref.shape[1]), gate_ref.shape[1])]
        return src, dst

    def mlp_sends(act):
        def one(s, tc, tz, fc, fz):
            for i in range(2):
                src, dst = mlp_copy(i, s, tc, tz)
                act(remote(src, dst, msend.at[i, s], mrecv.at[i, s], (tc, tz)))

        exchange_loop(c, z, one)

    keeps = []
    for i in range(2):
        src, dst = mlp_copy(i, 0, c, z)
        keeps.append(pltpu.make_async_copy(src, dst, lsem.at[1 + i]))
    for cp in keeps:
        cp.start()
    mlp_sends(lambda cp: cp.start())
    for arrived, sends in zip(plane.arrive(), plane.second()):
        arrived.wait_recv()
        for cp in sends:
            cp.start()
    for cp in plane.diagonal():
        cp.wait_recv()
    plane.third().start()
    for cp in plane.across():
        cp.wait_recv()

    def heads(i, _):
        at = pl.ds(pl.multiple_of(i * ROWS_AT_ONCE, ROWS_AT_ONCE), ROWS_AT_ONCE)
        g = gb[pl.ds(i * 2, 2)].reshape(ROWS_AT_ONCE, width)
        ga[at, :] = lax.dot_general(g, wout_ref[...], CONTRACT_COLS, preferred_element_type=F32).astype(BF16)
        return 0

    lax.fori_loop(0, tokens // ROWS_AT_ONCE, heads, 0)
    gk[...] = jnp.zeros_like(gk)
    gv[...] = jnp.zeros_like(gv)

    def attend(i, _):
        at = pl.ds(pl.multiple_of(i * ROWS_AT_ONCE, ROWS_AT_ONCE), ROWS_AT_ONCE)
        k, v = k_ref[...], v_ref[...]
        cosine, sine = cos_ref[at, :], sin_ref[at, :]
        first, place, keys = first_ref[at, :], place_ref[at, :], keys_ref[...]
        for h in range(QUERY_HEADS // KEY_VALUE_HEADS):
            lanes = slice(h * HEAD_SIZE, (h + 1) * HEAD_SIZE)
            q, g = q_ref[at, lanes], ga[at, lanes]
            probs = block_probs(q, k, first, place, keys)
            g_probs = lax.dot_general(g, v, CONTRACT_COLS, preferred_element_type=F32)
            delta = jnp.sum(probs * g_probs, axis=-1, keepdims=True)
            g_scores = (probs * (g_probs - delta)).astype(BF16)
            g_q = jnp.dot(g_scores, k, preferred_element_type=F32) * HEAD_SIZE ** (-0.5)
            gqkv[at, lanes] = turn(g_q, cosine, -sine).astype(BF16)
            gk[...] += lax.dot_general(g_scores, q, CONTRACT_ROWS, preferred_element_type=F32)
            gv[...] += lax.dot_general(probs.astype(BF16), g, CONTRACT_ROWS, preferred_element_type=F32)
        return 0

    lax.fori_loop(0, tokens // ROWS_AT_ONCE, attend, 0)
    qcols = q_ref.shape[1]
    g_k = gk[...] * HEAD_SIZE ** (-0.5)
    gqkv[:, qcols : qcols + HEAD_SIZE] = turn(g_k, cos_ref[...], -sin_ref[...]).astype(BF16)
    gqkv[:, qcols + HEAD_SIZE :] = gv[...].astype(BF16)

    fetch.wait()
    piece = 512

    def project(i, _):
        at = pl.ds(pl.multiple_of(i * piece, piece), piece)
        qkvg[at, :] = lax.dot_general(normed[:, at], gqkv[...], CONTRACT_ROWS, preferred_element_type=F32).astype(BF16)
        return 0

    lax.fori_loop(0, width // piece, project, 0)
    cols = qkvg.shape[1]

    def qkv_copy(tc, tz):
        src = qkvg.at[pl.ds(pl.multiple_of((tc * NZ + tz) * share, share), share)]
        return src, qkv_o.at[z, :, pl.ds(pl.multiple_of(c * cols, cols), cols)]

    def qkv_sends(act):
        def one(s, tc, tz, fc, fz):
            src, dst = qkv_copy(tc, tz)
            act(remote(src, dst, qsend.at[s], qrecv.at[s], (tc, tz)))

        exchange_loop(c, z, one)

    qkv_sends(lambda cp: cp.start())
    src, dst = qkv_copy(c, z)
    keep_q = pltpu.make_async_copy(src, dst, lsem.at[4])
    keep_q.start()

    for b in (3, 1, 2, 0):
        chip = chip_at(c, b)
        at = pl.ds(pl.multiple_of(chip * ROWS_AT_ONCE, ROWS_AT_ONCE), ROWS_AT_ONCE)
        p = lax.dot_general(gqkv[at, :], wqkv_ref[...], CONTRACT_COLS, preferred_element_type=F32).astype(BF16)
        sums.part[0, b] = p.reshape(2, rows, width)
        sums.cross(0, b).start()
    sums.one(0)

    def outs(i, _):
        at = pl.ds(pl.multiple_of(i * piece, piece), piece)
        g = gb[:, :, at].reshape(tokens, piece)
        outg[:, at] = lax.dot_general(attn_ref[...], g, CONTRACT_ROWS, preferred_element_type=F32).astype(BF16)
        return 0

    lax.fori_loop(0, width // piece, outs, 0)
    out_sends = []
    for s in (1, 2, 3):
        to = lax.rem(z + s, NZ)
        src = outg.at[pl.ds(pl.multiple_of(to * share, share), share)]
        out_sends.append(remote(src, out_o.at[z], osend.at[s], orecv.at[s], (c, to)))
    for cp in out_sends:
        cp.start()
    keep_o = pltpu.make_async_copy(outg.at[pl.ds(pl.multiple_of(z * share, share), share)], out_o.at[z], lsem.at[5])
    keep_o.start()
    sums.two(0)
    sums.three(0, o_ref)
    sums.end(o_ref)
    for cp in plane.first(g_ref) + plane.second()[0] + plane.second()[1] + [plane.third()]:
        cp.wait_send()
    mlp_sends(lambda cp: cp.wait())

    for cp in out_sends:
        cp.wait()
    qkv_sends(lambda cp: cp.wait())
    for cp in keeps + [keep_q, keep_o]:
        cp.wait()


def attention_back(g, q, k, v, attn, cosine, sine, first, place, keys, w_qkv, w_out, normed, gate_g, up_g):
    rows, width = g.shape
    tokens = q.shape[0]
    any_ = pl.BlockSpec(memory_space=pl.ANY)
    vmem = pl.BlockSpec(memory_space=pltpu.VMEM)
    dma, buf = pltpu.SemaphoreType.DMA, pltpu.VMEM
    share = width // 32
    cols = w_qkv.shape[1]
    return pl.pallas_call(
        back_kernel,
        out_shape=(
            jax.ShapeDtypeStruct((rows, width), F32),
            jax.ShapeDtypeStruct((2, share, 32 * gate_g.shape[1]), BF16),
            jax.ShapeDtypeStruct((NZ, share, 8 * cols), BF16),
            jax.ShapeDtypeStruct((NZ, share, width), BF16),
        ),
        in_specs=[vmem] * 12 + [any_] * 3,
        out_specs=(vmem,) + (any_,) * 3,
        scratch_shapes=[
            buf((8, rows, width), BF16), buf(q.shape, BF16), buf((tokens, cols), BF16), buf(k.shape, F32), buf(v.shape, F32),
            buf(w_out.shape, BF16), buf((width, cols), BF16), buf(normed.shape, BF16),
            dma((2, 32)), dma((2, 32)), dma((32,)), dma((32,)), dma((4,)), dma((4,)), dma((6,)), dma((8,)), dma((8,)),
        ] + scatter_scratch(1, rows, width),
        compiler_params=pltpu.CompilerParams(collective_id=6, has_side_effects=True, vmem_limit_bytes=60 << 20),
        cost_estimate=takes(110),
        name="attention_back",
    )(g, q, k, v, attn, cosine, sine, first, place, keys, w_qkv, w_out, normed, gate_g, up_g)


class Line:
    def __init__(self, c, z, slot, send, recv):
        self.c, self.z, self.slot, self.send, self.recv = c, z, slot, send, recv
        self.order = plane_order(z)

    def hop(self, up, t):
        zz = self.order[t]
        row = 0 if up else 1
        return remote(
            self.slot(zz), self.slot(zz), self.send.at[row, zz], self.recv.at[zz], (self.c, self.z + (1 if up else -1))
        )

    def hops(self, t, act):
        zz, z = self.order[t], self.z

        @pl.when((zz <= z) & (z < NZ - 1))
        def _():
            act(self.hop(True, t))

        @pl.when((zz >= z) & (z > 0))
        def _():
            act(self.hop(False, t))

    def step(self, t):
        if t > 0:
            self.hop(True, t).wait_recv()
        self.hops(t, lambda cp: cp.start())

    def end(self):
        for t in range(NZ):
            self.hops(t, lambda cp: cp.wait_send())


def front_kernel(
    x_ref, g_ref, wq_ref, wk_ref, wv_ref, wo_ref, wd_ref, cos_ref, sin_ref, first_ref, place_ref, keys_ref,
    o_ref, norm_o, wqkv, go_ref, outr, downr, q_ref, k_ref, v_ref, attn_ref,
    normed, nall, acc, tmp_o, tmp_d,
    lsem, gsend, grecv, qzsend, qzrecv, ozsend, ozrecv, dsend, drecv, o2send, o2recv, d2send, d2recv, psend, precv, *scat
):
    here = place_on_plane()
    c, z, sib, xn, yn, diag = here
    rows, width = x_ref.shape
    tokens = 8 * rows
    wide = tmp_o.shape[2]
    mates = [lax.rem(c + s, 8) for s in range(1, 8)]
    others = [lax.rem(z + s, NZ) for s in (1, 2, 3)]
    meet([(m, z) for m in mates] + [(c, t) for t in others])
    sums = Scatter(here, [z], *scat)
    plane = Plane(here, lambda j: nall.at[j], psend, precv, rows // 2)
    line_q = Line(c, z, lambda zz: wqkv.at[zz], qzsend, qzrecv)
    line_o = Line(c, z, lambda zz: tmp_o.at[zz], ozsend, ozrecv)
    own_cols = pl.ds(pl.multiple_of(c * wide, wide), wide)

    def narrow(ref, n):
        return ref.at[:, pl.ds(pl.multiple_of(c * n, n), n)]

    q_keeps = [
        pltpu.make_async_copy(narrow(wq_ref, wide), wqkv.at[z, :, pl.ds(0, wide)], lsem.at[0]),
        pltpu.make_async_copy(narrow(wk_ref, HEAD_SIZE), wqkv.at[z, :, pl.ds(wide, HEAD_SIZE)], lsem.at[1]),
        pltpu.make_async_copy(narrow(wv_ref, HEAD_SIZE), wqkv.at[z, :, pl.ds(wide + HEAD_SIZE, HEAD_SIZE)], lsem.at[2]),
    ]
    o_keep = pltpu.make_async_copy(wo_ref.at[:, own_cols], tmp_o.at[z], lsem.at[3])
    d_keeps, downs = [], []
    for core in range(2):
        for hop in range(NZ):
            to = lax.rem(z + hop, NZ)
            src = wd_ref.at[pl.ds(pl.multiple_of((core * NZ + to) * wide, wide), wide), own_cols]
            if hop == 0:
                d_keeps.append(pltpu.make_async_copy(src, tmp_d.at[z, core], lsem.at[4 + core]))
            else:
                downs.append(remote(src, tmp_d.at[z, core], dsend.at[core, hop], drecv.at[core, hop], (c, to)))
    for cp in q_keeps + [o_keep] + d_keeps:
        cp.start()
    go_ref[z] = g_ref[...]
    gains = [remote(g_ref, go_ref.at[z], gsend.at[s], grecv.at[s], (c, t)) for s, t in enumerate(others)]
    for cp in gains:
        cp.start()
    for cp in q_keeps:
        cp.wait()
    line_q.step(0)

    x = x_ref[...].astype(F32)
    scaled = x * lax.rsqrt(jnp.mean(x * x, axis=-1, keepdims=True) + EPS)
    for cp in gains:
        cp.wait()
    piece = width // NZ
    for zz in range(NZ):
        normed[:, zz * piece : (zz + 1) * piece] = (
            scaled[:, zz * piece : (zz + 1) * piece] * go_ref[zz, 0:1, :]
        ).astype(BF16)
    for cp in plane.first(normed):
        cp.start()
    nall[c] = normed[...]
    line_q.step(1)
    for arrived, sends in zip(plane.arrive(), plane.second()):
        arrived.wait_recv()
        for cp in sends:
            cp.start()
    line_q.step(2)
    o_keep.wait()
    line_o.step(0)
    for cp in plane.diagonal():
        cp.wait_recv()
    plane.third().start()
    for cp in plane.across():
        cp.wait_recv()
    norm_keep = pltpu.make_async_copy(nall, norm_o, lsem.at[6])
    norm_keep.start()

    def project(t):
        zz = line_q.order[t]
        at = pl.ds(pl.multiple_of(zz * piece, piece), piece)
        term = jnp.dot(nall[:, :, at].reshape(tokens, piece), wqkv[zz], preferred_element_type=F32)
        acc[...] = term if t == 0 else acc[...] + term

    for t in range(3):
        project(t)
    line_q.step(3)
    line_o.step(1)
    project(3)

    def heads(i, _):
        at = pl.ds(pl.multiple_of(i * ROWS_AT_ONCE, ROWS_AT_ONCE), ROWS_AT_ONCE)
        cosine, sine = cos_ref[at, :], sin_ref[at, :]
        for h in range(wide // HEAD_SIZE):
            lanes = slice(h * HEAD_SIZE, (h + 1) * HEAD_SIZE)
            q_ref[at, lanes] = turn(acc[at, lanes], cosine, sine).astype(BF16)
        k_ref[at, :] = turn(acc[at, wide : wide + HEAD_SIZE], cosine, sine).astype(BF16)
        v_ref[at, :] = acc[at, wide + HEAD_SIZE :].astype(BF16)
        return 0

    lax.fori_loop(0, tokens // ROWS_AT_ONCE, heads, 0)
    line_o.step(2)

    def attend(i, _):
        at = pl.ds(pl.multiple_of(i * ROWS_AT_ONCE, ROWS_AT_ONCE), ROWS_AT_ONCE)
        k, v = k_ref[...], v_ref[...]
        first, place, keys = first_ref[at, :], place_ref[at, :], keys_ref[...]
        for h in range(wide // HEAD_SIZE):
            lanes = slice(h * HEAD_SIZE, (h + 1) * HEAD_SIZE)
            probs = block_probs(q_ref[at, lanes], k, first, place, keys)
            attn_ref[at, lanes] = jnp.dot(probs.astype(BF16), v, preferred_element_type=F32).astype(BF16)
        return 0

    lax.fori_loop(0, 2, attend, 0)
    line_o.step(3)
    for cp in downs:
        cp.start()

    def regroup(buf, dst, send, recv, lrow):
        def block(j):
            return buf(j // 2, lax.rem(j, 2))

        out = [remote(block(m), dst.at[:, own_cols], send.at[s], recv.at[s], (m, z)) for s, m in enumerate(mates)]
        keep = pltpu.make_async_copy(block(c), dst.at[:, own_cols], lsem.at[lrow])
        for cp in out + [keep]:
            cp.start()
        return out + [keep]

    moved_o = regroup(lambda p, core: tmp_o.at[p, pl.ds(pl.multiple_of(core * wide, wide), wide)], outr, o2send, o2recv, 7)
    lax.fori_loop(2, tokens // ROWS_AT_ONCE, attend, 0)
    for cp in moved_o:
        cp.wait()
    for b in (3, 1, 2, 0):
        at = pl.ds(pl.multiple_of(chip_at(c, b) * ROWS_AT_ONCE, ROWS_AT_ONCE), ROWS_AT_ONCE)
        p = jnp.dot(attn_ref[at, :], outr[...], preferred_element_type=F32).astype(BF16)
        sums.part[0, b] = p.reshape(2, rows, width)
        sums.cross(0, b).start()
    sums.one(0)
    sums.two(0)
    for cp in d_keeps + downs:
        cp.wait()
    moved_d = regroup(lambda p, core: tmp_d.at[p, core], downr, d2send, d2recv, 8)
    sums.three(0, o_ref)
    sums.end(o_ref)
    for cp in moved_d:
        cp.wait()
    for cp in plane.first(normed) + plane.second()[0] + plane.second()[1] + [plane.third()]:
        cp.wait_send()
    line_q.end()
    line_o.end()
    norm_keep.wait()


def attention_front(x, gains, w_query, w_key, value_weight, w_output, w_down, cosine, sine, first, place, keys):
    rows, width = x.shape
    tokens = 8 * rows
    depth = w_query.shape[0]
    wide = width // 8
    any_ = pl.BlockSpec(memory_space=pl.ANY)
    vmem = pl.BlockSpec(memory_space=pltpu.VMEM)
    dma, buf, out = pltpu.SemaphoreType.DMA, pltpu.VMEM, jax.ShapeDtypeStruct
    return pl.pallas_call(
        front_kernel,
        out_shape=(
            out((rows, width), F32),
            out((8, rows, width), BF16),
            out((NZ, depth, 2 * wide), BF16),
            out((NZ,) + gains.shape, F32),
            out((wide, width), BF16),
            out((wide, width), BF16),
            out((tokens, wide), BF16),
            out((tokens, HEAD_SIZE), BF16),
            out((tokens, HEAD_SIZE), BF16),
            out((tokens, wide), BF16),
        ),
        in_specs=[vmem] * 2 + [any_] * 5 + [vmem] * 5,
        out_specs=(vmem, any_) + (vmem,) * 8,
        scratch_shapes=[
            buf((rows, width), BF16), buf((8, rows, width), BF16), buf((tokens, 2 * wide), F32), buf((NZ, depth, wide), BF16),
            buf((NZ, 2, wide, wide), BF16),
            dma((9,)), dma((3,)), dma((3,)), dma((2, 4)), dma((4,)), dma((2, 4)), dma((4,)), dma((2, 4)), dma((2, 4)),
            dma((7,)), dma((7,)), dma((7,)), dma((7,)), dma((8,)), dma((8,)),
        ] + scatter_scratch(1, rows, width),
        compiler_params=pltpu.CompilerParams(collective_id=8, has_side_effects=True, vmem_limit_bytes=60 << 20),
        cost_estimate=takes(95),
        name="attention_front",
    )(x, gains, w_query, w_key, value_weight, w_output, w_down, cosine, sine, first, place, keys)


def tile_of(value):
    return jnp.full((8, 128), value, F32)


def heads_and_columns(
    hidden_in,
    cotangent,
    teacher,
    valid_mask,
    doc_starts,
    attn_gain,
    w_query,
    w_key,
    value_weight,
    w_output,
    mlp_gain,
    w_gate,
    w_up,
    w_down,
):
    rows, width = hidden_in.shape[1:]
    c = lax.axis_index("ctx")
    z = lax.axis_index("fsdp")
    devices = lax.axis_size("ctx")
    tokens = rows * devices
    group = QUERY_HEADS // KEY_VALUE_HEADS
    qcols = group * HEAD_SIZE
    ffcols = FF // (devices * NZ)

    layer_input = hidden_in[0].astype(F32)
    gains = jnp.concatenate(
        [attn_gain.astype(F32)[None], mlp_gain.astype(F32)[None], jnp.zeros((6, attn_gain.shape[0]), F32)]
    )
    place, segment, offset = stream_places(tokens, rows, devices, doc_starts[0])
    freq = ROPE_BASE ** (-(jnp.arange(HEAD_SIZE // 2, dtype=F32) * 2.0 / HEAD_SIZE))
    angle = offset.astype(F32)[:, None] * freq[None, :]
    cosine = jnp.concatenate([jnp.cos(angle)] * 2, axis=1)
    sine = jnp.concatenate([-jnp.sin(angle), jnp.sin(angle)], axis=1)
    columns = ((place - offset)[:, None], place[:, None], place[None, :])
    branch, normed_all, w_qkv, gains_all, out_rows, down_rows, q, k, v, attn = attention_front(
        hidden_in[0], gains, w_query, w_key, value_weight, w_output, w_down, cosine, sine, *columns
    )
    attn_scale = gains_all[:, 0, :].reshape(1, width)
    mlp_scale = gains_all[:, 1, :].reshape(1, width)
    residual = layer_input + branch

    r2 = rms_norm_scale(residual)
    hat2 = residual * r2
    normed2 = (hat2 * mlp_scale).astype(BF16)
    maskf = valid_mask[0].astype(F32)
    mlp_out, normed2_all, counts, gate_up, w_mlp = feed_forward(
        normed2, tile_of(jnp.sum(maskf)), w_gate, w_up, down_rows
    )
    count = jnp.sum(counts[:, 0, 0])
    outf = residual + mlp_out

    diff = outf - teacher[0].astype(F32)
    error_here = jnp.sum(maskf * jnp.mean(diff * diff, axis=-1))
    g_out = cotangent[0].astype(F32) + maskf[:, None] * diff * (2.0 / (count * width))
    g_norm2, _, errors, gate_grads, up_grads, down_grads = feed_back(
        g_out.astype(BF16), tile_of(error_here), w_mlp, down_rows, normed2_all, gate_up
    )
    loss = jnp.sum(errors[:, 0, 0]) / count
    g_hat2 = g_norm2 * mlp_scale
    g_residual = g_out + r2 * (g_hat2 - hat2 * jnp.mean(g_hat2 * hat2, axis=-1, keepdims=True))
    g_norm1, got, got_qkv, got_out = attention_back(
        g_residual.astype(BF16), q, k, v, attn, cosine, sine, *columns, w_qkv.reshape(width, -1), out_rows,
        normed_all.reshape(tokens, width),
        gate_grads, up_grads,
    )

    r1 = rms_norm_scale(layer_input)
    hat1 = layer_input * r1
    g_hat1 = g_norm1 * attn_scale
    g_input = g_residual + r1 * (g_hat1 - hat1 * jnp.mean(g_hat1 * hat1, axis=-1, keepdims=True))

    both = ("ctx", "fsdp")
    parts = devices * NZ

    share = width // parts
    got = got.astype(F32)
    got_qkv = jnp.sum(got_qkv.astype(F32), axis=0).reshape(share, devices, 2 * qcols)
    got_out = jnp.sum(got_out.astype(F32), axis=0)
    gain_terms = jnp.stack([jnp.sum(g_norm1 * hat1, axis=0), jnp.sum(g_norm2 * hat2, axis=0)])
    gain_terms = gain_terms.reshape(2, parts, share).transpose(1, 0, 2).reshape(parts, 1, 2 * share)
    got_gains = jnp.sum(lax.all_to_all(gain_terms, both, 0, 0, tiled=True), axis=(0, 1))
    return (
        loss,
        outf.astype(BF16)[None],
        g_input.astype(BF16)[None],
        got_gains[:share],
        got_qkv[:, :, :qcols].reshape(share, QUERY_HEADS * HEAD_SIZE),
        got_qkv[:, :, qcols : qcols + HEAD_SIZE].reshape(share, KEY_VALUE_HEADS * HEAD_SIZE),
        got_qkv[:, :, qcols + HEAD_SIZE :].reshape(share, KEY_VALUE_HEADS * HEAD_SIZE),
        got_out,
        got_gains[share:],
        got[0],
        got[1],
        down_grads,
    )


def solution(mesh):
    small = dict(mesh.shape) == {"ctx": KEY_VALUE_HEADS, "fsdp": NZ}
    in_specs = (
        P("fsdp", "ctx", None),
        P("fsdp", "ctx", None),
        P("fsdp", "ctx", None),
        P("fsdp", "ctx"),
        P("fsdp", None),
        P("fsdp"),
        P("fsdp", None),
        P("fsdp", None),
        P("fsdp", None),
        P("fsdp", None),
        P("fsdp"),
        P("fsdp", None),
        P("fsdp", None),
        P("fsdp", None),
    )
    out_specs = (
        P(),
        P("fsdp", "ctx", None),
        P("fsdp", "ctx", None),
        P(("ctx", "fsdp")),
        P(("ctx", "fsdp"), None),
        P(("ctx", "fsdp"), None),
        P(("ctx", "fsdp"), None),
        P(("ctx", "fsdp"), None),
        P(("ctx", "fsdp")),
        P(("ctx", "fsdp"), None),
        P(("ctx", "fsdp"), None),
        P(("ctx", "fsdp"), None),
    )
    return jax.shard_map(
        heads_and_columns if small else per_device, mesh=mesh, in_specs=in_specs, out_specs=out_specs, check_vma=False
    )
```

```python
import functools

import jax
import jax.numpy as jnp
from jax import lax
from jax.experimental import pallas as pl
from jax.experimental.pallas import tpu as pltpu
from jax.sharding import PartitionSpec as P

QUERY_HEADS = 16
KEY_VALUE_HEADS = 8
HEAD_SIZE = 128
FF = 8192


EPS = 1e-05
ROPE_BASE = 1000000.0
NEG = -1e30
CONTRACT_ROWS = (((0,), (0,)), ((), ()))
CONTRACT_COLS = (((1,), (1,)), ((), ()))


def stream_places(rows, local_token_count, devices, starts):
    span = local_token_count // 2
    rowid = jnp.arange(rows, dtype=jnp.int32)
    device = rowid // local_token_count
    within = rowid % local_token_count
    span_id = jnp.where(within < span, device, 2 * devices - 1 - device)
    place = span_id * span + within % span
    before = starts[None, :] <= place[:, None]
    segment = jnp.sum(before.astype(jnp.int32), axis=1) - 1
    first = jnp.max(jnp.where(before, starts[None, :], 0), axis=1)
    return (place, segment, place - first)


def rotary_embed(values, token_offset, sign):
    half = HEAD_SIZE // 2
    freq = ROPE_BASE ** (-(jnp.arange(half, dtype=jnp.float32) * 2.0 / HEAD_SIZE))
    angle = token_offset.astype(jnp.float32)[:, None] * freq[None, :]
    cosine = jnp.cos(angle)[:, None, :]
    sine = sign * jnp.sin(angle)[:, None, :]
    first = values[..., :half]
    second = values[..., half:]
    return jnp.concatenate(
        [first * cosine - second * sine, second * cosine + first * sine], axis=-1
    )


def rms_norm_scale(values):
    return lax.rsqrt(jnp.mean(values * values, axis=-1, keepdims=True) + EPS)


def head_scores(query_rows, key_rows, allowed):
    attention_scores = jnp.einsum(
        "trd,sd->rts", query_rows, key_rows, preferred_element_type=jnp.float32
    ) * HEAD_SIZE ** (-0.5)
    return jnp.where(allowed[None], attention_scores, NEG)


def per_device(
    hidden_in,
    cotangent,
    teacher,
    valid_mask,
    doc_starts,
    attn_gain,
    w_query,
    w_key,
    value_weight,
    w_output,
    mlp_gain,
    w_gate,
    w_up,
    w_down,
):
    local_token_count = hidden_in.shape[1]
    width = hidden_in.shape[2]
    devices = lax.axis_size("ctx")
    index = lax.axis_index("ctx")
    packed_stream_rows = local_token_count * devices
    query_group = QUERY_HEADS // KEY_VALUE_HEADS
    place, segment, token_offset = stream_places(
        packed_stream_rows, local_token_count, devices, doc_starts[0]
    )
    own_start = index * local_token_count
    my_place = lax.dynamic_slice_in_dim(place, own_start, local_token_count)
    my_segment = lax.dynamic_slice_in_dim(segment, own_start, local_token_count)
    local_stream_offset = lax.dynamic_slice_in_dim(token_offset, own_start, local_token_count)
    allowed = (my_segment[:, None] == segment[None, :]) & (place[None, :] <= my_place[:, None])
    layer_input = hidden_in[0].astype(jnp.float32)
    attn_whole = (
        lax.all_gather(attn_gain, "fsdp", axis=0, tiled=True),
        lax.all_gather(w_query, "fsdp", axis=0, tiled=True),
        lax.all_gather(w_key, "fsdp", axis=0, tiled=True),
        lax.all_gather(value_weight, "fsdp", axis=0, tiled=True),
        lax.all_gather(w_output, "fsdp", axis=0, tiled=True),
    )
    first_norm_scale = attn_whole[0].astype(jnp.float32)
    first_inverse_norm = rms_norm_scale(layer_input)
    first_normalized_input = layer_input * first_inverse_norm
    first_normed = (first_normalized_input * first_norm_scale).astype(jnp.bfloat16)
    qproj = jnp.dot(first_normed, attn_whole[1], preferred_element_type=jnp.float32)
    key_projected = jnp.dot(first_normed, attn_whole[2], preferred_element_type=jnp.float32)
    vproj = jnp.dot(first_normed, attn_whole[3], preferred_element_type=jnp.float32).astype(
        jnp.bfloat16
    )
    query_rows = rotary_embed(
        qproj.reshape(local_token_count, QUERY_HEADS, HEAD_SIZE), local_stream_offset, 1.0
    ).astype(jnp.bfloat16)
    key_rows = (
        rotary_embed(
            key_projected.reshape(local_token_count, KEY_VALUE_HEADS, HEAD_SIZE),
            local_stream_offset,
            1.0,
        )
        .reshape(local_token_count, KEY_VALUE_HEADS * HEAD_SIZE)
        .astype(jnp.bfloat16)
    )
    every_key_row, every_value_row = (
        lax.all_gather(key_rows, "ctx", axis=0, tiled=True),
        lax.all_gather(vproj, "ctx", axis=0, tiled=True),
    )
    key_head_rows = every_key_row.reshape(packed_stream_rows, KEY_VALUE_HEADS, HEAD_SIZE).transpose(
        1, 0, 2
    )
    value_head_rows = every_value_row.reshape(
        packed_stream_rows, KEY_VALUE_HEADS, HEAD_SIZE
    ).transpose(1, 0, 2)
    query_head_rows = query_rows.reshape(
        local_token_count, KEY_VALUE_HEADS, query_group, HEAD_SIZE
    ).transpose(1, 0, 2, 3)

    def attend_head(parts):
        head_query, head_key, head_val = parts
        attention_scores = head_scores(head_query, head_key, allowed)
        top = jnp.max(attention_scores, axis=-1, keepdims=True)
        lse = top + jnp.log(jnp.sum(jnp.exp(attention_scores - top), axis=-1, keepdims=True))
        attention_probabilities = jnp.exp(attention_scores - lse)
        mixed_heads = jnp.einsum(
            "rts,sd->trd",
            attention_probabilities.astype(jnp.bfloat16),
            head_val,
            preferred_element_type=jnp.float32,
        )
        return (mixed_heads, lse)

    mixed_heads, lse = lax.map(attend_head, (query_head_rows, key_head_rows, value_head_rows))
    attn = (
        mixed_heads.transpose(1, 0, 2, 3)
        .reshape(local_token_count, QUERY_HEADS * HEAD_SIZE)
        .astype(jnp.bfloat16)
    )
    residual_state = layer_input + jnp.dot(attn, attn_whole[4], preferred_element_type=jnp.float32)
    mlp_whole = (
        lax.all_gather(mlp_gain, "fsdp", axis=0, tiled=True),
        lax.all_gather(w_gate, "fsdp", axis=0, tiled=True),
        lax.all_gather(w_up, "fsdp", axis=0, tiled=True),
        lax.all_gather(w_down, "fsdp", axis=0, tiled=True),
    )
    second_norm_scale = mlp_whole[0].astype(jnp.float32)
    second_inverse_norm = rms_norm_scale(residual_state)
    second_normalized_input = residual_state * second_inverse_norm
    second_normed = (second_normalized_input * second_norm_scale).astype(jnp.bfloat16)
    gate = jnp.dot(second_normed, mlp_whole[1], preferred_element_type=jnp.float32)
    up_val = jnp.dot(second_normed, mlp_whole[2], preferred_element_type=jnp.float32)
    sigma = jax.nn.sigmoid(gate)
    act = (gate * sigma * up_val).astype(jnp.bfloat16)
    outf = residual_state + jnp.dot(act, mlp_whole[3], preferred_element_type=jnp.float32)
    maskf = valid_mask[0].astype(jnp.float32)
    diff = outf - teacher[0].astype(jnp.float32)
    count_here = jnp.sum(maskf)
    error_here = jnp.sum(maskf * jnp.mean(diff * diff, axis=-1))
    count, error_total = lax.psum((count_here, error_here), ("ctx", "fsdp"))
    loss = error_total / count
    output_gradient = cotangent[0].astype(jnp.float32) + maskf[:, None] * diff * (
        2.0 / (count * width)
    )
    g_mo = output_gradient.astype(jnp.bfloat16)
    mlp_back = (
        lax.all_gather(mlp_gain, "fsdp", axis=0, tiled=True),
        lax.all_gather(w_gate, "fsdp", axis=0, tiled=True),
        lax.all_gather(w_up, "fsdp", axis=0, tiled=True),
        lax.all_gather(w_down, "fsdp", axis=0, tiled=True),
    )
    g_act = lax.dot_general(g_mo, mlp_back[3], CONTRACT_COLS, preferred_element_type=jnp.float32)
    g_gate = (g_act * up_val * sigma * (1.0 + gate * (1.0 - sigma))).astype(jnp.bfloat16)
    g_up = (g_act * gate * sigma).astype(jnp.bfloat16)
    gate_up_gradient = jnp.concatenate([g_gate, g_up], axis=1)
    second_norm_gradient = lax.dot_general(
        g_gate, mlp_back[1], CONTRACT_COLS, preferred_element_type=jnp.float32
    )
    second_norm_gradient = second_norm_gradient + lax.dot_general(
        g_up, mlp_back[2], CONTRACT_COLS, preferred_element_type=jnp.float32
    )
    second_hat_gradient = second_norm_gradient * second_norm_scale
    residual_gradient = output_gradient + second_inverse_norm * (
        second_hat_gradient
        - second_normalized_input
        * jnp.mean(second_hat_gradient * second_normalized_input, axis=-1, keepdims=True)
    )
    mlp_share = lax.psum_scatter(
        lax.dot_general(
            second_normed, gate_up_gradient, CONTRACT_ROWS, preferred_element_type=jnp.float32
        ),
        ("ctx", "fsdp"),
        scatter_dimension=0,
        tiled=True,
    )
    down_share = lax.psum_scatter(
        lax.dot_general(act, g_mo, CONTRACT_ROWS, preferred_element_type=jnp.float32),
        ("ctx", "fsdp"),
        scatter_dimension=0,
        tiled=True,
    )
    g_branch = residual_gradient.astype(jnp.bfloat16)
    attn_back = (
        lax.all_gather(attn_gain, "fsdp", axis=0, tiled=True),
        lax.all_gather(w_query, "fsdp", axis=0, tiled=True),
        lax.all_gather(w_key, "fsdp", axis=0, tiled=True),
        lax.all_gather(value_weight, "fsdp", axis=0, tiled=True),
        lax.all_gather(w_output, "fsdp", axis=0, tiled=True),
    )
    attention_gradient = lax.dot_general(
        g_branch, attn_back[4], CONTRACT_COLS, preferred_element_type=jnp.float32
    ).astype(jnp.bfloat16)
    heads_gradient = attention_gradient.reshape(
        local_token_count, KEY_VALUE_HEADS, query_group, HEAD_SIZE
    ).transpose(1, 0, 2, 3)

    def attend_back(parts):
        head_query, head_key, head_val, head_lse, head_grad = parts
        attention_probabilities = jnp.exp(head_scores(head_query, head_key, allowed) - head_lse)
        g_probs = jnp.einsum("trd,sd->rts", head_grad, head_val, preferred_element_type=jnp.float32)
        delta = jnp.sum(attention_probabilities * g_probs, axis=-1, keepdims=True)
        g_scores = (attention_probabilities * (g_probs - delta)).astype(jnp.bfloat16)
        g_query = jnp.einsum(
            "rts,sd->trd", g_scores, head_key, preferred_element_type=jnp.float32
        ) * HEAD_SIZE ** (-0.5)
        key_gradient = jnp.einsum(
            "rts,trd->sd", g_scores, head_query, preferred_element_type=jnp.float32
        ) * HEAD_SIZE ** (-0.5)
        value_gradient = jnp.einsum(
            "rts,trd->sd",
            attention_probabilities.astype(jnp.bfloat16),
            head_grad,
            preferred_element_type=jnp.float32,
        )
        return (g_query, key_gradient, value_gradient)

    g_query, key_gradient, value_gradient = lax.map(
        attend_back, (query_head_rows, key_head_rows, value_head_rows, lse, heads_gradient)
    )
    key_gradient_terms = key_gradient.transpose(1, 0, 2).reshape(
        packed_stream_rows, KEY_VALUE_HEADS * HEAD_SIZE
    )
    value_gradient_terms = value_gradient.transpose(1, 0, 2).reshape(
        packed_stream_rows, KEY_VALUE_HEADS * HEAD_SIZE
    )
    key_rows_gradient, g_vals = (
        lax.psum_scatter(
            key_gradient_terms.astype(jnp.bfloat16), "ctx", scatter_dimension=0, tiled=True
        ).astype(jnp.float32),
        lax.psum_scatter(
            value_gradient_terms.astype(jnp.bfloat16), "ctx", scatter_dimension=0, tiled=True
        ).astype(jnp.float32),
    )
    g_qproj = (
        rotary_embed(
            g_query.transpose(1, 0, 2, 3).reshape(local_token_count, QUERY_HEADS, HEAD_SIZE),
            local_stream_offset,
            -1.0,
        )
        .reshape(local_token_count, QUERY_HEADS * HEAD_SIZE)
        .astype(jnp.bfloat16)
    )
    g_kproj = (
        rotary_embed(
            key_rows_gradient.reshape(local_token_count, KEY_VALUE_HEADS, HEAD_SIZE),
            local_stream_offset,
            -1.0,
        )
        .reshape(local_token_count, KEY_VALUE_HEADS * HEAD_SIZE)
        .astype(jnp.bfloat16)
    )
    g_vproj = g_vals.astype(jnp.bfloat16)
    first_norm_gradient = lax.dot_general(
        g_qproj, attn_back[1], CONTRACT_COLS, preferred_element_type=jnp.float32
    )
    first_norm_gradient = first_norm_gradient + lax.dot_general(
        g_kproj, attn_back[2], CONTRACT_COLS, preferred_element_type=jnp.float32
    )
    first_norm_gradient = first_norm_gradient + lax.dot_general(
        g_vproj, attn_back[3], CONTRACT_COLS, preferred_element_type=jnp.float32
    )
    first_hat_gradient = first_norm_gradient * first_norm_scale
    g_input = residual_gradient + first_inverse_norm * (
        first_hat_gradient
        - first_normalized_input
        * jnp.mean(first_hat_gradient * first_normalized_input, axis=-1, keepdims=True)
    )
    key_value_proj_gradient = jnp.concatenate([g_kproj, g_vproj], axis=1)
    query_term = lax.dot_general(
        first_normed, g_qproj, CONTRACT_ROWS, preferred_element_type=jnp.float32
    )
    key_value_term = lax.dot_general(
        first_normed, key_value_proj_gradient, CONTRACT_ROWS, preferred_element_type=jnp.float32
    )
    output_term = lax.dot_general(attn, g_branch, CONTRACT_ROWS, preferred_element_type=jnp.float32)
    scale_gradient_terms = jnp.stack(
        [
            jnp.sum(first_norm_gradient * first_normalized_input, axis=0),
            jnp.sum(second_norm_gradient * second_normalized_input, axis=0),
        ]
    )
    query_share, key_value_share, output_share, gain_share = (
        lax.psum_scatter(query_term, ("ctx", "fsdp"), scatter_dimension=0, tiled=True),
        lax.psum_scatter(key_value_term, ("ctx", "fsdp"), scatter_dimension=0, tiled=True),
        lax.psum_scatter(output_term, ("ctx", "fsdp"), scatter_dimension=0, tiled=True),
        lax.psum_scatter(scale_gradient_terms, ("ctx", "fsdp"), scatter_dimension=1, tiled=True),
    )
    key_value_columns = KEY_VALUE_HEADS * HEAD_SIZE
    return (
        loss,
        outf.astype(jnp.bfloat16)[None],
        g_input.astype(jnp.bfloat16)[None],
        gain_share[0],
        query_share,
        key_value_share[:, :key_value_columns],
        key_value_share[:, key_value_columns:],
        output_share,
        gain_share[1],
        mlp_share[:, :FF],
        mlp_share[:, FF:],
        down_share,
    )


MESH = pl.DeviceIdType.MESH
F32 = jnp.float32
BF16 = jnp.bfloat16
NZ = 4


def place_on_plane():
    c = lax.axis_index("ctx")
    z = lax.axis_index("fsdp")
    sib = c + 1 - 2 * lax.rem(c, 2)
    xn = c + 2 - 4 * lax.rem(c // 2, 2)
    yn = c + 4 - 8 * (c // 4)
    diag = xn + yn - c
    return c, z, sib, xn, yn, diag


def meet(devices):
    barrier = pltpu.get_barrier_semaphore()
    for d in devices:
        pl.semaphore_signal(barrier, inc=1, device_id=d, device_id_type=MESH)
    pl.semaphore_wait(barrier, len(devices))


def remote(src, dst, send, recv, device):
    return pltpu.make_async_remote_copy(
        src_ref=src, dst_ref=dst, send_sem=send, recv_sem=recv, device_id=device, device_id_type=MESH
    )


def takes(micros):
    return pl.CostEstimate(flops=0, bytes_accessed=micros * 3_500_000, transcendentals=0)


class Plane:
    def __init__(self, here, slot, send, recv, half):
        self.c, self.z, self.sib, self.xn, self.yn, self.diag = here
        self.slot, self.send, self.recv, self.half = slot, send, recv, half

    def copy(self, kind, src, dst, to):
        return remote(src, dst, self.send.at[kind], self.recv.at[kind], (to, self.z))

    def first(self, src):
        mine = self.slot(self.c)
        return [self.copy(0, src, mine, self.xn), self.copy(1, src, mine, self.yn), self.copy(2, src, mine, self.sib)]

    def arrive(self):
        s = self.slot
        return [self.copy(0, s(self.xn), s(self.xn), self.xn), self.copy(1, s(self.yn), s(self.yn), self.yn)]

    def second(self):
        h = self.half
        s = self.slot
        ybot = s(self.yn).at[pl.ds(0, h)]
        xtop = s(self.xn).at[pl.ds(h, h)]
        return (
            [self.copy(4, xtop, xtop, self.yn), self.copy(5, s(self.xn), s(self.xn), self.sib)],
            [self.copy(3, ybot, ybot, self.xn), self.copy(6, s(self.yn), s(self.yn), self.sib)],
        )

    def diagonal(self):
        h = self.half
        lo, hi = self.slot(self.diag).at[pl.ds(0, h)], self.slot(self.diag).at[pl.ds(h, h)]
        return [self.copy(3, lo, lo, self.xn), self.copy(4, hi, hi, self.yn)]

    def third(self):
        d = self.slot(self.diag)
        return self.copy(7, d, d, self.sib)

    def across(self):
        s = self.slot
        return [self.copy(k, s(j), s(j), self.sib) for k, j in ((2, self.sib), (5, self.xn + self.sib - self.c), (6, self.yn + self.sib - self.c), (7, self.diag + self.sib - self.c))]


def add_rows(dst, parts, chunk=16):
    n = dst.shape[0] // chunk

    def body(i, _):
        at = pl.ds(pl.multiple_of(i * chunk, chunk), chunk)
        total = parts[0][at, :].astype(F32)
        for p in parts[1:]:
            total = total + p[at, :].astype(F32)
        dst[at, :] = total.astype(dst.dtype)
        return 0

    lax.fori_loop(0, n, body, 0)


def plane_order(z):
    pick = jnp.where
    return [z, pick(z == 0, 1, z - 1), pick(z == 3, 1, pick(z == 2, 3, 2)), pick(z < 2, 3, 0)]


def chip_at(c, b):
    x, y = lax.rem(c // 2, 2), c // 4
    xb, yb = lax.rem(b, 2), b // 2
    return (x + xb - 2 * x * xb) + 2 * (y + yb - 2 * y * yb)


def chunk_order(i):
    return jnp.where(i == 0, 3, jnp.where(i == 3, 0, i))


class Gather:
    def __init__(self, here, x_ref, o_ref, keep, zsend, zrecv, send, recv):
        self.here, self.x, self.o = here, x_ref, o_ref
        self.c, self.z = here[0], here[1]
        self.order = plane_order(self.z)
        self.zsend, self.zrecv = zsend, zrecv
        self.planes = [
            Plane(here, functools.partial(lambda zz, j: o_ref.at[zz, j], zz), send.at[zz], recv.at[zz], x_ref.shape[0] // 2)
            for zz in self.order
        ]
        self.keep = pltpu.make_async_copy(x_ref, o_ref.at[self.z, self.c], keep)

    def hop(self, up, t):
        zz = self.order[t]
        src = self.x if t == 0 else self.o.at[zz, self.c]
        row = 0 if up else 1
        return remote(
            src, self.o.at[zz, self.c], self.zsend.at[row, zz], self.zrecv.at[zz], (self.c, self.z + (1 if up else -1))
        )

    def hops(self, t, act):
        zz, z = self.order[t], self.z

        @pl.when((zz <= z) & (z < NZ - 1))
        def _():
            act(self.hop(True, t))

        @pl.when((zz >= z) & (z > 0))
        def _():
            act(self.hop(False, t))

    def spread(self, t):
        if t > 0:
            self.hop(True, t).wait_recv()
        self.hops(t, lambda cp: cp.start())
        for cp in self.planes[t].first(self.source(t)):
            cp.start()

    def source(self, t):
        return self.x if t == 0 else self.o.at[self.order[t], self.c]

    def onward(self, t):
        p = self.planes[t]
        for arrived, sends in zip(p.arrive(), p.second()):
            arrived.wait_recv()
            for cp in sends:
                cp.start()

    def close(self, t):
        p = self.planes[t]
        for cp in p.diagonal():
            cp.wait_recv()
        p.third().start()
        for cp in p.across():
            cp.wait_recv()
        if t == 0:
            self.keep.wait()

    def end(self):
        for t, p in enumerate(self.planes):
            for cp in p.first(self.source(t)) + p.second()[0] + p.second()[1] + [p.third()]:
                cp.wait_send()
            self.hops(t, lambda cp: cp.wait_send())


class Scatter:
    def __init__(self, here, order, part, sibr, xh, yh, xf, yf, zr, bsend, brecv, hsend, hrecv, fsend, frecv, zsend, zrecv):
        self.c, self.z, self.sib, self.xn, self.yn, self.diag = here
        self.k = lax.rem(self.c, 2)
        self.order = order
        self.part, self.sibr, self.xh, self.yh, self.xf, self.yf, self.zr = part, sibr, xh, yh, xf, yf, zr
        self.sems = (bsend, brecv, hsend, hrecv, fsend, frecv, zsend, zrecv)
        self.h = part.shape[3] // 2

    def mine(self, t, b):
        return self.part.at[t, b, self.k]

    def cross(self, t, b):
        send, recv = self.sems[0:2]
        return remote(self.part.at[t, b, 1 - self.k], self.sibr.at[t, b], send.at[t, b], recv.at[t, b], (self.sib, self.z))

    def halves(self, t):
        send, recv = self.sems[2:4]
        src = self.mine(t, 3)
        return (
            remote(src.at[pl.ds(0, self.h)], self.xh.at[t], send.at[t, 0], recv.at[t, 0], (self.xn, self.z)),
            remote(src.at[pl.ds(self.h, self.h)], self.yh.at[t], send.at[t, 1], recv.at[t, 1], (self.yn, self.z)),
        )

    def fulls(self, t):
        send, recv = self.sems[4:6]
        return (
            remote(self.mine(t, 1), self.xf.at[t], send.at[t, 0], recv.at[t, 0], (self.xn, self.z)),
            remote(self.mine(t, 2), self.yf.at[t], send.at[t, 1], recv.at[t, 1], (self.yn, self.z)),
        )

    def hop(self, t):
        send, recv = self.sems[6:8]
        return remote(self.mine(t, 0), self.zr.at[self.z], send.at[t], recv.at[self.z], (self.c, self.order[t]))

    def came(self, t):
        send, recv = self.sems[6:8]
        zz = self.order[t]
        return remote(self.zr.at[zz], self.zr.at[zz], send.at[t], recv.at[zz], (self.c, zz))

    def one(self, t):
        self.cross(t, 3).wait_recv()
        add_rows(self.mine(t, 3), [self.mine(t, 3), self.sibr.at[t, 3]])
        for cp in self.halves(t):
            cp.start()

    def two(self, t):
        h = self.h
        top, low = pl.ds(0, h), pl.ds(h, h)
        hx, hy = self.halves(t)
        fx, fy = self.fulls(t)
        self.cross(t, 1).wait_recv()
        m, s = self.mine(t, 1), self.sibr.at[t, 1]
        add_rows(m.at[top], [m.at[top], s.at[top]])
        hy.wait_recv()
        add_rows(m.at[low], [m.at[low], s.at[low], self.yh.at[t]])
        fx.start()
        self.cross(t, 2).wait_recv()
        m, s = self.mine(t, 2), self.sibr.at[t, 2]
        add_rows(m.at[low], [m.at[low], s.at[low]])
        hx.wait_recv()
        add_rows(m.at[top], [m.at[top], s.at[top], self.xh.at[t]])
        fy.start()

    def three(self, t, o_ref):
        self.cross(t, 0).wait_recv()
        for cp in self.fulls(t):
            cp.wait_recv()
        parts = [self.mine(t, 0), self.sibr.at[t, 0], self.xf.at[t], self.yf.at[t]]
        if t == 0:
            add_rows(o_ref, parts)
        else:
            add_rows(self.mine(t, 0), parts)
            self.hop(t).start()

    def end(self, o_ref):
        n = len(self.order)
        for t in range(1, n):
            self.came(t).wait_recv()
        if n > 1:
            add_rows(o_ref, [o_ref] + [self.zr.at[self.order[t]] for t in range(1, n)])
        for t in range(n):
            for b in range(4):
                self.cross(t, b).wait_send()
            for cp in self.halves(t) + self.fulls(t):
                cp.wait_send()
            if t > 0:
                self.hop(t).wait_send()


def scatter_scratch(n, rows, width):
    v, dma = pltpu.VMEM, pltpu.SemaphoreType.DMA
    return [
        v((n, 4, 2, rows, width), BF16), v((n, 4, rows, width), BF16),
        v((n, rows // 2, width), BF16), v((n, rows // 2, width), BF16),
        v((n, rows, width), BF16), v((n, rows, width), BF16), v((NZ, rows, width), BF16),
        dma((n, 4)), dma((n, 4)), dma((n, 2)), dma((n, 2)), dma((n, 2)), dma((n, 2)), dma((NZ,)), dma((NZ,)),
    ]


def everyone_else(c, z):
    flat = c * NZ + z
    others = [lax.rem(flat + s, 32) for s in range(1, 32)]
    return flat, [(o // NZ, lax.rem(o, NZ)) for o in others]


def feed_kernel(
    x_ref, st_ref, gate_in, wu_ref, d_in, o_ref, all_ref, so_ref, gu_ref, w_out,
    w_ref, d_ref, xs, gs, xsem, gsem, wsend, wrecv, wkeep, keep, zsend, zrecv, send, recv, ssend, srecv, *scat
):
    here = place_on_plane()
    c, z = here[0], here[1]
    flat, everyone = everyone_else(c, z)
    meet(everyone)
    gather_ = Gather(here, x_ref, all_ref, keep.at[0], zsend, zrecv, send, recv)
    order = gather_.order
    sums = Scatter(here, order, *scat)
    ff = d_ref.shape[0]
    gather_.keep.start()
    gather_.spread(0)
    keep_s = pltpu.make_async_copy(st_ref, so_ref.at[flat], keep.at[1])
    keep_s.start()
    stat = [remote(st_ref, so_ref.at[flat], ssend.at[s], srecv.at[s], d) for s, d in enumerate(everyone)]
    for cp in stat:
        cp.start()

    def load(t, b):
        src = all_ref.at[order[t], pl.ds(2 * chip_at(c, b), 2)]
        return pltpu.make_async_copy(src, xs.at[b], xsem.at[b])

    def store(t, b):
        return pltpu.make_async_copy(gs.at[b], gu_ref.at[order[t], chip_at(c, b)], gsem.at[b])

    def work(t, lo, hi):
        for b in (3, 1, 2, 0)[lo:hi]:
            load(t, b).start()

        def body(i, _):
            b = chunk_order(i)
            load(t, b).wait()
            if t != 1:
                store(1, b).wait()
            x = xs[b].reshape(-1, xs.shape[-1])
            gu = jnp.dot(x, w_ref[...].reshape(x.shape[1], -1), preferred_element_type=F32)
            gs[b] = gu
            store(t, b).start()
            gate, up = gu[:, :ff], gu[:, ff:]
            act = (gate * jax.nn.sigmoid(gate) * up).astype(BF16)
            p = jnp.dot(act, d_ref[...], preferred_element_type=F32).astype(BF16)
            sums.part[t, b] = p.reshape(sums.part.shape[2:])
            sums.cross(t, b).start()
            return 0

        lax.fori_loop(lo, hi, body, 0)

    weights = []
    keeps = [pltpu.make_async_copy(d_in, d_ref, wkeep.at[0])]
    keeps.append(pltpu.make_async_copy(gate_in, w_ref.at[:, :, pl.ds(0, ff)], wkeep.at[1]))
    for hop in range(NZ):
        to = lax.rem(z + hop, NZ)
        src = wu_ref.at[:, pl.ds(pl.multiple_of((c * NZ + to) * ff, ff), ff)]
        dst = w_ref.at[z, :, pl.ds(ff, ff)]
        if hop == 0:
            keeps.append(pltpu.make_async_copy(src, dst, wkeep.at[2]))
        else:
            weights.append(remote(src, dst, wsend.at[hop], wrecv.at[hop], (c, to)))
    w_keep = pltpu.make_async_copy(w_ref, w_out, wkeep.at[3])

    def early():
        for cp in keeps + weights:
            cp.start()

    def ready():
        for cp in keeps + weights:
            cp.wait()
        w_keep.start()

    fused_steps(gather_, sums, work, o_ref, False, early=early, ready=ready)
    for b in range(4):
        store(0, b).wait()
    w_keep.wait()
    keep_s.wait()
    for cp in stat:
        cp.wait()


def fused_steps(gather_, sums, work, o_ref, own_first, more=lambda t: None, early=lambda: None, ready=lambda: None):
    gather_.spread(1)
    gather_.onward(0)
    early()
    gather_.spread(2)
    if own_first:
        ready()
        gather_.close(0)
        work(0, 0, 2)
    gather_.onward(1)
    if own_first:
        work(0, 2, 4)
    gather_.spread(3)
    if own_first:
        more(0)
    gather_.onward(2)
    if not own_first:
        ready()
    gather_.close(1)
    work(1, 0, 2)
    gather_.onward(3)
    sums.one(1)
    work(1, 2, 4)
    more(1)
    gather_.close(2)
    work(2, 0, 2)
    sums.two(1)
    sums.one(2)
    work(2, 2, 4)
    more(2)
    gather_.close(3)
    work(3, 0, 2)
    sums.two(2)
    sums.one(3)
    work(3, 2, 4)
    sums.three(1, o_ref)
    more(3)
    sums.two(3)
    sums.three(2, o_ref)
    if not own_first:
        gather_.close(0)
        work(0, 0, 2)
    sums.one(0)
    if not own_first:
        work(0, 2, 4)
    sums.three(3, o_ref)
    sums.two(0)
    if not own_first:
        more(0)
    sums.three(0, o_ref)
    sums.end(o_ref)
    gather_.end()


def gather_sems():
    dma = pltpu.SemaphoreType.DMA
    return [dma((2,)), dma((2, 4)), dma((4,)), dma((4, 8)), dma((4, 8)), dma((31,)), dma((31,))]


def feed_forward(x, stats, gate, w_up, d):
    rows, width = x.shape
    depth, cols = w_up.shape[0], 2 * d.shape[0]
    any_ = pl.BlockSpec(memory_space=pl.ANY)
    vmem = pl.BlockSpec(memory_space=pltpu.VMEM)
    dma = pltpu.SemaphoreType.DMA
    return pl.pallas_call(
        feed_kernel,
        out_shape=(
            jax.ShapeDtypeStruct((rows, width), F32),
            jax.ShapeDtypeStruct((NZ, 8, rows, width), BF16),
            jax.ShapeDtypeStruct((32, 8, 128), F32),
            jax.ShapeDtypeStruct((NZ, 4, 2 * rows, cols), F32),
            jax.ShapeDtypeStruct((NZ, depth, cols), BF16),
        ),
        in_specs=[vmem, any_, any_, any_, any_],
        out_specs=(vmem, any_, any_, any_, any_),
        scratch_shapes=[
            pltpu.VMEM((NZ, depth, cols), BF16), pltpu.VMEM(d.shape, BF16),
            pltpu.VMEM((4, 2, rows, width), BF16), pltpu.VMEM((4, 2 * rows, cols), F32), dma((4,)), dma((4,)),
            dma((4,)), dma((4,)), dma((4,)),
        ] + gather_sems() + scatter_scratch(NZ, rows, width),
        compiler_params=pltpu.CompilerParams(collective_id=5, has_side_effects=True, vmem_limit_bytes=60 << 20),
        cost_estimate=takes(180),
        name="feed_forward",
    )(x, stats, gate, w_up, d)


def feed_back_kernel(
    x_ref, st_ref, w_in, d_in, n_ref, gu_ref, o_ref, all_ref, so_ref, gate_out, up_out, down_out,
    w_ref, d_ref, gate_o, up_o, down_o, wsem, gsend, grecv, xs, ns, gs, gg, acts, total, xsem, nsem, gsem, keep, zsend, zrecv, send, recv, ssend, srecv, *scat
):
    here = place_on_plane()
    c, z = here[0], here[1]
    flat, everyone = everyone_else(c, z)
    meet(everyone)
    gather_ = Gather(here, x_ref, all_ref, keep.at[0], zsend, zrecv, send, recv)
    order = gather_.order
    sums = Scatter(here, order, *scat)
    ff = d_ref.shape[0]
    tokens = 8 * x_ref.shape[0]
    gather_.keep.start()
    gather_.spread(0)
    keep_s = pltpu.make_async_copy(st_ref, so_ref.at[flat], keep.at[1])
    keep_s.start()
    stat = [remote(st_ref, so_ref.at[flat], ssend.at[s], srecv.at[s], d) for s, d in enumerate(everyone)]
    for cp in stat:
        cp.start()

    def loads(t, b):
        chip = chip_at(c, b)
        pair = pl.ds(2 * chip, 2)
        return (
            pltpu.make_async_copy(gu_ref.at[order[t], chip], gs.at[b], gsem.at[b]),
            pltpu.make_async_copy(all_ref.at[order[t], pair], xs.at[b], xsem.at[b]),
            pltpu.make_async_copy(n_ref.at[order[t], pair], ns.at[b], nsem.at[b]),
        )

    def work(t, lo, hi):
        for b in (3, 1, 2, 0)[lo:hi]:
            for cp in loads(t, b):
                cp.start()

        def body(i, _):
            b = chunk_order(i)
            stored, tokens_in, _ = loads(t, b)
            stored.wait()
            tokens_in.wait()
            g = xs[b].reshape(-1, xs.shape[-1])
            g_act = lax.dot_general(g, d_ref[...], CONTRACT_COLS, preferred_element_type=F32)
            gate, up = gs[b, :, :ff], gs[b, :, ff:]
            sg = jax.nn.sigmoid(gate)
            acts[b] = (gate * sg * up).astype(BF16)
            gg[b, :, :ff] = (g_act * up * sg * (1.0 + gate * (1.0 - sg))).astype(BF16)
            gg[b, :, ff:] = (g_act * gate * sg).astype(BF16)
            p = lax.dot_general(gg[b], w_ref[...].reshape(o_ref.shape[1], -1), CONTRACT_COLS, preferred_element_type=F32).astype(BF16)
            sums.part[t, b] = p.reshape(sums.part.shape[2:])
            sums.cross(t, b).start()
            return 0

        lax.fori_loop(lo, hi, body, 0)

    piece = 512

    def more(t):
        for b in range(4):
            loads(t, b)[2].wait()

        def body(i, _):
            at = pl.ds(pl.multiple_of(i * piece, piece), piece)
            n = ns[:, :, :, at].reshape(tokens, piece)
            w_term = lax.dot_general(n, gg[...].reshape(tokens, -1), CONTRACT_ROWS, preferred_element_type=F32)
            g = xs[:, :, :, at].reshape(tokens, piece)
            d_term = lax.dot_general(acts[...].reshape(tokens, -1), g, CONTRACT_ROWS, preferred_element_type=F32)
            if t > 0:
                w_term = w_term + total[at, :]
                d_term = d_term + down_o[:, at]
            down_o[:, at] = d_term
            if t < NZ - 1:
                total[at, :] = w_term
            else:
                pair = pl.ds(2 * i, 2)
                gate_o[pair] = w_term[:, :ff].astype(BF16).reshape((2,) + gate_o.shape[1:])
                up_o[pair] = w_term[:, ff:].astype(BF16).reshape((2,) + up_o.shape[1:])
            return 0

        lax.fori_loop(0, o_ref.shape[1] // piece, body, 0)

    keeps = [pltpu.make_async_copy(w_in, w_ref, wsem.at[0]), pltpu.make_async_copy(d_in, d_ref, wsem.at[1])]
    saved = [
        pltpu.make_async_copy(src, dst, wsem.at[2 + i])
        for i, (src, dst) in enumerate(((gate_o.at[:, z], gate_out.at[:, z]), (up_o, up_out), (down_o, down_out)))
    ]
    gate_z = []
    for s in (1, 2, 3):
        to = lax.rem(z + s, NZ)
        gate_z.append(remote(gate_o.at[:, to], gate_out.at[:, z], gsend.at[s], grecv.at[s], (c, to)))

    def early():
        for cp in keeps:
            cp.start()

    def ready():
        for cp in keeps:
            cp.wait()

    def more_and_save(t):
        more(t)
        if t == NZ - 1:
            for cp in gate_z + saved:
                cp.start()

    fused_steps(gather_, sums, work, o_ref, True, more_and_save, early, ready)
    for cp in saved + gate_z:
        cp.wait()
    keep_s.wait()
    for cp in stat:
        cp.wait()


def feed_back(x, stats, w, d, normed, gate_up):
    rows, width = x.shape
    cols = w.shape[2]
    ff = d.shape[0]
    by_owner = (8, NZ, width // 32, ff)
    any_ = pl.BlockSpec(memory_space=pl.ANY)
    vmem = pl.BlockSpec(memory_space=pltpu.VMEM)
    dma, buf = pltpu.SemaphoreType.DMA, pltpu.VMEM
    return pl.pallas_call(
        feed_back_kernel,
        out_shape=(
            jax.ShapeDtypeStruct((rows, width), F32),
            jax.ShapeDtypeStruct((NZ, 8, rows, width), BF16),
            jax.ShapeDtypeStruct((32, 8, 128), F32),
            jax.ShapeDtypeStruct(by_owner, BF16),
            jax.ShapeDtypeStruct(by_owner, BF16),
            jax.ShapeDtypeStruct((ff, width), F32),
        ),
        in_specs=[vmem] + [any_] * 5,
        out_specs=(vmem,) + (any_,) * 5,
        scratch_shapes=[
            buf(w.shape, BF16), buf(d.shape, BF16), buf(by_owner, BF16), buf(by_owner, BF16), buf((ff, width), F32),
            dma((5,)), dma((4,)), dma((4,)), buf((4, 2, rows, width), BF16), buf((4, 2, rows, width), BF16), buf((4, 2 * rows, cols), F32),
            buf((4, 2 * rows, cols), BF16), buf((4, 2 * rows, ff), BF16), buf((width, cols), F32),
            dma((4,)), dma((4,)), dma((4,)),
        ] + gather_sems() + scatter_scratch(NZ, rows, width),
        compiler_params=pltpu.CompilerParams(collective_id=7, has_side_effects=True, vmem_limit_bytes=63 << 20),
        cost_estimate=takes(180),
        name="feed_back",
    )(x, stats, w, d, normed, gate_up)


ROWS_AT_ONCE = 256


def turn(u, cosine, sine):
    return u * cosine + pltpu.roll(u, HEAD_SIZE // 2, 1) * sine


def block_probs(q, k, first, place, keys_place):
    scores = lax.dot_general(q, k, CONTRACT_COLS, preferred_element_type=F32) * HEAD_SIZE ** (-0.5)
    allowed = (keys_place >= first) & (keys_place <= place)
    scores = jnp.where(allowed, scores, NEG)
    raised = jnp.exp(scores - jnp.max(scores, axis=-1, keepdims=True))
    return raised / jnp.sum(raised, axis=-1, keepdims=True)


def fetches(pairs, sems):
    copies = [pltpu.make_async_copy(src, dst, sems.at[i]) for i, (src, dst) in enumerate(pairs)]
    for cp in copies:
        cp.start()
    return copies


def exchange_loop(c, z, act):
    flat = c * NZ + z

    def body(s, _):
        to = lax.rem(flat + s, 32)
        act(s, to // NZ, lax.rem(to, NZ))
        return 0

    lax.fori_loop(1, 32, body, 0)


def back_kernel(
    g_ref, q_in, k_in, v_in, attn_in, cos_in, sin_in, first_in, place_in, keys_in, wqkv_in, wout_in, gain_in,
    norm_in, gate_ref, up_ref,
    o_ref, mlp_o, qkv_o, out_o, gain_o,
    q_ref, k_ref, v_ref, attn_ref, cos_ref, sin_ref, first_ref, place_ref, keys_ref, wqkv_ref, wout_ref, gain_ref, normed, isem,
    gb, ga, gqkv, gk, gv, outg, qkvg, mt, qt, qs, gsrc,
    msend, mrecv, m2send, m2recv, qsend, qrecv, q2send, q2recv, osend, orecv, ssend, srecv, lsem, psend, precv, *scat
):
    here = place_on_plane()
    c, z, sib, xn, yn, diag = here
    flat, everyone = everyone_else(c, z)
    meet(everyone)
    rows, width = g_ref.shape
    tokens = 8 * rows
    share = width // 32
    plane = Plane(here, lambda j: gb.at[j], psend, precv, rows // 2)
    sums = Scatter(here, [z], *scat)
    mates = [lax.rem(c + s, 8) for s in range(1, 8)]
    others = [(s, lax.rem(z + s, NZ)) for s in (1, 2, 3)]
    for cp in plane.first(g_ref):
        cp.start()

    mlp_z = [remote(up_ref.at[:, to], mt.at[:, z], msend.at[s], mrecv.at[s], (c, to)) for s, to in others]
    keep = pltpu.make_async_copy(up_ref.at[:, z], mt.at[:, z], lsem.at[1])
    for cp in mlp_z + [keep]:
        cp.start()
    from_me = pl.ds(pl.multiple_of(c * NZ, NZ), NZ)

    def over_plane(i, ref):
        out = [
            remote(ref.at[m], mlp_o.at[i, from_me], m2send.at[i, s], m2recv.at[i, s], (m, z)) for s, m in enumerate(mates)
        ]
        out.append(pltpu.make_async_copy(ref.at[c], mlp_o.at[i, from_me], lsem.at[2 + i]))
        for cp in out:
            cp.start()
        return out

    got = fetches(
        [
            (wout_in, wout_ref), (q_in, q_ref), (k_in, k_ref), (v_in, v_ref), (cos_in, cos_ref), (sin_in, sin_ref),
            (first_in, first_ref), (place_in, place_ref), (keys_in, keys_ref),
            (attn_in, attn_ref), (norm_in, normed), (wqkv_in, wqkv_ref), (gain_in, gain_ref),
        ],
        isem,
    )
    gb[c] = g_ref[...]
    gk[...] = jnp.zeros_like(gk)
    gv[...] = jnp.zeros_like(gv)

    def attend(b):
        chip = chip_at(c, b)
        at = pl.ds(pl.multiple_of(chip * ROWS_AT_ONCE, ROWS_AT_ONCE), ROWS_AT_ONCE)
        g_rows = gb[pl.ds(chip * 2, 2)].reshape(ROWS_AT_ONCE, width)
        ga[at, :] = lax.dot_general(g_rows, wout_ref[...], CONTRACT_COLS, preferred_element_type=F32).astype(BF16)
        k, v = k_ref[...], v_ref[...]
        cosine, sine = cos_ref[at, :], sin_ref[at, :]
        first, place, keys = first_ref[at, :], place_ref[at, :], keys_ref[...]
        for h in range(QUERY_HEADS // KEY_VALUE_HEADS):
            lanes = slice(h * HEAD_SIZE, (h + 1) * HEAD_SIZE)
            q, g = q_ref[at, lanes], ga[at, lanes]
            probs = block_probs(q, k, first, place, keys)
            g_probs = lax.dot_general(g, v, CONTRACT_COLS, preferred_element_type=F32)
            delta = jnp.sum(probs * g_probs, axis=-1, keepdims=True)
            g_scores = (probs * (g_probs - delta)).astype(BF16)
            g_q = jnp.dot(g_scores, k, preferred_element_type=F32) * HEAD_SIZE ** (-0.5)
            gqkv[at, lanes] = turn(g_q, cosine, -sine).astype(BF16)
            gk[...] += lax.dot_general(g_scores, q, CONTRACT_ROWS, preferred_element_type=F32)
            gv[...] += lax.dot_general(probs.astype(BF16), g, CONTRACT_ROWS, preferred_element_type=F32)

    came = plane.across()
    for cp in got[:9]:
        cp.wait()
    came[0].wait_recv()
    attend(0)
    for arrived, sends in zip(plane.arrive(), plane.second()):
        arrived.wait_recv()
        for cp in sends:
            cp.start()
    came[1].wait_recv()
    attend(1)
    for cp in plane.diagonal():
        cp.wait_recv()
    plane.third().start()
    came[2].wait_recv()
    attend(2)
    came[3].wait_recv()
    mlp_c = over_plane(0, gate_ref)
    got[9].wait()
    piece = 512

    def outs(i, _):
        at = pl.ds(pl.multiple_of(i * piece, piece), piece)
        g = gb[:, :, at].reshape(tokens, piece)
        outg[:, at] = lax.dot_general(attn_ref[...], g, CONTRACT_ROWS, preferred_element_type=F32).astype(BF16)
        return 0

    lax.fori_loop(0, width // piece, outs, 0)
    out_sends = []
    for s, to in others:
        src = outg.at[pl.ds(pl.multiple_of(to * share, share), share)]
        out_sends.append(remote(src, out_o.at[z], osend.at[s], orecv.at[s], (c, to)))
    for cp in out_sends:
        cp.start()
    keep_o = pltpu.make_async_copy(outg.at[pl.ds(pl.multiple_of(z * share, share), share)], out_o.at[z], lsem.at[5])
    keep_o.start()
    attend(3)
    qcols = q_ref.shape[1]
    g_k = gk[...] * HEAD_SIZE ** (-0.5)
    gqkv[:, qcols : qcols + HEAD_SIZE] = turn(g_k, cos_ref[...], -sin_ref[...]).astype(BF16)
    gqkv[:, qcols + HEAD_SIZE :] = gv[...].astype(BF16)

    for cp in got[10:]:
        cp.wait()
    cols = gqkv.shape[1]

    def project(i, _):
        at = pl.ds(pl.multiple_of(i * piece, piece), piece)
        term = lax.dot_general(normed[:, at], gqkv[...], CONTRACT_ROWS, preferred_element_type=F32).astype(BF16)
        qkvg[pl.ds(2 * i, 2)] = term.reshape(2, NZ, share, cols)
        return 0

    lax.fori_loop(0, width // piece, project, 0)
    qkv_z = [remote(qkvg.at[:, to], qt.at[s], qsend.at[s], qrecv.at[s], (c, to)) for s, to in others]
    for cp in qkv_z:
        cp.start()

    gsrc[...] = jnp.zeros_like(gsrc)
    gsrc[1:2, :] = gain_ref[...]
    for b in (3, 1, 2, 0):
        chip = chip_at(c, b)
        at = pl.ds(pl.multiple_of(chip * ROWS_AT_ONCE, ROWS_AT_ONCE), ROWS_AT_ONCE)
        p = lax.dot_general(gqkv[at, :], wqkv_ref[...], CONTRACT_COLS, preferred_element_type=F32)
        sums.part[0, b] = p.astype(BF16).reshape(2, rows, width)
        sums.cross(0, b).start()
        gsrc[0:1, :] += jnp.sum(p * normed[at, :].astype(F32), axis=0, keepdims=True)

    def gain_sends(act):
        def one(s, tc, tz):
            lanes = pl.ds(pl.multiple_of((tc * NZ + tz) // 2 * 128, 128), 128)
            act(remote(gsrc.at[:, lanes], gain_o.at[flat], ssend.at[s], srecv.at[s], (tc, tz)))

        exchange_loop(c, z, one)

    gain_sends(lambda cp: cp.start())
    own_lanes = pl.ds(pl.multiple_of(flat // 2 * 128, 128), 128)
    gain_keep = pltpu.make_async_copy(gsrc.at[:, own_lanes], gain_o.at[flat], lsem.at[4])
    gain_keep.start()
    sums.one(0)
    for cp in mlp_z + [keep]:
        cp.wait()
    mlp_c += over_plane(1, mt)
    sums.two(0)

    sums.three(0, o_ref)

    for cp in qkv_z:
        cp.wait()

    def gathered(j, _):
        total = qkvg[j, z].astype(F32)
        for s in (1, 2, 3):
            total = total + qt[s, j].astype(F32)
        qs[j] = total.astype(BF16)
        return 0

    lax.fori_loop(0, 8, gathered, 0)
    qkv_c = [remote(qs.at[m], qkv_o.at[c], q2send.at[s], q2recv.at[s], (m, z)) for s, m in enumerate(mates)]
    qkv_keep = pltpu.make_async_copy(qs.at[c], qkv_o.at[c], lsem.at[6])
    for cp in qkv_c + [qkv_keep]:
        cp.start()
    sums.end(o_ref)
    for cp in plane.first(g_ref) + plane.second()[0] + plane.second()[1] + [plane.third()]:
        cp.wait_send()
    gain_sends(lambda cp: cp.wait())
    for cp in mlp_c + out_sends + qkv_c + [keep_o, qkv_keep, gain_keep]:
        cp.wait()


def attention_back(g, q, k, v, attn, cosine, sine, first, place, keys, w_qkv, w_out, gain, normed, gate_g, up_g):
    rows, width = g.shape
    tokens = q.shape[0]
    any_ = pl.BlockSpec(memory_space=pl.ANY)
    vmem = pl.BlockSpec(memory_space=pltpu.VMEM)
    dma, buf, out = pltpu.SemaphoreType.DMA, pltpu.VMEM, jax.ShapeDtypeStruct
    share = width // 32
    cols = w_qkv.shape[1]
    by_owner = gate_g.shape
    ff = by_owner[3]
    return pl.pallas_call(
        back_kernel,
        out_shape=(
            out((rows, width), F32),
            out((2, 32, share, ff), BF16),
            out((8, share, cols), BF16),
            out((NZ, share, width), BF16),
            out((32, 8, 128), F32),
        ),
        in_specs=[vmem] + [any_] * 15,
        out_specs=(vmem,) + (any_,) * 4,
        scratch_shapes=[
            buf(a.shape, a.dtype)
            for a in (q, k, v, attn, cosine, sine, first, place, keys, w_qkv, w_out, gain, normed)
        ] + [
            dma((13,)),
            buf((8, rows, width), BF16), buf(q.shape, BF16), buf((tokens, cols), BF16), buf(k.shape, F32), buf(v.shape, F32),
            buf(w_out.shape, BF16), buf((8, NZ, share, cols), BF16),
            buf(by_owner, BF16), buf((NZ, 8, share, cols), BF16), buf((8, share, cols), BF16), buf((8, width), F32),
            dma((4,)), dma((4,)), dma((2, 7)), dma((2, 7)), dma((4,)), dma((4,)), dma((7,)), dma((7,)), dma((4,)), dma((4,)),
            dma((32,)), dma((32,)), dma((7,)), dma((8,)), dma((8,)),
        ] + scatter_scratch(1, rows, width),
        compiler_params=pltpu.CompilerParams(collective_id=6, has_side_effects=True, vmem_limit_bytes=60 << 20),
        cost_estimate=takes(110),
        name="attention_back",
    )(g, q, k, v, attn, cosine, sine, first, place, keys, w_qkv, w_out, gain, normed, gate_g, up_g)


class Line:
    def __init__(self, c, z, slot, send, recv):
        self.c, self.z, self.slot, self.send, self.recv = c, z, slot, send, recv
        self.order = plane_order(z)

    def hop(self, up, t):
        zz = self.order[t]
        row = 0 if up else 1
        return remote(
            self.slot(zz), self.slot(zz), self.send.at[row, zz], self.recv.at[zz], (self.c, self.z + (1 if up else -1))
        )

    def hops(self, t, act):
        zz, z = self.order[t], self.z

        @pl.when((zz <= z) & (z < NZ - 1))
        def _():
            act(self.hop(True, t))

        @pl.when((zz >= z) & (z > 0))
        def _():
            act(self.hop(False, t))

    def step(self, t):
        if t > 0:
            self.hop(True, t).wait_recv()
        self.hops(t, lambda cp: cp.start())

    def end(self):
        for t in range(NZ):
            self.hops(t, lambda cp: cp.wait_send())


def front_kernel(
    x_ref, g_ref, wq_ref, wk_ref, wv_ref, wo_ref, wd_ref, wg_ref, cos_in, sin_in, first_in, place_in, keys_in,
    o_ref, go_ref, norm_o, wqkv_o, outr_o, downr_o, gate_o, q_o, k_o, v_o, attn_o,
    wqkv, outr, downr, gatew, q_ref, k_ref, v_ref, attn_ref, cos_ref, sin_ref, first_ref, place_ref, keys_ref,
    normed, nall, acc, tmp_o, tmp_d, isem, osem, wgsend, wgrecv,
    lsem, gsend, grecv, qzsend, qzrecv, ozsend, ozrecv, dsend, drecv, o2send, o2recv, d2send, d2recv, psend, precv, *scat
):
    here = place_on_plane()
    c, z, sib, xn, yn, diag = here
    rows, width = x_ref.shape
    tokens = 8 * rows
    wide = tmp_o.shape[2]
    mates = [lax.rem(c + s, 8) for s in range(1, 8)]
    others = [lax.rem(z + s, NZ) for s in (1, 2, 3)]
    meet([(m, z) for m in mates] + [(c, t) for t in others])
    sums = Scatter(here, [z], *scat)
    plane = Plane(here, lambda j: nall.at[j], psend, precv, rows // 2)
    line_q = Line(c, z, lambda zz: wqkv.at[zz], qzsend, qzrecv)
    line_o = Line(c, z, lambda zz: tmp_o.at[zz], ozsend, ozrecv)
    own_cols = pl.ds(pl.multiple_of(c * wide, wide), wide)

    def narrow(ref, n):
        return ref.at[:, pl.ds(pl.multiple_of(c * n, n), n)]

    q_keeps = [
        pltpu.make_async_copy(narrow(wq_ref, wide), wqkv.at[z, :, pl.ds(0, wide)], lsem.at[0]),
        pltpu.make_async_copy(narrow(wk_ref, HEAD_SIZE), wqkv.at[z, :, pl.ds(wide, HEAD_SIZE)], lsem.at[1]),
        pltpu.make_async_copy(narrow(wv_ref, HEAD_SIZE), wqkv.at[z, :, pl.ds(wide + HEAD_SIZE, HEAD_SIZE)], lsem.at[2]),
    ]
    o_keep = pltpu.make_async_copy(wo_ref.at[:, own_cols], tmp_o.at[z], lsem.at[3])
    d_keeps, downs = [], []
    for core in range(2):
        for hop in range(NZ):
            to = lax.rem(z + hop, NZ)
            src = wd_ref.at[pl.ds(pl.multiple_of((core * NZ + to) * wide, wide), wide), own_cols]
            if hop == 0:
                d_keeps.append(pltpu.make_async_copy(src, tmp_d.at[z, core], lsem.at[4 + core]))
            else:
                downs.append(remote(src, tmp_d.at[z, core], dsend.at[core, hop], drecv.at[core, hop], (c, to)))
    gate_cols = wg_ref.shape[1] // 32
    gates = []
    for hop in range(NZ):
        to = lax.rem(z + hop, NZ)
        src = wg_ref.at[:, pl.ds(pl.multiple_of((c * NZ + to) * gate_cols, gate_cols), gate_cols)]
        if hop == 0:
            g_keep = pltpu.make_async_copy(src, gatew.at[z], lsem.at[9])
        else:
            gates.append(remote(src, gatew.at[z], wgsend.at[hop], wgrecv.at[hop], (c, to)))
    for cp in [o_keep] + q_keeps + d_keeps + [g_keep]:
        cp.start()
    go_ref[z] = g_ref[...]
    gains = [remote(g_ref, go_ref.at[z], gsend.at[s], grecv.at[s], (c, t)) for s, t in enumerate(others)]
    for cp in gains:
        cp.start()
    o_keep.wait()
    line_o.step(0)
    got = fetches(
        [(cos_in, cos_ref), (sin_in, sin_ref), (first_in, first_ref), (place_in, place_ref), (keys_in, keys_ref)], isem
    )
    x = x_ref[...].astype(F32)
    scaled = x * lax.rsqrt(jnp.mean(x * x, axis=-1, keepdims=True) + EPS)
    for cp in gains:
        cp.wait()
    piece = width // NZ
    for zz in range(NZ):
        normed[:, zz * piece : (zz + 1) * piece] = (
            scaled[:, zz * piece : (zz + 1) * piece] * go_ref[zz, 0:1, :]
        ).astype(BF16)
    for cp in plane.first(normed):
        cp.start()
    nall[c] = normed[...]
    line_o.step(1)
    for cp in q_keeps:
        cp.wait()
    line_q.step(0)
    line_o.step(2)
    for arrived, sends in zip(plane.arrive(), plane.second()):
        arrived.wait_recv()
        for cp in sends:
            cp.start()
    line_o.step(3)

    def regroup(buf, dst, send, recv, lrow):
        def block(j):
            return buf(j // 2, lax.rem(j, 2))

        out = [remote(block(m), dst.at[:, own_cols], send.at[s], recv.at[s], (m, z)) for s, m in enumerate(mates)]
        keep = pltpu.make_async_copy(block(c), dst.at[:, own_cols], lsem.at[lrow])
        for cp in out + [keep]:
            cp.start()
        return out + [keep]

    moved_o = regroup(lambda p, core: tmp_o.at[p, pl.ds(pl.multiple_of(core * wide, wide), wide)], outr, o2send, o2recv, 7)
    line_q.step(1)
    for cp in plane.diagonal():
        cp.wait_recv()
    plane.third().start()
    for cp in plane.across():
        cp.wait_recv()
    line_q.step(2)
    norm_keep = pltpu.make_async_copy(nall, norm_o, lsem.at[6])
    norm_keep.start()

    def project(t):
        zz = line_q.order[t]
        at = pl.ds(pl.multiple_of(zz * piece, piece), piece)
        term = jnp.dot(nall[:, :, at].reshape(tokens, piece), wqkv[zz], preferred_element_type=F32)
        acc[...] = term if t == 0 else acc[...] + term

    for t in range(3):
        project(t)
    line_q.step(3)
    for cp in downs:
        cp.start()
    project(3)
    for cp in got:
        cp.wait()

    def heads(i, _):
        at = pl.ds(pl.multiple_of(i * ROWS_AT_ONCE, ROWS_AT_ONCE), ROWS_AT_ONCE)
        cosine, sine = cos_ref[at, :], sin_ref[at, :]
        for h in range(wide // HEAD_SIZE):
            lanes = slice(h * HEAD_SIZE, (h + 1) * HEAD_SIZE)
            q_ref[at, lanes] = turn(acc[at, lanes], cosine, sine).astype(BF16)
        k_ref[at, :] = turn(acc[at, wide : wide + HEAD_SIZE], cosine, sine).astype(BF16)
        v_ref[at, :] = acc[at, wide + HEAD_SIZE :].astype(BF16)
        return 0

    lax.fori_loop(0, tokens // ROWS_AT_ONCE, heads, 0)

    saved = fetches([(wqkv, wqkv_o), (q_ref, q_o), (k_ref, k_o), (v_ref, v_o)], osem)

    def attend(b):
        at = pl.ds(pl.multiple_of(chip_at(c, b) * ROWS_AT_ONCE, ROWS_AT_ONCE), ROWS_AT_ONCE)
        k, v = k_ref[...], v_ref[...]
        first, place, keys = first_ref[at, :], place_ref[at, :], keys_ref[...]
        for h in range(wide // HEAD_SIZE):
            lanes = slice(h * HEAD_SIZE, (h + 1) * HEAD_SIZE)
            probs = block_probs(q_ref[at, lanes], k, first, place, keys)
            attn_ref[at, lanes] = jnp.dot(probs.astype(BF16), v, preferred_element_type=F32).astype(BF16)
        p = jnp.dot(attn_ref[at, :], outr[...], preferred_element_type=F32).astype(BF16)
        sums.part[0, b] = p.reshape(2, rows, width)
        sums.cross(0, b).start()

    for cp in moved_o:
        cp.wait()
    attend(3)
    attend(1)
    sums.one(0)
    attend(2)
    attend(0)
    saved += fetches([(outr, outr_o), (attn_ref, attn_o)], osem.at[pl.ds(4, 2)])
    sums.two(0)
    for cp in d_keeps + downs:
        cp.wait()
    moved_d = regroup(lambda p, core: tmp_d.at[p, core], downr, d2send, d2recv, 8)
    for cp in gates:
        cp.start()
    sums.three(0, o_ref)
    sums.end(o_ref)
    for cp in moved_d:
        cp.wait()
    saved += fetches([(downr, downr_o)], osem.at[pl.ds(6, 1)])
    for cp in gates + [g_keep]:
        cp.wait()
    saved += fetches([(gatew, gate_o)], osem.at[pl.ds(7, 1)])
    for cp in plane.first(normed) + plane.second()[0] + plane.second()[1] + [plane.third()]:
        cp.wait_send()
    line_q.end()
    line_o.end()
    for cp in saved + [norm_keep]:
        cp.wait()


def attention_front(x, gains, w_query, w_key, value_weight, w_output, w_down, w_gate, cosine, sine, first, place, keys):
    rows, width = x.shape
    tokens = 8 * rows
    depth = w_query.shape[0]
    wide = width // 8
    any_ = pl.BlockSpec(memory_space=pl.ANY)
    vmem = pl.BlockSpec(memory_space=pltpu.VMEM)
    dma, buf, out = pltpu.SemaphoreType.DMA, pltpu.VMEM, jax.ShapeDtypeStruct
    results = (
        out((NZ, depth, 2 * wide), BF16),
        out((wide, width), BF16),
        out((wide, width), BF16),
        out((NZ, depth, w_gate.shape[1] // 32), BF16),
        out((tokens, wide), BF16),
        out((tokens, HEAD_SIZE), BF16),
        out((tokens, HEAD_SIZE), BF16),
        out((tokens, wide), BF16),
    )
    return pl.pallas_call(
        front_kernel,
        out_shape=(out((rows, width), F32), out((NZ,) + gains.shape, F32), out((8, rows, width), BF16)) + results,
        in_specs=[vmem] * 2 + [any_] * 11,
        out_specs=(vmem, vmem) + (any_,) * 9,
        scratch_shapes=[buf(r.shape, r.dtype) for r in results]
        + [buf(a.shape, a.dtype) for a in (cosine, sine, first, place, keys)]
        + [
            buf((rows, width), BF16), buf((8, rows, width), BF16), buf((tokens, 2 * wide), F32), buf((NZ, depth, wide), BF16),
            buf((NZ, 2, wide, wide), BF16), dma((5,)), dma((8,)), dma((NZ,)), dma((NZ,)),
            dma((10,)), dma((3,)), dma((3,)), dma((2, 4)), dma((4,)), dma((2, 4)), dma((4,)), dma((2, 4)), dma((2, 4)),
            dma((7,)), dma((7,)), dma((7,)), dma((7,)), dma((8,)), dma((8,)),
        ] + scatter_scratch(1, rows, width),
        compiler_params=pltpu.CompilerParams(collective_id=8, has_side_effects=True, vmem_limit_bytes=60 << 20),
        cost_estimate=takes(95),
        name="attention_front",
    )(x, gains, w_query, w_key, value_weight, w_output, w_down, w_gate, cosine, sine, first, place, keys)


def tile_of(value):
    return jnp.full((8, 128), value, F32)


def heads_and_columns(
    hidden_in,
    cotangent,
    teacher,
    valid_mask,
    doc_starts,
    attn_gain,
    w_query,
    w_key,
    value_weight,
    w_output,
    mlp_gain,
    w_gate,
    w_up,
    w_down,
):
    rows, width = hidden_in.shape[1:]
    c = lax.axis_index("ctx")
    z = lax.axis_index("fsdp")
    devices = lax.axis_size("ctx")
    tokens = rows * devices
    group = QUERY_HEADS // KEY_VALUE_HEADS
    qcols = group * HEAD_SIZE
    ffcols = FF // (devices * NZ)

    layer_input = hidden_in[0].astype(F32)
    gains = jnp.concatenate(
        [attn_gain.astype(F32)[None], mlp_gain.astype(F32)[None], jnp.zeros((6, attn_gain.shape[0]), F32)]
    )
    place, segment, offset = stream_places(tokens, rows, devices, doc_starts[0])
    freq = ROPE_BASE ** (-(jnp.arange(HEAD_SIZE // 2, dtype=F32) * 2.0 / HEAD_SIZE))
    angle = offset.astype(F32)[:, None] * freq[None, :]
    cosine = jnp.concatenate([jnp.cos(angle)] * 2, axis=1)
    sine = jnp.concatenate([-jnp.sin(angle), jnp.sin(angle)], axis=1)
    columns = ((place - offset)[:, None], place[:, None], place[None, :])
    branch, gains_all, normed_all, w_qkv, out_rows, down_rows, gate_cols, q, k, v, attn = attention_front(
        hidden_in[0], gains, w_query, w_key, value_weight, w_output, w_down, w_gate, cosine, sine, *columns
    )
    attn_scale = gains_all[:, 0, :].reshape(1, width)
    mlp_scale = gains_all[:, 1, :].reshape(1, width)
    residual = layer_input + branch

    r2 = rms_norm_scale(residual)
    hat2 = residual * r2
    normed2 = (hat2 * mlp_scale).astype(BF16)
    maskf = valid_mask[0].astype(F32)
    mlp_out, normed2_all, counts, gate_up, w_mlp = feed_forward(
        normed2, tile_of(jnp.sum(maskf)), gate_cols, w_up, down_rows
    )
    count = jnp.sum(counts[:, 0, 0])
    outf = residual + mlp_out

    diff = outf - teacher[0].astype(F32)
    error_here = jnp.sum(maskf * jnp.mean(diff * diff, axis=-1))
    g_out = cotangent[0].astype(F32) + maskf[:, None] * diff * (2.0 / (count * width))
    g_norm2, _, errors, gate_grads, up_grads, down_grads = feed_back(
        g_out.astype(BF16), tile_of(error_here), w_mlp, down_rows, normed2_all, gate_up
    )
    loss = jnp.sum(errors[:, 0, 0]) / count
    g_hat2 = g_norm2 * mlp_scale
    g_residual = g_out + r2 * (g_hat2 - hat2 * jnp.mean(g_hat2 * hat2, axis=-1, keepdims=True))
    mlp_gain_term = jnp.sum(g_norm2 * hat2, axis=0, keepdims=True)
    g_norm1, got, got_qkv, got_out, got_gains = attention_back(
        g_residual.astype(BF16), q, k, v, attn, cosine, sine, *columns, w_qkv.reshape(width, -1), out_rows, mlp_gain_term,
        normed_all.reshape(tokens, width), gate_grads, up_grads,
    )

    r1 = rms_norm_scale(layer_input)
    hat1 = layer_input * r1
    g_hat1 = g_norm1 * attn_scale
    g_input = g_residual + r1 * (g_hat1 - hat1 * jnp.mean(g_hat1 * hat1, axis=-1, keepdims=True))

    parts = devices * NZ
    share = width // parts
    got = got.astype(F32).transpose(0, 2, 1, 3).reshape(2, share, FF)
    got_qkv = got_qkv.astype(F32).transpose(1, 0, 2)
    got_out = jnp.sum(got_out.astype(F32), axis=0)
    flat = c * NZ + z
    got_gains = lax.dynamic_slice_in_dim(jnp.sum(got_gains, axis=0), flat % 2 * share, share, axis=1)
    own_scale = lax.dynamic_slice_in_dim(attn_scale[0], flat * share, share)

    return (
        loss,
        outf.astype(BF16)[None],
        g_input.astype(BF16)[None],
        got_gains[0] / own_scale,
        got_qkv[:, :, :qcols].reshape(share, QUERY_HEADS * HEAD_SIZE),
        got_qkv[:, :, qcols : qcols + HEAD_SIZE].reshape(share, KEY_VALUE_HEADS * HEAD_SIZE),
        got_qkv[:, :, qcols + HEAD_SIZE :].reshape(share, KEY_VALUE_HEADS * HEAD_SIZE),
        got_out,
        got_gains[1],
        got[0],
        got[1],
        down_grads,
    )


def solution(mesh):
    small = dict(mesh.shape) == {"ctx": KEY_VALUE_HEADS, "fsdp": NZ}
    in_specs = (
        P("fsdp", "ctx", None),
        P("fsdp", "ctx", None),
        P("fsdp", "ctx", None),
        P("fsdp", "ctx"),
        P("fsdp", None),
        P("fsdp"),
        P("fsdp", None),
        P("fsdp", None),
        P("fsdp", None),
        P("fsdp", None),
        P("fsdp"),
        P("fsdp", None),
        P("fsdp", None),
        P("fsdp", None),
    )
    out_specs = (
        P(),
        P("fsdp", "ctx", None),
        P("fsdp", "ctx", None),
        P(("ctx", "fsdp")),
        P(("ctx", "fsdp"), None),
        P(("ctx", "fsdp"), None),
        P(("ctx", "fsdp"), None),
        P(("ctx", "fsdp"), None),
        P(("ctx", "fsdp")),
        P(("ctx", "fsdp"), None),
        P(("ctx", "fsdp"), None),
        P(("ctx", "fsdp"), None),
    )
    return jax.shard_map(
        heads_and_columns if small else per_device, mesh=mesh, in_specs=in_specs, out_specs=out_specs, check_vma=False
    )
```

```python
import functools

import jax
import jax.numpy as jnp
from jax import lax
from jax.experimental import pallas as pl
from jax.experimental.pallas import tpu as pltpu
from jax.sharding import PartitionSpec as P

QUERY_HEADS = 16
KEY_VALUE_HEADS = 8
HEAD_SIZE = 128
FF = 8192


EPS = 1e-05
ROPE_BASE = 1000000.0
NEG = -1e30
CONTRACT_ROWS = (((0,), (0,)), ((), ()))
CONTRACT_COLS = (((1,), (1,)), ((), ()))


def stream_places(rows, local_token_count, devices, starts):
    span = local_token_count // 2
    rowid = jnp.arange(rows, dtype=jnp.int32)
    device = rowid // local_token_count
    within = rowid % local_token_count
    span_id = jnp.where(within < span, device, 2 * devices - 1 - device)
    place = span_id * span + within % span
    before = starts[None, :] <= place[:, None]
    segment = jnp.sum(before.astype(jnp.int32), axis=1) - 1
    first = jnp.max(jnp.where(before, starts[None, :], 0), axis=1)
    return (place, segment, place - first)


def rotary_embed(values, token_offset, sign):
    half = HEAD_SIZE // 2
    freq = ROPE_BASE ** (-(jnp.arange(half, dtype=jnp.float32) * 2.0 / HEAD_SIZE))
    angle = token_offset.astype(jnp.float32)[:, None] * freq[None, :]
    cosine = jnp.cos(angle)[:, None, :]
    sine = sign * jnp.sin(angle)[:, None, :]
    first = values[..., :half]
    second = values[..., half:]
    return jnp.concatenate(
        [first * cosine - second * sine, second * cosine + first * sine], axis=-1
    )


def rms_norm_scale(values):
    return lax.rsqrt(jnp.mean(values * values, axis=-1, keepdims=True) + EPS)


def head_scores(query_rows, key_rows, allowed):
    attention_scores = jnp.einsum(
        "trd,sd->rts", query_rows, key_rows, preferred_element_type=jnp.float32
    ) * HEAD_SIZE ** (-0.5)
    return jnp.where(allowed[None], attention_scores, NEG)


def per_device(
    hidden_in,
    cotangent,
    teacher,
    valid_mask,
    doc_starts,
    attn_gain,
    w_query,
    w_key,
    value_weight,
    w_output,
    mlp_gain,
    w_gate,
    w_up,
    w_down,
):
    local_token_count = hidden_in.shape[1]
    width = hidden_in.shape[2]
    devices = lax.axis_size("ctx")
    index = lax.axis_index("ctx")
    packed_stream_rows = local_token_count * devices
    query_group = QUERY_HEADS // KEY_VALUE_HEADS
    place, segment, token_offset = stream_places(
        packed_stream_rows, local_token_count, devices, doc_starts[0]
    )
    own_start = index * local_token_count
    my_place = lax.dynamic_slice_in_dim(place, own_start, local_token_count)
    my_segment = lax.dynamic_slice_in_dim(segment, own_start, local_token_count)
    local_stream_offset = lax.dynamic_slice_in_dim(token_offset, own_start, local_token_count)
    allowed = (my_segment[:, None] == segment[None, :]) & (place[None, :] <= my_place[:, None])
    layer_input = hidden_in[0].astype(jnp.float32)
    attn_whole = (
        lax.all_gather(attn_gain, "fsdp", axis=0, tiled=True),
        lax.all_gather(w_query, "fsdp", axis=0, tiled=True),
        lax.all_gather(w_key, "fsdp", axis=0, tiled=True),
        lax.all_gather(value_weight, "fsdp", axis=0, tiled=True),
        lax.all_gather(w_output, "fsdp", axis=0, tiled=True),
    )
    first_norm_scale = attn_whole[0].astype(jnp.float32)
    first_inverse_norm = rms_norm_scale(layer_input)
    first_normalized_input = layer_input * first_inverse_norm
    first_normed = (first_normalized_input * first_norm_scale).astype(jnp.bfloat16)
    qproj = jnp.dot(first_normed, attn_whole[1], preferred_element_type=jnp.float32)
    key_projected = jnp.dot(first_normed, attn_whole[2], preferred_element_type=jnp.float32)
    vproj = jnp.dot(first_normed, attn_whole[3], preferred_element_type=jnp.float32).astype(
        jnp.bfloat16
    )
    query_rows = rotary_embed(
        qproj.reshape(local_token_count, QUERY_HEADS, HEAD_SIZE), local_stream_offset, 1.0
    ).astype(jnp.bfloat16)
    key_rows = (
        rotary_embed(
            key_projected.reshape(local_token_count, KEY_VALUE_HEADS, HEAD_SIZE),
            local_stream_offset,
            1.0,
        )
        .reshape(local_token_count, KEY_VALUE_HEADS * HEAD_SIZE)
        .astype(jnp.bfloat16)
    )
    every_key_row, every_value_row = (
        lax.all_gather(key_rows, "ctx", axis=0, tiled=True),
        lax.all_gather(vproj, "ctx", axis=0, tiled=True),
    )
    key_head_rows = every_key_row.reshape(packed_stream_rows, KEY_VALUE_HEADS, HEAD_SIZE).transpose(
        1, 0, 2
    )
    value_head_rows = every_value_row.reshape(
        packed_stream_rows, KEY_VALUE_HEADS, HEAD_SIZE
    ).transpose(1, 0, 2)
    query_head_rows = query_rows.reshape(
        local_token_count, KEY_VALUE_HEADS, query_group, HEAD_SIZE
    ).transpose(1, 0, 2, 3)

    def attend_head(parts):
        head_query, head_key, head_val = parts
        attention_scores = head_scores(head_query, head_key, allowed)
        top = jnp.max(attention_scores, axis=-1, keepdims=True)
        lse = top + jnp.log(jnp.sum(jnp.exp(attention_scores - top), axis=-1, keepdims=True))
        attention_probabilities = jnp.exp(attention_scores - lse)
        mixed_heads = jnp.einsum(
            "rts,sd->trd",
            attention_probabilities.astype(jnp.bfloat16),
            head_val,
            preferred_element_type=jnp.float32,
        )
        return (mixed_heads, lse)

    mixed_heads, lse = lax.map(attend_head, (query_head_rows, key_head_rows, value_head_rows))
    attn = (
        mixed_heads.transpose(1, 0, 2, 3)
        .reshape(local_token_count, QUERY_HEADS * HEAD_SIZE)
        .astype(jnp.bfloat16)
    )
    residual_state = layer_input + jnp.dot(attn, attn_whole[4], preferred_element_type=jnp.float32)
    mlp_whole = (
        lax.all_gather(mlp_gain, "fsdp", axis=0, tiled=True),
        lax.all_gather(w_gate, "fsdp", axis=0, tiled=True),
        lax.all_gather(w_up, "fsdp", axis=0, tiled=True),
        lax.all_gather(w_down, "fsdp", axis=0, tiled=True),
    )
    second_norm_scale = mlp_whole[0].astype(jnp.float32)
    second_inverse_norm = rms_norm_scale(residual_state)
    second_normalized_input = residual_state * second_inverse_norm
    second_normed = (second_normalized_input * second_norm_scale).astype(jnp.bfloat16)
    gate = jnp.dot(second_normed, mlp_whole[1], preferred_element_type=jnp.float32)
    up_val = jnp.dot(second_normed, mlp_whole[2], preferred_element_type=jnp.float32)
    sigma = jax.nn.sigmoid(gate)
    act = (gate * sigma * up_val).astype(jnp.bfloat16)
    outf = residual_state + jnp.dot(act, mlp_whole[3], preferred_element_type=jnp.float32)
    maskf = valid_mask[0].astype(jnp.float32)
    diff = outf - teacher[0].astype(jnp.float32)
    count_here = jnp.sum(maskf)
    error_here = jnp.sum(maskf * jnp.mean(diff * diff, axis=-1))
    count, error_total = lax.psum((count_here, error_here), ("ctx", "fsdp"))
    loss = error_total / count
    output_gradient = cotangent[0].astype(jnp.float32) + maskf[:, None] * diff * (
        2.0 / (count * width)
    )
    g_mo = output_gradient.astype(jnp.bfloat16)
    mlp_back = (
        lax.all_gather(mlp_gain, "fsdp", axis=0, tiled=True),
        lax.all_gather(w_gate, "fsdp", axis=0, tiled=True),
        lax.all_gather(w_up, "fsdp", axis=0, tiled=True),
        lax.all_gather(w_down, "fsdp", axis=0, tiled=True),
    )
    g_act = lax.dot_general(g_mo, mlp_back[3], CONTRACT_COLS, preferred_element_type=jnp.float32)
    g_gate = (g_act * up_val * sigma * (1.0 + gate * (1.0 - sigma))).astype(jnp.bfloat16)
    g_up = (g_act * gate * sigma).astype(jnp.bfloat16)
    gate_up_gradient = jnp.concatenate([g_gate, g_up], axis=1)
    second_norm_gradient = lax.dot_general(
        g_gate, mlp_back[1], CONTRACT_COLS, preferred_element_type=jnp.float32
    )
    second_norm_gradient = second_norm_gradient + lax.dot_general(
        g_up, mlp_back[2], CONTRACT_COLS, preferred_element_type=jnp.float32
    )
    second_hat_gradient = second_norm_gradient * second_norm_scale
    residual_gradient = output_gradient + second_inverse_norm * (
        second_hat_gradient
        - second_normalized_input
        * jnp.mean(second_hat_gradient * second_normalized_input, axis=-1, keepdims=True)
    )
    mlp_share = lax.psum_scatter(
        lax.dot_general(
            second_normed, gate_up_gradient, CONTRACT_ROWS, preferred_element_type=jnp.float32
        ),
        ("ctx", "fsdp"),
        scatter_dimension=0,
        tiled=True,
    )
    down_share = lax.psum_scatter(
        lax.dot_general(act, g_mo, CONTRACT_ROWS, preferred_element_type=jnp.float32),
        ("ctx", "fsdp"),
        scatter_dimension=0,
        tiled=True,
    )
    g_branch = residual_gradient.astype(jnp.bfloat16)
    attn_back = (
        lax.all_gather(attn_gain, "fsdp", axis=0, tiled=True),
        lax.all_gather(w_query, "fsdp", axis=0, tiled=True),
        lax.all_gather(w_key, "fsdp", axis=0, tiled=True),
        lax.all_gather(value_weight, "fsdp", axis=0, tiled=True),
        lax.all_gather(w_output, "fsdp", axis=0, tiled=True),
    )
    attention_gradient = lax.dot_general(
        g_branch, attn_back[4], CONTRACT_COLS, preferred_element_type=jnp.float32
    ).astype(jnp.bfloat16)
    heads_gradient = attention_gradient.reshape(
        local_token_count, KEY_VALUE_HEADS, query_group, HEAD_SIZE
    ).transpose(1, 0, 2, 3)

    def attend_back(parts):
        head_query, head_key, head_val, head_lse, head_grad = parts
        attention_probabilities = jnp.exp(head_scores(head_query, head_key, allowed) - head_lse)
        g_probs = jnp.einsum("trd,sd->rts", head_grad, head_val, preferred_element_type=jnp.float32)
        delta = jnp.sum(attention_probabilities * g_probs, axis=-1, keepdims=True)
        g_scores = (attention_probabilities * (g_probs - delta)).astype(jnp.bfloat16)
        g_query = jnp.einsum(
            "rts,sd->trd", g_scores, head_key, preferred_element_type=jnp.float32
        ) * HEAD_SIZE ** (-0.5)
        key_gradient = jnp.einsum(
            "rts,trd->sd", g_scores, head_query, preferred_element_type=jnp.float32
        ) * HEAD_SIZE ** (-0.5)
        value_gradient = jnp.einsum(
            "rts,trd->sd",
            attention_probabilities.astype(jnp.bfloat16),
            head_grad,
            preferred_element_type=jnp.float32,
        )
        return (g_query, key_gradient, value_gradient)

    g_query, key_gradient, value_gradient = lax.map(
        attend_back, (query_head_rows, key_head_rows, value_head_rows, lse, heads_gradient)
    )
    key_gradient_terms = key_gradient.transpose(1, 0, 2).reshape(
        packed_stream_rows, KEY_VALUE_HEADS * HEAD_SIZE
    )
    value_gradient_terms = value_gradient.transpose(1, 0, 2).reshape(
        packed_stream_rows, KEY_VALUE_HEADS * HEAD_SIZE
    )
    key_rows_gradient, g_vals = (
        lax.psum_scatter(
            key_gradient_terms.astype(jnp.bfloat16), "ctx", scatter_dimension=0, tiled=True
        ).astype(jnp.float32),
        lax.psum_scatter(
            value_gradient_terms.astype(jnp.bfloat16), "ctx", scatter_dimension=0, tiled=True
        ).astype(jnp.float32),
    )
    g_qproj = (
        rotary_embed(
            g_query.transpose(1, 0, 2, 3).reshape(local_token_count, QUERY_HEADS, HEAD_SIZE),
            local_stream_offset,
            -1.0,
        )
        .reshape(local_token_count, QUERY_HEADS * HEAD_SIZE)
        .astype(jnp.bfloat16)
    )
    g_kproj = (
        rotary_embed(
            key_rows_gradient.reshape(local_token_count, KEY_VALUE_HEADS, HEAD_SIZE),
            local_stream_offset,
            -1.0,
        )
        .reshape(local_token_count, KEY_VALUE_HEADS * HEAD_SIZE)
        .astype(jnp.bfloat16)
    )
    g_vproj = g_vals.astype(jnp.bfloat16)
    first_norm_gradient = lax.dot_general(
        g_qproj, attn_back[1], CONTRACT_COLS, preferred_element_type=jnp.float32
    )
    first_norm_gradient = first_norm_gradient + lax.dot_general(
        g_kproj, attn_back[2], CONTRACT_COLS, preferred_element_type=jnp.float32
    )
    first_norm_gradient = first_norm_gradient + lax.dot_general(
        g_vproj, attn_back[3], CONTRACT_COLS, preferred_element_type=jnp.float32
    )
    first_hat_gradient = first_norm_gradient * first_norm_scale
    g_input = residual_gradient + first_inverse_norm * (
        first_hat_gradient
        - first_normalized_input
        * jnp.mean(first_hat_gradient * first_normalized_input, axis=-1, keepdims=True)
    )
    key_value_proj_gradient = jnp.concatenate([g_kproj, g_vproj], axis=1)
    query_term = lax.dot_general(
        first_normed, g_qproj, CONTRACT_ROWS, preferred_element_type=jnp.float32
    )
    key_value_term = lax.dot_general(
        first_normed, key_value_proj_gradient, CONTRACT_ROWS, preferred_element_type=jnp.float32
    )
    output_term = lax.dot_general(attn, g_branch, CONTRACT_ROWS, preferred_element_type=jnp.float32)
    scale_gradient_terms = jnp.stack(
        [
            jnp.sum(first_norm_gradient * first_normalized_input, axis=0),
            jnp.sum(second_norm_gradient * second_normalized_input, axis=0),
        ]
    )
    query_share, key_value_share, output_share, gain_share = (
        lax.psum_scatter(query_term, ("ctx", "fsdp"), scatter_dimension=0, tiled=True),
        lax.psum_scatter(key_value_term, ("ctx", "fsdp"), scatter_dimension=0, tiled=True),
        lax.psum_scatter(output_term, ("ctx", "fsdp"), scatter_dimension=0, tiled=True),
        lax.psum_scatter(scale_gradient_terms, ("ctx", "fsdp"), scatter_dimension=1, tiled=True),
    )
    key_value_columns = KEY_VALUE_HEADS * HEAD_SIZE
    return (
        loss,
        outf.astype(jnp.bfloat16)[None],
        g_input.astype(jnp.bfloat16)[None],
        gain_share[0],
        query_share,
        key_value_share[:, :key_value_columns],
        key_value_share[:, key_value_columns:],
        output_share,
        gain_share[1],
        mlp_share[:, :FF],
        mlp_share[:, FF:],
        down_share,
    )


MESH = pl.DeviceIdType.MESH
F32 = jnp.float32
BF16 = jnp.bfloat16
NZ = 4


def place_on_plane():
    c = lax.axis_index("ctx")
    z = lax.axis_index("fsdp")
    sib = c + 1 - 2 * lax.rem(c, 2)
    xn = c + 2 - 4 * lax.rem(c // 2, 2)
    yn = c + 4 - 8 * (c // 4)
    diag = xn + yn - c
    return c, z, sib, xn, yn, diag


def meet(devices):
    barrier = pltpu.get_barrier_semaphore()
    for d in devices:
        pl.semaphore_signal(barrier, inc=1, device_id=d, device_id_type=MESH)
    pl.semaphore_wait(barrier, len(devices))


def remote(src, dst, send, recv, device):
    return pltpu.make_async_remote_copy(
        src_ref=src, dst_ref=dst, send_sem=send, recv_sem=recv, device_id=device, device_id_type=MESH
    )


def takes(micros):
    return pl.CostEstimate(flops=0, bytes_accessed=micros * 3_500_000, transcendentals=0)


class Plane:
    def __init__(self, here, slot, send, recv, half):
        self.c, self.z, self.sib, self.xn, self.yn, self.diag = here
        self.slot, self.send, self.recv, self.half = slot, send, recv, half

    def copy(self, kind, src, dst, to):
        return remote(src, dst, self.send.at[kind], self.recv.at[kind], (to, self.z))

    def first(self, src):
        mine = self.slot(self.c)
        return [self.copy(0, src, mine, self.xn), self.copy(1, src, mine, self.yn), self.copy(2, src, mine, self.sib)]

    def arrive(self):
        s = self.slot
        return [self.copy(0, s(self.xn), s(self.xn), self.xn), self.copy(1, s(self.yn), s(self.yn), self.yn)]

    def second(self):
        h = self.half
        s = self.slot
        ybot = s(self.yn).at[pl.ds(0, h)]
        xtop = s(self.xn).at[pl.ds(h, h)]
        return (
            [self.copy(4, xtop, xtop, self.yn), self.copy(5, s(self.xn), s(self.xn), self.sib)],
            [self.copy(3, ybot, ybot, self.xn), self.copy(6, s(self.yn), s(self.yn), self.sib)],
        )

    def diagonal(self):
        h = self.half
        lo, hi = self.slot(self.diag).at[pl.ds(0, h)], self.slot(self.diag).at[pl.ds(h, h)]
        return [self.copy(3, lo, lo, self.xn), self.copy(4, hi, hi, self.yn)]

    def third(self):
        d = self.slot(self.diag)
        return self.copy(7, d, d, self.sib)

    def across(self):
        s = self.slot
        return [self.copy(k, s(j), s(j), self.sib) for k, j in ((2, self.sib), (5, self.xn + self.sib - self.c), (6, self.yn + self.sib - self.c), (7, self.diag + self.sib - self.c))]


def add_rows(dst, parts, chunk=16):
    n = dst.shape[0] // chunk

    def body(i, _):
        at = pl.ds(pl.multiple_of(i * chunk, chunk), chunk)
        total = parts[0][at, :].astype(F32)
        for p in parts[1:]:
            total = total + p[at, :].astype(F32)
        dst[at, :] = total.astype(dst.dtype)
        return 0

    lax.fori_loop(0, n, body, 0)


def plane_order(z):
    pick = jnp.where
    return [z, pick(z == 0, 1, z - 1), pick(z == 3, 1, pick(z == 2, 3, 2)), pick(z < 2, 3, 0)]


def chip_at(c, b):
    x, y = lax.rem(c // 2, 2), c // 4
    xb, yb = lax.rem(b, 2), b // 2
    return (x + xb - 2 * x * xb) + 2 * (y + yb - 2 * y * yb)


def chunk_order(i):
    return jnp.where(i == 0, 3, jnp.where(i == 3, 0, i))


class Gather:
    def __init__(self, here, x_ref, o_ref, keep, zsend, zrecv, send, recv):
        self.here, self.x, self.o = here, x_ref, o_ref
        self.c, self.z = here[0], here[1]
        self.order = plane_order(self.z)
        self.zsend, self.zrecv = zsend, zrecv
        self.planes = [
            Plane(here, functools.partial(lambda zz, j: o_ref.at[zz, j], zz), send.at[zz], recv.at[zz], x_ref.shape[0] // 2)
            for zz in self.order
        ]
        self.keep = pltpu.make_async_copy(x_ref, o_ref.at[self.z, self.c], keep)

    def hop(self, up, t):
        zz = self.order[t]
        src = self.x if t == 0 else self.o.at[zz, self.c]
        row = 0 if up else 1
        return remote(
            src, self.o.at[zz, self.c], self.zsend.at[row, zz], self.zrecv.at[zz], (self.c, self.z + (1 if up else -1))
        )

    def hops(self, t, act):
        zz, z = self.order[t], self.z

        @pl.when((zz <= z) & (z < NZ - 1))
        def _():
            act(self.hop(True, t))

        @pl.when((zz >= z) & (z > 0))
        def _():
            act(self.hop(False, t))

    def spread(self, t):
        if t > 0:
            self.hop(True, t).wait_recv()
        self.hops(t, lambda cp: cp.start())
        for cp in self.planes[t].first(self.source(t)):
            cp.start()

    def source(self, t):
        return self.x if t == 0 else self.o.at[self.order[t], self.c]

    def onward(self, t):
        p = self.planes[t]
        for arrived, sends in zip(p.arrive(), p.second()):
            arrived.wait_recv()
            for cp in sends:
                cp.start()

    def close(self, t):
        p = self.planes[t]
        for cp in p.diagonal():
            cp.wait_recv()
        p.third().start()
        for cp in p.across():
            cp.wait_recv()
        if t == 0:
            self.keep.wait()

    def end(self):
        for t, p in enumerate(self.planes):
            for cp in p.first(self.source(t)) + p.second()[0] + p.second()[1] + [p.third()]:
                cp.wait_send()
            self.hops(t, lambda cp: cp.wait_send())


class Scatter:
    def __init__(self, here, order, part, sibr, xh, yh, xf, yf, zr, bsend, brecv, hsend, hrecv, fsend, frecv, zsend, zrecv):
        self.c, self.z, self.sib, self.xn, self.yn, self.diag = here
        self.k = lax.rem(self.c, 2)
        self.order = order
        self.part, self.sibr, self.xh, self.yh, self.xf, self.yf, self.zr = part, sibr, xh, yh, xf, yf, zr
        self.sems = (bsend, brecv, hsend, hrecv, fsend, frecv, zsend, zrecv)
        self.h = part.shape[3] // 2

    def mine(self, t, b):
        return self.part.at[t, b, self.k]

    def cross(self, t, b):
        send, recv = self.sems[0:2]
        return remote(self.part.at[t, b, 1 - self.k], self.sibr.at[t, b], send.at[t, b], recv.at[t, b], (self.sib, self.z))

    def halves(self, t):
        send, recv = self.sems[2:4]
        src = self.mine(t, 3)
        return (
            remote(src.at[pl.ds(0, self.h)], self.xh.at[t], send.at[t, 0], recv.at[t, 0], (self.xn, self.z)),
            remote(src.at[pl.ds(self.h, self.h)], self.yh.at[t], send.at[t, 1], recv.at[t, 1], (self.yn, self.z)),
        )

    def fulls(self, t):
        send, recv = self.sems[4:6]
        return (
            remote(self.mine(t, 1), self.xf.at[t], send.at[t, 0], recv.at[t, 0], (self.xn, self.z)),
            remote(self.mine(t, 2), self.yf.at[t], send.at[t, 1], recv.at[t, 1], (self.yn, self.z)),
        )

    def hop(self, t):
        send, recv = self.sems[6:8]
        return remote(self.mine(t, 0), self.zr.at[self.z], send.at[t], recv.at[self.z], (self.c, self.order[t]))

    def came(self, t):
        send, recv = self.sems[6:8]
        zz = self.order[t]
        return remote(self.zr.at[zz], self.zr.at[zz], send.at[t], recv.at[zz], (self.c, zz))

    def one(self, t):
        self.cross(t, 3).wait_recv()
        add_rows(self.mine(t, 3), [self.mine(t, 3), self.sibr.at[t, 3]])
        for cp in self.halves(t):
            cp.start()

    def two(self, t):
        h = self.h
        top, low = pl.ds(0, h), pl.ds(h, h)
        hx, hy = self.halves(t)
        fx, fy = self.fulls(t)
        self.cross(t, 1).wait_recv()
        m, s = self.mine(t, 1), self.sibr.at[t, 1]
        add_rows(m.at[top], [m.at[top], s.at[top]])
        hy.wait_recv()
        add_rows(m.at[low], [m.at[low], s.at[low], self.yh.at[t]])
        fx.start()
        self.cross(t, 2).wait_recv()
        m, s = self.mine(t, 2), self.sibr.at[t, 2]
        add_rows(m.at[low], [m.at[low], s.at[low]])
        hx.wait_recv()
        add_rows(m.at[top], [m.at[top], s.at[top], self.xh.at[t]])
        fy.start()

    def three(self, t, o_ref):
        self.cross(t, 0).wait_recv()
        for cp in self.fulls(t):
            cp.wait_recv()
        parts = [self.mine(t, 0), self.sibr.at[t, 0], self.xf.at[t], self.yf.at[t]]
        if t == 0:
            add_rows(o_ref, parts)
        else:
            add_rows(self.mine(t, 0), parts)
            self.hop(t).start()

    def end(self, o_ref):
        n = len(self.order)
        for t in range(1, n):
            self.came(t).wait_recv()
        if n > 1:
            add_rows(o_ref, [o_ref] + [self.zr.at[self.order[t]] for t in range(1, n)])
        for t in range(n):
            for b in range(4):
                self.cross(t, b).wait_send()
            for cp in self.halves(t) + self.fulls(t):
                cp.wait_send()
            if t > 0:
                self.hop(t).wait_send()


def scatter_scratch(n, rows, width):
    v, dma = pltpu.VMEM, pltpu.SemaphoreType.DMA
    return [
        v((n, 4, 2, rows, width), BF16), v((n, 4, rows, width), BF16),
        v((n, rows // 2, width), BF16), v((n, rows // 2, width), BF16),
        v((n, rows, width), BF16), v((n, rows, width), BF16), v((NZ, rows, width), BF16),
        dma((n, 4)), dma((n, 4)), dma((n, 2)), dma((n, 2)), dma((n, 2)), dma((n, 2)), dma((NZ,)), dma((NZ,)),
    ]


def neighbours(here):
    c, z, sib, xn, yn, diag = here
    return [(sib, z), (xn, z), (yn, z)] + [(c, lax.rem(z + s, NZ)) for s in (1, 2, 3)]


def everyone_else(c, z):
    flat = c * NZ + z
    others = [lax.rem(flat + s, 32) for s in range(1, 32)]
    return flat, [(o // NZ, lax.rem(o, NZ)) for o in others]


def feed_kernel(
    x_ref, gate_in, wu_ref, d_in, o_ref, all_ref, gu_ref, w_out,
    w_ref, d_ref, xs, gs, xsem, gsem, wsend, wrecv, wkeep, keep, zsend, zrecv, send, recv, *scat
):
    here = place_on_plane()
    c, z = here[0], here[1]
    meet(neighbours(here))
    gather_ = Gather(here, x_ref, all_ref, keep.at[0], zsend, zrecv, send, recv)
    order = gather_.order
    sums = Scatter(here, order, *scat)
    ff = d_ref.shape[0]
    gather_.keep.start()
    gather_.spread(0)

    def load(t, b):
        src = all_ref.at[order[t], pl.ds(2 * chip_at(c, b), 2)]
        return pltpu.make_async_copy(src, xs.at[b], xsem.at[b])

    def store(t, b):
        return pltpu.make_async_copy(gs.at[b], gu_ref.at[order[t], chip_at(c, b)], gsem.at[b])

    def work(t, lo, hi):
        for b in (3, 1, 2, 0)[lo:hi]:
            load(t, b).start()

        def body(i, _):
            b = chunk_order(i)
            load(t, b).wait()
            if t != 1:
                store(1, b).wait()
            x = xs[b].reshape(-1, xs.shape[-1])
            gu = jnp.dot(x, w_ref[...].reshape(x.shape[1], -1), preferred_element_type=F32)
            gs[b] = gu
            store(t, b).start()
            gate, up = gu[:, :ff], gu[:, ff:]
            act = (gate * jax.nn.sigmoid(gate) * up).astype(BF16)
            p = jnp.dot(act, d_ref[...], preferred_element_type=F32).astype(BF16)
            sums.part[t, b] = p.reshape(sums.part.shape[2:])
            sums.cross(t, b).start()
            return 0

        lax.fori_loop(lo, hi, body, 0)

    weights = []
    keeps = [pltpu.make_async_copy(d_in, d_ref, wkeep.at[0])]
    keeps.append(pltpu.make_async_copy(gate_in, w_ref.at[:, :, pl.ds(0, ff)], wkeep.at[1]))
    for hop in range(NZ):
        to = lax.rem(z + hop, NZ)
        src = wu_ref.at[:, pl.ds(pl.multiple_of((c * NZ + to) * ff, ff), ff)]
        dst = w_ref.at[z, :, pl.ds(ff, ff)]
        if hop == 0:
            keeps.append(pltpu.make_async_copy(src, dst, wkeep.at[2]))
        else:
            weights.append(remote(src, dst, wsend.at[hop], wrecv.at[hop], (c, to)))
    w_keep = pltpu.make_async_copy(w_ref, w_out, wkeep.at[3])

    def early():
        for cp in keeps + weights:
            cp.start()

    def ready():
        for cp in keeps + weights:
            cp.wait()
        w_keep.start()

    fused_steps(gather_, sums, work, o_ref, False, early=early, ready=ready)
    for b in range(4):
        store(0, b).wait()
    w_keep.wait()


def fused_steps(gather_, sums, work, o_ref, own_first, more=lambda t: None, early=lambda: None, ready=lambda: None):
    gather_.spread(1)
    gather_.onward(0)
    early()
    gather_.spread(2)
    if own_first:
        ready()
        gather_.close(0)
        work(0, 0, 2)
    gather_.onward(1)
    if own_first:
        work(0, 2, 4)
    gather_.spread(3)
    if own_first:
        more(0)
    gather_.onward(2)
    if not own_first:
        ready()
    gather_.close(1)
    work(1, 0, 4)
    gather_.onward(3)
    sums.one(1)
    if own_first:
        sums.one(0)
    more(1)
    gather_.close(2)
    work(2, 0, 2)
    sums.one(2)
    work(2, 2, 4)
    sums.two(2)
    more(2)
    gather_.close(3)
    work(3, 0, 2)
    sums.one(3)
    work(3, 2, 4)
    sums.three(2, o_ref)
    sums.two(3)
    more(3)
    if not own_first:
        gather_.close(0)
        work(0, 0, 4)
    sums.three(3, o_ref)
    if not own_first:
        sums.one(0)
        more(0)
    sums.two(1)
    sums.three(1, o_ref)
    sums.two(0)
    sums.three(0, o_ref)
    sums.end(o_ref)
    gather_.end()


def gather_sems():
    dma = pltpu.SemaphoreType.DMA
    return [dma((1,)), dma((2, 4)), dma((4,)), dma((4, 8)), dma((4, 8))]


def feed_forward(x, gate, w_up, d):
    rows, width = x.shape
    depth, cols = w_up.shape[0], 2 * d.shape[0]
    any_ = pl.BlockSpec(memory_space=pl.ANY)
    vmem = pl.BlockSpec(memory_space=pltpu.VMEM)
    dma = pltpu.SemaphoreType.DMA
    return pl.pallas_call(
        feed_kernel,
        out_shape=(
            jax.ShapeDtypeStruct((rows, width), F32),
            jax.ShapeDtypeStruct((NZ, 8, rows, width), BF16),
            jax.ShapeDtypeStruct((NZ, 4, 2 * rows, cols), F32),
            jax.ShapeDtypeStruct((NZ, depth, cols), BF16),
        ),
        in_specs=[vmem, any_, any_, any_],
        out_specs=(vmem, any_, any_, any_),
        scratch_shapes=[
            pltpu.VMEM((NZ, depth, cols), BF16), pltpu.VMEM(d.shape, BF16),
            pltpu.VMEM((4, 2, rows, width), BF16), pltpu.VMEM((4, 2 * rows, cols), F32), dma((4,)), dma((4,)),
            dma((4,)), dma((4,)), dma((4,)),
        ] + gather_sems() + scatter_scratch(NZ, rows, width),
        compiler_params=pltpu.CompilerParams(collective_id=5, has_side_effects=True, vmem_limit_bytes=60 << 20),
        cost_estimate=takes(180),
        name="feed_forward",
    )(x, gate, w_up, d)


def feed_back_kernel(
    x_ref, w_in, d_in, n_ref, gu_ref, o_ref, all_ref, gate_out, up_out, down_out,
    w_ref, d_ref, gate_o, up_o, down_o, wsem, gsend, grecv, xs, ns, gs, gg, acts, total, xsem, nsem, gsem, keep, zsend, zrecv, send, recv, *scat
):
    here = place_on_plane()
    c, z = here[0], here[1]
    meet(neighbours(here))
    gather_ = Gather(here, x_ref, all_ref, keep.at[0], zsend, zrecv, send, recv)
    order = gather_.order
    sums = Scatter(here, order, *scat)
    ff = d_ref.shape[0]
    tokens = 8 * x_ref.shape[0]
    gather_.keep.start()
    gather_.spread(0)

    def loads(t, b):
        chip = chip_at(c, b)
        pair = pl.ds(2 * chip, 2)
        return (
            pltpu.make_async_copy(gu_ref.at[order[t], chip], gs.at[b], gsem.at[b]),
            pltpu.make_async_copy(all_ref.at[order[t], pair], xs.at[b], xsem.at[b]),
            pltpu.make_async_copy(n_ref.at[order[t], pair], ns.at[b], nsem.at[b]),
        )

    def work(t, lo, hi):
        for b in (3, 1, 2, 0)[lo:hi]:
            for cp in loads(t, b):
                cp.start()

        def body(i, _):
            b = chunk_order(i)
            stored, tokens_in, _ = loads(t, b)
            stored.wait()
            tokens_in.wait()
            g = xs[b].reshape(-1, xs.shape[-1])
            g_act = lax.dot_general(g, d_ref[...], CONTRACT_COLS, preferred_element_type=F32)
            gate, up = gs[b, :, :ff], gs[b, :, ff:]
            sg = jax.nn.sigmoid(gate)
            acts[b] = (gate * sg * up).astype(BF16)
            gg[b, :, :ff] = (g_act * up * sg * (1.0 + gate * (1.0 - sg))).astype(BF16)
            gg[b, :, ff:] = (g_act * gate * sg).astype(BF16)
            p = lax.dot_general(gg[b], w_ref[...].reshape(o_ref.shape[1], -1), CONTRACT_COLS, preferred_element_type=F32).astype(BF16)
            sums.part[t, b] = p.reshape(sums.part.shape[2:])
            sums.cross(t, b).start()
            return 0

        lax.fori_loop(lo, hi, body, 0)

    piece = 512

    def more(t):
        for b in range(4):
            loads(t, b)[2].wait()

        def body(i, _):
            at = pl.ds(pl.multiple_of(i * piece, piece), piece)
            n = ns[:, :, :, at].reshape(tokens, piece)
            w_term = lax.dot_general(n, gg[...].reshape(tokens, -1), CONTRACT_ROWS, preferred_element_type=F32)
            g = xs[:, :, :, at].reshape(tokens, piece)
            d_term = lax.dot_general(acts[...].reshape(tokens, -1), g, CONTRACT_ROWS, preferred_element_type=F32)
            if t > 0:
                w_term = w_term + total[at, :]
                d_term = d_term + down_o[:, at]
            down_o[:, at] = d_term
            if t < NZ - 1:
                total[at, :] = w_term
            else:
                pair = pl.ds(2 * i, 2)
                gate_o[pair] = w_term[:, :ff].astype(BF16).reshape((2,) + gate_o.shape[1:])
                up_o[pair] = w_term[:, ff:].astype(BF16).reshape((2,) + up_o.shape[1:])
            return 0

        lax.fori_loop(0, o_ref.shape[1] // piece, body, 0)

    keeps = [pltpu.make_async_copy(w_in, w_ref, wsem.at[0]), pltpu.make_async_copy(d_in, d_ref, wsem.at[1])]
    saved = [
        pltpu.make_async_copy(src, dst, wsem.at[2 + i])
        for i, (src, dst) in enumerate(((gate_o.at[:, z], gate_out.at[:, z]), (up_o, up_out), (down_o, down_out)))
    ]
    gate_z = []
    for s in (1, 2, 3):
        to = lax.rem(z + s, NZ)
        gate_z.append(remote(gate_o.at[:, to], gate_out.at[:, z], gsend.at[s], grecv.at[s], (c, to)))

    def early():
        for cp in keeps:
            cp.start()

    def ready():
        for cp in keeps:
            cp.wait()

    def more_and_save(t):
        more(t)
        if t == NZ - 1:
            for cp in gate_z + saved:
                cp.start()

    fused_steps(gather_, sums, work, o_ref, True, more_and_save, early, ready)
    for cp in saved + gate_z:
        cp.wait()


def feed_back(x, w, d, normed, gate_up):
    rows, width = x.shape
    cols = w.shape[2]
    ff = d.shape[0]
    by_owner = (8, NZ, width // 32, ff)
    any_ = pl.BlockSpec(memory_space=pl.ANY)
    vmem = pl.BlockSpec(memory_space=pltpu.VMEM)
    dma, buf = pltpu.SemaphoreType.DMA, pltpu.VMEM
    return pl.pallas_call(
        feed_back_kernel,
        out_shape=(
            jax.ShapeDtypeStruct((rows, width), F32),
            jax.ShapeDtypeStruct((NZ, 8, rows, width), BF16),
            jax.ShapeDtypeStruct(by_owner, BF16),
            jax.ShapeDtypeStruct(by_owner, BF16),
            jax.ShapeDtypeStruct((ff, width), F32),
        ),
        in_specs=[vmem] + [any_] * 4,
        out_specs=(vmem,) + (any_,) * 4,
        scratch_shapes=[
            buf(w.shape, BF16), buf(d.shape, BF16), buf(by_owner, BF16), buf(by_owner, BF16), buf((ff, width), F32),
            dma((5,)), dma((4,)), dma((4,)), buf((4, 2, rows, width), BF16), buf((4, 2, rows, width), BF16), buf((4, 2 * rows, cols), F32),
            buf((4, 2 * rows, cols), BF16), buf((4, 2 * rows, ff), BF16), buf((width, cols), F32),
            dma((4,)), dma((4,)), dma((4,)),
        ] + gather_sems() + scatter_scratch(NZ, rows, width),
        compiler_params=pltpu.CompilerParams(collective_id=7, has_side_effects=True, vmem_limit_bytes=63 << 20),
        cost_estimate=takes(180),
        name="feed_back",
    )(x, w, d, normed, gate_up)


ROWS_AT_ONCE = 256


def turn(u, cosine, sine):
    return u * cosine + pltpu.roll(u, HEAD_SIZE // 2, 1) * sine


def block_probs(q, k, first, place, keys_place):
    scores = lax.dot_general(q, k, CONTRACT_COLS, preferred_element_type=F32) * HEAD_SIZE ** (-0.5)
    allowed = (keys_place >= first) & (keys_place <= place)
    scores = jnp.where(allowed, scores, NEG)
    raised = jnp.exp(scores - jnp.max(scores, axis=-1, keepdims=True))
    return raised / jnp.sum(raised, axis=-1, keepdims=True)


def fetches(pairs, sems):
    copies = [pltpu.make_async_copy(src, dst, sems.at[i]) for i, (src, dst) in enumerate(pairs)]
    for cp in copies:
        cp.start()
    return copies


def exchange_loop(c, z, act):
    flat = c * NZ + z

    def body(s, _):
        to = lax.rem(flat + s, 32)
        act(s, to // NZ, lax.rem(to, NZ))
        return 0

    lax.fori_loop(1, 32, body, 0)


def back_kernel(
    g_ref, err_ref, q_in, k_in, v_in, attn_in, cos_in, sin_in, first_in, place_in, keys_in, wqkv_in, wout_in, gain_in,
    norm_in, gate_ref, up_ref,
    o_ref, gate_o, up_o, qkv_o, out_o, gain_o,
    q_ref, k_ref, v_ref, attn_ref, cos_ref, sin_ref, first_ref, place_ref, keys_ref, wqkv_ref, wout_ref, gain_ref, normed, isem,
    gb, ga, gqkv, gk, gv, outg, qkvg, mt, qt, qs, gsrc,
    msend, mrecv, m2send, m2recv, qsend, qrecv, q2send, q2recv, osend, orecv, ssend, srecv, lsem, psend, precv, *scat
):
    here = place_on_plane()
    c, z, sib, xn, yn, diag = here
    flat, everyone = everyone_else(c, z)
    meet(everyone)
    rows, width = g_ref.shape
    tokens = 8 * rows
    share = width // 32
    plane = Plane(here, lambda j: gb.at[j], psend, precv, rows // 2)
    sums = Scatter(here, [z], *scat)
    mates = [lax.rem(c + s, 8) for s in range(1, 8)]
    others = [(s, lax.rem(z + s, NZ)) for s in (1, 2, 3)]
    for cp in plane.first(g_ref):
        cp.start()

    mlp_z = [remote(up_ref.at[:, to], mt.at[:, z], msend.at[s], mrecv.at[s], (c, to)) for s, to in others]
    keep = pltpu.make_async_copy(up_ref.at[:, z], mt.at[:, z], lsem.at[1])
    for cp in mlp_z + [keep]:
        cp.start()
    from_me = pl.ds(pl.multiple_of(c * NZ, NZ), NZ)

    def over_plane(i, ref):
        dst = (gate_o, up_o)[i]
        out = [
            remote(ref.at[m], dst.at[from_me], m2send.at[i, s], m2recv.at[i, s], (m, z)) for s, m in enumerate(mates)
        ]
        out.append(pltpu.make_async_copy(ref.at[c], dst.at[from_me], lsem.at[2 + i]))
        for cp in out:
            cp.start()
        return out

    got = fetches(
        [
            (wout_in, wout_ref), (q_in, q_ref), (k_in, k_ref), (v_in, v_ref), (cos_in, cos_ref), (sin_in, sin_ref),
            (first_in, first_ref), (place_in, place_ref), (keys_in, keys_ref),
            (attn_in, attn_ref), (norm_in, normed), (wqkv_in, wqkv_ref), (gain_in, gain_ref),
        ],
        isem,
    )
    gb[c] = g_ref[...]
    gk[...] = jnp.zeros_like(gk)
    gv[...] = jnp.zeros_like(gv)

    def attend(b):
        chip = chip_at(c, b)
        at = pl.ds(pl.multiple_of(chip * ROWS_AT_ONCE, ROWS_AT_ONCE), ROWS_AT_ONCE)
        g_rows = gb[pl.ds(chip * 2, 2)].reshape(ROWS_AT_ONCE, width)
        ga[at, :] = lax.dot_general(g_rows, wout_ref[...], CONTRACT_COLS, preferred_element_type=F32).astype(BF16)
        k, v = k_ref[...], v_ref[...]
        cosine, sine = cos_ref[at, :], sin_ref[at, :]
        first, place, keys = first_ref[at, :], place_ref[at, :], keys_ref[...]
        for h in range(QUERY_HEADS // KEY_VALUE_HEADS):
            lanes = slice(h * HEAD_SIZE, (h + 1) * HEAD_SIZE)
            q, g = q_ref[at, lanes], ga[at, lanes]
            probs = block_probs(q, k, first, place, keys)
            g_probs = lax.dot_general(g, v, CONTRACT_COLS, preferred_element_type=F32)
            delta = jnp.sum(probs * g_probs, axis=-1, keepdims=True)
            g_scores = (probs * (g_probs - delta)).astype(BF16)
            g_q = jnp.dot(g_scores, k, preferred_element_type=F32) * HEAD_SIZE ** (-0.5)
            gqkv[at, lanes] = turn(g_q, cosine, -sine).astype(BF16)
            gk[...] += lax.dot_general(g_scores, q, CONTRACT_ROWS, preferred_element_type=F32)
            gv[...] += lax.dot_general(probs.astype(BF16), g, CONTRACT_ROWS, preferred_element_type=F32)

    came = plane.across()
    for cp in got[:9]:
        cp.wait()
    came[0].wait_recv()
    attend(0)
    for arrived, sends in zip(plane.arrive(), plane.second()):
        arrived.wait_recv()
        for cp in sends:
            cp.start()
    came[1].wait_recv()
    attend(1)
    for cp in plane.diagonal():
        cp.wait_recv()
    plane.third().start()
    came[2].wait_recv()
    attend(2)
    came[3].wait_recv()
    mlp_c = over_plane(0, gate_ref)
    got[9].wait()
    piece = 512

    def outs(i, _):
        at = pl.ds(pl.multiple_of(i * piece, piece), piece)
        g = gb[:, :, at].reshape(tokens, piece)
        outg[:, at] = lax.dot_general(attn_ref[...], g, CONTRACT_ROWS, preferred_element_type=F32).astype(BF16)
        return 0

    lax.fori_loop(0, width // piece, outs, 0)
    out_sends = []
    for s, to in others:
        src = outg.at[pl.ds(pl.multiple_of(to * share, share), share)]
        out_sends.append(remote(src, out_o.at[z], osend.at[s], orecv.at[s], (c, to)))
    for cp in out_sends:
        cp.start()
    keep_o = pltpu.make_async_copy(outg.at[pl.ds(pl.multiple_of(z * share, share), share)], out_o.at[z], lsem.at[5])
    keep_o.start()
    attend(3)
    qcols = q_ref.shape[1]
    g_k = gk[...] * HEAD_SIZE ** (-0.5)
    gqkv[:, qcols : qcols + HEAD_SIZE] = turn(g_k, cos_ref[...], -sin_ref[...]).astype(BF16)
    gqkv[:, qcols + HEAD_SIZE :] = gv[...].astype(BF16)

    for cp in got[10:]:
        cp.wait()
    cols = gqkv.shape[1]

    def project(i, _):
        at = pl.ds(pl.multiple_of(i * piece, piece), piece)
        term = lax.dot_general(normed[:, at], gqkv[...], CONTRACT_ROWS, preferred_element_type=F32).astype(BF16)
        qkvg[pl.ds(2 * i, 2)] = term.reshape(2, NZ, share, cols)
        return 0

    lax.fori_loop(0, width // piece, project, 0)
    qkv_z = [remote(qkvg.at[:, to], qt.at[s], qsend.at[s], qrecv.at[s], (c, to)) for s, to in others]
    for cp in qkv_z:
        cp.start()

    gsrc[...] = jnp.zeros_like(gsrc)
    gsrc[1:2, :] = gain_ref[...]
    gsrc[2:3, :] = jnp.full((1, width), err_ref[0, 0], F32)
    for b in (3, 1, 2, 0):
        chip = chip_at(c, b)
        at = pl.ds(pl.multiple_of(chip * ROWS_AT_ONCE, ROWS_AT_ONCE), ROWS_AT_ONCE)
        p = lax.dot_general(gqkv[at, :], wqkv_ref[...], CONTRACT_COLS, preferred_element_type=F32)
        sums.part[0, b] = p.astype(BF16).reshape(2, rows, width)
        sums.cross(0, b).start()
        gsrc[0:1, :] += jnp.sum(p * normed[at, :].astype(F32), axis=0, keepdims=True)

    def gain_sends(act):
        def one(s, tc, tz):
            lanes = pl.ds(pl.multiple_of((tc * NZ + tz) // 2 * 128, 128), 128)
            act(remote(gsrc.at[:, lanes], gain_o.at[flat], ssend.at[s], srecv.at[s], (tc, tz)))

        exchange_loop(c, z, one)

    gain_sends(lambda cp: cp.start())
    own_lanes = pl.ds(pl.multiple_of(flat // 2 * 128, 128), 128)
    gain_keep = pltpu.make_async_copy(gsrc.at[:, own_lanes], gain_o.at[flat], lsem.at[4])
    gain_keep.start()
    sums.one(0)
    for cp in mlp_z + [keep]:
        cp.wait()
    mlp_c += over_plane(1, mt)
    sums.two(0)

    sums.three(0, o_ref)

    for cp in qkv_z:
        cp.wait()

    def gathered(j, _):
        total = qkvg[j, z].astype(F32)
        for s in (1, 2, 3):
            total = total + qt[s, j].astype(F32)
        qs[j] = total.astype(BF16)
        return 0

    lax.fori_loop(0, 8, gathered, 0)
    qkv_c = [remote(qs.at[m], qkv_o.at[c], q2send.at[s], q2recv.at[s], (m, z)) for s, m in enumerate(mates)]
    qkv_keep = pltpu.make_async_copy(qs.at[c], qkv_o.at[c], lsem.at[6])
    for cp in qkv_c + [qkv_keep]:
        cp.start()
    sums.end(o_ref)
    for cp in plane.first(g_ref) + plane.second()[0] + plane.second()[1] + [plane.third()]:
        cp.wait_send()
    gain_sends(lambda cp: cp.wait())
    for cp in mlp_c + out_sends + qkv_c + [keep_o, qkv_keep, gain_keep]:
        cp.wait()


def attention_back(g, err, q, k, v, attn, cosine, sine, first, place, keys, w_qkv, w_out, gain, normed, gate_g, up_g):
    rows, width = g.shape
    tokens = q.shape[0]
    any_ = pl.BlockSpec(memory_space=pl.ANY)
    vmem = pl.BlockSpec(memory_space=pltpu.VMEM)
    dma, buf, out = pltpu.SemaphoreType.DMA, pltpu.VMEM, jax.ShapeDtypeStruct
    share = width // 32
    cols = w_qkv.shape[1]
    by_owner = gate_g.shape
    ff = by_owner[3]
    return pl.pallas_call(
        back_kernel,
        out_shape=(
            out((rows, width), F32),
            out((32, share, ff), BF16),
            out((32, share, ff), BF16),
            out((8, share, cols), BF16),
            out((NZ, share, width), BF16),
            out((32, 8, 128), F32),
        ),
        in_specs=[vmem, pl.BlockSpec(memory_space=pltpu.SMEM)] + [any_] * 15,
        out_specs=(vmem,) + (any_,) * 5,
        scratch_shapes=[
            buf(a.shape, a.dtype)
            for a in (q, k, v, attn, cosine, sine, first, place, keys, w_qkv, w_out, gain, normed)
        ] + [
            dma((13,)),
            buf((8, rows, width), BF16), buf(q.shape, BF16), buf((tokens, cols), BF16), buf(k.shape, F32), buf(v.shape, F32),
            buf(w_out.shape, BF16), buf((8, NZ, share, cols), BF16),
            buf(by_owner, BF16), buf((NZ, 8, share, cols), BF16), buf((8, share, cols), BF16), buf((8, width), F32),
            dma((4,)), dma((4,)), dma((2, 7)), dma((2, 7)), dma((4,)), dma((4,)), dma((7,)), dma((7,)), dma((4,)), dma((4,)),
            dma((32,)), dma((32,)), dma((7,)), dma((8,)), dma((8,)),
        ] + scatter_scratch(1, rows, width),
        compiler_params=pltpu.CompilerParams(collective_id=6, has_side_effects=True, vmem_limit_bytes=60 << 20),
        cost_estimate=takes(110),
        name="attention_back",
    )(g, err, q, k, v, attn, cosine, sine, first, place, keys, w_qkv, w_out, gain, normed, gate_g, up_g)


class Line:
    def __init__(self, c, z, slot, send, recv):
        self.c, self.z, self.slot, self.send, self.recv = c, z, slot, send, recv
        self.order = plane_order(z)

    def hop(self, up, t):
        zz = self.order[t]
        row = 0 if up else 1
        return remote(
            self.slot(zz), self.slot(zz), self.send.at[row, zz], self.recv.at[zz], (self.c, self.z + (1 if up else -1))
        )

    def hops(self, t, act):
        zz, z = self.order[t], self.z

        @pl.when((zz <= z) & (z < NZ - 1))
        def _():
            act(self.hop(True, t))

        @pl.when((zz >= z) & (z > 0))
        def _():
            act(self.hop(False, t))

    def step(self, t):
        if t > 0:
            self.hop(True, t).wait_recv()
        self.hops(t, lambda cp: cp.start())

    def end(self):
        for t in range(NZ):
            self.hops(t, lambda cp: cp.wait_send())


def front_kernel(
    x_ref, g_ref, mask_ref, wq_ref, wk_ref, wv_ref, wo_ref, wd_ref, wg_ref, cos_in, sin_in, first_in, place_in, keys_in,
    o_ref, go_ref, so_ref, norm_o, wqkv_o, outr_o, downr_o, gate_o, q_o, k_o, v_o, attn_o,
    wqkv, outr, downr, gatew, q_ref, k_ref, v_ref, attn_ref, cos_ref, sin_ref, first_ref, place_ref, keys_ref,
    normed, nall, acc, tmp_o, tmp_d, st_ref, isem, osem, wgsend, wgrecv, ssend, srecv,
    lsem, gsend, grecv, qzsend, qzrecv, ozsend, ozrecv, dsend, drecv, o2send, o2recv, d2send, d2recv, psend, precv, *scat
):
    here = place_on_plane()
    c, z, sib, xn, yn, diag = here
    rows, width = x_ref.shape
    tokens = 8 * rows
    wide = tmp_o.shape[2]
    mates = [lax.rem(c + s, 8) for s in range(1, 8)]
    others = [lax.rem(z + s, NZ) for s in (1, 2, 3)]
    flat, everyone = everyone_else(c, z)
    meet(everyone)
    sums = Scatter(here, [z], *scat)
    plane = Plane(here, lambda j: nall.at[j], psend, precv, rows // 2)
    line_q = Line(c, z, lambda zz: wqkv.at[zz], qzsend, qzrecv)
    line_o = Line(c, z, lambda zz: tmp_o.at[zz], ozsend, ozrecv)
    own_cols = pl.ds(pl.multiple_of(c * wide, wide), wide)

    def narrow(ref, n):
        return ref.at[:, pl.ds(pl.multiple_of(c * n, n), n)]

    q_keeps = [
        pltpu.make_async_copy(narrow(wq_ref, wide), wqkv.at[z, :, pl.ds(0, wide)], lsem.at[0]),
        pltpu.make_async_copy(narrow(wk_ref, HEAD_SIZE), wqkv.at[z, :, pl.ds(wide, HEAD_SIZE)], lsem.at[1]),
        pltpu.make_async_copy(narrow(wv_ref, HEAD_SIZE), wqkv.at[z, :, pl.ds(wide + HEAD_SIZE, HEAD_SIZE)], lsem.at[2]),
    ]
    o_keep = pltpu.make_async_copy(wo_ref.at[:, own_cols], tmp_o.at[z], lsem.at[3])
    d_keeps, downs = [], []
    for core in range(2):
        for hop in range(NZ):
            to = lax.rem(z + hop, NZ)
            src = wd_ref.at[pl.ds(pl.multiple_of((core * NZ + to) * wide, wide), wide), own_cols]
            if hop == 0:
                d_keeps.append(pltpu.make_async_copy(src, tmp_d.at[z, core], lsem.at[4 + core]))
            else:
                downs.append(remote(src, tmp_d.at[z, core], dsend.at[core, hop], drecv.at[core, hop], (c, to)))
    gate_cols = wg_ref.shape[1] // 32
    gates = []
    for hop in range(NZ):
        to = lax.rem(z + hop, NZ)
        src = wg_ref.at[:, pl.ds(pl.multiple_of((c * NZ + to) * gate_cols, gate_cols), gate_cols)]
        if hop == 0:
            g_keep = pltpu.make_async_copy(src, gatew.at[z], lsem.at[9])
        else:
            gates.append(remote(src, gatew.at[z], wgsend.at[hop], wgrecv.at[hop], (c, to)))
    for cp in [o_keep] + q_keeps + d_keeps + [g_keep]:
        cp.start()
    go_ref[z] = g_ref[...]
    gains = [remote(g_ref, go_ref.at[z], gsend.at[s], grecv.at[s], (c, t)) for s, t in enumerate(others)]
    for cp in gains:
        cp.start()
    o_keep.wait()
    line_o.step(0)
    got = fetches(
        [(cos_in, cos_ref), (sin_in, sin_ref), (first_in, first_ref), (place_in, place_ref), (keys_in, keys_ref)], isem
    )
    st_ref[...] = jnp.full(st_ref.shape, jnp.sum(mask_ref[...].astype(F32)), F32)
    so_ref[flat] = st_ref[...]

    def counts(act):
        def one(s, tc, tz):
            act(remote(st_ref, so_ref.at[flat], ssend.at[s], srecv.at[s], (tc, tz)))

        exchange_loop(c, z, one)

    x = x_ref[...].astype(F32)
    scaled = x * lax.rsqrt(jnp.mean(x * x, axis=-1, keepdims=True) + EPS)
    for cp in gains:
        cp.wait()
    piece = width // NZ
    for zz in range(NZ):
        normed[:, zz * piece : (zz + 1) * piece] = (
            scaled[:, zz * piece : (zz + 1) * piece] * go_ref[zz, 0:1, :]
        ).astype(BF16)
    for cp in plane.first(normed):
        cp.start()
    nall[c] = normed[...]
    counts(lambda cp: cp.start())
    line_o.step(1)
    for cp in q_keeps:
        cp.wait()
    line_q.step(0)
    line_o.step(2)
    for arrived, sends in zip(plane.arrive(), plane.second()):
        arrived.wait_recv()
        for cp in sends:
            cp.start()
    line_o.step(3)

    def regroup(buf, dst, send, recv, lrow):
        def block(j):
            return buf(j // 2, lax.rem(j, 2))

        out = [remote(block(m), dst.at[:, own_cols], send.at[s], recv.at[s], (m, z)) for s, m in enumerate(mates)]
        keep = pltpu.make_async_copy(block(c), dst.at[:, own_cols], lsem.at[lrow])
        for cp in out + [keep]:
            cp.start()
        return out + [keep]

    moved_o = regroup(lambda p, core: tmp_o.at[p, pl.ds(pl.multiple_of(core * wide, wide), wide)], outr, o2send, o2recv, 7)
    line_q.step(1)
    for cp in plane.diagonal():
        cp.wait_recv()
    plane.third().start()
    for cp in plane.across():
        cp.wait_recv()
    line_q.step(2)
    norm_keep = pltpu.make_async_copy(nall, norm_o, lsem.at[6])
    norm_keep.start()

    def project(t):
        zz = line_q.order[t]
        at = pl.ds(pl.multiple_of(zz * piece, piece), piece)
        term = jnp.dot(nall[:, :, at].reshape(tokens, piece), wqkv[zz], preferred_element_type=F32)
        acc[...] = term if t == 0 else acc[...] + term

    for t in range(3):
        project(t)
    line_q.step(3)
    for cp in downs:
        cp.start()
    project(3)
    for cp in got:
        cp.wait()

    def heads(i, _):
        at = pl.ds(pl.multiple_of(i * ROWS_AT_ONCE, ROWS_AT_ONCE), ROWS_AT_ONCE)
        cosine, sine = cos_ref[at, :], sin_ref[at, :]
        for h in range(wide // HEAD_SIZE):
            lanes = slice(h * HEAD_SIZE, (h + 1) * HEAD_SIZE)
            q_ref[at, lanes] = turn(acc[at, lanes], cosine, sine).astype(BF16)
        k_ref[at, :] = turn(acc[at, wide : wide + HEAD_SIZE], cosine, sine).astype(BF16)
        v_ref[at, :] = acc[at, wide + HEAD_SIZE :].astype(BF16)
        return 0

    lax.fori_loop(0, tokens // ROWS_AT_ONCE, heads, 0)

    saved = fetches([(wqkv, wqkv_o), (q_ref, q_o), (k_ref, k_o), (v_ref, v_o)], osem)

    def attend(b):
        at = pl.ds(pl.multiple_of(chip_at(c, b) * ROWS_AT_ONCE, ROWS_AT_ONCE), ROWS_AT_ONCE)
        k, v = k_ref[...], v_ref[...]
        first, place, keys = first_ref[at, :], place_ref[at, :], keys_ref[...]
        for h in range(wide // HEAD_SIZE):
            lanes = slice(h * HEAD_SIZE, (h + 1) * HEAD_SIZE)
            probs = block_probs(q_ref[at, lanes], k, first, place, keys)
            attn_ref[at, lanes] = jnp.dot(probs.astype(BF16), v, preferred_element_type=F32).astype(BF16)
        p = jnp.dot(attn_ref[at, :], outr[...], preferred_element_type=F32).astype(BF16)
        sums.part[0, b] = p.reshape(2, rows, width)
        sums.cross(0, b).start()

    for cp in moved_o:
        cp.wait()
    attend(3)
    attend(1)
    sums.one(0)
    attend(2)
    attend(0)
    saved += fetches([(outr, outr_o), (attn_ref, attn_o)], osem.at[pl.ds(4, 2)])
    sums.two(0)
    for cp in d_keeps + downs:
        cp.wait()
    moved_d = regroup(lambda p, core: tmp_d.at[p, core], downr, d2send, d2recv, 8)
    for cp in gates:
        cp.start()
    sums.three(0, o_ref)
    sums.end(o_ref)
    for cp in moved_d:
        cp.wait()
    saved += fetches([(downr, downr_o)], osem.at[pl.ds(6, 1)])
    for cp in gates + [g_keep]:
        cp.wait()
    saved += fetches([(gatew, gate_o)], osem.at[pl.ds(7, 1)])
    for cp in plane.first(normed) + plane.second()[0] + plane.second()[1] + [plane.third()]:
        cp.wait_send()
    line_q.end()
    line_o.end()
    counts(lambda cp: cp.wait())
    for cp in saved + [norm_keep]:
        cp.wait()


def attention_front(x, gains, mask, w_query, w_key, value_weight, w_output, w_down, w_gate, cosine, sine, first, place, keys):
    rows, width = x.shape
    tokens = 8 * rows
    depth = w_query.shape[0]
    wide = width // 8
    any_ = pl.BlockSpec(memory_space=pl.ANY)
    vmem = pl.BlockSpec(memory_space=pltpu.VMEM)
    dma, buf, out = pltpu.SemaphoreType.DMA, pltpu.VMEM, jax.ShapeDtypeStruct
    results = (
        out((NZ, depth, 2 * wide), BF16),
        out((wide, width), BF16),
        out((wide, width), BF16),
        out((NZ, depth, w_gate.shape[1] // 32), BF16),
        out((tokens, wide), BF16),
        out((tokens, HEAD_SIZE), BF16),
        out((tokens, HEAD_SIZE), BF16),
        out((tokens, wide), BF16),
    )
    return pl.pallas_call(
        front_kernel,
        out_shape=(
            out((rows, width), F32), out((NZ,) + gains.shape, F32), out((32, 8, 128), F32), out((8, rows, width), BF16)
        ) + results,
        in_specs=[vmem] * 3 + [any_] * 11,
        out_specs=(vmem,) * 3 + (any_,) * 9,
        scratch_shapes=[buf(r.shape, r.dtype) for r in results]
        + [buf(a.shape, a.dtype) for a in (cosine, sine, first, place, keys)]
        + [
            buf((rows, width), BF16), buf((8, rows, width), BF16), buf((tokens, 2 * wide), F32), buf((NZ, depth, wide), BF16),
            buf((NZ, 2, wide, wide), BF16), buf((8, 128), F32), dma((5,)), dma((8,)), dma((NZ,)), dma((NZ,)),
            dma((32,)), dma((32,)),
            dma((10,)), dma((3,)), dma((3,)), dma((2, 4)), dma((4,)), dma((2, 4)), dma((4,)), dma((2, 4)), dma((2, 4)),
            dma((7,)), dma((7,)), dma((7,)), dma((7,)), dma((8,)), dma((8,)),
        ] + scatter_scratch(1, rows, width),
        compiler_params=pltpu.CompilerParams(collective_id=8, has_side_effects=True, vmem_limit_bytes=60 << 20),
        cost_estimate=takes(95),
        name="attention_front",
    )(x, gains, mask, w_query, w_key, value_weight, w_output, w_down, w_gate, cosine, sine, first, place, keys)


def heads_and_columns(
    hidden_in,
    cotangent,
    teacher,
    valid_mask,
    doc_starts,
    attn_gain,
    w_query,
    w_key,
    value_weight,
    w_output,
    mlp_gain,
    w_gate,
    w_up,
    w_down,
):
    rows, width = hidden_in.shape[1:]
    c = lax.axis_index("ctx")
    z = lax.axis_index("fsdp")
    devices = lax.axis_size("ctx")
    tokens = rows * devices
    group = QUERY_HEADS // KEY_VALUE_HEADS
    qcols = group * HEAD_SIZE
    ffcols = FF // (devices * NZ)

    layer_input = hidden_in[0].astype(F32)
    gains = jnp.concatenate(
        [attn_gain.astype(F32)[None], mlp_gain.astype(F32)[None], jnp.zeros((6, attn_gain.shape[0]), F32)]
    )
    place, segment, offset = stream_places(tokens, rows, devices, doc_starts[0])
    freq = ROPE_BASE ** (-(jnp.arange(HEAD_SIZE // 2, dtype=F32) * 2.0 / HEAD_SIZE))
    angle = offset.astype(F32)[:, None] * freq[None, :]
    cosine = jnp.concatenate([jnp.cos(angle)] * 2, axis=1)
    sine = jnp.concatenate([-jnp.sin(angle), jnp.sin(angle)], axis=1)
    columns = ((place - offset)[:, None], place[:, None], place[None, :])
    branch, gains_all, counts, normed_all, w_qkv, out_rows, down_rows, gate_cols, q, k, v, attn = attention_front(
        hidden_in[0], gains, valid_mask, w_query, w_key, value_weight, w_output, w_down, w_gate, cosine, sine, *columns
    )
    attn_scale = gains_all[:, 0, :].reshape(1, width)
    mlp_scale = gains_all[:, 1, :].reshape(1, width)
    residual = layer_input + branch

    r2 = rms_norm_scale(residual)
    hat2 = residual * r2
    normed2 = (hat2 * mlp_scale).astype(BF16)
    maskf = valid_mask[0].astype(F32)
    mlp_out, normed2_all, gate_up, w_mlp = feed_forward(normed2, gate_cols, w_up, down_rows)
    count = jnp.sum(counts[:, 0, 0])
    outf = residual + mlp_out

    diff = outf - teacher[0].astype(F32)
    error_here = jnp.sum(maskf * jnp.mean(diff * diff, axis=-1))
    g_out = cotangent[0].astype(F32) + maskf[:, None] * diff * (2.0 / (count * width))
    g_norm2, _, gate_grads, up_grads, down_grads = feed_back(g_out.astype(BF16), w_mlp, down_rows, normed2_all, gate_up)

    g_hat2 = g_norm2 * mlp_scale
    g_residual = g_out + r2 * (g_hat2 - hat2 * jnp.mean(g_hat2 * hat2, axis=-1, keepdims=True))
    mlp_gain_term = jnp.sum(g_norm2 * hat2, axis=0, keepdims=True)
    g_norm1, got_gate, got_up, got_qkv, got_out, got_gains = attention_back(
        g_residual.astype(BF16), error_here.reshape(1, 1), q, k, v, attn, cosine, sine, *columns, w_qkv.reshape(width, -1), out_rows, mlp_gain_term,
        normed_all.reshape(tokens, width), gate_grads, up_grads,
    )

    r1 = rms_norm_scale(layer_input)
    hat1 = layer_input * r1
    g_hat1 = g_norm1 * attn_scale
    g_input = g_residual + r1 * (g_hat1 - hat1 * jnp.mean(g_hat1 * hat1, axis=-1, keepdims=True))

    parts = devices * NZ
    share = width // parts
    got_gate, got_up = (g.astype(F32).transpose(1, 0, 2).reshape(share, FF) for g in (got_gate, got_up))
    got_qkv = got_qkv.astype(F32).transpose(1, 0, 2)
    got_out = jnp.sum(got_out.astype(F32), axis=0)
    flat = c * NZ + z
    got_gains = jnp.sum(got_gains, axis=0)
    loss = got_gains[2, 0] / count
    got_gains = lax.dynamic_slice_in_dim(got_gains, flat % 2 * share, share, axis=1)
    own_scale = lax.dynamic_slice_in_dim(attn_scale[0], flat * share, share)

    return (
        loss,
        outf.astype(BF16)[None],
        g_input.astype(BF16)[None],
        got_gains[0] / own_scale,
        got_qkv[:, :, :qcols].reshape(share, QUERY_HEADS * HEAD_SIZE),
        got_qkv[:, :, qcols : qcols + HEAD_SIZE].reshape(share, KEY_VALUE_HEADS * HEAD_SIZE),
        got_qkv[:, :, qcols + HEAD_SIZE :].reshape(share, KEY_VALUE_HEADS * HEAD_SIZE),
        got_out,
        got_gains[1],
        got_gate,
        got_up,
        down_grads,
    )


def solution(mesh):
    small = dict(mesh.shape) == {"ctx": KEY_VALUE_HEADS, "fsdp": NZ}
    in_specs = (
        P("fsdp", "ctx", None),
        P("fsdp", "ctx", None),
        P("fsdp", "ctx", None),
        P("fsdp", "ctx"),
        P("fsdp", None),
        P("fsdp"),
        P("fsdp", None),
        P("fsdp", None),
        P("fsdp", None),
        P("fsdp", None),
        P("fsdp"),
        P("fsdp", None),
        P("fsdp", None),
        P("fsdp", None),
    )
    out_specs = (
        P(),
        P("fsdp", "ctx", None),
        P("fsdp", "ctx", None),
        P(("ctx", "fsdp")),
        P(("ctx", "fsdp"), None),
        P(("ctx", "fsdp"), None),
        P(("ctx", "fsdp"), None),
        P(("ctx", "fsdp"), None),
        P(("ctx", "fsdp")),
        P(("ctx", "fsdp"), None),
        P(("ctx", "fsdp"), None),
        P(("ctx", "fsdp"), None),
    )
    return jax.shard_map(
        heads_and_columns if small else per_device, mesh=mesh, in_specs=in_specs, out_specs=out_specs, check_vma=False
    )
```

```python
import functools

import jax
import jax.numpy as jnp
from jax import lax
from jax.experimental import pallas as pl
from jax.experimental.pallas import tpu as pltpu
from jax.sharding import PartitionSpec as P

QUERY_HEADS = 16
KEY_VALUE_HEADS = 8
HEAD_SIZE = 128
FF = 8192


EPS = 1e-05
ROPE_BASE = 1000000.0
NEG = -1e30
CONTRACT_ROWS = (((0,), (0,)), ((), ()))
CONTRACT_COLS = (((1,), (1,)), ((), ()))


def stream_places(rows, local_token_count, devices, starts):
    span = local_token_count // 2
    rowid = jnp.arange(rows, dtype=jnp.int32)
    device = rowid // local_token_count
    within = rowid % local_token_count
    span_id = jnp.where(within < span, device, 2 * devices - 1 - device)
    place = span_id * span + within % span
    before = starts[None, :] <= place[:, None]
    segment = jnp.sum(before.astype(jnp.int32), axis=1) - 1
    first = jnp.max(jnp.where(before, starts[None, :], 0), axis=1)
    return (place, segment, place - first)


def rotary_embed(values, token_offset, sign):
    half = HEAD_SIZE // 2
    freq = ROPE_BASE ** (-(jnp.arange(half, dtype=jnp.float32) * 2.0 / HEAD_SIZE))
    angle = token_offset.astype(jnp.float32)[:, None] * freq[None, :]
    cosine = jnp.cos(angle)[:, None, :]
    sine = sign * jnp.sin(angle)[:, None, :]
    first = values[..., :half]
    second = values[..., half:]
    return jnp.concatenate(
        [first * cosine - second * sine, second * cosine + first * sine], axis=-1
    )


def rms_norm_scale(values):
    return lax.rsqrt(jnp.mean(values * values, axis=-1, keepdims=True) + EPS)


def head_scores(query_rows, key_rows, allowed):
    attention_scores = jnp.einsum(
        "trd,sd->rts", query_rows, key_rows, preferred_element_type=jnp.float32
    ) * HEAD_SIZE ** (-0.5)
    return jnp.where(allowed[None], attention_scores, NEG)


def per_device(
    hidden_in,
    cotangent,
    teacher,
    valid_mask,
    doc_starts,
    attn_gain,
    w_query,
    w_key,
    value_weight,
    w_output,
    mlp_gain,
    w_gate,
    w_up,
    w_down,
):
    local_token_count = hidden_in.shape[1]
    width = hidden_in.shape[2]
    devices = lax.axis_size("ctx")
    index = lax.axis_index("ctx")
    packed_stream_rows = local_token_count * devices
    query_group = QUERY_HEADS // KEY_VALUE_HEADS
    place, segment, token_offset = stream_places(
        packed_stream_rows, local_token_count, devices, doc_starts[0]
    )
    own_start = index * local_token_count
    my_place = lax.dynamic_slice_in_dim(place, own_start, local_token_count)
    my_segment = lax.dynamic_slice_in_dim(segment, own_start, local_token_count)
    local_stream_offset = lax.dynamic_slice_in_dim(token_offset, own_start, local_token_count)
    allowed = (my_segment[:, None] == segment[None, :]) & (place[None, :] <= my_place[:, None])
    layer_input = hidden_in[0].astype(jnp.float32)
    attn_whole = (
        lax.all_gather(attn_gain, "fsdp", axis=0, tiled=True),
        lax.all_gather(w_query, "fsdp", axis=0, tiled=True),
        lax.all_gather(w_key, "fsdp", axis=0, tiled=True),
        lax.all_gather(value_weight, "fsdp", axis=0, tiled=True),
        lax.all_gather(w_output, "fsdp", axis=0, tiled=True),
    )
    first_norm_scale = attn_whole[0].astype(jnp.float32)
    first_inverse_norm = rms_norm_scale(layer_input)
    first_normalized_input = layer_input * first_inverse_norm
    first_normed = (first_normalized_input * first_norm_scale).astype(jnp.bfloat16)
    qproj = jnp.dot(first_normed, attn_whole[1], preferred_element_type=jnp.float32)
    key_projected = jnp.dot(first_normed, attn_whole[2], preferred_element_type=jnp.float32)
    vproj = jnp.dot(first_normed, attn_whole[3], preferred_element_type=jnp.float32).astype(
        jnp.bfloat16
    )
    query_rows = rotary_embed(
        qproj.reshape(local_token_count, QUERY_HEADS, HEAD_SIZE), local_stream_offset, 1.0
    ).astype(jnp.bfloat16)
    key_rows = (
        rotary_embed(
            key_projected.reshape(local_token_count, KEY_VALUE_HEADS, HEAD_SIZE),
            local_stream_offset,
            1.0,
        )
        .reshape(local_token_count, KEY_VALUE_HEADS * HEAD_SIZE)
        .astype(jnp.bfloat16)
    )
    every_key_row, every_value_row = (
        lax.all_gather(key_rows, "ctx", axis=0, tiled=True),
        lax.all_gather(vproj, "ctx", axis=0, tiled=True),
    )
    key_head_rows = every_key_row.reshape(packed_stream_rows, KEY_VALUE_HEADS, HEAD_SIZE).transpose(
        1, 0, 2
    )
    value_head_rows = every_value_row.reshape(
        packed_stream_rows, KEY_VALUE_HEADS, HEAD_SIZE
    ).transpose(1, 0, 2)
    query_head_rows = query_rows.reshape(
        local_token_count, KEY_VALUE_HEADS, query_group, HEAD_SIZE
    ).transpose(1, 0, 2, 3)

    def attend_head(parts):
        head_query, head_key, head_val = parts
        attention_scores = head_scores(head_query, head_key, allowed)
        top = jnp.max(attention_scores, axis=-1, keepdims=True)
        lse = top + jnp.log(jnp.sum(jnp.exp(attention_scores - top), axis=-1, keepdims=True))
        attention_probabilities = jnp.exp(attention_scores - lse)
        mixed_heads = jnp.einsum(
            "rts,sd->trd",
            attention_probabilities.astype(jnp.bfloat16),
            head_val,
            preferred_element_type=jnp.float32,
        )
        return (mixed_heads, lse)

    mixed_heads, lse = lax.map(attend_head, (query_head_rows, key_head_rows, value_head_rows))
    attn = (
        mixed_heads.transpose(1, 0, 2, 3)
        .reshape(local_token_count, QUERY_HEADS * HEAD_SIZE)
        .astype(jnp.bfloat16)
    )
    residual_state = layer_input + jnp.dot(attn, attn_whole[4], preferred_element_type=jnp.float32)
    mlp_whole = (
        lax.all_gather(mlp_gain, "fsdp", axis=0, tiled=True),
        lax.all_gather(w_gate, "fsdp", axis=0, tiled=True),
        lax.all_gather(w_up, "fsdp", axis=0, tiled=True),
        lax.all_gather(w_down, "fsdp", axis=0, tiled=True),
    )
    second_norm_scale = mlp_whole[0].astype(jnp.float32)
    second_inverse_norm = rms_norm_scale(residual_state)
    second_normalized_input = residual_state * second_inverse_norm
    second_normed = (second_normalized_input * second_norm_scale).astype(jnp.bfloat16)
    gate = jnp.dot(second_normed, mlp_whole[1], preferred_element_type=jnp.float32)
    up_val = jnp.dot(second_normed, mlp_whole[2], preferred_element_type=jnp.float32)
    sigma = jax.nn.sigmoid(gate)
    act = (gate * sigma * up_val).astype(jnp.bfloat16)
    outf = residual_state + jnp.dot(act, mlp_whole[3], preferred_element_type=jnp.float32)
    maskf = valid_mask[0].astype(jnp.float32)
    diff = outf - teacher[0].astype(jnp.float32)
    count_here = jnp.sum(maskf)
    error_here = jnp.sum(maskf * jnp.mean(diff * diff, axis=-1))
    count, error_total = lax.psum((count_here, error_here), ("ctx", "fsdp"))
    loss = error_total / count
    output_gradient = cotangent[0].astype(jnp.float32) + maskf[:, None] * diff * (
        2.0 / (count * width)
    )
    g_mo = output_gradient.astype(jnp.bfloat16)
    mlp_back = (
        lax.all_gather(mlp_gain, "fsdp", axis=0, tiled=True),
        lax.all_gather(w_gate, "fsdp", axis=0, tiled=True),
        lax.all_gather(w_up, "fsdp", axis=0, tiled=True),
        lax.all_gather(w_down, "fsdp", axis=0, tiled=True),
    )
    g_act = lax.dot_general(g_mo, mlp_back[3], CONTRACT_COLS, preferred_element_type=jnp.float32)
    g_gate = (g_act * up_val * sigma * (1.0 + gate * (1.0 - sigma))).astype(jnp.bfloat16)
    g_up = (g_act * gate * sigma).astype(jnp.bfloat16)
    gate_up_gradient = jnp.concatenate([g_gate, g_up], axis=1)
    second_norm_gradient = lax.dot_general(
        g_gate, mlp_back[1], CONTRACT_COLS, preferred_element_type=jnp.float32
    )
    second_norm_gradient = second_norm_gradient + lax.dot_general(
        g_up, mlp_back[2], CONTRACT_COLS, preferred_element_type=jnp.float32
    )
    second_hat_gradient = second_norm_gradient * second_norm_scale
    residual_gradient = output_gradient + second_inverse_norm * (
        second_hat_gradient
        - second_normalized_input
        * jnp.mean(second_hat_gradient * second_normalized_input, axis=-1, keepdims=True)
    )
    mlp_share = lax.psum_scatter(
        lax.dot_general(
            second_normed, gate_up_gradient, CONTRACT_ROWS, preferred_element_type=jnp.float32
        ),
        ("ctx", "fsdp"),
        scatter_dimension=0,
        tiled=True,
    )
    down_share = lax.psum_scatter(
        lax.dot_general(act, g_mo, CONTRACT_ROWS, preferred_element_type=jnp.float32),
        ("ctx", "fsdp"),
        scatter_dimension=0,
        tiled=True,
    )
    g_branch = residual_gradient.astype(jnp.bfloat16)
    attn_back = (
        lax.all_gather(attn_gain, "fsdp", axis=0, tiled=True),
        lax.all_gather(w_query, "fsdp", axis=0, tiled=True),
        lax.all_gather(w_key, "fsdp", axis=0, tiled=True),
        lax.all_gather(value_weight, "fsdp", axis=0, tiled=True),
        lax.all_gather(w_output, "fsdp", axis=0, tiled=True),
    )
    attention_gradient = lax.dot_general(
        g_branch, attn_back[4], CONTRACT_COLS, preferred_element_type=jnp.float32
    ).astype(jnp.bfloat16)
    heads_gradient = attention_gradient.reshape(
        local_token_count, KEY_VALUE_HEADS, query_group, HEAD_SIZE
    ).transpose(1, 0, 2, 3)

    def attend_back(parts):
        head_query, head_key, head_val, head_lse, head_grad = parts
        attention_probabilities = jnp.exp(head_scores(head_query, head_key, allowed) - head_lse)
        g_probs = jnp.einsum("trd,sd->rts", head_grad, head_val, preferred_element_type=jnp.float32)
        delta = jnp.sum(attention_probabilities * g_probs, axis=-1, keepdims=True)
        g_scores = (attention_probabilities * (g_probs - delta)).astype(jnp.bfloat16)
        g_query = jnp.einsum(
            "rts,sd->trd", g_scores, head_key, preferred_element_type=jnp.float32
        ) * HEAD_SIZE ** (-0.5)
        key_gradient = jnp.einsum(
            "rts,trd->sd", g_scores, head_query, preferred_element_type=jnp.float32
        ) * HEAD_SIZE ** (-0.5)
        value_gradient = jnp.einsum(
            "rts,trd->sd",
            attention_probabilities.astype(jnp.bfloat16),
            head_grad,
            preferred_element_type=jnp.float32,
        )
        return (g_query, key_gradient, value_gradient)

    g_query, key_gradient, value_gradient = lax.map(
        attend_back, (query_head_rows, key_head_rows, value_head_rows, lse, heads_gradient)
    )
    key_gradient_terms = key_gradient.transpose(1, 0, 2).reshape(
        packed_stream_rows, KEY_VALUE_HEADS * HEAD_SIZE
    )
    value_gradient_terms = value_gradient.transpose(1, 0, 2).reshape(
        packed_stream_rows, KEY_VALUE_HEADS * HEAD_SIZE
    )
    key_rows_gradient, g_vals = (
        lax.psum_scatter(
            key_gradient_terms.astype(jnp.bfloat16), "ctx", scatter_dimension=0, tiled=True
        ).astype(jnp.float32),
        lax.psum_scatter(
            value_gradient_terms.astype(jnp.bfloat16), "ctx", scatter_dimension=0, tiled=True
        ).astype(jnp.float32),
    )
    g_qproj = (
        rotary_embed(
            g_query.transpose(1, 0, 2, 3).reshape(local_token_count, QUERY_HEADS, HEAD_SIZE),
            local_stream_offset,
            -1.0,
        )
        .reshape(local_token_count, QUERY_HEADS * HEAD_SIZE)
        .astype(jnp.bfloat16)
    )
    g_kproj = (
        rotary_embed(
            key_rows_gradient.reshape(local_token_count, KEY_VALUE_HEADS, HEAD_SIZE),
            local_stream_offset,
            -1.0,
        )
        .reshape(local_token_count, KEY_VALUE_HEADS * HEAD_SIZE)
        .astype(jnp.bfloat16)
    )
    g_vproj = g_vals.astype(jnp.bfloat16)
    first_norm_gradient = lax.dot_general(
        g_qproj, attn_back[1], CONTRACT_COLS, preferred_element_type=jnp.float32
    )
    first_norm_gradient = first_norm_gradient + lax.dot_general(
        g_kproj, attn_back[2], CONTRACT_COLS, preferred_element_type=jnp.float32
    )
    first_norm_gradient = first_norm_gradient + lax.dot_general(
        g_vproj, attn_back[3], CONTRACT_COLS, preferred_element_type=jnp.float32
    )
    first_hat_gradient = first_norm_gradient * first_norm_scale
    g_input = residual_gradient + first_inverse_norm * (
        first_hat_gradient
        - first_normalized_input
        * jnp.mean(first_hat_gradient * first_normalized_input, axis=-1, keepdims=True)
    )
    key_value_proj_gradient = jnp.concatenate([g_kproj, g_vproj], axis=1)
    query_term = lax.dot_general(
        first_normed, g_qproj, CONTRACT_ROWS, preferred_element_type=jnp.float32
    )
    key_value_term = lax.dot_general(
        first_normed, key_value_proj_gradient, CONTRACT_ROWS, preferred_element_type=jnp.float32
    )
    output_term = lax.dot_general(attn, g_branch, CONTRACT_ROWS, preferred_element_type=jnp.float32)
    scale_gradient_terms = jnp.stack(
        [
            jnp.sum(first_norm_gradient * first_normalized_input, axis=0),
            jnp.sum(second_norm_gradient * second_normalized_input, axis=0),
        ]
    )
    query_share, key_value_share, output_share, gain_share = (
        lax.psum_scatter(query_term, ("ctx", "fsdp"), scatter_dimension=0, tiled=True),
        lax.psum_scatter(key_value_term, ("ctx", "fsdp"), scatter_dimension=0, tiled=True),
        lax.psum_scatter(output_term, ("ctx", "fsdp"), scatter_dimension=0, tiled=True),
        lax.psum_scatter(scale_gradient_terms, ("ctx", "fsdp"), scatter_dimension=1, tiled=True),
    )
    key_value_columns = KEY_VALUE_HEADS * HEAD_SIZE
    return (
        loss,
        outf.astype(jnp.bfloat16)[None],
        g_input.astype(jnp.bfloat16)[None],
        gain_share[0],
        query_share,
        key_value_share[:, :key_value_columns],
        key_value_share[:, key_value_columns:],
        output_share,
        gain_share[1],
        mlp_share[:, :FF],
        mlp_share[:, FF:],
        down_share,
    )


MESH = pl.DeviceIdType.MESH
F32 = jnp.float32
BF16 = jnp.bfloat16
NZ = 4


def place_on_plane():
    c = lax.axis_index("ctx")
    z = lax.axis_index("fsdp")
    sib = c + 1 - 2 * lax.rem(c, 2)
    xn = c + 2 - 4 * lax.rem(c // 2, 2)
    yn = c + 4 - 8 * (c // 4)
    diag = xn + yn - c
    return c, z, sib, xn, yn, diag


def meet(devices):
    barrier = pltpu.get_barrier_semaphore()
    for d in devices:
        pl.semaphore_signal(barrier, inc=1, device_id=d, device_id_type=MESH)
    pl.semaphore_wait(barrier, len(devices))


def remote(src, dst, send, recv, device):
    return pltpu.make_async_remote_copy(
        src_ref=src, dst_ref=dst, send_sem=send, recv_sem=recv, device_id=device, device_id_type=MESH
    )


def takes(micros):
    return pl.CostEstimate(flops=0, bytes_accessed=micros * 3_500_000, transcendentals=0)


class Plane:
    def __init__(self, here, slot, send, recv, half):
        self.c, self.z, self.sib, self.xn, self.yn, self.diag = here
        self.slot, self.send, self.recv, self.half = slot, send, recv, half

    def copy(self, kind, src, dst, to):
        return remote(src, dst, self.send.at[kind], self.recv.at[kind], (to, self.z))

    def first(self, src):
        mine = self.slot(self.c)
        return [self.copy(0, src, mine, self.xn), self.copy(1, src, mine, self.yn), self.copy(2, src, mine, self.sib)]

    def arrive(self):
        s = self.slot
        return [self.copy(0, s(self.xn), s(self.xn), self.xn), self.copy(1, s(self.yn), s(self.yn), self.yn)]

    def second(self):
        h = self.half
        s = self.slot
        ybot = s(self.yn).at[pl.ds(0, h)]
        xtop = s(self.xn).at[pl.ds(h, h)]
        return (
            [self.copy(4, xtop, xtop, self.yn), self.copy(5, s(self.xn), s(self.xn), self.sib)],
            [self.copy(3, ybot, ybot, self.xn), self.copy(6, s(self.yn), s(self.yn), self.sib)],
        )

    def diagonal(self):
        h = self.half
        lo, hi = self.slot(self.diag).at[pl.ds(0, h)], self.slot(self.diag).at[pl.ds(h, h)]
        return [self.copy(3, lo, lo, self.xn), self.copy(4, hi, hi, self.yn)]

    def third(self):
        d = self.slot(self.diag)
        return self.copy(7, d, d, self.sib)

    def across(self):
        s = self.slot
        return [self.copy(k, s(j), s(j), self.sib) for k, j in ((2, self.sib), (5, self.xn + self.sib - self.c), (6, self.yn + self.sib - self.c), (7, self.diag + self.sib - self.c))]


def add_rows(dst, parts, chunk=16):
    n = dst.shape[0] // chunk

    def body(i, _):
        at = pl.ds(pl.multiple_of(i * chunk, chunk), chunk)
        total = parts[0][at, :].astype(F32)
        for p in parts[1:]:
            total = total + p[at, :].astype(F32)
        dst[at, :] = total.astype(dst.dtype)
        return 0

    lax.fori_loop(0, n, body, 0)


def plane_order(z):
    pick = jnp.where
    return [z, pick(z == 0, 1, z - 1), pick(z == 3, 1, pick(z == 2, 3, 2)), pick(z < 2, 3, 0)]


def chip_at(c, b):
    x, y = lax.rem(c // 2, 2), c // 4
    xb, yb = lax.rem(b, 2), b // 2
    return (x + xb - 2 * x * xb) + 2 * (y + yb - 2 * y * yb)


def chunk_order(i):
    return jnp.where(i == 0, 3, jnp.where(i == 3, 0, i))


class Gather:
    def __init__(self, here, x_ref, o_ref, keep, zsend, zrecv, send, recv):
        self.here, self.x, self.o = here, x_ref, o_ref
        self.c, self.z = here[0], here[1]
        self.order = plane_order(self.z)
        self.zsend, self.zrecv = zsend, zrecv
        self.planes = [
            Plane(here, functools.partial(lambda zz, j: o_ref.at[zz, j], zz), send.at[zz], recv.at[zz], x_ref.shape[0] // 2)
            for zz in self.order
        ]
        self.keep = pltpu.make_async_copy(x_ref, o_ref.at[self.z, self.c], keep)

    def hop(self, up, t):
        zz = self.order[t]
        src = self.x if t == 0 else self.o.at[zz, self.c]
        row = 0 if up else 1
        return remote(
            src, self.o.at[zz, self.c], self.zsend.at[row, zz], self.zrecv.at[zz], (self.c, self.z + (1 if up else -1))
        )

    def hops(self, t, act):
        zz, z = self.order[t], self.z

        @pl.when((zz <= z) & (z < NZ - 1))
        def _():
            act(self.hop(True, t))

        @pl.when((zz >= z) & (z > 0))
        def _():
            act(self.hop(False, t))

    def spread(self, t):
        if t > 0:
            self.hop(True, t).wait_recv()
        self.hops(t, lambda cp: cp.start())
        for cp in self.planes[t].first(self.source(t)):
            cp.start()

    def source(self, t):
        return self.x if t == 0 else self.o.at[self.order[t], self.c]

    def onward(self, t):
        p = self.planes[t]
        for arrived, sends in zip(p.arrive(), p.second()):
            arrived.wait_recv()
            for cp in sends:
                cp.start()

    def close(self, t):
        p = self.planes[t]
        for cp in p.diagonal():
            cp.wait_recv()
        p.third().start()
        for cp in p.across():
            cp.wait_recv()
        if t == 0:
            self.keep.wait()

    def end(self):
        for t, p in enumerate(self.planes):
            for cp in p.first(self.source(t)) + p.second()[0] + p.second()[1] + [p.third()]:
                cp.wait_send()
            self.hops(t, lambda cp: cp.wait_send())


class Scatter:
    def __init__(self, here, order, part, sibr, xh, yh, xf, yf, zr, bsend, brecv, hsend, hrecv, fsend, frecv, zsend, zrecv):
        self.c, self.z, self.sib, self.xn, self.yn, self.diag = here
        self.k = lax.rem(self.c, 2)
        self.order = order
        self.part, self.sibr, self.xh, self.yh, self.xf, self.yf, self.zr = part, sibr, xh, yh, xf, yf, zr
        self.sems = (bsend, brecv, hsend, hrecv, fsend, frecv, zsend, zrecv)
        self.h = part.shape[3] // 2

    def mine(self, t, b):
        return self.part.at[t, b, self.k]

    def cross(self, t, b):
        send, recv = self.sems[0:2]
        return remote(self.part.at[t, b, 1 - self.k], self.sibr.at[t, b], send.at[t, b], recv.at[t, b], (self.sib, self.z))

    def halves(self, t):
        send, recv = self.sems[2:4]
        src = self.mine(t, 3)
        return (
            remote(src.at[pl.ds(0, self.h)], self.xh.at[t], send.at[t, 0], recv.at[t, 0], (self.xn, self.z)),
            remote(src.at[pl.ds(self.h, self.h)], self.yh.at[t], send.at[t, 1], recv.at[t, 1], (self.yn, self.z)),
        )

    def fulls(self, t):
        send, recv = self.sems[4:6]
        return (
            remote(self.mine(t, 1), self.xf.at[t], send.at[t, 0], recv.at[t, 0], (self.xn, self.z)),
            remote(self.mine(t, 2), self.yf.at[t], send.at[t, 1], recv.at[t, 1], (self.yn, self.z)),
        )

    def hop(self, t):
        send, recv = self.sems[6:8]
        return remote(self.mine(t, 0), self.zr.at[self.z], send.at[t], recv.at[self.z], (self.c, self.order[t]))

    def came(self, t):
        send, recv = self.sems[6:8]
        zz = self.order[t]
        return remote(self.zr.at[zz], self.zr.at[zz], send.at[t], recv.at[zz], (self.c, zz))

    def one(self, t):
        self.cross(t, 3).wait_recv()
        add_rows(self.mine(t, 3), [self.mine(t, 3), self.sibr.at[t, 3]])
        for cp in self.halves(t):
            cp.start()

    def two(self, t):
        h = self.h
        top, low = pl.ds(0, h), pl.ds(h, h)
        hx, hy = self.halves(t)
        fx, fy = self.fulls(t)
        self.cross(t, 1).wait_recv()
        m, s = self.mine(t, 1), self.sibr.at[t, 1]
        add_rows(m.at[top], [m.at[top], s.at[top]])
        hy.wait_recv()
        add_rows(m.at[low], [m.at[low], s.at[low], self.yh.at[t]])
        fx.start()
        self.cross(t, 2).wait_recv()
        m, s = self.mine(t, 2), self.sibr.at[t, 2]
        add_rows(m.at[low], [m.at[low], s.at[low]])
        hx.wait_recv()
        add_rows(m.at[top], [m.at[top], s.at[top], self.xh.at[t]])
        fy.start()

    def three(self, t, o_ref):
        self.cross(t, 0).wait_recv()
        for cp in self.fulls(t):
            cp.wait_recv()
        parts = [self.mine(t, 0), self.sibr.at[t, 0], self.xf.at[t], self.yf.at[t]]
        if t == 0:
            add_rows(o_ref, parts)
        else:
            add_rows(self.mine(t, 0), parts)
            self.hop(t).start()

    def end(self, o_ref):
        n = len(self.order)
        for t in range(1, n):
            self.came(t).wait_recv()
        if n > 1:
            add_rows(o_ref, [o_ref] + [self.zr.at[self.order[t]] for t in range(1, n)])
        for t in range(n):
            for b in range(4):
                self.cross(t, b).wait_send()
            for cp in self.halves(t) + self.fulls(t):
                cp.wait_send()
            if t > 0:
                self.hop(t).wait_send()


def scatter_scratch(n, rows, width):
    v, dma = pltpu.VMEM, pltpu.SemaphoreType.DMA
    return [
        v((n, 4, 2, rows, width), BF16), v((n, 4, rows, width), BF16),
        v((n, rows // 2, width), BF16), v((n, rows // 2, width), BF16),
        v((n, rows, width), BF16), v((n, rows, width), BF16), v((NZ, rows, width), BF16),
        dma((n, 4)), dma((n, 4)), dma((n, 2)), dma((n, 2)), dma((n, 2)), dma((n, 2)), dma((NZ,)), dma((NZ,)),
    ]


def neighbours(here):
    c, z, sib, xn, yn, diag = here
    return [(sib, z), (xn, z), (yn, z)] + [(c, lax.rem(z + s, NZ)) for s in (1, 2, 3)]


def everyone_else(c, z):
    flat = c * NZ + z
    others = [lax.rem(flat + s, 32) for s in range(1, 32)]
    return flat, [(o // NZ, lax.rem(o, NZ)) for o in others]


def feed_kernel(
    x_ref, gate_in, wu_ref, d_in, o_ref, all_ref, gu_ref, w_out,
    w_ref, d_ref, xs, gs, xsem, gsem, wsend, wrecv, wkeep, keep, zsend, zrecv, send, recv, *scat
):
    here = place_on_plane()
    c, z = here[0], here[1]
    meet(neighbours(here))
    gather_ = Gather(here, x_ref, all_ref, keep.at[0], zsend, zrecv, send, recv)
    order = gather_.order
    sums = Scatter(here, order, *scat)
    ff = d_ref.shape[0]
    gather_.keep.start()
    gather_.spread(0)

    def load(t, b):
        src = all_ref.at[order[t], pl.ds(2 * chip_at(c, b), 2)]
        return pltpu.make_async_copy(src, xs.at[b], xsem.at[b])

    def store(t, b):
        return pltpu.make_async_copy(gs.at[b], gu_ref.at[order[t], chip_at(c, b)], gsem.at[b])

    def work(t, lo, hi):
        for b in (3, 1, 2, 0)[lo:hi]:
            load(t, b).start()

        def body(i, _):
            b = chunk_order(i)
            load(t, b).wait()
            if t != 1:
                store(1, b).wait()
            x = xs[b].reshape(-1, xs.shape[-1])
            gu = jnp.dot(x, w_ref[...].reshape(x.shape[1], -1), preferred_element_type=F32)
            gs[b] = gu
            store(t, b).start()
            gate, up = gu[:, :ff], gu[:, ff:]
            act = (gate * jax.nn.sigmoid(gate) * up).astype(BF16)
            p = jnp.dot(act, d_ref[...], preferred_element_type=F32).astype(BF16)
            sums.part[t, b] = p.reshape(sums.part.shape[2:])
            sums.cross(t, b).start()
            return 0

        lax.fori_loop(lo, hi, body, 0)

    weights = []
    keeps = [pltpu.make_async_copy(d_in, d_ref, wkeep.at[0])]
    keeps.append(pltpu.make_async_copy(gate_in, w_ref.at[:, :, pl.ds(0, ff)], wkeep.at[1]))
    for hop in range(NZ):
        to = lax.rem(z + hop, NZ)
        src = wu_ref.at[:, pl.ds(pl.multiple_of((c * NZ + to) * ff, ff), ff)]
        dst = w_ref.at[z, :, pl.ds(ff, ff)]
        if hop == 0:
            keeps.append(pltpu.make_async_copy(src, dst, wkeep.at[2]))
        else:
            weights.append(remote(src, dst, wsend.at[hop], wrecv.at[hop], (c, to)))
    w_keep = pltpu.make_async_copy(w_ref, w_out, wkeep.at[3])

    def early():
        for cp in keeps + weights:
            cp.start()

    def ready():
        for cp in keeps + weights:
            cp.wait()
        w_keep.start()

    fused_steps(gather_, sums, work, o_ref, False, early=early, ready=ready)
    for b in range(4):
        store(0, b).wait()
    w_keep.wait()


def fused_steps(gather_, sums, work, o_ref, own_first, more=lambda t: None, early=lambda: None, ready=lambda: None):
    gather_.spread(1)
    gather_.onward(0)
    early()
    gather_.spread(2)
    if own_first:
        ready()
        gather_.close(0)
        work(0, 0, 2)
    gather_.onward(1)
    if own_first:
        work(0, 2, 4)
    gather_.spread(3)
    if own_first:
        more(0)
    gather_.onward(2)
    if not own_first:
        ready()
    gather_.close(1)
    work(1, 0, 4)
    gather_.onward(3)
    if not own_first:
        sums.one(1)
    more(1)
    gather_.close(2)
    work(2, 0, 2)
    sums.one(2)
    work(2, 2, 4)
    sums.two(2)
    more(2)
    gather_.close(3)
    work(3, 0, 2)
    sums.one(3)
    work(3, 2, 4)
    sums.three(2, o_ref)
    sums.two(3)
    more(3)
    if own_first:
        sums.one(1)
    else:
        gather_.close(0)
        work(0, 0, 4)
    sums.three(3, o_ref)
    if own_first:
        sums.two(1)
        sums.one(0)
    else:
        sums.one(0)
        more(0)
        sums.two(1)
    sums.three(1, o_ref)
    sums.two(0)
    sums.three(0, o_ref)
    sums.end(o_ref)
    gather_.end()


def gather_sems():
    dma = pltpu.SemaphoreType.DMA
    return [dma((1,)), dma((2, 4)), dma((4,)), dma((4, 8)), dma((4, 8))]


def feed_forward(x, gate, w_up, d):
    rows, width = x.shape
    depth, cols = w_up.shape[0], 2 * d.shape[0]
    any_ = pl.BlockSpec(memory_space=pl.ANY)
    vmem = pl.BlockSpec(memory_space=pltpu.VMEM)
    dma = pltpu.SemaphoreType.DMA
    return pl.pallas_call(
        feed_kernel,
        out_shape=(
            jax.ShapeDtypeStruct((rows, width), F32),
            jax.ShapeDtypeStruct((NZ, 8, rows, width), BF16),
            jax.ShapeDtypeStruct((NZ, 4, 2 * rows, cols), F32),
            jax.ShapeDtypeStruct((NZ, depth, cols), BF16),
        ),
        in_specs=[vmem, any_, any_, any_],
        out_specs=(vmem, any_, any_, any_),
        scratch_shapes=[
            pltpu.VMEM((NZ, depth, cols), BF16), pltpu.VMEM(d.shape, BF16),
            pltpu.VMEM((4, 2, rows, width), BF16), pltpu.VMEM((4, 2 * rows, cols), F32), dma((4,)), dma((4,)),
            dma((4,)), dma((4,)), dma((4,)),
        ] + gather_sems() + scatter_scratch(NZ, rows, width),
        compiler_params=pltpu.CompilerParams(collective_id=5, has_side_effects=True, vmem_limit_bytes=60 << 20),
        cost_estimate=takes(180),
        name="feed_forward",
    )(x, gate, w_up, d)


def feed_back_kernel(
    x_ref, w_in, d_in, n_ref, gu_ref, o_ref, all_ref, gate_out, up_out, down_out,
    w_ref, d_ref, gate_o, up_o, down_o, wsem, gsend, grecv, xs, ns, gs, gg, acts, total, xsem, nsem, gsem, keep, zsend, zrecv, send, recv, *scat
):
    here = place_on_plane()
    c, z = here[0], here[1]
    meet(neighbours(here))
    gather_ = Gather(here, x_ref, all_ref, keep.at[0], zsend, zrecv, send, recv)
    order = gather_.order
    sums = Scatter(here, order, *scat)
    ff = d_ref.shape[0]
    tokens = 8 * x_ref.shape[0]
    gather_.keep.start()
    gather_.spread(0)

    def loads(t, b):
        chip = chip_at(c, b)
        pair = pl.ds(2 * chip, 2)
        return (
            pltpu.make_async_copy(gu_ref.at[order[t], chip], gs.at[b], gsem.at[b]),
            pltpu.make_async_copy(all_ref.at[order[t], pair], xs.at[b], xsem.at[b]),
            pltpu.make_async_copy(n_ref.at[order[t], pair], ns.at[b], nsem.at[b]),
        )

    def work(t, lo, hi):
        for b in (3, 1, 2, 0)[lo:hi]:
            for cp in loads(t, b):
                cp.start()

        def body(i, _):
            b = chunk_order(i)
            stored, tokens_in, _ = loads(t, b)
            stored.wait()
            tokens_in.wait()
            g = xs[b].reshape(-1, xs.shape[-1])
            g_act = lax.dot_general(g, d_ref[...], CONTRACT_COLS, preferred_element_type=F32)
            gate, up = gs[b, :, :ff], gs[b, :, ff:]
            sg = jax.nn.sigmoid(gate)
            acts[b] = (gate * sg * up).astype(BF16)
            gg[b, :, :ff] = (g_act * up * sg * (1.0 + gate * (1.0 - sg))).astype(BF16)
            gg[b, :, ff:] = (g_act * gate * sg).astype(BF16)
            p = lax.dot_general(gg[b], w_ref[...].reshape(o_ref.shape[1], -1), CONTRACT_COLS, preferred_element_type=F32).astype(BF16)
            sums.part[t, b] = p.reshape(sums.part.shape[2:])
            sums.cross(t, b).start()
            return 0

        lax.fori_loop(lo, hi, body, 0)

    piece = 512

    def more(t):
        for b in range(4):
            loads(t, b)[2].wait()

        def body(i, _):
            at = pl.ds(pl.multiple_of(i * piece, piece), piece)
            n = ns[:, :, :, at].reshape(tokens, piece)
            w_term = lax.dot_general(n, gg[...].reshape(tokens, -1), CONTRACT_ROWS, preferred_element_type=F32)
            g = xs[:, :, :, at].reshape(tokens, piece)
            d_term = lax.dot_general(acts[...].reshape(tokens, -1), g, CONTRACT_ROWS, preferred_element_type=F32)
            if t > 0:
                w_term = w_term + total[at, :]
                d_term = d_term + down_o[:, at]
            down_o[:, at] = d_term
            if t < NZ - 1:
                total[at, :] = w_term
            else:
                pair = pl.ds(2 * i, 2)
                gate_o[pair] = w_term[:, :ff].astype(BF16).reshape((2,) + gate_o.shape[1:])
                up_o[pair] = w_term[:, ff:].astype(BF16).reshape((2,) + up_o.shape[1:])
            return 0

        lax.fori_loop(0, o_ref.shape[1] // piece, body, 0)

    keeps = [pltpu.make_async_copy(w_in, w_ref, wsem.at[0]), pltpu.make_async_copy(d_in, d_ref, wsem.at[1])]
    saved = [
        pltpu.make_async_copy(src, dst, wsem.at[2 + i])
        for i, (src, dst) in enumerate(((gate_o.at[:, z], gate_out.at[:, z]), (up_o, up_out), (down_o, down_out)))
    ]
    gate_z = []
    for s in (1, 2, 3):
        to = lax.rem(z + s, NZ)
        gate_z.append(remote(gate_o.at[:, to], gate_out.at[:, z], gsend.at[s], grecv.at[s], (c, to)))

    def early():
        for cp in keeps:
            cp.start()

    def ready():
        for cp in keeps:
            cp.wait()

    def more_and_save(t):
        more(t)
        if t == NZ - 1:
            for cp in gate_z + saved:
                cp.start()

    fused_steps(gather_, sums, work, o_ref, True, more_and_save, early, ready)
    for cp in saved + gate_z:
        cp.wait()


def feed_back(x, w, d, normed, gate_up):
    rows, width = x.shape
    cols = w.shape[2]
    ff = d.shape[0]
    by_owner = (8, NZ, width // 32, ff)
    any_ = pl.BlockSpec(memory_space=pl.ANY)
    vmem = pl.BlockSpec(memory_space=pltpu.VMEM)
    dma, buf = pltpu.SemaphoreType.DMA, pltpu.VMEM
    return pl.pallas_call(
        feed_back_kernel,
        out_shape=(
            jax.ShapeDtypeStruct((rows, width), F32),
            jax.ShapeDtypeStruct((NZ, 8, rows, width), BF16),
            jax.ShapeDtypeStruct(by_owner, BF16),
            jax.ShapeDtypeStruct(by_owner, BF16),
            jax.ShapeDtypeStruct((ff, width), F32),
        ),
        in_specs=[vmem] + [any_] * 4,
        out_specs=(vmem,) + (any_,) * 4,
        scratch_shapes=[
            buf(w.shape, BF16), buf(d.shape, BF16), buf(by_owner, BF16), buf(by_owner, BF16), buf((ff, width), F32),
            dma((5,)), dma((4,)), dma((4,)), buf((4, 2, rows, width), BF16), buf((4, 2, rows, width), BF16), buf((4, 2 * rows, cols), F32),
            buf((4, 2 * rows, cols), BF16), buf((4, 2 * rows, ff), BF16), buf((width, cols), F32),
            dma((4,)), dma((4,)), dma((4,)),
        ] + gather_sems() + scatter_scratch(NZ, rows, width),
        compiler_params=pltpu.CompilerParams(collective_id=7, has_side_effects=True, vmem_limit_bytes=63 << 20),
        cost_estimate=takes(180),
        name="feed_back",
    )(x, w, d, normed, gate_up)


ROWS_AT_ONCE = 256


def turn(u, cosine, sine):
    return u * cosine + pltpu.roll(u, HEAD_SIZE // 2, 1) * sine


def block_probs(q, k, first, place, keys_place):
    scores = lax.dot_general(q, k, CONTRACT_COLS, preferred_element_type=F32) * HEAD_SIZE ** (-0.5)
    allowed = (keys_place >= first) & (keys_place <= place)
    scores = jnp.where(allowed, scores, NEG)
    raised = jnp.exp(scores - jnp.max(scores, axis=-1, keepdims=True))
    return raised / jnp.sum(raised, axis=-1, keepdims=True)


def fetches(pairs, sems):
    copies = [pltpu.make_async_copy(src, dst, sems.at[i]) for i, (src, dst) in enumerate(pairs)]
    for cp in copies:
        cp.start()
    return copies


def exchange_loop(c, z, act):
    flat = c * NZ + z

    def body(s, _):
        to = lax.rem(flat + s, 32)
        act(s, to // NZ, lax.rem(to, NZ))
        return 0

    lax.fori_loop(1, 32, body, 0)


def back_kernel(
    g_ref, err_ref, q_in, k_in, v_in, attn_in, cos_in, sin_in, first_in, place_in, keys_in, wqkv_in, wout_in, gain_in,
    norm_in, gate_ref, up_ref,
    o_ref, gate_o, up_o, qkv_o, out_o, gain_o,
    q_ref, k_ref, v_ref, attn_ref, cos_ref, sin_ref, first_ref, place_ref, keys_ref, wqkv_ref, wout_ref, gain_ref, normed, isem,
    gb, ga, gqkv, gk, gv, outg, qkvg, mt, qt, qs, gsrc,
    msend, mrecv, m2send, m2recv, qsend, qrecv, q2send, q2recv, osend, orecv, ssend, srecv, lsem, psend, precv, *scat
):
    here = place_on_plane()
    c, z, sib, xn, yn, diag = here
    flat, everyone = everyone_else(c, z)
    meet(everyone)
    rows, width = g_ref.shape
    tokens = 8 * rows
    share = width // 32
    plane = Plane(here, lambda j: gb.at[j], psend, precv, rows // 2)
    sums = Scatter(here, [z], *scat)
    mates = [lax.rem(c + s, 8) for s in range(1, 8)]
    others = [(s, lax.rem(z + s, NZ)) for s in (1, 2, 3)]
    for cp in plane.first(g_ref):
        cp.start()

    mlp_z = [remote(up_ref.at[:, to], mt.at[:, z], msend.at[s], mrecv.at[s], (c, to)) for s, to in others]
    keep = pltpu.make_async_copy(up_ref.at[:, z], mt.at[:, z], lsem.at[1])
    for cp in mlp_z + [keep]:
        cp.start()
    from_me = pl.ds(pl.multiple_of(c * NZ, NZ), NZ)

    def over_plane(i, ref):
        dst = (gate_o, up_o)[i]
        out = [
            remote(ref.at[m], dst.at[from_me], m2send.at[i, s], m2recv.at[i, s], (m, z)) for s, m in enumerate(mates)
        ]
        out.append(pltpu.make_async_copy(ref.at[c], dst.at[from_me], lsem.at[2 + i]))
        for cp in out:
            cp.start()
        return out

    got = fetches(
        [
            (wout_in, wout_ref), (q_in, q_ref), (k_in, k_ref), (v_in, v_ref), (cos_in, cos_ref), (sin_in, sin_ref),
            (first_in, first_ref), (place_in, place_ref), (keys_in, keys_ref),
            (attn_in, attn_ref), (norm_in, normed), (wqkv_in, wqkv_ref), (gain_in, gain_ref),
        ],
        isem,
    )
    gb[c] = g_ref[...]
    gk[...] = jnp.zeros_like(gk)
    gv[...] = jnp.zeros_like(gv)

    def attend(b):
        chip = chip_at(c, b)
        at = pl.ds(pl.multiple_of(chip * ROWS_AT_ONCE, ROWS_AT_ONCE), ROWS_AT_ONCE)
        g_rows = gb[pl.ds(chip * 2, 2)].reshape(ROWS_AT_ONCE, width)
        ga[at, :] = lax.dot_general(g_rows, wout_ref[...], CONTRACT_COLS, preferred_element_type=F32).astype(BF16)
        k, v = k_ref[...], v_ref[...]
        cosine, sine = cos_ref[at, :], sin_ref[at, :]
        first, place, keys = first_ref[at, :], place_ref[at, :], keys_ref[...]
        for h in range(QUERY_HEADS // KEY_VALUE_HEADS):
            lanes = slice(h * HEAD_SIZE, (h + 1) * HEAD_SIZE)
            q, g = q_ref[at, lanes], ga[at, lanes]
            probs = block_probs(q, k, first, place, keys)
            g_probs = lax.dot_general(g, v, CONTRACT_COLS, preferred_element_type=F32)
            delta = jnp.sum(probs * g_probs, axis=-1, keepdims=True)
            g_scores = (probs * (g_probs - delta)).astype(BF16)
            g_q = jnp.dot(g_scores, k, preferred_element_type=F32) * HEAD_SIZE ** (-0.5)
            gqkv[at, lanes] = turn(g_q, cosine, -sine).astype(BF16)
            gk[...] += lax.dot_general(g_scores, q, CONTRACT_ROWS, preferred_element_type=F32)
            gv[...] += lax.dot_general(probs.astype(BF16), g, CONTRACT_ROWS, preferred_element_type=F32)

    came = plane.across()
    for cp in got[:9]:
        cp.wait()
    came[0].wait_recv()
    attend(0)
    for arrived, sends in zip(plane.arrive(), plane.second()):
        arrived.wait_recv()
        for cp in sends:
            cp.start()
    came[1].wait_recv()
    attend(1)
    for cp in plane.diagonal():
        cp.wait_recv()
    plane.third().start()
    came[2].wait_recv()
    attend(2)
    came[3].wait_recv()
    mlp_c = over_plane(0, gate_ref)
    got[9].wait()
    piece = 512

    def outs(i, _):
        at = pl.ds(pl.multiple_of(i * piece, piece), piece)
        g = gb[:, :, at].reshape(tokens, piece)
        outg[:, at] = lax.dot_general(attn_ref[...], g, CONTRACT_ROWS, preferred_element_type=F32).astype(BF16)
        return 0

    lax.fori_loop(0, width // piece, outs, 0)
    out_sends = []
    for s, to in others:
        src = outg.at[pl.ds(pl.multiple_of(to * share, share), share)]
        out_sends.append(remote(src, out_o.at[z], osend.at[s], orecv.at[s], (c, to)))
    for cp in out_sends:
        cp.start()
    keep_o = pltpu.make_async_copy(outg.at[pl.ds(pl.multiple_of(z * share, share), share)], out_o.at[z], lsem.at[5])
    keep_o.start()
    attend(3)
    qcols = q_ref.shape[1]
    g_k = gk[...] * HEAD_SIZE ** (-0.5)
    gqkv[:, qcols : qcols + HEAD_SIZE] = turn(g_k, cos_ref[...], -sin_ref[...]).astype(BF16)
    gqkv[:, qcols + HEAD_SIZE :] = gv[...].astype(BF16)

    for cp in got[10:]:
        cp.wait()
    cols = gqkv.shape[1]

    def project(i, _):
        at = pl.ds(pl.multiple_of(i * piece, piece), piece)
        term = lax.dot_general(normed[:, at], gqkv[...], CONTRACT_ROWS, preferred_element_type=F32).astype(BF16)
        qkvg[pl.ds(2 * i, 2)] = term.reshape(2, NZ, share, cols)
        return 0

    lax.fori_loop(0, width // piece, project, 0)
    qkv_z = [remote(qkvg.at[:, to], qt.at[s], qsend.at[s], qrecv.at[s], (c, to)) for s, to in others]
    for cp in qkv_z:
        cp.start()

    gsrc[...] = jnp.zeros_like(gsrc)
    gsrc[1:2, :] = gain_ref[...]
    gsrc[2:3, :] = jnp.full((1, width), err_ref[0, 0], F32)
    for b in (3, 1, 2, 0):
        chip = chip_at(c, b)
        at = pl.ds(pl.multiple_of(chip * ROWS_AT_ONCE, ROWS_AT_ONCE), ROWS_AT_ONCE)
        p = lax.dot_general(gqkv[at, :], wqkv_ref[...], CONTRACT_COLS, preferred_element_type=F32)
        sums.part[0, b] = p.astype(BF16).reshape(2, rows, width)
        sums.cross(0, b).start()
        gsrc[0:1, :] += jnp.sum(p * normed[at, :].astype(F32), axis=0, keepdims=True)

    def gain_sends(act):
        def one(s, tc, tz):
            lanes = pl.ds(pl.multiple_of((tc * NZ + tz) // 2 * 128, 128), 128)
            act(remote(gsrc.at[:, lanes], gain_o.at[flat], ssend.at[s], srecv.at[s], (tc, tz)))

        exchange_loop(c, z, one)

    gain_sends(lambda cp: cp.start())
    own_lanes = pl.ds(pl.multiple_of(flat // 2 * 128, 128), 128)
    gain_keep = pltpu.make_async_copy(gsrc.at[:, own_lanes], gain_o.at[flat], lsem.at[4])
    gain_keep.start()
    sums.one(0)
    for cp in mlp_z + [keep]:
        cp.wait()
    mlp_c += over_plane(1, mt)
    sums.two(0)

    sums.three(0, o_ref)

    for cp in qkv_z:
        cp.wait()

    def gathered(j, _):
        total = qkvg[j, z].astype(F32)
        for s in (1, 2, 3):
            total = total + qt[s, j].astype(F32)
        qs[j] = total.astype(BF16)
        return 0

    lax.fori_loop(0, 8, gathered, 0)
    qkv_c = [remote(qs.at[m], qkv_o.at[c], q2send.at[s], q2recv.at[s], (m, z)) for s, m in enumerate(mates)]
    qkv_keep = pltpu.make_async_copy(qs.at[c], qkv_o.at[c], lsem.at[6])
    for cp in qkv_c + [qkv_keep]:
        cp.start()
    sums.end(o_ref)
    for cp in plane.first(g_ref) + plane.second()[0] + plane.second()[1] + [plane.third()]:
        cp.wait_send()
    gain_sends(lambda cp: cp.wait())
    for cp in mlp_c + out_sends + qkv_c + [keep_o, qkv_keep, gain_keep]:
        cp.wait()


def attention_back(g, err, q, k, v, attn, cosine, sine, first, place, keys, w_qkv, w_out, gain, normed, gate_g, up_g):
    rows, width = g.shape
    tokens = q.shape[0]
    any_ = pl.BlockSpec(memory_space=pl.ANY)
    vmem = pl.BlockSpec(memory_space=pltpu.VMEM)
    dma, buf, out = pltpu.SemaphoreType.DMA, pltpu.VMEM, jax.ShapeDtypeStruct
    share = width // 32
    cols = w_qkv.shape[1]
    by_owner = gate_g.shape
    ff = by_owner[3]
    return pl.pallas_call(
        back_kernel,
        out_shape=(
            out((rows, width), F32),
            out((32, share, ff), BF16),
            out((32, share, ff), BF16),
            out((8, share, cols), BF16),
            out((NZ, share, width), BF16),
            out((32, 8, 128), F32),
        ),
        in_specs=[vmem, pl.BlockSpec(memory_space=pltpu.SMEM)] + [any_] * 15,
        out_specs=(vmem,) + (any_,) * 5,
        scratch_shapes=[
            buf(a.shape, a.dtype)
            for a in (q, k, v, attn, cosine, sine, first, place, keys, w_qkv, w_out, gain, normed)
        ] + [
            dma((13,)),
            buf((8, rows, width), BF16), buf(q.shape, BF16), buf((tokens, cols), BF16), buf(k.shape, F32), buf(v.shape, F32),
            buf(w_out.shape, BF16), buf((8, NZ, share, cols), BF16),
            buf(by_owner, BF16), buf((NZ, 8, share, cols), BF16), buf((8, share, cols), BF16), buf((8, width), F32),
            dma((4,)), dma((4,)), dma((2, 7)), dma((2, 7)), dma((4,)), dma((4,)), dma((7,)), dma((7,)), dma((4,)), dma((4,)),
            dma((32,)), dma((32,)), dma((7,)), dma((8,)), dma((8,)),
        ] + scatter_scratch(1, rows, width),
        compiler_params=pltpu.CompilerParams(collective_id=6, has_side_effects=True, vmem_limit_bytes=60 << 20),
        cost_estimate=takes(110),
        name="attention_back",
    )(g, err, q, k, v, attn, cosine, sine, first, place, keys, w_qkv, w_out, gain, normed, gate_g, up_g)


class Line:
    def __init__(self, c, z, slot, send, recv):
        self.c, self.z, self.slot, self.send, self.recv = c, z, slot, send, recv
        self.order = plane_order(z)

    def hop(self, up, t):
        zz = self.order[t]
        row = 0 if up else 1
        return remote(
            self.slot(zz), self.slot(zz), self.send.at[row, zz], self.recv.at[zz], (self.c, self.z + (1 if up else -1))
        )

    def hops(self, t, act):
        zz, z = self.order[t], self.z

        @pl.when((zz <= z) & (z < NZ - 1))
        def _():
            act(self.hop(True, t))

        @pl.when((zz >= z) & (z > 0))
        def _():
            act(self.hop(False, t))

    def step(self, t):
        if t > 0:
            self.hop(True, t).wait_recv()
        self.hops(t, lambda cp: cp.start())

    def end(self):
        for t in range(NZ):
            self.hops(t, lambda cp: cp.wait_send())


def front_kernel(
    x_ref, g_ref, mask_ref, wq_ref, wk_ref, wv_ref, wo_ref, wd_ref, wg_ref, cos_in, sin_in, first_in, place_in, keys_in,
    o_ref, go_ref, so_ref, norm_o, wqkv_o, outr_o, downr_o, gate_o, q_o, k_o, v_o, attn_o,
    wqkv, outr, downr, gatew, q_ref, k_ref, v_ref, attn_ref, cos_ref, sin_ref, first_ref, place_ref, keys_ref,
    normed, nall, acc, tmp_o, tmp_d, st_ref, isem, osem, wgsend, wgrecv, ssend, srecv,
    lsem, gsend, grecv, qzsend, qzrecv, ozsend, ozrecv, dsend, drecv, o2send, o2recv, d2send, d2recv, psend, precv, *scat
):
    here = place_on_plane()
    c, z, sib, xn, yn, diag = here
    rows, width = x_ref.shape
    tokens = 8 * rows
    wide = tmp_o.shape[2]
    mates = [lax.rem(c + s, 8) for s in range(1, 8)]
    others = [lax.rem(z + s, NZ) for s in (1, 2, 3)]
    flat, everyone = everyone_else(c, z)
    meet(everyone)
    sums = Scatter(here, [z], *scat)
    plane = Plane(here, lambda j: nall.at[j], psend, precv, rows // 2)
    line_q = Line(c, z, lambda zz: wqkv.at[zz], qzsend, qzrecv)
    line_o = Line(c, z, lambda zz: tmp_o.at[zz], ozsend, ozrecv)
    own_cols = pl.ds(pl.multiple_of(c * wide, wide), wide)

    def narrow(ref, n):
        return ref.at[:, pl.ds(pl.multiple_of(c * n, n), n)]

    q_keeps = [
        pltpu.make_async_copy(narrow(wq_ref, wide), wqkv.at[z, :, pl.ds(0, wide)], lsem.at[0]),
        pltpu.make_async_copy(narrow(wk_ref, HEAD_SIZE), wqkv.at[z, :, pl.ds(wide, HEAD_SIZE)], lsem.at[1]),
        pltpu.make_async_copy(narrow(wv_ref, HEAD_SIZE), wqkv.at[z, :, pl.ds(wide + HEAD_SIZE, HEAD_SIZE)], lsem.at[2]),
    ]
    o_keep = pltpu.make_async_copy(wo_ref.at[:, own_cols], tmp_o.at[z], lsem.at[3])
    d_keeps, downs = [], []
    for core in range(2):
        for hop in range(NZ):
            to = lax.rem(z + hop, NZ)
            src = wd_ref.at[pl.ds(pl.multiple_of((core * NZ + to) * wide, wide), wide), own_cols]
            if hop == 0:
                d_keeps.append(pltpu.make_async_copy(src, tmp_d.at[z, core], lsem.at[4 + core]))
            else:
                downs.append(remote(src, tmp_d.at[z, core], dsend.at[core, hop], drecv.at[core, hop], (c, to)))
    gate_cols = wg_ref.shape[1] // 32
    gates = []
    for hop in range(NZ):
        to = lax.rem(z + hop, NZ)
        src = wg_ref.at[:, pl.ds(pl.multiple_of((c * NZ + to) * gate_cols, gate_cols), gate_cols)]
        if hop == 0:
            g_keep = pltpu.make_async_copy(src, gatew.at[z], lsem.at[9])
        else:
            gates.append(remote(src, gatew.at[z], wgsend.at[hop], wgrecv.at[hop], (c, to)))
    for cp in [o_keep] + q_keeps + d_keeps + [g_keep]:
        cp.start()
    go_ref[z] = g_ref[...]
    gains = [remote(g_ref, go_ref.at[z], gsend.at[s], grecv.at[s], (c, t)) for s, t in enumerate(others)]
    for cp in gains:
        cp.start()
    o_keep.wait()
    line_o.step(0)
    got = fetches(
        [(cos_in, cos_ref), (sin_in, sin_ref), (first_in, first_ref), (place_in, place_ref), (keys_in, keys_ref)], isem
    )
    st_ref[...] = jnp.full(st_ref.shape, jnp.sum(mask_ref[...].astype(F32)), F32)
    so_ref[flat] = st_ref[...]

    def counts(act):
        def one(s, tc, tz):
            act(remote(st_ref, so_ref.at[flat], ssend.at[s], srecv.at[s], (tc, tz)))

        exchange_loop(c, z, one)

    x = x_ref[...].astype(F32)
    scaled = x * lax.rsqrt(jnp.mean(x * x, axis=-1, keepdims=True) + EPS)
    for cp in gains:
        cp.wait()
    piece = width // NZ
    for zz in range(NZ):
        normed[:, zz * piece : (zz + 1) * piece] = (
            scaled[:, zz * piece : (zz + 1) * piece] * go_ref[zz, 0:1, :]
        ).astype(BF16)
    for cp in plane.first(normed):
        cp.start()
    nall[c] = normed[...]
    counts(lambda cp: cp.start())
    line_o.step(1)
    for cp in q_keeps:
        cp.wait()
    line_q.step(0)
    line_o.step(2)
    for arrived, sends in zip(plane.arrive(), plane.second()):
        arrived.wait_recv()
        for cp in sends:
            cp.start()
    line_o.step(3)

    def regroup(buf, dst, send, recv, lrow):
        def block(j):
            return buf(j // 2, lax.rem(j, 2))

        out = [remote(block(m), dst.at[:, own_cols], send.at[s], recv.at[s], (m, z)) for s, m in enumerate(mates)]
        keep = pltpu.make_async_copy(block(c), dst.at[:, own_cols], lsem.at[lrow])
        for cp in out + [keep]:
            cp.start()
        return out + [keep]

    moved_o = regroup(lambda p, core: tmp_o.at[p, pl.ds(pl.multiple_of(core * wide, wide), wide)], outr, o2send, o2recv, 7)
    line_q.step(1)
    for cp in plane.diagonal():
        cp.wait_recv()
    plane.third().start()
    for cp in plane.across():
        cp.wait_recv()
    line_q.step(2)
    norm_keep = pltpu.make_async_copy(nall, norm_o, lsem.at[6])
    norm_keep.start()

    def project(t):
        zz = line_q.order[t]
        at = pl.ds(pl.multiple_of(zz * piece, piece), piece)
        term = jnp.dot(nall[:, :, at].reshape(tokens, piece), wqkv[zz], preferred_element_type=F32)
        acc[...] = term if t == 0 else acc[...] + term

    for t in range(3):
        project(t)
    line_q.step(3)
    for cp in downs:
        cp.start()
    project(3)
    for cp in got:
        cp.wait()

    def heads(i, _):
        at = pl.ds(pl.multiple_of(i * ROWS_AT_ONCE, ROWS_AT_ONCE), ROWS_AT_ONCE)
        cosine, sine = cos_ref[at, :], sin_ref[at, :]
        for h in range(wide // HEAD_SIZE):
            lanes = slice(h * HEAD_SIZE, (h + 1) * HEAD_SIZE)
            q_ref[at, lanes] = turn(acc[at, lanes], cosine, sine).astype(BF16)
        k_ref[at, :] = turn(acc[at, wide : wide + HEAD_SIZE], cosine, sine).astype(BF16)
        v_ref[at, :] = acc[at, wide + HEAD_SIZE :].astype(BF16)
        return 0

    lax.fori_loop(0, tokens // ROWS_AT_ONCE, heads, 0)

    saved = fetches([(wqkv, wqkv_o), (q_ref, q_o), (k_ref, k_o), (v_ref, v_o)], osem)

    def attend(b):
        at = pl.ds(pl.multiple_of(chip_at(c, b) * ROWS_AT_ONCE, ROWS_AT_ONCE), ROWS_AT_ONCE)
        k, v = k_ref[...], v_ref[...]
        first, place, keys = first_ref[at, :], place_ref[at, :], keys_ref[...]
        for h in range(wide // HEAD_SIZE):
            lanes = slice(h * HEAD_SIZE, (h + 1) * HEAD_SIZE)
            probs = block_probs(q_ref[at, lanes], k, first, place, keys)
            attn_ref[at, lanes] = jnp.dot(probs.astype(BF16), v, preferred_element_type=F32).astype(BF16)
        p = jnp.dot(attn_ref[at, :], outr[...], preferred_element_type=F32).astype(BF16)
        sums.part[0, b] = p.reshape(2, rows, width)
        sums.cross(0, b).start()

    for cp in moved_o:
        cp.wait()
    attend(3)
    attend(1)
    sums.one(0)
    attend(2)
    attend(0)
    saved += fetches([(outr, outr_o), (attn_ref, attn_o)], osem.at[pl.ds(4, 2)])
    sums.two(0)
    for cp in d_keeps + downs:
        cp.wait()
    moved_d = regroup(lambda p, core: tmp_d.at[p, core], downr, d2send, d2recv, 8)
    for cp in gates:
        cp.start()
    sums.three(0, o_ref)
    sums.end(o_ref)
    for cp in moved_d:
        cp.wait()
    saved += fetches([(downr, downr_o)], osem.at[pl.ds(6, 1)])
    for cp in gates + [g_keep]:
        cp.wait()
    saved += fetches([(gatew, gate_o)], osem.at[pl.ds(7, 1)])
    for cp in plane.first(normed) + plane.second()[0] + plane.second()[1] + [plane.third()]:
        cp.wait_send()
    line_q.end()
    line_o.end()
    counts(lambda cp: cp.wait())
    for cp in saved + [norm_keep]:
        cp.wait()


def attention_front(x, gains, mask, w_query, w_key, value_weight, w_output, w_down, w_gate, cosine, sine, first, place, keys):
    rows, width = x.shape
    tokens = 8 * rows
    depth = w_query.shape[0]
    wide = width // 8
    any_ = pl.BlockSpec(memory_space=pl.ANY)
    vmem = pl.BlockSpec(memory_space=pltpu.VMEM)
    dma, buf, out = pltpu.SemaphoreType.DMA, pltpu.VMEM, jax.ShapeDtypeStruct
    results = (
        out((NZ, depth, 2 * wide), BF16),
        out((wide, width), BF16),
        out((wide, width), BF16),
        out((NZ, depth, w_gate.shape[1] // 32), BF16),
        out((tokens, wide), BF16),
        out((tokens, HEAD_SIZE), BF16),
        out((tokens, HEAD_SIZE), BF16),
        out((tokens, wide), BF16),
    )
    return pl.pallas_call(
        front_kernel,
        out_shape=(
            out((rows, width), F32), out((NZ,) + gains.shape, F32), out((32, 8, 128), F32), out((8, rows, width), BF16)
        ) + results,
        in_specs=[vmem] * 3 + [any_] * 11,
        out_specs=(vmem,) * 3 + (any_,) * 9,
        scratch_shapes=[buf(r.shape, r.dtype) for r in results]
        + [buf(a.shape, a.dtype) for a in (cosine, sine, first, place, keys)]
        + [
            buf((rows, width), BF16), buf((8, rows, width), BF16), buf((tokens, 2 * wide), F32), buf((NZ, depth, wide), BF16),
            buf((NZ, 2, wide, wide), BF16), buf((8, 128), F32), dma((5,)), dma((8,)), dma((NZ,)), dma((NZ,)),
            dma((32,)), dma((32,)),
            dma((10,)), dma((3,)), dma((3,)), dma((2, 4)), dma((4,)), dma((2, 4)), dma((4,)), dma((2, 4)), dma((2, 4)),
            dma((7,)), dma((7,)), dma((7,)), dma((7,)), dma((8,)), dma((8,)),
        ] + scatter_scratch(1, rows, width),
        compiler_params=pltpu.CompilerParams(collective_id=8, has_side_effects=True, vmem_limit_bytes=60 << 20),
        cost_estimate=takes(95),
        name="attention_front",
    )(x, gains, mask, w_query, w_key, value_weight, w_output, w_down, w_gate, cosine, sine, first, place, keys)


def heads_and_columns(
    hidden_in,
    cotangent,
    teacher,
    valid_mask,
    doc_starts,
    attn_gain,
    w_query,
    w_key,
    value_weight,
    w_output,
    mlp_gain,
    w_gate,
    w_up,
    w_down,
):
    rows, width = hidden_in.shape[1:]
    c = lax.axis_index("ctx")
    z = lax.axis_index("fsdp")
    devices = lax.axis_size("ctx")
    tokens = rows * devices
    group = QUERY_HEADS // KEY_VALUE_HEADS
    qcols = group * HEAD_SIZE
    ffcols = FF // (devices * NZ)

    layer_input = hidden_in[0].astype(F32)
    gains = jnp.concatenate(
        [attn_gain.astype(F32)[None], mlp_gain.astype(F32)[None], jnp.zeros((6, attn_gain.shape[0]), F32)]
    )
    place, segment, offset = stream_places(tokens, rows, devices, doc_starts[0])
    freq = ROPE_BASE ** (-(jnp.arange(HEAD_SIZE // 2, dtype=F32) * 2.0 / HEAD_SIZE))
    angle = offset.astype(F32)[:, None] * freq[None, :]
    cosine = jnp.concatenate([jnp.cos(angle)] * 2, axis=1)
    sine = jnp.concatenate([-jnp.sin(angle), jnp.sin(angle)], axis=1)
    columns = ((place - offset)[:, None], place[:, None], place[None, :])
    branch, gains_all, counts, normed_all, w_qkv, out_rows, down_rows, gate_cols, q, k, v, attn = attention_front(
        hidden_in[0], gains, valid_mask, w_query, w_key, value_weight, w_output, w_down, w_gate, cosine, sine, *columns
    )
    attn_scale = gains_all[:, 0, :].reshape(1, width)
    mlp_scale = gains_all[:, 1, :].reshape(1, width)
    residual = layer_input + branch

    r2 = rms_norm_scale(residual)
    hat2 = residual * r2
    normed2 = (hat2 * mlp_scale).astype(BF16)
    maskf = valid_mask[0].astype(F32)
    mlp_out, normed2_all, gate_up, w_mlp = feed_forward(normed2, gate_cols, w_up, down_rows)
    count = jnp.sum(counts[:, 0, 0])
    outf = residual + mlp_out

    diff = outf - teacher[0].astype(F32)
    error_here = jnp.sum(maskf * jnp.mean(diff * diff, axis=-1))
    g_out = cotangent[0].astype(F32) + maskf[:, None] * diff * (2.0 / (count * width))
    g_norm2, _, gate_grads, up_grads, down_grads = feed_back(g_out.astype(BF16), w_mlp, down_rows, normed2_all, gate_up)

    g_hat2 = g_norm2 * mlp_scale
    g_residual = g_out + r2 * (g_hat2 - hat2 * jnp.mean(g_hat2 * hat2, axis=-1, keepdims=True))
    mlp_gain_term = jnp.sum(g_norm2 * hat2, axis=0, keepdims=True)
    g_norm1, got_gate, got_up, got_qkv, got_out, got_gains = attention_back(
        g_residual.astype(BF16), error_here.reshape(1, 1), q, k, v, attn, cosine, sine, *columns, w_qkv.reshape(width, -1), out_rows, mlp_gain_term,
        normed_all.reshape(tokens, width), gate_grads, up_grads,
    )

    r1 = rms_norm_scale(layer_input)
    hat1 = layer_input * r1
    g_hat1 = g_norm1 * attn_scale
    g_input = g_residual + r1 * (g_hat1 - hat1 * jnp.mean(g_hat1 * hat1, axis=-1, keepdims=True))

    parts = devices * NZ
    share = width // parts
    got_gate, got_up = (g.astype(F32).transpose(1, 0, 2).reshape(share, FF) for g in (got_gate, got_up))
    got_qkv = got_qkv.astype(F32).transpose(1, 0, 2)
    got_out = jnp.sum(got_out.astype(F32), axis=0)
    flat = c * NZ + z
    got_gains = jnp.sum(got_gains, axis=0)
    loss = got_gains[2, 0] / count
    got_gains = lax.dynamic_slice_in_dim(got_gains, flat % 2 * share, share, axis=1)
    own_scale = lax.dynamic_slice_in_dim(attn_scale[0], flat * share, share)

    return (
        loss,
        outf.astype(BF16)[None],
        g_input.astype(BF16)[None],
        got_gains[0] / own_scale,
        got_qkv[:, :, :qcols].reshape(share, QUERY_HEADS * HEAD_SIZE),
        got_qkv[:, :, qcols : qcols + HEAD_SIZE].reshape(share, KEY_VALUE_HEADS * HEAD_SIZE),
        got_qkv[:, :, qcols + HEAD_SIZE :].reshape(share, KEY_VALUE_HEADS * HEAD_SIZE),
        got_out,
        got_gains[1],
        got_gate,
        got_up,
        down_grads,
    )


def solution(mesh):
    small = dict(mesh.shape) == {"ctx": KEY_VALUE_HEADS, "fsdp": NZ}
    in_specs = (
        P("fsdp", "ctx", None),
        P("fsdp", "ctx", None),
        P("fsdp", "ctx", None),
        P("fsdp", "ctx"),
        P("fsdp", None),
        P("fsdp"),
        P("fsdp", None),
        P("fsdp", None),
        P("fsdp", None),
        P("fsdp", None),
        P("fsdp"),
        P("fsdp", None),
        P("fsdp", None),
        P("fsdp", None),
    )
    out_specs = (
        P(),
        P("fsdp", "ctx", None),
        P("fsdp", "ctx", None),
        P(("ctx", "fsdp")),
        P(("ctx", "fsdp"), None),
        P(("ctx", "fsdp"), None),
        P(("ctx", "fsdp"), None),
        P(("ctx", "fsdp"), None),
        P(("ctx", "fsdp")),
        P(("ctx", "fsdp"), None),
        P(("ctx", "fsdp"), None),
        P(("ctx", "fsdp"), None),
    )
    return jax.shard_map(
        heads_and_columns if small else per_device, mesh=mesh, in_specs=in_specs, out_specs=out_specs, check_vma=False
    )
```

```python
import functools

import jax
import jax.numpy as jnp
from jax import lax
from jax.experimental import pallas as pl
from jax.experimental.pallas import tpu as pltpu
from jax.sharding import PartitionSpec as P

QUERY_HEADS = 16
KEY_VALUE_HEADS = 8
HEAD_SIZE = 128
FF = 8192


EPS = 1e-05
ROPE_BASE = 1000000.0
NEG = -1e30
CONTRACT_ROWS = (((0,), (0,)), ((), ()))
CONTRACT_COLS = (((1,), (1,)), ((), ()))


def stream_places(rows, local_token_count, devices, starts):
    span = local_token_count // 2
    rowid = jnp.arange(rows, dtype=jnp.int32)
    device = rowid // local_token_count
    within = rowid % local_token_count
    span_id = jnp.where(within < span, device, 2 * devices - 1 - device)
    place = span_id * span + within % span
    before = starts[None, :] <= place[:, None]
    segment = jnp.sum(before.astype(jnp.int32), axis=1) - 1
    first = jnp.max(jnp.where(before, starts[None, :], 0), axis=1)
    return (place, segment, place - first)


def rotary_embed(values, token_offset, sign):
    half = HEAD_SIZE // 2
    freq = ROPE_BASE ** (-(jnp.arange(half, dtype=jnp.float32) * 2.0 / HEAD_SIZE))
    angle = token_offset.astype(jnp.float32)[:, None] * freq[None, :]
    cosine = jnp.cos(angle)[:, None, :]
    sine = sign * jnp.sin(angle)[:, None, :]
    first = values[..., :half]
    second = values[..., half:]
    return jnp.concatenate(
        [first * cosine - second * sine, second * cosine + first * sine], axis=-1
    )


def rms_norm_scale(values):
    return lax.rsqrt(jnp.mean(values * values, axis=-1, keepdims=True) + EPS)


def head_scores(query_rows, key_rows, allowed):
    attention_scores = jnp.einsum(
        "trd,sd->rts", query_rows, key_rows, preferred_element_type=jnp.float32
    ) * HEAD_SIZE ** (-0.5)
    return jnp.where(allowed[None], attention_scores, NEG)


def per_device(
    hidden_in,
    cotangent,
    teacher,
    valid_mask,
    doc_starts,
    attn_gain,
    w_query,
    w_key,
    value_weight,
    w_output,
    mlp_gain,
    w_gate,
    w_up,
    w_down,
):
    local_token_count = hidden_in.shape[1]
    width = hidden_in.shape[2]
    devices = lax.axis_size("ctx")
    index = lax.axis_index("ctx")
    packed_stream_rows = local_token_count * devices
    query_group = QUERY_HEADS // KEY_VALUE_HEADS
    place, segment, token_offset = stream_places(
        packed_stream_rows, local_token_count, devices, doc_starts[0]
    )
    own_start = index * local_token_count
    my_place = lax.dynamic_slice_in_dim(place, own_start, local_token_count)
    my_segment = lax.dynamic_slice_in_dim(segment, own_start, local_token_count)
    local_stream_offset = lax.dynamic_slice_in_dim(token_offset, own_start, local_token_count)
    allowed = (my_segment[:, None] == segment[None, :]) & (place[None, :] <= my_place[:, None])
    layer_input = hidden_in[0].astype(jnp.float32)
    attn_whole = (
        lax.all_gather(attn_gain, "fsdp", axis=0, tiled=True),
        lax.all_gather(w_query, "fsdp", axis=0, tiled=True),
        lax.all_gather(w_key, "fsdp", axis=0, tiled=True),
        lax.all_gather(value_weight, "fsdp", axis=0, tiled=True),
        lax.all_gather(w_output, "fsdp", axis=0, tiled=True),
    )
    first_norm_scale = attn_whole[0].astype(jnp.float32)
    first_inverse_norm = rms_norm_scale(layer_input)
    first_normalized_input = layer_input * first_inverse_norm
    first_normed = (first_normalized_input * first_norm_scale).astype(jnp.bfloat16)
    qproj = jnp.dot(first_normed, attn_whole[1], preferred_element_type=jnp.float32)
    key_projected = jnp.dot(first_normed, attn_whole[2], preferred_element_type=jnp.float32)
    vproj = jnp.dot(first_normed, attn_whole[3], preferred_element_type=jnp.float32).astype(
        jnp.bfloat16
    )
    query_rows = rotary_embed(
        qproj.reshape(local_token_count, QUERY_HEADS, HEAD_SIZE), local_stream_offset, 1.0
    ).astype(jnp.bfloat16)
    key_rows = (
        rotary_embed(
            key_projected.reshape(local_token_count, KEY_VALUE_HEADS, HEAD_SIZE),
            local_stream_offset,
            1.0,
        )
        .reshape(local_token_count, KEY_VALUE_HEADS * HEAD_SIZE)
        .astype(jnp.bfloat16)
    )
    every_key_row, every_value_row = (
        lax.all_gather(key_rows, "ctx", axis=0, tiled=True),
        lax.all_gather(vproj, "ctx", axis=0, tiled=True),
    )
    key_head_rows = every_key_row.reshape(packed_stream_rows, KEY_VALUE_HEADS, HEAD_SIZE).transpose(
        1, 0, 2
    )
    value_head_rows = every_value_row.reshape(
        packed_stream_rows, KEY_VALUE_HEADS, HEAD_SIZE
    ).transpose(1, 0, 2)
    query_head_rows = query_rows.reshape(
        local_token_count, KEY_VALUE_HEADS, query_group, HEAD_SIZE
    ).transpose(1, 0, 2, 3)

    def attend_head(parts):
        head_query, head_key, head_val = parts
        attention_scores = head_scores(head_query, head_key, allowed)
        top = jnp.max(attention_scores, axis=-1, keepdims=True)
        lse = top + jnp.log(jnp.sum(jnp.exp(attention_scores - top), axis=-1, keepdims=True))
        attention_probabilities = jnp.exp(attention_scores - lse)
        mixed_heads = jnp.einsum(
            "rts,sd->trd",
            attention_probabilities.astype(jnp.bfloat16),
            head_val,
            preferred_element_type=jnp.float32,
        )
        return (mixed_heads, lse)

    mixed_heads, lse = lax.map(attend_head, (query_head_rows, key_head_rows, value_head_rows))
    attn = (
        mixed_heads.transpose(1, 0, 2, 3)
        .reshape(local_token_count, QUERY_HEADS * HEAD_SIZE)
        .astype(jnp.bfloat16)
    )
    residual_state = layer_input + jnp.dot(attn, attn_whole[4], preferred_element_type=jnp.float32)
    mlp_whole = (
        lax.all_gather(mlp_gain, "fsdp", axis=0, tiled=True),
        lax.all_gather(w_gate, "fsdp", axis=0, tiled=True),
        lax.all_gather(w_up, "fsdp", axis=0, tiled=True),
        lax.all_gather(w_down, "fsdp", axis=0, tiled=True),
    )
    second_norm_scale = mlp_whole[0].astype(jnp.float32)
    second_inverse_norm = rms_norm_scale(residual_state)
    second_normalized_input = residual_state * second_inverse_norm
    second_normed = (second_normalized_input * second_norm_scale).astype(jnp.bfloat16)
    gate = jnp.dot(second_normed, mlp_whole[1], preferred_element_type=jnp.float32)
    up_val = jnp.dot(second_normed, mlp_whole[2], preferred_element_type=jnp.float32)
    sigma = jax.nn.sigmoid(gate)
    act = (gate * sigma * up_val).astype(jnp.bfloat16)
    outf = residual_state + jnp.dot(act, mlp_whole[3], preferred_element_type=jnp.float32)
    maskf = valid_mask[0].astype(jnp.float32)
    diff = outf - teacher[0].astype(jnp.float32)
    count_here = jnp.sum(maskf)
    error_here = jnp.sum(maskf * jnp.mean(diff * diff, axis=-1))
    count, error_total = lax.psum((count_here, error_here), ("ctx", "fsdp"))
    loss = error_total / count
    output_gradient = cotangent[0].astype(jnp.float32) + maskf[:, None] * diff * (
        2.0 / (count * width)
    )
    g_mo = output_gradient.astype(jnp.bfloat16)
    mlp_back = (
        lax.all_gather(mlp_gain, "fsdp", axis=0, tiled=True),
        lax.all_gather(w_gate, "fsdp", axis=0, tiled=True),
        lax.all_gather(w_up, "fsdp", axis=0, tiled=True),
        lax.all_gather(w_down, "fsdp", axis=0, tiled=True),
    )
    g_act = lax.dot_general(g_mo, mlp_back[3], CONTRACT_COLS, preferred_element_type=jnp.float32)
    g_gate = (g_act * up_val * sigma * (1.0 + gate * (1.0 - sigma))).astype(jnp.bfloat16)
    g_up = (g_act * gate * sigma).astype(jnp.bfloat16)
    gate_up_gradient = jnp.concatenate([g_gate, g_up], axis=1)
    second_norm_gradient = lax.dot_general(
        g_gate, mlp_back[1], CONTRACT_COLS, preferred_element_type=jnp.float32
    )
    second_norm_gradient = second_norm_gradient + lax.dot_general(
        g_up, mlp_back[2], CONTRACT_COLS, preferred_element_type=jnp.float32
    )
    second_hat_gradient = second_norm_gradient * second_norm_scale
    residual_gradient = output_gradient + second_inverse_norm * (
        second_hat_gradient
        - second_normalized_input
        * jnp.mean(second_hat_gradient * second_normalized_input, axis=-1, keepdims=True)
    )
    mlp_share = lax.psum_scatter(
        lax.dot_general(
            second_normed, gate_up_gradient, CONTRACT_ROWS, preferred_element_type=jnp.float32
        ),
        ("ctx", "fsdp"),
        scatter_dimension=0,
        tiled=True,
    )
    down_share = lax.psum_scatter(
        lax.dot_general(act, g_mo, CONTRACT_ROWS, preferred_element_type=jnp.float32),
        ("ctx", "fsdp"),
        scatter_dimension=0,
        tiled=True,
    )
    g_branch = residual_gradient.astype(jnp.bfloat16)
    attn_back = (
        lax.all_gather(attn_gain, "fsdp", axis=0, tiled=True),
        lax.all_gather(w_query, "fsdp", axis=0, tiled=True),
        lax.all_gather(w_key, "fsdp", axis=0, tiled=True),
        lax.all_gather(value_weight, "fsdp", axis=0, tiled=True),
        lax.all_gather(w_output, "fsdp", axis=0, tiled=True),
    )
    attention_gradient = lax.dot_general(
        g_branch, attn_back[4], CONTRACT_COLS, preferred_element_type=jnp.float32
    ).astype(jnp.bfloat16)
    heads_gradient = attention_gradient.reshape(
        local_token_count, KEY_VALUE_HEADS, query_group, HEAD_SIZE
    ).transpose(1, 0, 2, 3)

    def attend_back(parts):
        head_query, head_key, head_val, head_lse, head_grad = parts
        attention_probabilities = jnp.exp(head_scores(head_query, head_key, allowed) - head_lse)
        g_probs = jnp.einsum("trd,sd->rts", head_grad, head_val, preferred_element_type=jnp.float32)
        delta = jnp.sum(attention_probabilities * g_probs, axis=-1, keepdims=True)
        g_scores = (attention_probabilities * (g_probs - delta)).astype(jnp.bfloat16)
        g_query = jnp.einsum(
            "rts,sd->trd", g_scores, head_key, preferred_element_type=jnp.float32
        ) * HEAD_SIZE ** (-0.5)
        key_gradient = jnp.einsum(
            "rts,trd->sd", g_scores, head_query, preferred_element_type=jnp.float32
        ) * HEAD_SIZE ** (-0.5)
        value_gradient = jnp.einsum(
            "rts,trd->sd",
            attention_probabilities.astype(jnp.bfloat16),
            head_grad,
            preferred_element_type=jnp.float32,
        )
        return (g_query, key_gradient, value_gradient)

    g_query, key_gradient, value_gradient = lax.map(
        attend_back, (query_head_rows, key_head_rows, value_head_rows, lse, heads_gradient)
    )
    key_gradient_terms = key_gradient.transpose(1, 0, 2).reshape(
        packed_stream_rows, KEY_VALUE_HEADS * HEAD_SIZE
    )
    value_gradient_terms = value_gradient.transpose(1, 0, 2).reshape(
        packed_stream_rows, KEY_VALUE_HEADS * HEAD_SIZE
    )
    key_rows_gradient, g_vals = (
        lax.psum_scatter(
            key_gradient_terms.astype(jnp.bfloat16), "ctx", scatter_dimension=0, tiled=True
        ).astype(jnp.float32),
        lax.psum_scatter(
            value_gradient_terms.astype(jnp.bfloat16), "ctx", scatter_dimension=0, tiled=True
        ).astype(jnp.float32),
    )
    g_qproj = (
        rotary_embed(
            g_query.transpose(1, 0, 2, 3).reshape(local_token_count, QUERY_HEADS, HEAD_SIZE),
            local_stream_offset,
            -1.0,
        )
        .reshape(local_token_count, QUERY_HEADS * HEAD_SIZE)
        .astype(jnp.bfloat16)
    )
    g_kproj = (
        rotary_embed(
            key_rows_gradient.reshape(local_token_count, KEY_VALUE_HEADS, HEAD_SIZE),
            local_stream_offset,
            -1.0,
        )
        .reshape(local_token_count, KEY_VALUE_HEADS * HEAD_SIZE)
        .astype(jnp.bfloat16)
    )
    g_vproj = g_vals.astype(jnp.bfloat16)
    first_norm_gradient = lax.dot_general(
        g_qproj, attn_back[1], CONTRACT_COLS, preferred_element_type=jnp.float32
    )
    first_norm_gradient = first_norm_gradient + lax.dot_general(
        g_kproj, attn_back[2], CONTRACT_COLS, preferred_element_type=jnp.float32
    )
    first_norm_gradient = first_norm_gradient + lax.dot_general(
        g_vproj, attn_back[3], CONTRACT_COLS, preferred_element_type=jnp.float32
    )
    first_hat_gradient = first_norm_gradient * first_norm_scale
    g_input = residual_gradient + first_inverse_norm * (
        first_hat_gradient
        - first_normalized_input
        * jnp.mean(first_hat_gradient * first_normalized_input, axis=-1, keepdims=True)
    )
    key_value_proj_gradient = jnp.concatenate([g_kproj, g_vproj], axis=1)
    query_term = lax.dot_general(
        first_normed, g_qproj, CONTRACT_ROWS, preferred_element_type=jnp.float32
    )
    key_value_term = lax.dot_general(
        first_normed, key_value_proj_gradient, CONTRACT_ROWS, preferred_element_type=jnp.float32
    )
    output_term = lax.dot_general(attn, g_branch, CONTRACT_ROWS, preferred_element_type=jnp.float32)
    scale_gradient_terms = jnp.stack(
        [
            jnp.sum(first_norm_gradient * first_normalized_input, axis=0),
            jnp.sum(second_norm_gradient * second_normalized_input, axis=0),
        ]
    )
    query_share, key_value_share, output_share, gain_share = (
        lax.psum_scatter(query_term, ("ctx", "fsdp"), scatter_dimension=0, tiled=True),
        lax.psum_scatter(key_value_term, ("ctx", "fsdp"), scatter_dimension=0, tiled=True),
        lax.psum_scatter(output_term, ("ctx", "fsdp"), scatter_dimension=0, tiled=True),
        lax.psum_scatter(scale_gradient_terms, ("ctx", "fsdp"), scatter_dimension=1, tiled=True),
    )
    key_value_columns = KEY_VALUE_HEADS * HEAD_SIZE
    return (
        loss,
        outf.astype(jnp.bfloat16)[None],
        g_input.astype(jnp.bfloat16)[None],
        gain_share[0],
        query_share,
        key_value_share[:, :key_value_columns],
        key_value_share[:, key_value_columns:],
        output_share,
        gain_share[1],
        mlp_share[:, :FF],
        mlp_share[:, FF:],
        down_share,
    )


MESH = pl.DeviceIdType.MESH
F32 = jnp.float32
BF16 = jnp.bfloat16
NZ = 4


def place_on_plane():
    c = lax.axis_index("ctx")
    z = lax.axis_index("fsdp")
    sib = c + 1 - 2 * lax.rem(c, 2)
    xn = c + 2 - 4 * lax.rem(c // 2, 2)
    yn = c + 4 - 8 * (c // 4)
    diag = xn + yn - c
    return c, z, sib, xn, yn, diag


def meet(devices):
    barrier = pltpu.get_barrier_semaphore()
    for d in devices:
        pl.semaphore_signal(barrier, inc=1, device_id=d, device_id_type=MESH)
    pl.semaphore_wait(barrier, len(devices))


def remote(src, dst, send, recv, device):
    return pltpu.make_async_remote_copy(
        src_ref=src, dst_ref=dst, send_sem=send, recv_sem=recv, device_id=device, device_id_type=MESH
    )


def takes(micros):
    return pl.CostEstimate(flops=0, bytes_accessed=micros * 3_500_000, transcendentals=0)


class Plane:
    def __init__(self, here, slot, send, recv, half):
        self.c, self.z, self.sib, self.xn, self.yn, self.diag = here
        self.slot, self.send, self.recv, self.half = slot, send, recv, half

    def copy(self, kind, src, dst, to):
        return remote(src, dst, self.send.at[kind], self.recv.at[kind], (to, self.z))

    def first(self, src):
        mine = self.slot(self.c)
        return [self.copy(0, src, mine, self.xn), self.copy(1, src, mine, self.yn), self.copy(2, src, mine, self.sib)]

    def arrive(self):
        s = self.slot
        return [self.copy(0, s(self.xn), s(self.xn), self.xn), self.copy(1, s(self.yn), s(self.yn), self.yn)]

    def second(self):
        h = self.half
        s = self.slot
        ybot = s(self.yn).at[pl.ds(0, h)]
        xtop = s(self.xn).at[pl.ds(h, h)]
        return (
            [self.copy(4, xtop, xtop, self.yn), self.copy(5, s(self.xn), s(self.xn), self.sib)],
            [self.copy(3, ybot, ybot, self.xn), self.copy(6, s(self.yn), s(self.yn), self.sib)],
        )

    def diagonal(self):
        h = self.half
        lo, hi = self.slot(self.diag).at[pl.ds(0, h)], self.slot(self.diag).at[pl.ds(h, h)]
        return [self.copy(3, lo, lo, self.xn), self.copy(4, hi, hi, self.yn)]

    def third(self):
        d = self.slot(self.diag)
        return self.copy(7, d, d, self.sib)

    def across(self):
        s = self.slot
        return [self.copy(k, s(j), s(j), self.sib) for k, j in ((2, self.sib), (5, self.xn + self.sib - self.c), (6, self.yn + self.sib - self.c), (7, self.diag + self.sib - self.c))]


def add_rows(dst, parts, chunk=16):
    n = dst.shape[0] // chunk

    def body(i, _):
        at = pl.ds(pl.multiple_of(i * chunk, chunk), chunk)
        total = parts[0][at, :].astype(F32)
        for p in parts[1:]:
            total = total + p[at, :].astype(F32)
        dst[at, :] = total.astype(dst.dtype)
        return 0

    lax.fori_loop(0, n, body, 0)


def plane_order(z):
    pick = jnp.where
    return [z, pick(z == 0, 1, z - 1), pick(z == 3, 1, pick(z == 2, 3, 2)), pick(z < 2, 3, 0)]


def chip_at(c, b):
    x, y = lax.rem(c // 2, 2), c // 4
    xb, yb = lax.rem(b, 2), b // 2
    return (x + xb - 2 * x * xb) + 2 * (y + yb - 2 * y * yb)


def chunk_order(i):
    return jnp.where(i == 0, 3, jnp.where(i == 3, 0, i))


class Gather:
    def __init__(self, here, x_ref, o_ref, keep, zsend, zrecv, send, recv):
        self.here, self.x, self.o = here, x_ref, o_ref
        self.c, self.z = here[0], here[1]
        self.order = plane_order(self.z)
        self.zsend, self.zrecv = zsend, zrecv
        self.planes = [
            Plane(here, functools.partial(lambda zz, j: o_ref.at[zz, j], zz), send.at[zz], recv.at[zz], x_ref.shape[0] // 2)
            for zz in self.order
        ]
        self.keep = pltpu.make_async_copy(x_ref, o_ref.at[self.z, self.c], keep)

    def hop(self, up, t):
        zz = self.order[t]
        src = self.x if t == 0 else self.o.at[zz, self.c]
        row = 0 if up else 1
        return remote(
            src, self.o.at[zz, self.c], self.zsend.at[row, zz], self.zrecv.at[zz], (self.c, self.z + (1 if up else -1))
        )

    def hops(self, t, act):
        zz, z = self.order[t], self.z

        @pl.when((zz <= z) & (z < NZ - 1))
        def _():
            act(self.hop(True, t))

        @pl.when((zz >= z) & (z > 0))
        def _():
            act(self.hop(False, t))

    def spread(self, t):
        if t > 0:
            self.hop(True, t).wait_recv()
        self.hops(t, lambda cp: cp.start())
        for cp in self.planes[t].first(self.source(t)):
            cp.start()

    def source(self, t):
        return self.x if t == 0 else self.o.at[self.order[t], self.c]

    def onward(self, t):
        p = self.planes[t]
        for arrived, sends in zip(p.arrive(), p.second()):
            arrived.wait_recv()
            for cp in sends:
                cp.start()

    def close(self, t):
        p = self.planes[t]
        for cp in p.diagonal():
            cp.wait_recv()
        p.third().start()
        for cp in p.across():
            cp.wait_recv()
        if t == 0:
            self.keep.wait()

    def end(self):
        for t, p in enumerate(self.planes):
            for cp in p.first(self.source(t)) + p.second()[0] + p.second()[1] + [p.third()]:
                cp.wait_send()
            self.hops(t, lambda cp: cp.wait_send())


class Scatter:
    def __init__(self, here, order, part, sibr, xh, yh, xf, yf, zr, bsend, brecv, hsend, hrecv, fsend, frecv, zsend, zrecv):
        self.c, self.z, self.sib, self.xn, self.yn, self.diag = here
        self.k = lax.rem(self.c, 2)
        self.order = order
        self.part, self.sibr, self.xh, self.yh, self.xf, self.yf, self.zr = part, sibr, xh, yh, xf, yf, zr
        self.sems = (bsend, brecv, hsend, hrecv, fsend, frecv, zsend, zrecv)
        self.h = part.shape[3] // 2

    def mine(self, t, b):
        return self.part.at[t, b, self.k]

    def cross(self, t, b):
        send, recv = self.sems[0:2]
        return remote(self.part.at[t, b, 1 - self.k], self.sibr.at[t, b], send.at[t, b], recv.at[t, b], (self.sib, self.z))

    def halves(self, t):
        send, recv = self.sems[2:4]
        src = self.mine(t, 3)
        return (
            remote(src.at[pl.ds(0, self.h)], self.xh.at[t], send.at[t, 0], recv.at[t, 0], (self.xn, self.z)),
            remote(src.at[pl.ds(self.h, self.h)], self.yh.at[t], send.at[t, 1], recv.at[t, 1], (self.yn, self.z)),
        )

    def fulls(self, t):
        send, recv = self.sems[4:6]
        return (
            remote(self.mine(t, 1), self.xf.at[t], send.at[t, 0], recv.at[t, 0], (self.xn, self.z)),
            remote(self.mine(t, 2), self.yf.at[t], send.at[t, 1], recv.at[t, 1], (self.yn, self.z)),
        )

    def hop(self, t):
        send, recv = self.sems[6:8]
        return remote(self.mine(t, 0), self.zr.at[self.z], send.at[t], recv.at[self.z], (self.c, self.order[t]))

    def came(self, t):
        send, recv = self.sems[6:8]
        zz = self.order[t]
        return remote(self.zr.at[zz], self.zr.at[zz], send.at[t], recv.at[zz], (self.c, zz))

    def one(self, t):
        self.cross(t, 3).wait_recv()
        add_rows(self.mine(t, 3), [self.mine(t, 3), self.sibr.at[t, 3]])
        for cp in self.halves(t):
            cp.start()

    def two(self, t):
        h = self.h
        top, low = pl.ds(0, h), pl.ds(h, h)
        hx, hy = self.halves(t)
        fx, fy = self.fulls(t)
        self.cross(t, 1).wait_recv()
        m, s = self.mine(t, 1), self.sibr.at[t, 1]
        add_rows(m.at[top], [m.at[top], s.at[top]])
        hy.wait_recv()
        add_rows(m.at[low], [m.at[low], s.at[low], self.yh.at[t]])
        fx.start()
        self.cross(t, 2).wait_recv()
        m, s = self.mine(t, 2), self.sibr.at[t, 2]
        add_rows(m.at[low], [m.at[low], s.at[low]])
        hx.wait_recv()
        add_rows(m.at[top], [m.at[top], s.at[top], self.xh.at[t]])
        fy.start()

    def three(self, t, o_ref):
        self.cross(t, 0).wait_recv()
        for cp in self.fulls(t):
            cp.wait_recv()
        parts = [self.mine(t, 0), self.sibr.at[t, 0], self.xf.at[t], self.yf.at[t]]
        if t == 0:
            add_rows(o_ref, parts)
        else:
            add_rows(self.mine(t, 0), parts)
            self.hop(t).start()

    def end(self, o_ref):
        n = len(self.order)
        for t in range(1, n):
            self.came(t).wait_recv()
        if n > 1:
            add_rows(o_ref, [o_ref] + [self.zr.at[self.order[t]] for t in range(1, n)])
        for t in range(n):
            for b in range(4):
                self.cross(t, b).wait_send()
            for cp in self.halves(t) + self.fulls(t):
                cp.wait_send()
            if t > 0:
                self.hop(t).wait_send()


def scatter_scratch(n, rows, width):
    v, dma = pltpu.VMEM, pltpu.SemaphoreType.DMA
    return [
        v((n, 4, 2, rows, width), BF16), v((n, 4, rows, width), BF16),
        v((n, rows // 2, width), BF16), v((n, rows // 2, width), BF16),
        v((n, rows, width), BF16), v((n, rows, width), BF16), v((NZ, rows, width), BF16),
        dma((n, 4)), dma((n, 4)), dma((n, 2)), dma((n, 2)), dma((n, 2)), dma((n, 2)), dma((NZ,)), dma((NZ,)),
    ]


def neighbours(here):
    c, z, sib, xn, yn, diag = here
    return [(sib, z), (xn, z), (yn, z)] + [(c, lax.rem(z + s, NZ)) for s in (1, 2, 3)]


def everyone_else(c, z):
    flat = c * NZ + z
    others = [lax.rem(flat + s, 32) for s in range(1, 32)]
    return flat, [(o // NZ, lax.rem(o, NZ)) for o in others]


def feed_kernel(
    x_ref, gate_in, wu_ref, d_in, o_ref, all_ref, gu_ref, w_out,
    w_ref, d_ref, xs, gs, xsem, gsem, wsend, wrecv, wkeep, keep, zsend, zrecv, send, recv, *scat
):
    here = place_on_plane()
    c, z = here[0], here[1]
    meet(neighbours(here))
    gather_ = Gather(here, x_ref, all_ref, keep.at[0], zsend, zrecv, send, recv)
    order = gather_.order
    sums = Scatter(here, order, *scat)
    ff = d_ref.shape[0]
    gather_.keep.start()
    gather_.spread(0)

    def load(t, b):
        src = all_ref.at[order[t], pl.ds(2 * chip_at(c, b), 2)]
        return pltpu.make_async_copy(src, xs.at[b], xsem.at[b])

    def store(t, b):
        return pltpu.make_async_copy(gs.at[b], gu_ref.at[order[t], chip_at(c, b)], gsem.at[b])

    def work(t, lo, hi):
        for b in (3, 1, 2, 0)[lo:hi]:
            load(t, b).start()

        def body(i, _):
            b = chunk_order(i)
            load(t, b).wait()
            if t != 1:
                store(1, b).wait()
            x = xs[b].reshape(-1, xs.shape[-1])
            gu = jnp.dot(x, w_ref[...].reshape(x.shape[1], -1), preferred_element_type=F32)
            gs[b] = gu
            store(t, b).start()
            gate, up = gu[:, :ff], gu[:, ff:]
            act = (gate * jax.nn.sigmoid(gate) * up).astype(BF16)
            p = jnp.dot(act, d_ref[...], preferred_element_type=F32).astype(BF16)
            sums.part[t, b] = p.reshape(sums.part.shape[2:])
            sums.cross(t, b).start()
            return 0

        lax.fori_loop(lo, hi, body, 0)

    weights = []
    keeps = [pltpu.make_async_copy(d_in, d_ref, wkeep.at[0])]
    keeps.append(pltpu.make_async_copy(gate_in, w_ref.at[:, :, pl.ds(0, ff)], wkeep.at[1]))
    for hop in range(NZ):
        to = lax.rem(z + hop, NZ)
        src = wu_ref.at[:, pl.ds(pl.multiple_of((c * NZ + to) * ff, ff), ff)]
        dst = w_ref.at[z, :, pl.ds(ff, ff)]
        if hop == 0:
            keeps.append(pltpu.make_async_copy(src, dst, wkeep.at[2]))
        else:
            weights.append(remote(src, dst, wsend.at[hop], wrecv.at[hop], (c, to)))
    w_keep = pltpu.make_async_copy(w_ref, w_out, wkeep.at[3])

    def early():
        for cp in keeps + weights:
            cp.start()

    def ready():
        for cp in keeps + weights:
            cp.wait()
        w_keep.start()

    fused_steps(gather_, sums, work, o_ref, False, early=early, ready=ready)
    for b in range(4):
        store(0, b).wait()
    w_keep.wait()


def fused_steps(gather_, sums, work, o_ref, own_first, more=lambda t: None, early=lambda: None, ready=lambda: None):
    gather_.spread(1)
    gather_.onward(0)
    early()
    gather_.spread(2)
    if own_first:
        ready()
        gather_.close(0)
        work(0, 0, 2)
    gather_.onward(1)
    if own_first:
        work(0, 2, 4)
    gather_.spread(3)
    if own_first:
        more(0)
    gather_.onward(2)
    if not own_first:
        ready()
    gather_.close(1)
    work(1, 0, 4)
    gather_.onward(3)
    if not own_first:
        sums.one(1)
    more(1)
    gather_.close(2)
    work(2, 0, 2)
    sums.one(2)
    work(2, 2, 4)
    sums.two(2)
    more(2)
    gather_.close(3)
    work(3, 0, 2)
    sums.one(3)
    work(3, 2, 4)
    sums.three(2, o_ref)
    sums.two(3)
    more(3)
    if own_first:
        sums.one(1)
    else:
        gather_.close(0)
        work(0, 0, 4)
    sums.three(3, o_ref)
    if own_first:
        sums.two(1)
        sums.one(0)
    else:
        sums.one(0)
        more(0)
        sums.two(1)
    sums.three(1, o_ref)
    sums.two(0)
    sums.three(0, o_ref)
    sums.end(o_ref)
    gather_.end()


def gather_sems():
    dma = pltpu.SemaphoreType.DMA
    return [dma((1,)), dma((2, 4)), dma((4,)), dma((4, 8)), dma((4, 8))]


def feed_forward(x, gate, w_up, d):
    rows, width = x.shape
    depth, cols = w_up.shape[0], 2 * d.shape[0]
    any_ = pl.BlockSpec(memory_space=pl.ANY)
    vmem = pl.BlockSpec(memory_space=pltpu.VMEM)
    dma = pltpu.SemaphoreType.DMA
    return pl.pallas_call(
        feed_kernel,
        out_shape=(
            jax.ShapeDtypeStruct((rows, width), F32),
            jax.ShapeDtypeStruct((NZ, 8, rows, width), BF16),
            jax.ShapeDtypeStruct((NZ, 4, 2 * rows, cols), F32),
            jax.ShapeDtypeStruct((NZ, depth, cols), BF16),
        ),
        in_specs=[vmem, any_, any_, any_],
        out_specs=(vmem, any_, any_, any_),
        scratch_shapes=[
            pltpu.VMEM((NZ, depth, cols), BF16), pltpu.VMEM(d.shape, BF16),
            pltpu.VMEM((4, 2, rows, width), BF16), pltpu.VMEM((4, 2 * rows, cols), F32), dma((4,)), dma((4,)),
            dma((4,)), dma((4,)), dma((4,)),
        ] + gather_sems() + scatter_scratch(NZ, rows, width),
        compiler_params=pltpu.CompilerParams(collective_id=5, has_side_effects=True, vmem_limit_bytes=60 << 20),
        cost_estimate=takes(180),
        name="feed_forward",
    )(x, gate, w_up, d)


def feed_back_kernel(
    x_ref, w_in, d_in, n_ref, gu_ref, o_ref, all_ref, gate_out, up_out, down_out,
    w_ref, d_ref, gate_o, up_o, down_o, wsem, gsend, grecv, xs, ns, gs, gg, acts, total, xsem, nsem, gsem, keep, zsend, zrecv, send, recv, *scat
):
    here = place_on_plane()
    c, z = here[0], here[1]
    meet(neighbours(here))
    gather_ = Gather(here, x_ref, all_ref, keep.at[0], zsend, zrecv, send, recv)
    order = gather_.order
    sums = Scatter(here, order, *scat)
    ff = d_ref.shape[0]
    tokens = 8 * x_ref.shape[0]
    gather_.keep.start()
    gather_.spread(0)

    def loads(t, b):
        chip = chip_at(c, b)
        pair = pl.ds(2 * chip, 2)
        return (
            pltpu.make_async_copy(gu_ref.at[order[t], chip], gs.at[b], gsem.at[b]),
            pltpu.make_async_copy(all_ref.at[order[t], pair], xs.at[b], xsem.at[b]),
            pltpu.make_async_copy(n_ref.at[order[t], pair], ns.at[b], nsem.at[b]),
        )

    def work(t, lo, hi):
        for b in (3, 1, 2, 0)[lo:hi]:
            for cp in loads(t, b):
                cp.start()

        def body(i, _):
            b = chunk_order(i)
            stored, tokens_in, _ = loads(t, b)
            stored.wait()
            tokens_in.wait()
            g = xs[b].reshape(-1, xs.shape[-1])
            g_act = lax.dot_general(g, d_ref[...], CONTRACT_COLS, preferred_element_type=F32)
            gate, up = gs[b, :, :ff], gs[b, :, ff:]
            sg = jax.nn.sigmoid(gate)
            acts[b] = (gate * sg * up).astype(BF16)
            gg[b, :, :ff] = (g_act * up * sg * (1.0 + gate * (1.0 - sg))).astype(BF16)
            gg[b, :, ff:] = (g_act * gate * sg).astype(BF16)
            p = lax.dot_general(gg[b], w_ref[...].reshape(o_ref.shape[1], -1), CONTRACT_COLS, preferred_element_type=F32).astype(BF16)
            sums.part[t, b] = p.reshape(sums.part.shape[2:])
            sums.cross(t, b).start()
            return 0

        lax.fori_loop(lo, hi, body, 0)

    piece = 512

    def more(t):
        for b in range(4):
            loads(t, b)[2].wait()

        def body(i, _):
            at = pl.ds(pl.multiple_of(i * piece, piece), piece)
            n = ns[:, :, :, at].reshape(tokens, piece)
            w_term = lax.dot_general(n, gg[...].reshape(tokens, -1), CONTRACT_ROWS, preferred_element_type=F32)
            g = xs[:, :, :, at].reshape(tokens, piece)
            d_term = lax.dot_general(acts[...].reshape(tokens, -1), g, CONTRACT_ROWS, preferred_element_type=F32)
            if t > 0:
                w_term = w_term + total[at, :]
                d_term = d_term + down_o[:, at]
            down_o[:, at] = d_term
            if t < NZ - 1:
                total[at, :] = w_term
            else:
                pair = pl.ds(2 * i, 2)
                gate_o[pair] = w_term[:, :ff].astype(BF16).reshape((2,) + gate_o.shape[1:])
                up_o[pair] = w_term[:, ff:].astype(BF16).reshape((2,) + up_o.shape[1:])
            return 0

        lax.fori_loop(0, o_ref.shape[1] // piece, body, 0)

    keeps = [pltpu.make_async_copy(w_in, w_ref, wsem.at[0]), pltpu.make_async_copy(d_in, d_ref, wsem.at[1])]
    saved = [
        pltpu.make_async_copy(src, dst, wsem.at[2 + i])
        for i, (src, dst) in enumerate(((gate_o.at[:, z], gate_out.at[:, z]), (up_o, up_out), (down_o, down_out)))
    ]
    gate_z = []
    for s in (1, 2, 3):
        to = lax.rem(z + s, NZ)
        gate_z.append(remote(gate_o.at[:, to], gate_out.at[:, z], gsend.at[s], grecv.at[s], (c, to)))

    def early():
        for cp in keeps:
            cp.start()

    def ready():
        for cp in keeps:
            cp.wait()

    def more_and_save(t):
        more(t)
        if t == NZ - 1:
            for cp in gate_z + saved:
                cp.start()

    fused_steps(gather_, sums, work, o_ref, True, more_and_save, early, ready)
    for cp in saved + gate_z:
        cp.wait()


def feed_back(x, w, d, normed, gate_up):
    rows, width = x.shape
    cols = w.shape[2]
    ff = d.shape[0]
    by_owner = (8, NZ, width // 32, ff)
    any_ = pl.BlockSpec(memory_space=pl.ANY)
    vmem = pl.BlockSpec(memory_space=pltpu.VMEM)
    dma, buf = pltpu.SemaphoreType.DMA, pltpu.VMEM
    return pl.pallas_call(
        feed_back_kernel,
        out_shape=(
            jax.ShapeDtypeStruct((rows, width), F32),
            jax.ShapeDtypeStruct((NZ, 8, rows, width), BF16),
            jax.ShapeDtypeStruct(by_owner, BF16),
            jax.ShapeDtypeStruct(by_owner, BF16),
            jax.ShapeDtypeStruct((ff, width), F32),
        ),
        in_specs=[vmem] + [any_] * 4,
        out_specs=(vmem,) + (any_,) * 4,
        scratch_shapes=[
            buf(w.shape, BF16), buf(d.shape, BF16), buf(by_owner, BF16), buf(by_owner, BF16), buf((ff, width), F32),
            dma((5,)), dma((4,)), dma((4,)), buf((4, 2, rows, width), BF16), buf((4, 2, rows, width), BF16), buf((4, 2 * rows, cols), F32),
            buf((4, 2 * rows, cols), BF16), buf((4, 2 * rows, ff), BF16), buf((width, cols), F32),
            dma((4,)), dma((4,)), dma((4,)),
        ] + gather_sems() + scatter_scratch(NZ, rows, width),
        compiler_params=pltpu.CompilerParams(collective_id=7, has_side_effects=True, vmem_limit_bytes=63 << 20),
        cost_estimate=takes(180),
        name="feed_back",
    )(x, w, d, normed, gate_up)


ROWS_AT_ONCE = 256


def turn(u, cosine, sine):
    return u * cosine + pltpu.roll(u, HEAD_SIZE // 2, 1) * sine


def block_probs(q, k, first, place, keys_place):
    scores = lax.dot_general(q, k, CONTRACT_COLS, preferred_element_type=F32) * HEAD_SIZE ** (-0.5)
    allowed = (keys_place >= first) & (keys_place <= place)
    scores = jnp.where(allowed, scores, NEG)
    raised = jnp.exp(scores - jnp.max(scores, axis=-1, keepdims=True))
    return raised / jnp.sum(raised, axis=-1, keepdims=True)


def fetches(pairs, sems):
    copies = [pltpu.make_async_copy(src, dst, sems.at[i]) for i, (src, dst) in enumerate(pairs)]
    for cp in copies:
        cp.start()
    return copies


def exchange_loop(c, z, act):
    flat = c * NZ + z

    def body(s, _):
        to = lax.rem(flat + s, 32)
        act(s, to // NZ, lax.rem(to, NZ))
        return 0

    lax.fori_loop(1, 32, body, 0)


def back_kernel(
    g_ref, err_ref, q_in, k_in, v_in, attn_in, cos_in, sin_in, first_in, place_in, keys_in, wqkv_in, wout_in, gain_in,
    norm_in, gate_ref, up_ref,
    o_ref, gate_o, up_o, q_o, k_o, v_o, out_o, gain_o,
    q_ref, k_ref, v_ref, attn_ref, cos_ref, sin_ref, first_ref, place_ref, keys_ref, wqkv_ref, wout_ref, gain_ref, normed, isem,
    gb, ga, gqkv, gk, gv, outg, qkvg, mt, qt, qs, gsrc,
    msend, mrecv, m2send, m2recv, m2keep, qsend, qrecv, q2send, q2recv, osend, orecv, ssend, srecv, lsem, psend, precv, *scat
):
    here = place_on_plane()
    c, z, sib, xn, yn, diag = here
    flat, everyone = everyone_else(c, z)
    meet(everyone)
    rows, width = g_ref.shape
    tokens = 8 * rows
    share = width // 32
    plane = Plane(here, lambda j: gb.at[j], psend, precv, rows // 2)
    sums = Scatter(here, [z], *scat)
    mates = [lax.rem(c + s, 8) for s in range(1, 8)]
    others = [(s, lax.rem(z + s, NZ)) for s in (1, 2, 3)]
    for cp in plane.first(g_ref):
        cp.start()

    mlp_z = [remote(up_ref.at[:, to], mt.at[:, z], msend.at[s], mrecv.at[s], (c, to)) for s, to in others]
    keep = pltpu.make_async_copy(up_ref.at[:, z], mt.at[:, z], lsem.at[1])
    for cp in mlp_z + [keep]:
        cp.start()
    ff = gate_ref.shape[3]

    def over_plane(i, ref):
        out = []
        for zz in range(NZ):
            dst = (gate_o, up_o)[i].at[:, pl.ds(pl.multiple_of((c * NZ + zz) * ff, ff), ff)]
            for s, m in enumerate(mates):
                out.append(remote(ref.at[m, zz], dst, m2send.at[i, zz, s], m2recv.at[i, zz, s], (m, z)))
            out.append(pltpu.make_async_copy(ref.at[c, zz], dst, m2keep.at[i, zz]))
        for cp in out:
            cp.start()
        return out

    got = fetches(
        [
            (wout_in, wout_ref), (q_in, q_ref), (k_in, k_ref), (v_in, v_ref), (cos_in, cos_ref), (sin_in, sin_ref),
            (first_in, first_ref), (place_in, place_ref), (keys_in, keys_ref),
            (attn_in, attn_ref), (norm_in, normed), (wqkv_in, wqkv_ref), (gain_in, gain_ref),
        ],
        isem,
    )
    gb[c] = g_ref[...]
    gk[...] = jnp.zeros_like(gk)
    gv[...] = jnp.zeros_like(gv)

    def attend(b):
        chip = chip_at(c, b)
        at = pl.ds(pl.multiple_of(chip * ROWS_AT_ONCE, ROWS_AT_ONCE), ROWS_AT_ONCE)
        g_rows = gb[pl.ds(chip * 2, 2)].reshape(ROWS_AT_ONCE, width)
        ga[at, :] = lax.dot_general(g_rows, wout_ref[...], CONTRACT_COLS, preferred_element_type=F32).astype(BF16)
        k, v = k_ref[...], v_ref[...]
        cosine, sine = cos_ref[at, :], sin_ref[at, :]
        first, place, keys = first_ref[at, :], place_ref[at, :], keys_ref[...]
        for h in range(QUERY_HEADS // KEY_VALUE_HEADS):
            lanes = slice(h * HEAD_SIZE, (h + 1) * HEAD_SIZE)
            q, g = q_ref[at, lanes], ga[at, lanes]
            probs = block_probs(q, k, first, place, keys)
            g_probs = lax.dot_general(g, v, CONTRACT_COLS, preferred_element_type=F32)
            delta = jnp.sum(probs * g_probs, axis=-1, keepdims=True)
            g_scores = (probs * (g_probs - delta)).astype(BF16)
            g_q = jnp.dot(g_scores, k, preferred_element_type=F32) * HEAD_SIZE ** (-0.5)
            gqkv[at, lanes] = turn(g_q, cosine, -sine).astype(BF16)
            gk[...] += lax.dot_general(g_scores, q, CONTRACT_ROWS, preferred_element_type=F32)
            gv[...] += lax.dot_general(probs.astype(BF16), g, CONTRACT_ROWS, preferred_element_type=F32)

    came = plane.across()
    for cp in got[:9]:
        cp.wait()
    came[0].wait_recv()
    attend(0)
    for arrived, sends in zip(plane.arrive(), plane.second()):
        arrived.wait_recv()
        for cp in sends:
            cp.start()
    came[1].wait_recv()
    attend(1)
    for cp in plane.diagonal():
        cp.wait_recv()
    plane.third().start()
    came[2].wait_recv()
    attend(2)
    came[3].wait_recv()
    mlp_c = over_plane(0, gate_ref)
    got[9].wait()
    piece = 512

    def outs(i, _):
        at = pl.ds(pl.multiple_of(i * piece, piece), piece)
        g = gb[:, :, at].reshape(tokens, piece)
        outg[:, at] = lax.dot_general(attn_ref[...], g, CONTRACT_ROWS, preferred_element_type=F32).astype(BF16)
        return 0

    lax.fori_loop(0, width // piece, outs, 0)
    out_sends = []
    for s, to in others:
        src = outg.at[pl.ds(pl.multiple_of(to * share, share), share)]
        out_sends.append(remote(src, out_o.at[z], osend.at[s], orecv.at[s], (c, to)))
    for cp in out_sends:
        cp.start()
    keep_o = pltpu.make_async_copy(outg.at[pl.ds(pl.multiple_of(z * share, share), share)], out_o.at[z], lsem.at[5])
    keep_o.start()
    attend(3)
    qcols = q_ref.shape[1]
    g_k = gk[...] * HEAD_SIZE ** (-0.5)
    gqkv[:, qcols : qcols + HEAD_SIZE] = turn(g_k, cos_ref[...], -sin_ref[...]).astype(BF16)
    gqkv[:, qcols + HEAD_SIZE :] = gv[...].astype(BF16)

    for cp in got[10:]:
        cp.wait()
    cols = gqkv.shape[1]

    def project(i, _):
        at = pl.ds(pl.multiple_of(i * piece, piece), piece)
        term = lax.dot_general(normed[:, at], gqkv[...], CONTRACT_ROWS, preferred_element_type=F32).astype(BF16)
        qkvg[pl.ds(2 * i, 2)] = term.reshape(2, NZ, share, cols)
        return 0

    lax.fori_loop(0, width // piece, project, 0)
    qkv_z = []
    for h in range(2):
        lanes = pl.ds(h * qcols, qcols)
        for s, to in others:
            src, dst = qkvg.at[:, to, :, lanes], qt.at[s, :, :, lanes]
            qkv_z.append(remote(src, dst, qsend.at[h, s], qrecv.at[h, s], (c, to)))
            qkv_z[-1].start()

    gsrc[...] = jnp.zeros_like(gsrc)
    gsrc[1:2, :] = gain_ref[...]
    gsrc[2:3, :] = jnp.full((1, width), err_ref[0, 0], F32)
    for b in (3, 1, 2, 0):
        chip = chip_at(c, b)
        at = pl.ds(pl.multiple_of(chip * ROWS_AT_ONCE, ROWS_AT_ONCE), ROWS_AT_ONCE)
        p = lax.dot_general(gqkv[at, :], wqkv_ref[...], CONTRACT_COLS, preferred_element_type=F32)
        sums.part[0, b] = p.astype(BF16).reshape(2, rows, width)
        sums.cross(0, b).start()
        gsrc[0:1, :] += jnp.sum(p * normed[at, :].astype(F32), axis=0, keepdims=True)

    def gain_sends(act):
        def one(s, tc, tz):
            lanes = pl.ds(pl.multiple_of((tc * NZ + tz) // 2 * 128, 128), 128)
            act(remote(gsrc.at[:, lanes], gain_o.at[flat], ssend.at[s], srecv.at[s], (tc, tz)))

        exchange_loop(c, z, one)

    gain_sends(lambda cp: cp.start())
    own_lanes = pl.ds(pl.multiple_of(flat // 2 * 128, 128), 128)
    gain_keep = pltpu.make_async_copy(gsrc.at[:, own_lanes], gain_o.at[flat], lsem.at[4])
    gain_keep.start()
    sums.one(0)
    for cp in mlp_z + [keep]:
        cp.wait()
    mlp_c += over_plane(1, mt)
    sums.two(0)

    sums.three(0, o_ref)

    qkv_c = []
    for h in range(2):
        lanes = pl.ds(h * qcols, qcols)
        for cp in qkv_z[3 * h : 3 * h + 3]:
            cp.wait()

        def gathered(j, _):
            total = qkvg[j, z, :, lanes].astype(F32)
            for s in (1, 2, 3):
                total = total + qt[s, j, :, lanes].astype(F32)
            qs[j, :, lanes] = total.astype(BF16)
            return 0

        lax.fori_loop(0, 8, gathered, 0)
        for n, out_ref, lo, wide in ((0, q_o, 0, qcols),) if h == 0 else (
            (1, k_o, qcols, HEAD_SIZE), (2, v_o, qcols + HEAD_SIZE, HEAD_SIZE)
        ):
            dst = out_ref.at[:, pl.ds(pl.multiple_of(c * wide, wide), wide)]
            part = pl.ds(lo, wide)
            qkv_c += [remote(qs.at[m, :, part], dst, q2send.at[n, s], q2recv.at[n, s], (m, z)) for s, m in enumerate(mates)]
            qkv_c.append(pltpu.make_async_copy(qs.at[c, :, part], dst, lsem.at[6 + n]))
        for cp in qkv_c[-8 if h == 0 else -16 :]:
            cp.start()
    sums.end(o_ref)
    for cp in plane.first(g_ref) + plane.second()[0] + plane.second()[1] + [plane.third()]:
        cp.wait_send()
    gain_sends(lambda cp: cp.wait())
    for cp in mlp_c + out_sends + qkv_c + [keep_o, gain_keep]:
        cp.wait()


def attention_back(g, err, q, k, v, attn, cosine, sine, first, place, keys, w_qkv, w_out, gain, normed, gate_g, up_g):
    rows, width = g.shape
    tokens = q.shape[0]
    any_ = pl.BlockSpec(memory_space=pl.ANY)
    vmem = pl.BlockSpec(memory_space=pltpu.VMEM)
    dma, buf, out = pltpu.SemaphoreType.DMA, pltpu.VMEM, jax.ShapeDtypeStruct
    share = width // 32
    cols = w_qkv.shape[1]
    by_owner = gate_g.shape
    ff = by_owner[3]
    return pl.pallas_call(
        back_kernel,
        out_shape=(
            out((rows, width), F32),
            out((share, 32 * ff), BF16),
            out((share, 32 * ff), BF16),
            out((share, 8 * q.shape[1]), BF16),
            out((share, 8 * k.shape[1]), BF16),
            out((share, 8 * v.shape[1]), BF16),
            out((NZ, share, width), BF16),
            out((32, 8, 128), F32),
        ),
        in_specs=[vmem, pl.BlockSpec(memory_space=pltpu.SMEM)] + [any_] * 15,
        out_specs=(vmem,) + (any_,) * 7,
        scratch_shapes=[
            buf(a.shape, a.dtype)
            for a in (q, k, v, attn, cosine, sine, first, place, keys, w_qkv, w_out, gain, normed)
        ] + [
            dma((13,)),
            buf((8, rows, width), BF16), buf(q.shape, BF16), buf((tokens, cols), BF16), buf(k.shape, F32), buf(v.shape, F32),
            buf(w_out.shape, BF16), buf((8, NZ, share, cols), BF16),
            buf(by_owner, BF16), buf((NZ, 8, share, cols), BF16), buf((8, share, cols), BF16), buf((8, width), F32),
            dma((4,)), dma((4,)), dma((2, 4, 7)), dma((2, 4, 7)), dma((2, 4)), dma((2, 4)), dma((2, 4)), dma((3, 7)), dma((3, 7)), dma((4,)), dma((4,)),
            dma((32,)), dma((32,)), dma((9,)), dma((8,)), dma((8,)),
        ] + scatter_scratch(1, rows, width),
        compiler_params=pltpu.CompilerParams(collective_id=6, has_side_effects=True, vmem_limit_bytes=60 << 20),
        cost_estimate=takes(110),
        name="attention_back",
    )(g, err, q, k, v, attn, cosine, sine, first, place, keys, w_qkv, w_out, gain, normed, gate_g, up_g)


class Line:
    def __init__(self, c, z, slot, send, recv):
        self.c, self.z, self.slot, self.send, self.recv = c, z, slot, send, recv
        self.order = plane_order(z)

    def hop(self, up, t):
        zz = self.order[t]
        row = 0 if up else 1
        return remote(
            self.slot(zz), self.slot(zz), self.send.at[row, zz], self.recv.at[zz], (self.c, self.z + (1 if up else -1))
        )

    def hops(self, t, act):
        zz, z = self.order[t], self.z

        @pl.when((zz <= z) & (z < NZ - 1))
        def _():
            act(self.hop(True, t))

        @pl.when((zz >= z) & (z > 0))
        def _():
            act(self.hop(False, t))

    def step(self, t):
        if t > 0:
            self.hop(True, t).wait_recv()
        self.hops(t, lambda cp: cp.start())

    def end(self):
        for t in range(NZ):
            self.hops(t, lambda cp: cp.wait_send())


def front_kernel(
    x_ref, g_ref, mask_ref, wq_ref, wk_ref, wv_ref, wo_ref, wd_ref, wg_ref, cos_in, sin_in, first_in, place_in, keys_in,
    o_ref, go_ref, so_ref, norm_o, wqkv_o, outr_o, downr_o, gate_o, q_o, k_o, v_o, attn_o,
    wqkv, outr, downr, gatew, q_ref, k_ref, v_ref, attn_ref, cos_ref, sin_ref, first_ref, place_ref, keys_ref,
    normed, nall, acc, tmp_o, tmp_d, st_ref, isem, osem, wgsend, wgrecv, ssend, srecv,
    lsem, gsend, grecv, qzsend, qzrecv, ozsend, ozrecv, dsend, drecv, o2send, o2recv, d2send, d2recv, psend, precv, *scat
):
    here = place_on_plane()
    c, z, sib, xn, yn, diag = here
    rows, width = x_ref.shape
    tokens = 8 * rows
    wide = tmp_o.shape[2]
    mates = [lax.rem(c + s, 8) for s in range(1, 8)]
    others = [lax.rem(z + s, NZ) for s in (1, 2, 3)]
    flat, everyone = everyone_else(c, z)
    meet(everyone)
    sums = Scatter(here, [z], *scat)
    plane = Plane(here, lambda j: nall.at[j], psend, precv, rows // 2)
    line_q = Line(c, z, lambda zz: wqkv.at[zz], qzsend, qzrecv)
    line_o = Line(c, z, lambda zz: tmp_o.at[zz], ozsend, ozrecv)
    own_cols = pl.ds(pl.multiple_of(c * wide, wide), wide)

    def narrow(ref, n):
        return ref.at[:, pl.ds(pl.multiple_of(c * n, n), n)]

    q_keeps = [
        pltpu.make_async_copy(narrow(wq_ref, wide), wqkv.at[z, :, pl.ds(0, wide)], lsem.at[0]),
        pltpu.make_async_copy(narrow(wk_ref, HEAD_SIZE), wqkv.at[z, :, pl.ds(wide, HEAD_SIZE)], lsem.at[1]),
        pltpu.make_async_copy(narrow(wv_ref, HEAD_SIZE), wqkv.at[z, :, pl.ds(wide + HEAD_SIZE, HEAD_SIZE)], lsem.at[2]),
    ]
    o_keep = pltpu.make_async_copy(wo_ref.at[:, own_cols], tmp_o.at[z], lsem.at[3])
    d_keeps, downs = [], []
    for core in range(2):
        for hop in range(NZ):
            to = lax.rem(z + hop, NZ)
            src = wd_ref.at[pl.ds(pl.multiple_of((core * NZ + to) * wide, wide), wide), own_cols]
            if hop == 0:
                d_keeps.append(pltpu.make_async_copy(src, tmp_d.at[z, core], lsem.at[4 + core]))
            else:
                downs.append(remote(src, tmp_d.at[z, core], dsend.at[core, hop], drecv.at[core, hop], (c, to)))
    gate_cols = wg_ref.shape[1] // 32
    gates = []
    for hop in range(NZ):
        to = lax.rem(z + hop, NZ)
        src = wg_ref.at[:, pl.ds(pl.multiple_of((c * NZ + to) * gate_cols, gate_cols), gate_cols)]
        if hop == 0:
            g_keep = pltpu.make_async_copy(src, gatew.at[z], lsem.at[9])
        else:
            gates.append(remote(src, gatew.at[z], wgsend.at[hop], wgrecv.at[hop], (c, to)))
    for cp in [o_keep] + q_keeps + d_keeps + [g_keep]:
        cp.start()
    go_ref[z] = g_ref[...]
    gains = [remote(g_ref, go_ref.at[z], gsend.at[s], grecv.at[s], (c, t)) for s, t in enumerate(others)]
    for cp in gains:
        cp.start()
    o_keep.wait()
    line_o.step(0)
    got = fetches(
        [(cos_in, cos_ref), (sin_in, sin_ref), (first_in, first_ref), (place_in, place_ref), (keys_in, keys_ref)], isem
    )
    st_ref[...] = jnp.full(st_ref.shape, jnp.sum(mask_ref[...].astype(F32)), F32)
    so_ref[flat] = st_ref[...]

    def counts(act):
        def one(s, tc, tz):
            act(remote(st_ref, so_ref.at[flat], ssend.at[s], srecv.at[s], (tc, tz)))

        exchange_loop(c, z, one)

    x = x_ref[...].astype(F32)
    scaled = x * lax.rsqrt(jnp.mean(x * x, axis=-1, keepdims=True) + EPS)
    for cp in gains:
        cp.wait()
    piece = width // NZ
    for zz in range(NZ):
        normed[:, zz * piece : (zz + 1) * piece] = (
            scaled[:, zz * piece : (zz + 1) * piece] * go_ref[zz, 0:1, :]
        ).astype(BF16)
    for cp in plane.first(normed):
        cp.start()
    nall[c] = normed[...]
    counts(lambda cp: cp.start())
    line_o.step(1)
    for cp in q_keeps:
        cp.wait()
    line_q.step(0)
    line_o.step(2)
    for arrived, sends in zip(plane.arrive(), plane.second()):
        arrived.wait_recv()
        for cp in sends:
            cp.start()
    line_o.step(3)

    def regroup(buf, dst, send, recv, lrow):
        def block(j):
            return buf(j // 2, lax.rem(j, 2))

        out = [remote(block(m), dst.at[:, own_cols], send.at[s], recv.at[s], (m, z)) for s, m in enumerate(mates)]
        keep = pltpu.make_async_copy(block(c), dst.at[:, own_cols], lsem.at[lrow])
        for cp in out + [keep]:
            cp.start()
        return out + [keep]

    moved_o = regroup(lambda p, core: tmp_o.at[p, pl.ds(pl.multiple_of(core * wide, wide), wide)], outr, o2send, o2recv, 7)
    line_q.step(1)
    for cp in plane.diagonal():
        cp.wait_recv()
    plane.third().start()
    for cp in plane.across():
        cp.wait_recv()
    line_q.step(2)
    norm_keep = pltpu.make_async_copy(nall, norm_o, lsem.at[6])
    norm_keep.start()

    def project(t):
        zz = line_q.order[t]
        at = pl.ds(pl.multiple_of(zz * piece, piece), piece)
        term = jnp.dot(nall[:, :, at].reshape(tokens, piece), wqkv[zz], preferred_element_type=F32)
        acc[...] = term if t == 0 else acc[...] + term

    for t in range(3):
        project(t)
    line_q.step(3)
    for cp in downs:
        cp.start()
    project(3)
    for cp in got:
        cp.wait()

    def heads(i, _):
        at = pl.ds(pl.multiple_of(i * ROWS_AT_ONCE, ROWS_AT_ONCE), ROWS_AT_ONCE)
        cosine, sine = cos_ref[at, :], sin_ref[at, :]
        for h in range(wide // HEAD_SIZE):
            lanes = slice(h * HEAD_SIZE, (h + 1) * HEAD_SIZE)
            q_ref[at, lanes] = turn(acc[at, lanes], cosine, sine).astype(BF16)
        k_ref[at, :] = turn(acc[at, wide : wide + HEAD_SIZE], cosine, sine).astype(BF16)
        v_ref[at, :] = acc[at, wide + HEAD_SIZE :].astype(BF16)
        return 0

    lax.fori_loop(0, tokens // ROWS_AT_ONCE, heads, 0)

    saved = fetches([(wqkv, wqkv_o), (q_ref, q_o), (k_ref, k_o), (v_ref, v_o)], osem)

    def attend(b):
        at = pl.ds(pl.multiple_of(chip_at(c, b) * ROWS_AT_ONCE, ROWS_AT_ONCE), ROWS_AT_ONCE)
        k, v = k_ref[...], v_ref[...]
        first, place, keys = first_ref[at, :], place_ref[at, :], keys_ref[...]
        for h in range(wide // HEAD_SIZE):
            lanes = slice(h * HEAD_SIZE, (h + 1) * HEAD_SIZE)
            probs = block_probs(q_ref[at, lanes], k, first, place, keys)
            attn_ref[at, lanes] = jnp.dot(probs.astype(BF16), v, preferred_element_type=F32).astype(BF16)
        p = jnp.dot(attn_ref[at, :], outr[...], preferred_element_type=F32).astype(BF16)
        sums.part[0, b] = p.reshape(2, rows, width)
        sums.cross(0, b).start()

    for cp in moved_o:
        cp.wait()
    attend(3)
    attend(1)
    sums.one(0)
    attend(2)
    attend(0)
    saved += fetches([(outr, outr_o), (attn_ref, attn_o)], osem.at[pl.ds(4, 2)])
    sums.two(0)
    for cp in d_keeps + downs:
        cp.wait()
    moved_d = regroup(lambda p, core: tmp_d.at[p, core], downr, d2send, d2recv, 8)
    for cp in gates:
        cp.start()
    sums.three(0, o_ref)
    sums.end(o_ref)
    for cp in moved_d:
        cp.wait()
    saved += fetches([(downr, downr_o)], osem.at[pl.ds(6, 1)])
    for cp in gates + [g_keep]:
        cp.wait()
    saved += fetches([(gatew, gate_o)], osem.at[pl.ds(7, 1)])
    for cp in plane.first(normed) + plane.second()[0] + plane.second()[1] + [plane.third()]:
        cp.wait_send()
    line_q.end()
    line_o.end()
    counts(lambda cp: cp.wait())
    for cp in saved + [norm_keep]:
        cp.wait()


def attention_front(x, gains, mask, w_query, w_key, value_weight, w_output, w_down, w_gate, cosine, sine, first, place, keys):
    rows, width = x.shape
    tokens = 8 * rows
    depth = w_query.shape[0]
    wide = width // 8
    any_ = pl.BlockSpec(memory_space=pl.ANY)
    vmem = pl.BlockSpec(memory_space=pltpu.VMEM)
    dma, buf, out = pltpu.SemaphoreType.DMA, pltpu.VMEM, jax.ShapeDtypeStruct
    results = (
        out((NZ, depth, 2 * wide), BF16),
        out((wide, width), BF16),
        out((wide, width), BF16),
        out((NZ, depth, w_gate.shape[1] // 32), BF16),
        out((tokens, wide), BF16),
        out((tokens, HEAD_SIZE), BF16),
        out((tokens, HEAD_SIZE), BF16),
        out((tokens, wide), BF16),
    )
    return pl.pallas_call(
        front_kernel,
        out_shape=(
            out((rows, width), F32), out((NZ,) + gains.shape, F32), out((32, 8, 128), F32), out((8, rows, width), BF16)
        ) + results,
        in_specs=[vmem] * 3 + [any_] * 11,
        out_specs=(vmem,) * 3 + (any_,) * 9,
        scratch_shapes=[buf(r.shape, r.dtype) for r in results]
        + [buf(a.shape, a.dtype) for a in (cosine, sine, first, place, keys)]
        + [
            buf((rows, width), BF16), buf((8, rows, width), BF16), buf((tokens, 2 * wide), F32), buf((NZ, depth, wide), BF16),
            buf((NZ, 2, wide, wide), BF16), buf((8, 128), F32), dma((5,)), dma((8,)), dma((NZ,)), dma((NZ,)),
            dma((32,)), dma((32,)),
            dma((10,)), dma((3,)), dma((3,)), dma((2, 4)), dma((4,)), dma((2, 4)), dma((4,)), dma((2, 4)), dma((2, 4)),
            dma((7,)), dma((7,)), dma((7,)), dma((7,)), dma((8,)), dma((8,)),
        ] + scatter_scratch(1, rows, width),
        compiler_params=pltpu.CompilerParams(collective_id=8, has_side_effects=True, vmem_limit_bytes=60 << 20),
        cost_estimate=takes(95),
        name="attention_front",
    )(x, gains, mask, w_query, w_key, value_weight, w_output, w_down, w_gate, cosine, sine, first, place, keys)


def heads_and_columns(
    hidden_in,
    cotangent,
    teacher,
    valid_mask,
    doc_starts,
    attn_gain,
    w_query,
    w_key,
    value_weight,
    w_output,
    mlp_gain,
    w_gate,
    w_up,
    w_down,
):
    rows, width = hidden_in.shape[1:]
    c = lax.axis_index("ctx")
    z = lax.axis_index("fsdp")
    devices = lax.axis_size("ctx")
    tokens = rows * devices
    group = QUERY_HEADS // KEY_VALUE_HEADS
    qcols = group * HEAD_SIZE
    ffcols = FF // (devices * NZ)

    layer_input = hidden_in[0].astype(F32)
    gains = jnp.concatenate(
        [attn_gain.astype(F32)[None], mlp_gain.astype(F32)[None], jnp.zeros((6, attn_gain.shape[0]), F32)]
    )
    place, segment, offset = stream_places(tokens, rows, devices, doc_starts[0])
    freq = ROPE_BASE ** (-(jnp.arange(HEAD_SIZE // 2, dtype=F32) * 2.0 / HEAD_SIZE))
    angle = offset.astype(F32)[:, None] * freq[None, :]
    cosine = jnp.concatenate([jnp.cos(angle)] * 2, axis=1)
    sine = jnp.concatenate([-jnp.sin(angle), jnp.sin(angle)], axis=1)
    columns = ((place - offset)[:, None], place[:, None], place[None, :])
    branch, gains_all, counts, normed_all, w_qkv, out_rows, down_rows, gate_cols, q, k, v, attn = attention_front(
        hidden_in[0], gains, valid_mask, w_query, w_key, value_weight, w_output, w_down, w_gate, cosine, sine, *columns
    )
    attn_scale = gains_all[:, 0, :].reshape(1, width)
    mlp_scale = gains_all[:, 1, :].reshape(1, width)
    residual = layer_input + branch

    r2 = rms_norm_scale(residual)
    hat2 = residual * r2
    normed2 = (hat2 * mlp_scale).astype(BF16)
    maskf = valid_mask[0].astype(F32)
    mlp_out, normed2_all, gate_up, w_mlp = feed_forward(normed2, gate_cols, w_up, down_rows)
    count = jnp.sum(counts[:, 0, 0])
    outf = residual + mlp_out

    diff = outf - teacher[0].astype(F32)
    error_here = jnp.sum(maskf * jnp.mean(diff * diff, axis=-1))
    g_out = cotangent[0].astype(F32) + maskf[:, None] * diff * (2.0 / (count * width))
    g_norm2, _, gate_grads, up_grads, down_grads = feed_back(g_out.astype(BF16), w_mlp, down_rows, normed2_all, gate_up)

    g_hat2 = g_norm2 * mlp_scale
    g_residual = g_out + r2 * (g_hat2 - hat2 * jnp.mean(g_hat2 * hat2, axis=-1, keepdims=True))
    mlp_gain_term = jnp.sum(g_norm2 * hat2, axis=0, keepdims=True)
    g_norm1, got_gate, got_up, got_q, got_k, got_v, got_out, got_gains = attention_back(
        g_residual.astype(BF16), error_here.reshape(1, 1), q, k, v, attn, cosine, sine, *columns, w_qkv.reshape(width, -1), out_rows, mlp_gain_term,
        normed_all.reshape(tokens, width), gate_grads, up_grads,
    )

    r1 = rms_norm_scale(layer_input)
    hat1 = layer_input * r1
    g_hat1 = g_norm1 * attn_scale
    g_input = g_residual + r1 * (g_hat1 - hat1 * jnp.mean(g_hat1 * hat1, axis=-1, keepdims=True))

    parts = devices * NZ
    share = width // parts
    got_out = jnp.sum(got_out.astype(F32), axis=0)
    flat = c * NZ + z
    got_gains = jnp.sum(got_gains, axis=0)
    loss = got_gains[2, 0] / count
    got_gains = lax.dynamic_slice_in_dim(got_gains, flat % 2 * share, share, axis=1)
    own_scale = lax.dynamic_slice_in_dim(attn_scale[0], flat * share, share)

    return (
        loss,
        outf.astype(BF16)[None],
        g_input.astype(BF16)[None],
        got_gains[0] / own_scale,
        got_q.astype(F32),
        got_k.astype(F32),
        got_v.astype(F32),
        got_out,
        got_gains[1],
        got_gate.astype(F32),
        got_up.astype(F32),
        down_grads,
    )


def solution(mesh):
    small = dict(mesh.shape) == {"ctx": KEY_VALUE_HEADS, "fsdp": NZ}
    in_specs = (
        P("fsdp", "ctx", None),
        P("fsdp", "ctx", None),
        P("fsdp", "ctx", None),
        P("fsdp", "ctx"),
        P("fsdp", None),
        P("fsdp"),
        P("fsdp", None),
        P("fsdp", None),
        P("fsdp", None),
        P("fsdp", None),
        P("fsdp"),
        P("fsdp", None),
        P("fsdp", None),
        P("fsdp", None),
    )
    out_specs = (
        P(),
        P("fsdp", "ctx", None),
        P("fsdp", "ctx", None),
        P(("ctx", "fsdp")),
        P(("ctx", "fsdp"), None),
        P(("ctx", "fsdp"), None),
        P(("ctx", "fsdp"), None),
        P(("ctx", "fsdp"), None),
        P(("ctx", "fsdp")),
        P(("ctx", "fsdp"), None),
        P(("ctx", "fsdp"), None),
        P(("ctx", "fsdp"), None),
    )
    return jax.shard_map(
        heads_and_columns if small else per_device, mesh=mesh, in_specs=in_specs, out_specs=out_specs, check_vma=False
    )
```

```python
import functools

import jax
import jax.numpy as jnp
from jax import lax
from jax.experimental import pallas as pl
from jax.experimental.pallas import tpu as pltpu
from jax.sharding import PartitionSpec as P

QUERY_HEADS = 16
KEY_VALUE_HEADS = 8
HEAD_SIZE = 128
FF = 8192


EPS = 1e-05
ROPE_BASE = 1000000.0
NEG = -1e30
CONTRACT_ROWS = (((0,), (0,)), ((), ()))
CONTRACT_COLS = (((1,), (1,)), ((), ()))


def stream_places(rows, local_token_count, devices, starts):
    span = local_token_count // 2
    rowid = jnp.arange(rows, dtype=jnp.int32)
    device = rowid // local_token_count
    within = rowid % local_token_count
    span_id = jnp.where(within < span, device, 2 * devices - 1 - device)
    place = span_id * span + within % span
    before = starts[None, :] <= place[:, None]
    segment = jnp.sum(before.astype(jnp.int32), axis=1) - 1
    first = jnp.max(jnp.where(before, starts[None, :], 0), axis=1)
    return (place, segment, place - first)


def rotary_embed(values, token_offset, sign):
    half = HEAD_SIZE // 2
    freq = ROPE_BASE ** (-(jnp.arange(half, dtype=jnp.float32) * 2.0 / HEAD_SIZE))
    angle = token_offset.astype(jnp.float32)[:, None] * freq[None, :]
    cosine = jnp.cos(angle)[:, None, :]
    sine = sign * jnp.sin(angle)[:, None, :]
    first = values[..., :half]
    second = values[..., half:]
    return jnp.concatenate(
        [first * cosine - second * sine, second * cosine + first * sine], axis=-1
    )


def rms_norm_scale(values):
    return lax.rsqrt(jnp.mean(values * values, axis=-1, keepdims=True) + EPS)


def head_scores(query_rows, key_rows, allowed):
    attention_scores = jnp.einsum(
        "trd,sd->rts", query_rows, key_rows, preferred_element_type=jnp.float32
    ) * HEAD_SIZE ** (-0.5)
    return jnp.where(allowed[None], attention_scores, NEG)


def per_device(
    hidden_in,
    cotangent,
    teacher,
    valid_mask,
    doc_starts,
    attn_gain,
    w_query,
    w_key,
    value_weight,
    w_output,
    mlp_gain,
    w_gate,
    w_up,
    w_down,
):
    local_token_count = hidden_in.shape[1]
    width = hidden_in.shape[2]
    devices = lax.axis_size("ctx")
    index = lax.axis_index("ctx")
    packed_stream_rows = local_token_count * devices
    query_group = QUERY_HEADS // KEY_VALUE_HEADS
    place, segment, token_offset = stream_places(
        packed_stream_rows, local_token_count, devices, doc_starts[0]
    )
    own_start = index * local_token_count
    my_place = lax.dynamic_slice_in_dim(place, own_start, local_token_count)
    my_segment = lax.dynamic_slice_in_dim(segment, own_start, local_token_count)
    local_stream_offset = lax.dynamic_slice_in_dim(token_offset, own_start, local_token_count)
    allowed = (my_segment[:, None] == segment[None, :]) & (place[None, :] <= my_place[:, None])
    layer_input = hidden_in[0].astype(jnp.float32)
    attn_whole = (
        lax.all_gather(attn_gain, "fsdp", axis=0, tiled=True),
        lax.all_gather(w_query, "fsdp", axis=0, tiled=True),
        lax.all_gather(w_key, "fsdp", axis=0, tiled=True),
        lax.all_gather(value_weight, "fsdp", axis=0, tiled=True),
        lax.all_gather(w_output, "fsdp", axis=0, tiled=True),
    )
    first_norm_scale = attn_whole[0].astype(jnp.float32)
    first_inverse_norm = rms_norm_scale(layer_input)
    first_normalized_input = layer_input * first_inverse_norm
    first_normed = (first_normalized_input * first_norm_scale).astype(jnp.bfloat16)
    qproj = jnp.dot(first_normed, attn_whole[1], preferred_element_type=jnp.float32)
    key_projected = jnp.dot(first_normed, attn_whole[2], preferred_element_type=jnp.float32)
    vproj = jnp.dot(first_normed, attn_whole[3], preferred_element_type=jnp.float32).astype(
        jnp.bfloat16
    )
    query_rows = rotary_embed(
        qproj.reshape(local_token_count, QUERY_HEADS, HEAD_SIZE), local_stream_offset, 1.0
    ).astype(jnp.bfloat16)
    key_rows = (
        rotary_embed(
            key_projected.reshape(local_token_count, KEY_VALUE_HEADS, HEAD_SIZE),
            local_stream_offset,
            1.0,
        )
        .reshape(local_token_count, KEY_VALUE_HEADS * HEAD_SIZE)
        .astype(jnp.bfloat16)
    )
    every_key_row, every_value_row = (
        lax.all_gather(key_rows, "ctx", axis=0, tiled=True),
        lax.all_gather(vproj, "ctx", axis=0, tiled=True),
    )
    key_head_rows = every_key_row.reshape(packed_stream_rows, KEY_VALUE_HEADS, HEAD_SIZE).transpose(
        1, 0, 2
    )
    value_head_rows = every_value_row.reshape(
        packed_stream_rows, KEY_VALUE_HEADS, HEAD_SIZE
    ).transpose(1, 0, 2)
    query_head_rows = query_rows.reshape(
        local_token_count, KEY_VALUE_HEADS, query_group, HEAD_SIZE
    ).transpose(1, 0, 2, 3)

    def attend_head(parts):
        head_query, head_key, head_val = parts
        attention_scores = head_scores(head_query, head_key, allowed)
        top = jnp.max(attention_scores, axis=-1, keepdims=True)
        lse = top + jnp.log(jnp.sum(jnp.exp(attention_scores - top), axis=-1, keepdims=True))
        attention_probabilities = jnp.exp(attention_scores - lse)
        mixed_heads = jnp.einsum(
            "rts,sd->trd",
            attention_probabilities.astype(jnp.bfloat16),
            head_val,
            preferred_element_type=jnp.float32,
        )
        return (mixed_heads, lse)

    mixed_heads, lse = lax.map(attend_head, (query_head_rows, key_head_rows, value_head_rows))
    attn = (
        mixed_heads.transpose(1, 0, 2, 3)
        .reshape(local_token_count, QUERY_HEADS * HEAD_SIZE)
        .astype(jnp.bfloat16)
    )
    residual_state = layer_input + jnp.dot(attn, attn_whole[4], preferred_element_type=jnp.float32)
    mlp_whole = (
        lax.all_gather(mlp_gain, "fsdp", axis=0, tiled=True),
        lax.all_gather(w_gate, "fsdp", axis=0, tiled=True),
        lax.all_gather(w_up, "fsdp", axis=0, tiled=True),
        lax.all_gather(w_down, "fsdp", axis=0, tiled=True),
    )
    second_norm_scale = mlp_whole[0].astype(jnp.float32)
    second_inverse_norm = rms_norm_scale(residual_state)
    second_normalized_input = residual_state * second_inverse_norm
    second_normed = (second_normalized_input * second_norm_scale).astype(jnp.bfloat16)
    gate = jnp.dot(second_normed, mlp_whole[1], preferred_element_type=jnp.float32)
    up_val = jnp.dot(second_normed, mlp_whole[2], preferred_element_type=jnp.float32)
    sigma = jax.nn.sigmoid(gate)
    act = (gate * sigma * up_val).astype(jnp.bfloat16)
    outf = residual_state + jnp.dot(act, mlp_whole[3], preferred_element_type=jnp.float32)
    maskf = valid_mask[0].astype(jnp.float32)
    diff = outf - teacher[0].astype(jnp.float32)
    count_here = jnp.sum(maskf)
    error_here = jnp.sum(maskf * jnp.mean(diff * diff, axis=-1))
    count, error_total = lax.psum((count_here, error_here), ("ctx", "fsdp"))
    loss = error_total / count
    output_gradient = cotangent[0].astype(jnp.float32) + maskf[:, None] * diff * (
        2.0 / (count * width)
    )
    g_mo = output_gradient.astype(jnp.bfloat16)
    mlp_back = (
        lax.all_gather(mlp_gain, "fsdp", axis=0, tiled=True),
        lax.all_gather(w_gate, "fsdp", axis=0, tiled=True),
        lax.all_gather(w_up, "fsdp", axis=0, tiled=True),
        lax.all_gather(w_down, "fsdp", axis=0, tiled=True),
    )
    g_act = lax.dot_general(g_mo, mlp_back[3], CONTRACT_COLS, preferred_element_type=jnp.float32)
    g_gate = (g_act * up_val * sigma * (1.0 + gate * (1.0 - sigma))).astype(jnp.bfloat16)
    g_up = (g_act * gate * sigma).astype(jnp.bfloat16)
    gate_up_gradient = jnp.concatenate([g_gate, g_up], axis=1)
    second_norm_gradient = lax.dot_general(
        g_gate, mlp_back[1], CONTRACT_COLS, preferred_element_type=jnp.float32
    )
    second_norm_gradient = second_norm_gradient + lax.dot_general(
        g_up, mlp_back[2], CONTRACT_COLS, preferred_element_type=jnp.float32
    )
    second_hat_gradient = second_norm_gradient * second_norm_scale
    residual_gradient = output_gradient + second_inverse_norm * (
        second_hat_gradient
        - second_normalized_input
        * jnp.mean(second_hat_gradient * second_normalized_input, axis=-1, keepdims=True)
    )
    mlp_share = lax.psum_scatter(
        lax.dot_general(
            second_normed, gate_up_gradient, CONTRACT_ROWS, preferred_element_type=jnp.float32
        ),
        ("ctx", "fsdp"),
        scatter_dimension=0,
        tiled=True,
    )
    down_share = lax.psum_scatter(
        lax.dot_general(act, g_mo, CONTRACT_ROWS, preferred_element_type=jnp.float32),
        ("ctx", "fsdp"),
        scatter_dimension=0,
        tiled=True,
    )
    g_branch = residual_gradient.astype(jnp.bfloat16)
    attn_back = (
        lax.all_gather(attn_gain, "fsdp", axis=0, tiled=True),
        lax.all_gather(w_query, "fsdp", axis=0, tiled=True),
        lax.all_gather(w_key, "fsdp", axis=0, tiled=True),
        lax.all_gather(value_weight, "fsdp", axis=0, tiled=True),
        lax.all_gather(w_output, "fsdp", axis=0, tiled=True),
    )
    attention_gradient = lax.dot_general(
        g_branch, attn_back[4], CONTRACT_COLS, preferred_element_type=jnp.float32
    ).astype(jnp.bfloat16)
    heads_gradient = attention_gradient.reshape(
        local_token_count, KEY_VALUE_HEADS, query_group, HEAD_SIZE
    ).transpose(1, 0, 2, 3)

    def attend_back(parts):
        head_query, head_key, head_val, head_lse, head_grad = parts
        attention_probabilities = jnp.exp(head_scores(head_query, head_key, allowed) - head_lse)
        g_probs = jnp.einsum("trd,sd->rts", head_grad, head_val, preferred_element_type=jnp.float32)
        delta = jnp.sum(attention_probabilities * g_probs, axis=-1, keepdims=True)
        g_scores = (attention_probabilities * (g_probs - delta)).astype(jnp.bfloat16)
        g_query = jnp.einsum(
            "rts,sd->trd", g_scores, head_key, preferred_element_type=jnp.float32
        ) * HEAD_SIZE ** (-0.5)
        key_gradient = jnp.einsum(
            "rts,trd->sd", g_scores, head_query, preferred_element_type=jnp.float32
        ) * HEAD_SIZE ** (-0.5)
        value_gradient = jnp.einsum(
            "rts,trd->sd",
            attention_probabilities.astype(jnp.bfloat16),
            head_grad,
            preferred_element_type=jnp.float32,
        )
        return (g_query, key_gradient, value_gradient)

    g_query, key_gradient, value_gradient = lax.map(
        attend_back, (query_head_rows, key_head_rows, value_head_rows, lse, heads_gradient)
    )
    key_gradient_terms = key_gradient.transpose(1, 0, 2).reshape(
        packed_stream_rows, KEY_VALUE_HEADS * HEAD_SIZE
    )
    value_gradient_terms = value_gradient.transpose(1, 0, 2).reshape(
        packed_stream_rows, KEY_VALUE_HEADS * HEAD_SIZE
    )
    key_rows_gradient, g_vals = (
        lax.psum_scatter(
            key_gradient_terms.astype(jnp.bfloat16), "ctx", scatter_dimension=0, tiled=True
        ).astype(jnp.float32),
        lax.psum_scatter(
            value_gradient_terms.astype(jnp.bfloat16), "ctx", scatter_dimension=0, tiled=True
        ).astype(jnp.float32),
    )
    g_qproj = (
        rotary_embed(
            g_query.transpose(1, 0, 2, 3).reshape(local_token_count, QUERY_HEADS, HEAD_SIZE),
            local_stream_offset,
            -1.0,
        )
        .reshape(local_token_count, QUERY_HEADS * HEAD_SIZE)
        .astype(jnp.bfloat16)
    )
    g_kproj = (
        rotary_embed(
            key_rows_gradient.reshape(local_token_count, KEY_VALUE_HEADS, HEAD_SIZE),
            local_stream_offset,
            -1.0,
        )
        .reshape(local_token_count, KEY_VALUE_HEADS * HEAD_SIZE)
        .astype(jnp.bfloat16)
    )
    g_vproj = g_vals.astype(jnp.bfloat16)
    first_norm_gradient = lax.dot_general(
        g_qproj, attn_back[1], CONTRACT_COLS, preferred_element_type=jnp.float32
    )
    first_norm_gradient = first_norm_gradient + lax.dot_general(
        g_kproj, attn_back[2], CONTRACT_COLS, preferred_element_type=jnp.float32
    )
    first_norm_gradient = first_norm_gradient + lax.dot_general(
        g_vproj, attn_back[3], CONTRACT_COLS, preferred_element_type=jnp.float32
    )
    first_hat_gradient = first_norm_gradient * first_norm_scale
    g_input = residual_gradient + first_inverse_norm * (
        first_hat_gradient
        - first_normalized_input
        * jnp.mean(first_hat_gradient * first_normalized_input, axis=-1, keepdims=True)
    )
    key_value_proj_gradient = jnp.concatenate([g_kproj, g_vproj], axis=1)
    query_term = lax.dot_general(
        first_normed, g_qproj, CONTRACT_ROWS, preferred_element_type=jnp.float32
    )
    key_value_term = lax.dot_general(
        first_normed, key_value_proj_gradient, CONTRACT_ROWS, preferred_element_type=jnp.float32
    )
    output_term = lax.dot_general(attn, g_branch, CONTRACT_ROWS, preferred_element_type=jnp.float32)
    scale_gradient_terms = jnp.stack(
        [
            jnp.sum(first_norm_gradient * first_normalized_input, axis=0),
            jnp.sum(second_norm_gradient * second_normalized_input, axis=0),
        ]
    )
    query_share, key_value_share, output_share, gain_share = (
        lax.psum_scatter(query_term, ("ctx", "fsdp"), scatter_dimension=0, tiled=True),
        lax.psum_scatter(key_value_term, ("ctx", "fsdp"), scatter_dimension=0, tiled=True),
        lax.psum_scatter(output_term, ("ctx", "fsdp"), scatter_dimension=0, tiled=True),
        lax.psum_scatter(scale_gradient_terms, ("ctx", "fsdp"), scatter_dimension=1, tiled=True),
    )
    key_value_columns = KEY_VALUE_HEADS * HEAD_SIZE
    return (
        loss,
        outf.astype(jnp.bfloat16)[None],
        g_input.astype(jnp.bfloat16)[None],
        gain_share[0],
        query_share,
        key_value_share[:, :key_value_columns],
        key_value_share[:, key_value_columns:],
        output_share,
        gain_share[1],
        mlp_share[:, :FF],
        mlp_share[:, FF:],
        down_share,
    )


MESH = pl.DeviceIdType.MESH
F32 = jnp.float32
BF16 = jnp.bfloat16
NZ = 4


def place_on_plane():
    c = lax.axis_index("ctx")
    z = lax.axis_index("fsdp")
    sib = c + 1 - 2 * lax.rem(c, 2)
    xn = c + 2 - 4 * lax.rem(c // 2, 2)
    yn = c + 4 - 8 * (c // 4)
    diag = xn + yn - c
    return c, z, sib, xn, yn, diag


def meet(devices):
    barrier = pltpu.get_barrier_semaphore()
    for d in devices:
        pl.semaphore_signal(barrier, inc=1, device_id=d, device_id_type=MESH)
    pl.semaphore_wait(barrier, len(devices))


def remote(src, dst, send, recv, device):
    return pltpu.make_async_remote_copy(
        src_ref=src, dst_ref=dst, send_sem=send, recv_sem=recv, device_id=device, device_id_type=MESH
    )


def takes(micros):
    return pl.CostEstimate(flops=0, bytes_accessed=micros * 3_500_000, transcendentals=0)


class Plane:
    def __init__(self, here, slot, send, recv, half):
        self.c, self.z, self.sib, self.xn, self.yn, self.diag = here
        self.slot, self.send, self.recv, self.half = slot, send, recv, half

    def copy(self, kind, src, dst, to):
        return remote(src, dst, self.send.at[kind], self.recv.at[kind], (to, self.z))

    def first(self, src):
        mine = self.slot(self.c)
        return [self.copy(0, src, mine, self.xn), self.copy(1, src, mine, self.yn), self.copy(2, src, mine, self.sib)]

    def arrive(self):
        s = self.slot
        return [self.copy(0, s(self.xn), s(self.xn), self.xn), self.copy(1, s(self.yn), s(self.yn), self.yn)]

    def second(self):
        h = self.half
        s = self.slot
        ybot = s(self.yn).at[pl.ds(0, h)]
        xtop = s(self.xn).at[pl.ds(h, h)]
        return (
            [self.copy(4, xtop, xtop, self.yn), self.copy(5, s(self.xn), s(self.xn), self.sib)],
            [self.copy(3, ybot, ybot, self.xn), self.copy(6, s(self.yn), s(self.yn), self.sib)],
        )

    def diagonal(self):
        h = self.half
        lo, hi = self.slot(self.diag).at[pl.ds(0, h)], self.slot(self.diag).at[pl.ds(h, h)]
        return [self.copy(3, lo, lo, self.xn), self.copy(4, hi, hi, self.yn)]

    def third(self):
        d = self.slot(self.diag)
        return self.copy(7, d, d, self.sib)

    def across(self):
        s = self.slot
        return [self.copy(k, s(j), s(j), self.sib) for k, j in ((2, self.sib), (5, self.xn + self.sib - self.c), (6, self.yn + self.sib - self.c), (7, self.diag + self.sib - self.c))]


def add_rows(dst, parts, chunk=16):
    n = dst.shape[0] // chunk

    def body(i, _):
        at = pl.ds(pl.multiple_of(i * chunk, chunk), chunk)
        total = parts[0][at, :].astype(F32)
        for p in parts[1:]:
            total = total + p[at, :].astype(F32)
        dst[at, :] = total.astype(dst.dtype)
        return 0

    lax.fori_loop(0, n, body, 0)


def plane_order(z):
    pick = jnp.where
    return [z, pick(z == 0, 1, z - 1), pick(z == 3, 1, pick(z == 2, 3, 2)), pick(z < 2, 3, 0)]


def chip_at(c, b):
    x, y = lax.rem(c // 2, 2), c // 4
    xb, yb = lax.rem(b, 2), b // 2
    return (x + xb - 2 * x * xb) + 2 * (y + yb - 2 * y * yb)


def chunk_order(i):
    return jnp.where(i == 0, 3, jnp.where(i == 3, 0, i))


class Gather:
    def __init__(self, here, x_ref, o_ref, keep, zsend, zrecv, send, recv):
        self.here, self.x, self.o = here, x_ref, o_ref
        self.c, self.z = here[0], here[1]
        self.order = plane_order(self.z)
        self.zsend, self.zrecv = zsend, zrecv
        self.planes = [
            Plane(here, functools.partial(lambda zz, j: o_ref.at[zz, j], zz), send.at[zz], recv.at[zz], x_ref.shape[0] // 2)
            for zz in self.order
        ]
        self.keep = pltpu.make_async_copy(x_ref, o_ref.at[self.z, self.c], keep)

    def hop(self, up, t):
        zz = self.order[t]
        src = self.x if t == 0 else self.o.at[zz, self.c]
        row = 0 if up else 1
        return remote(
            src, self.o.at[zz, self.c], self.zsend.at[row, zz], self.zrecv.at[zz], (self.c, self.z + (1 if up else -1))
        )

    def hops(self, t, act):
        zz, z = self.order[t], self.z

        @pl.when((zz <= z) & (z < NZ - 1))
        def _():
            act(self.hop(True, t))

        @pl.when((zz >= z) & (z > 0))
        def _():
            act(self.hop(False, t))

    def spread(self, t):
        if t > 0:
            self.hop(True, t).wait_recv()
        self.hops(t, lambda cp: cp.start())
        for cp in self.planes[t].first(self.source(t)):
            cp.start()

    def source(self, t):
        return self.x if t == 0 else self.o.at[self.order[t], self.c]

    def onward(self, t):
        p = self.planes[t]
        for arrived, sends in zip(p.arrive(), p.second()):
            arrived.wait_recv()
            for cp in sends:
                cp.start()

    def close(self, t):
        p = self.planes[t]
        for cp in p.diagonal():
            cp.wait_recv()
        p.third().start()
        for cp in p.across():
            cp.wait_recv()
        if t == 0:
            self.keep.wait()

    def end(self):
        for t, p in enumerate(self.planes):
            for cp in p.first(self.source(t)) + p.second()[0] + p.second()[1] + [p.third()]:
                cp.wait_send()
            self.hops(t, lambda cp: cp.wait_send())


class Scatter:
    def __init__(self, here, order, part, sibr, xh, yh, xf, yf, zr, bsend, brecv, hsend, hrecv, fsend, frecv, zsend, zrecv):
        self.c, self.z, self.sib, self.xn, self.yn, self.diag = here
        self.k = lax.rem(self.c, 2)
        self.order = order
        self.part, self.sibr, self.xh, self.yh, self.xf, self.yf, self.zr = part, sibr, xh, yh, xf, yf, zr
        self.sems = (bsend, brecv, hsend, hrecv, fsend, frecv, zsend, zrecv)
        self.h = part.shape[3] // 2

    def mine(self, t, b):
        return self.part.at[t, b, self.k]

    def cross(self, t, b):
        send, recv = self.sems[0:2]
        return remote(self.part.at[t, b, 1 - self.k], self.sibr.at[t, b], send.at[t, b], recv.at[t, b], (self.sib, self.z))

    def halves(self, t):
        send, recv = self.sems[2:4]
        src = self.mine(t, 3)
        return (
            remote(src.at[pl.ds(0, self.h)], self.xh.at[t], send.at[t, 0], recv.at[t, 0], (self.xn, self.z)),
            remote(src.at[pl.ds(self.h, self.h)], self.yh.at[t], send.at[t, 1], recv.at[t, 1], (self.yn, self.z)),
        )

    def fulls(self, t):
        send, recv = self.sems[4:6]
        return (
            remote(self.mine(t, 1), self.xf.at[t], send.at[t, 0], recv.at[t, 0], (self.xn, self.z)),
            remote(self.mine(t, 2), self.yf.at[t], send.at[t, 1], recv.at[t, 1], (self.yn, self.z)),
        )

    def hop(self, t):
        send, recv = self.sems[6:8]
        return remote(self.mine(t, 0), self.zr.at[self.z], send.at[t], recv.at[self.z], (self.c, self.order[t]))

    def came(self, t):
        send, recv = self.sems[6:8]
        zz = self.order[t]
        return remote(self.zr.at[zz], self.zr.at[zz], send.at[t], recv.at[zz], (self.c, zz))

    def one(self, t):
        self.cross(t, 3).wait_recv()
        add_rows(self.mine(t, 3), [self.mine(t, 3), self.sibr.at[t, 3]])
        for cp in self.halves(t):
            cp.start()

    def two(self, t):
        h = self.h
        top, low = pl.ds(0, h), pl.ds(h, h)
        hx, hy = self.halves(t)
        fx, fy = self.fulls(t)
        self.cross(t, 1).wait_recv()
        m, s = self.mine(t, 1), self.sibr.at[t, 1]
        add_rows(m.at[top], [m.at[top], s.at[top]])
        hy.wait_recv()
        add_rows(m.at[low], [m.at[low], s.at[low], self.yh.at[t]])
        fx.start()
        self.cross(t, 2).wait_recv()
        m, s = self.mine(t, 2), self.sibr.at[t, 2]
        add_rows(m.at[low], [m.at[low], s.at[low]])
        hx.wait_recv()
        add_rows(m.at[top], [m.at[top], s.at[top], self.xh.at[t]])
        fy.start()

    def three(self, t, o_ref):
        self.cross(t, 0).wait_recv()
        for cp in self.fulls(t):
            cp.wait_recv()
        parts = [self.mine(t, 0), self.sibr.at[t, 0], self.xf.at[t], self.yf.at[t]]
        if t == 0:
            add_rows(o_ref, parts)
        else:
            add_rows(self.mine(t, 0), parts)
            self.hop(t).start()

    def end(self, o_ref):
        n = len(self.order)
        for t in range(1, n):
            self.came(t).wait_recv()
        if n > 1:
            add_rows(o_ref, [o_ref] + [self.zr.at[self.order[t]] for t in range(1, n)])
        for t in range(n):
            for b in range(4):
                self.cross(t, b).wait_send()
            for cp in self.halves(t) + self.fulls(t):
                cp.wait_send()
            if t > 0:
                self.hop(t).wait_send()


def scatter_scratch(n, rows, width):
    v, dma = pltpu.VMEM, pltpu.SemaphoreType.DMA
    return [
        v((n, 4, 2, rows, width), BF16), v((n, 4, rows, width), BF16),
        v((n, rows // 2, width), BF16), v((n, rows // 2, width), BF16),
        v((n, rows, width), BF16), v((n, rows, width), BF16), v((NZ, rows, width), BF16),
        dma((n, 4)), dma((n, 4)), dma((n, 2)), dma((n, 2)), dma((n, 2)), dma((n, 2)), dma((NZ,)), dma((NZ,)),
    ]


def neighbours(here):
    c, z, sib, xn, yn, diag = here
    return [(sib, z), (xn, z), (yn, z)] + [(c, lax.rem(z + s, NZ)) for s in (1, 2, 3)]


def everyone_else(c, z):
    flat = c * NZ + z
    others = [lax.rem(flat + s, 32) for s in range(1, 32)]
    return flat, [(o // NZ, lax.rem(o, NZ)) for o in others]


def feed_kernel(
    x_ref, gate_in, wu_ref, d_in, o_ref, all_ref, gu_ref, w_out,
    w_ref, d_ref, xs, gs, xsem, gsem, wsend, wrecv, wkeep, keep, zsend, zrecv, send, recv, *scat
):
    here = place_on_plane()
    c, z = here[0], here[1]
    meet(neighbours(here))
    gather_ = Gather(here, x_ref, all_ref, keep.at[0], zsend, zrecv, send, recv)
    order = gather_.order
    sums = Scatter(here, order, *scat)
    ff = d_ref.shape[0]
    gather_.keep.start()
    gather_.spread(0)

    def load(t, b):
        src = all_ref.at[order[t], pl.ds(2 * chip_at(c, b), 2)]
        return pltpu.make_async_copy(src, xs.at[b], xsem.at[b])

    def store(t, b):
        return pltpu.make_async_copy(gs.at[b], gu_ref.at[order[t], chip_at(c, b)], gsem.at[b])

    def work(t, lo, hi):
        for b in (3, 1, 2, 0)[lo:hi]:
            load(t, b).start()

        def body(i, _):
            b = chunk_order(i)
            load(t, b).wait()
            if t != 1:
                store(1, b).wait()
            x = xs[b].reshape(-1, xs.shape[-1])
            gu = jnp.dot(x, w_ref[...].reshape(x.shape[1], -1), preferred_element_type=F32)
            gs[b] = gu
            store(t, b).start()
            gate, up = gu[:, :ff], gu[:, ff:]
            act = (gate * jax.nn.sigmoid(gate) * up).astype(BF16)
            p = jnp.dot(act, d_ref[...], preferred_element_type=F32).astype(BF16)
            sums.part[t, b] = p.reshape(sums.part.shape[2:])
            sums.cross(t, b).start()
            return 0

        lax.fori_loop(lo, hi, body, 0)

    weights = []
    keeps = [pltpu.make_async_copy(d_in, d_ref, wkeep.at[0])]
    keeps.append(pltpu.make_async_copy(gate_in, w_ref.at[:, :, pl.ds(0, ff)], wkeep.at[1]))
    for hop in range(NZ):
        to = lax.rem(z + hop, NZ)
        src = wu_ref.at[:, pl.ds(pl.multiple_of((c * NZ + to) * ff, ff), ff)]
        dst = w_ref.at[z, :, pl.ds(ff, ff)]
        if hop == 0:
            keeps.append(pltpu.make_async_copy(src, dst, wkeep.at[2]))
        else:
            weights.append(remote(src, dst, wsend.at[hop], wrecv.at[hop], (c, to)))
    w_keep = pltpu.make_async_copy(w_ref, w_out, wkeep.at[3])

    def early():
        for cp in keeps + weights:
            cp.start()

    def ready():
        for cp in keeps + weights:
            cp.wait()
        w_keep.start()

    fused_steps(gather_, sums, work, o_ref, False, early=early, ready=ready)
    for b in range(4):
        store(0, b).wait()
    w_keep.wait()


def fused_steps(gather_, sums, work, o_ref, own_first, more=lambda t: None, early=lambda: None, ready=lambda: None):
    gather_.spread(1)
    gather_.onward(0)
    gather_.spread(2)
    early()
    if own_first:
        ready()
        gather_.close(0)
        work(0, 0, 2)
    gather_.onward(1)
    if own_first:
        work(0, 2, 4)
    gather_.spread(3)
    if own_first:
        more(0)
    gather_.onward(2)
    if not own_first:
        ready()
    gather_.close(1)
    work(1, 0, 4)
    gather_.onward(3)
    if not own_first:
        sums.one(1)
    more(1)
    gather_.close(2)
    work(2, 0, 2)
    sums.one(2)
    work(2, 2, 4)
    sums.two(2)
    more(2)
    gather_.close(3)
    work(3, 0, 2)
    sums.one(3)
    work(3, 2, 4)
    sums.three(2, o_ref)
    sums.two(3)
    more(3)
    if own_first:
        sums.one(1)
    else:
        gather_.close(0)
        work(0, 0, 4)
    sums.three(3, o_ref)
    if own_first:
        sums.two(1)
        sums.one(0)
    else:
        sums.one(0)
        more(0)
        sums.two(1)
    sums.three(1, o_ref)
    sums.two(0)
    sums.three(0, o_ref)
    sums.end(o_ref)
    gather_.end()


def gather_sems():
    dma = pltpu.SemaphoreType.DMA
    return [dma((1,)), dma((2, 4)), dma((4,)), dma((4, 8)), dma((4, 8))]


def feed_forward(x, gate, w_up, d):
    rows, width = x.shape
    depth, cols = w_up.shape[0], 2 * d.shape[0]
    any_ = pl.BlockSpec(memory_space=pl.ANY)
    vmem = pl.BlockSpec(memory_space=pltpu.VMEM)
    dma = pltpu.SemaphoreType.DMA
    return pl.pallas_call(
        feed_kernel,
        out_shape=(
            jax.ShapeDtypeStruct((rows, width), F32),
            jax.ShapeDtypeStruct((NZ, 8, rows, width), BF16),
            jax.ShapeDtypeStruct((NZ, 4, 2 * rows, cols), F32),
            jax.ShapeDtypeStruct((NZ, depth, cols), BF16),
        ),
        in_specs=[vmem, any_, any_, any_],
        out_specs=(vmem, any_, any_, any_),
        scratch_shapes=[
            pltpu.VMEM((NZ, depth, cols), BF16), pltpu.VMEM(d.shape, BF16),
            pltpu.VMEM((4, 2, rows, width), BF16), pltpu.VMEM((4, 2 * rows, cols), F32), dma((4,)), dma((4,)),
            dma((4,)), dma((4,)), dma((4,)),
        ] + gather_sems() + scatter_scratch(NZ, rows, width),
        compiler_params=pltpu.CompilerParams(collective_id=5, has_side_effects=True, vmem_limit_bytes=60 << 20),
        cost_estimate=takes(180),
        name="feed_forward",
    )(x, gate, w_up, d)


def feed_back_kernel(
    x_ref, w_in, d_in, n_ref, gu_ref, o_ref, all_ref, gate_out, up_out, down_out,
    w_ref, d_ref, gate_o, up_o, down_o, wsem, gsend, grecv, xs, ns, gs, gg, acts, total, xsem, nsem, gsem, keep, zsend, zrecv, send, recv, *scat
):
    here = place_on_plane()
    c, z = here[0], here[1]
    meet(neighbours(here))
    gather_ = Gather(here, x_ref, all_ref, keep.at[0], zsend, zrecv, send, recv)
    order = gather_.order
    sums = Scatter(here, order, *scat)
    ff = d_ref.shape[0]
    tokens = 8 * x_ref.shape[0]
    gather_.keep.start()
    gather_.spread(0)

    def loads(t, b):
        chip = chip_at(c, b)
        pair = pl.ds(2 * chip, 2)
        return (
            pltpu.make_async_copy(gu_ref.at[order[t], chip], gs.at[b], gsem.at[b]),
            pltpu.make_async_copy(all_ref.at[order[t], pair], xs.at[b], xsem.at[b]),
            pltpu.make_async_copy(n_ref.at[order[t], pair], ns.at[b], nsem.at[b]),
        )

    def work(t, lo, hi):
        for b in (3, 1, 2, 0)[lo:hi]:
            for cp in loads(t, b):
                cp.start()

        def body(i, _):
            b = chunk_order(i)
            stored, tokens_in, _ = loads(t, b)
            stored.wait()
            tokens_in.wait()
            g = xs[b].reshape(-1, xs.shape[-1])
            g_act = lax.dot_general(g, d_ref[...], CONTRACT_COLS, preferred_element_type=F32)
            gate, up = gs[b, :, :ff], gs[b, :, ff:]
            sg = jax.nn.sigmoid(gate)
            acts[b] = (gate * sg * up).astype(BF16)
            gg[b, :, :ff] = (g_act * up * sg * (1.0 + gate * (1.0 - sg))).astype(BF16)
            gg[b, :, ff:] = (g_act * gate * sg).astype(BF16)
            p = lax.dot_general(gg[b], w_ref[...].reshape(o_ref.shape[1], -1), CONTRACT_COLS, preferred_element_type=F32).astype(BF16)
            sums.part[t, b] = p.reshape(sums.part.shape[2:])
            sums.cross(t, b).start()
            return 0

        lax.fori_loop(lo, hi, body, 0)

    piece = 512

    def more(t):
        for b in range(4):
            loads(t, b)[2].wait()

        def body(i, _):
            at = pl.ds(pl.multiple_of(i * piece, piece), piece)
            n = ns[:, :, :, at].reshape(tokens, piece)
            w_term = lax.dot_general(n, gg[...].reshape(tokens, -1), CONTRACT_ROWS, preferred_element_type=F32)
            g = xs[:, :, :, at].reshape(tokens, piece)
            d_term = lax.dot_general(acts[...].reshape(tokens, -1), g, CONTRACT_ROWS, preferred_element_type=F32)
            if t > 0:
                w_term = w_term + total[at, :]
                d_term = d_term + down_o[:, at]
            down_o[:, at] = d_term
            if t < NZ - 1:
                total[at, :] = w_term
            else:
                pair = pl.ds(2 * i, 2)
                gate_o[pair] = w_term[:, :ff].astype(BF16).reshape((2,) + gate_o.shape[1:])
                up_o[pair] = w_term[:, ff:].astype(BF16).reshape((2,) + up_o.shape[1:])
            return 0

        lax.fori_loop(0, o_ref.shape[1] // piece, body, 0)

    keeps = [pltpu.make_async_copy(w_in, w_ref, wsem.at[0]), pltpu.make_async_copy(d_in, d_ref, wsem.at[1])]
    saved = [
        pltpu.make_async_copy(src, dst, wsem.at[2 + i])
        for i, (src, dst) in enumerate(((gate_o.at[:, z], gate_out.at[:, z]), (up_o, up_out), (down_o, down_out)))
    ]
    gate_z = []
    for s in (1, 2, 3):
        to = lax.rem(z + s, NZ)
        gate_z.append(remote(gate_o.at[:, to], gate_out.at[:, z], gsend.at[s], grecv.at[s], (c, to)))

    def early():
        for cp in keeps:
            cp.start()

    def ready():
        for cp in keeps:
            cp.wait()

    def more_and_save(t):
        more(t)
        if t == NZ - 1:
            for cp in gate_z + saved:
                cp.start()

    fused_steps(gather_, sums, work, o_ref, True, more_and_save, early, ready)
    for cp in saved + gate_z:
        cp.wait()


def feed_back(x, w, d, normed, gate_up):
    rows, width = x.shape
    cols = w.shape[2]
    ff = d.shape[0]
    by_owner = (8, NZ, width // 32, ff)
    any_ = pl.BlockSpec(memory_space=pl.ANY)
    vmem = pl.BlockSpec(memory_space=pltpu.VMEM)
    dma, buf = pltpu.SemaphoreType.DMA, pltpu.VMEM
    return pl.pallas_call(
        feed_back_kernel,
        out_shape=(
            jax.ShapeDtypeStruct((rows, width), F32),
            jax.ShapeDtypeStruct((NZ, 8, rows, width), BF16),
            jax.ShapeDtypeStruct(by_owner, BF16),
            jax.ShapeDtypeStruct(by_owner, BF16),
            jax.ShapeDtypeStruct((ff, width), F32),
        ),
        in_specs=[vmem] + [any_] * 4,
        out_specs=(vmem,) + (any_,) * 4,
        scratch_shapes=[
            buf(w.shape, BF16), buf(d.shape, BF16), buf(by_owner, BF16), buf(by_owner, BF16), buf((ff, width), F32),
            dma((5,)), dma((4,)), dma((4,)), buf((4, 2, rows, width), BF16), buf((4, 2, rows, width), BF16), buf((4, 2 * rows, cols), F32),
            buf((4, 2 * rows, cols), BF16), buf((4, 2 * rows, ff), BF16), buf((width, cols), F32),
            dma((4,)), dma((4,)), dma((4,)),
        ] + gather_sems() + scatter_scratch(NZ, rows, width),
        compiler_params=pltpu.CompilerParams(collective_id=7, has_side_effects=True, vmem_limit_bytes=63 << 20),
        cost_estimate=takes(180),
        name="feed_back",
    )(x, w, d, normed, gate_up)


ROWS_AT_ONCE = 256


def turn(u, cosine, sine):
    return u * cosine + pltpu.roll(u, HEAD_SIZE // 2, 1) * sine


def block_probs(q, k, first, place, keys_place):
    scores = lax.dot_general(q, k, CONTRACT_COLS, preferred_element_type=F32) * HEAD_SIZE ** (-0.5)
    allowed = (keys_place >= first) & (keys_place <= place)
    scores = jnp.where(allowed, scores, NEG)
    raised = jnp.exp(scores - jnp.max(scores, axis=-1, keepdims=True))
    return raised / jnp.sum(raised, axis=-1, keepdims=True)


def fetches(pairs, sems):
    copies = [pltpu.make_async_copy(src, dst, sems.at[i]) for i, (src, dst) in enumerate(pairs)]
    for cp in copies:
        cp.start()
    return copies


def exchange_loop(c, z, act):
    flat = c * NZ + z

    def body(s, _):
        to = lax.rem(flat + s, 32)
        act(s, to // NZ, lax.rem(to, NZ))
        return 0

    lax.fori_loop(1, 32, body, 0)


def back_kernel(
    g_ref, err_ref, q_in, k_in, v_in, attn_in, cos_in, sin_in, first_in, place_in, keys_in, wqkv_in, wout_in, gain_in,
    norm_in, gate_ref, up_ref,
    o_ref, gate_o, up_o, q_o, k_o, v_o, out_o, gain_o,
    q_ref, k_ref, v_ref, attn_ref, cos_ref, sin_ref, first_ref, place_ref, keys_ref, wqkv_ref, wout_ref, gain_ref, normed, isem,
    gb, ga, gqkv, gk, gv, outg, qkvg, mt, qt, qs, gsrc,
    msend, mrecv, m2send, m2recv, m2keep, qsend, qrecv, q2send, q2recv, osend, orecv, ssend, srecv, lsem, psend, precv, *scat
):
    here = place_on_plane()
    c, z, sib, xn, yn, diag = here
    flat, everyone = everyone_else(c, z)
    meet(everyone)
    rows, width = g_ref.shape
    tokens = 8 * rows
    share = width // 32
    plane = Plane(here, lambda j: gb.at[j], psend, precv, rows // 2)
    sums = Scatter(here, [z], *scat)
    mates = [lax.rem(c + s, 8) for s in range(1, 8)]
    others = [(s, lax.rem(z + s, NZ)) for s in (1, 2, 3)]
    for cp in plane.first(g_ref):
        cp.start()

    mlp_z = [remote(up_ref.at[:, to], mt.at[:, z], msend.at[s], mrecv.at[s], (c, to)) for s, to in others]
    keep = pltpu.make_async_copy(up_ref.at[:, z], mt.at[:, z], lsem.at[1])
    for cp in mlp_z + [keep]:
        cp.start()
    ff = gate_ref.shape[3]

    def over_plane(i, ref):
        out = []
        for zz in range(NZ):
            dst = (gate_o, up_o)[i].at[:, pl.ds(pl.multiple_of((c * NZ + zz) * ff, ff), ff)]
            for s, m in enumerate(mates):
                out.append(remote(ref.at[m, zz], dst, m2send.at[i, zz, s], m2recv.at[i, zz, s], (m, z)))
            out.append(pltpu.make_async_copy(ref.at[c, zz], dst, m2keep.at[i, zz]))
        for cp in out:
            cp.start()
        return out

    got = fetches(
        [
            (wout_in, wout_ref), (q_in, q_ref), (k_in, k_ref), (v_in, v_ref), (cos_in, cos_ref), (sin_in, sin_ref),
            (first_in, first_ref), (place_in, place_ref), (keys_in, keys_ref),
            (attn_in, attn_ref), (norm_in, normed), (wqkv_in, wqkv_ref), (gain_in, gain_ref),
        ],
        isem,
    )
    gb[c] = g_ref[...]
    gk[...] = jnp.zeros_like(gk)
    gv[...] = jnp.zeros_like(gv)

    def attend(b):
        chip = chip_at(c, b)
        at = pl.ds(pl.multiple_of(chip * ROWS_AT_ONCE, ROWS_AT_ONCE), ROWS_AT_ONCE)
        g_rows = gb[pl.ds(chip * 2, 2)].reshape(ROWS_AT_ONCE, width)
        ga[at, :] = lax.dot_general(g_rows, wout_ref[...], CONTRACT_COLS, preferred_element_type=F32).astype(BF16)
        k, v = k_ref[...], v_ref[...]
        cosine, sine = cos_ref[at, :], sin_ref[at, :]
        first, place, keys = first_ref[at, :], place_ref[at, :], keys_ref[...]
        for h in range(QUERY_HEADS // KEY_VALUE_HEADS):
            lanes = slice(h * HEAD_SIZE, (h + 1) * HEAD_SIZE)
            q, g = q_ref[at, lanes], ga[at, lanes]
            probs = block_probs(q, k, first, place, keys)
            g_probs = lax.dot_general(g, v, CONTRACT_COLS, preferred_element_type=F32)
            delta = jnp.sum(probs * g_probs, axis=-1, keepdims=True)
            g_scores = (probs * (g_probs - delta)).astype(BF16)
            g_q = jnp.dot(g_scores, k, preferred_element_type=F32) * HEAD_SIZE ** (-0.5)
            gqkv[at, lanes] = turn(g_q, cosine, -sine).astype(BF16)
            gk[...] += lax.dot_general(g_scores, q, CONTRACT_ROWS, preferred_element_type=F32)
            gv[...] += lax.dot_general(probs.astype(BF16), g, CONTRACT_ROWS, preferred_element_type=F32)

    came = plane.across()
    for cp in got[:9]:
        cp.wait()
    came[0].wait_recv()
    attend(0)
    for arrived, sends in zip(plane.arrive(), plane.second()):
        arrived.wait_recv()
        for cp in sends:
            cp.start()
    came[1].wait_recv()
    attend(1)
    for cp in plane.diagonal():
        cp.wait_recv()
    plane.third().start()
    came[2].wait_recv()
    attend(2)
    came[3].wait_recv()
    mlp_c = over_plane(0, gate_ref)
    got[9].wait()
    piece = 512

    def outs(i, _):
        at = pl.ds(pl.multiple_of(i * piece, piece), piece)
        g = gb[:, :, at].reshape(tokens, piece)
        outg[:, at] = lax.dot_general(attn_ref[...], g, CONTRACT_ROWS, preferred_element_type=F32).astype(BF16)
        return 0

    lax.fori_loop(0, width // piece, outs, 0)
    out_sends = []
    for s, to in others:
        src = outg.at[pl.ds(pl.multiple_of(to * share, share), share)]
        out_sends.append(remote(src, out_o.at[z], osend.at[s], orecv.at[s], (c, to)))
    for cp in out_sends:
        cp.start()
    keep_o = pltpu.make_async_copy(outg.at[pl.ds(pl.multiple_of(z * share, share), share)], out_o.at[z], lsem.at[5])
    keep_o.start()
    attend(3)
    qcols = q_ref.shape[1]
    g_k = gk[...] * HEAD_SIZE ** (-0.5)
    gqkv[:, qcols : qcols + HEAD_SIZE] = turn(g_k, cos_ref[...], -sin_ref[...]).astype(BF16)
    gqkv[:, qcols + HEAD_SIZE :] = gv[...].astype(BF16)

    for cp in got[10:]:
        cp.wait()
    cols = gqkv.shape[1]

    def project(i, _):
        at = pl.ds(pl.multiple_of(i * piece, piece), piece)
        term = lax.dot_general(normed[:, at], gqkv[...], CONTRACT_ROWS, preferred_element_type=F32).astype(BF16)
        qkvg[pl.ds(2 * i, 2)] = term.reshape(2, NZ, share, cols)
        return 0

    lax.fori_loop(0, width // piece, project, 0)
    qkv_z = []
    for h in range(2):
        lanes = pl.ds(h * qcols, qcols)
        for s, to in others:
            src, dst = qkvg.at[:, to, :, lanes], qt.at[s, :, :, lanes]
            qkv_z.append(remote(src, dst, qsend.at[h, s], qrecv.at[h, s], (c, to)))
            qkv_z[-1].start()

    gsrc[...] = jnp.zeros_like(gsrc)
    gsrc[1:2, :] = gain_ref[...]
    gsrc[2:3, :] = jnp.full((1, width), err_ref[0, 0], F32)
    for b in (3, 1, 2, 0):
        chip = chip_at(c, b)
        at = pl.ds(pl.multiple_of(chip * ROWS_AT_ONCE, ROWS_AT_ONCE), ROWS_AT_ONCE)
        p = lax.dot_general(gqkv[at, :], wqkv_ref[...], CONTRACT_COLS, preferred_element_type=F32)
        sums.part[0, b] = p.astype(BF16).reshape(2, rows, width)
        sums.cross(0, b).start()
        gsrc[0:1, :] += jnp.sum(p * normed[at, :].astype(F32), axis=0, keepdims=True)

    def gain_sends(act):
        def one(s, tc, tz):
            lanes = pl.ds(pl.multiple_of((tc * NZ + tz) // 2 * 128, 128), 128)
            act(remote(gsrc.at[:, lanes], gain_o.at[flat], ssend.at[s], srecv.at[s], (tc, tz)))

        exchange_loop(c, z, one)

    gain_sends(lambda cp: cp.start())
    own_lanes = pl.ds(pl.multiple_of(flat // 2 * 128, 128), 128)
    gain_keep = pltpu.make_async_copy(gsrc.at[:, own_lanes], gain_o.at[flat], lsem.at[4])
    gain_keep.start()
    sums.one(0)
    for cp in mlp_z + [keep]:
        cp.wait()
    mlp_c += over_plane(1, mt)
    sums.two(0)

    sums.three(0, o_ref)

    qkv_c = []
    for h in range(2):
        lanes = pl.ds(h * qcols, qcols)
        for cp in qkv_z[3 * h : 3 * h + 3]:
            cp.wait()

        def gathered(j, _):
            total = qkvg[j, z, :, lanes].astype(F32)
            for s in (1, 2, 3):
                total = total + qt[s, j, :, lanes].astype(F32)
            qs[j, :, lanes] = total.astype(BF16)
            return 0

        lax.fori_loop(0, 8, gathered, 0)
        for n, out_ref, lo, wide in ((0, q_o, 0, qcols),) if h == 0 else (
            (1, k_o, qcols, HEAD_SIZE), (2, v_o, qcols + HEAD_SIZE, HEAD_SIZE)
        ):
            dst = out_ref.at[:, pl.ds(pl.multiple_of(c * wide, wide), wide)]
            part = pl.ds(lo, wide)
            qkv_c += [remote(qs.at[m, :, part], dst, q2send.at[n, s], q2recv.at[n, s], (m, z)) for s, m in enumerate(mates)]
            qkv_c.append(pltpu.make_async_copy(qs.at[c, :, part], dst, lsem.at[6 + n]))
        for cp in qkv_c[-8 if h == 0 else -16 :]:
            cp.start()
    sums.end(o_ref)
    for cp in plane.first(g_ref) + plane.second()[0] + plane.second()[1] + [plane.third()]:
        cp.wait_send()
    gain_sends(lambda cp: cp.wait())
    for cp in mlp_c + out_sends + qkv_c + [keep_o, gain_keep]:
        cp.wait()


def attention_back(g, err, q, k, v, attn, cosine, sine, first, place, keys, w_qkv, w_out, gain, normed, gate_g, up_g):
    rows, width = g.shape
    tokens = q.shape[0]
    any_ = pl.BlockSpec(memory_space=pl.ANY)
    vmem = pl.BlockSpec(memory_space=pltpu.VMEM)
    dma, buf, out = pltpu.SemaphoreType.DMA, pltpu.VMEM, jax.ShapeDtypeStruct
    share = width // 32
    cols = w_qkv.shape[1]
    by_owner = gate_g.shape
    ff = by_owner[3]
    return pl.pallas_call(
        back_kernel,
        out_shape=(
            out((rows, width), F32),
            out((share, 32 * ff), BF16),
            out((share, 32 * ff), BF16),
            out((share, 8 * q.shape[1]), BF16),
            out((share, 8 * k.shape[1]), BF16),
            out((share, 8 * v.shape[1]), BF16),
            out((NZ, share, width), BF16),
            out((32, 8, 128), F32),
        ),
        in_specs=[vmem, pl.BlockSpec(memory_space=pltpu.SMEM)] + [any_] * 15,
        out_specs=(vmem,) + (any_,) * 7,
        scratch_shapes=[
            buf(a.shape, a.dtype)
            for a in (q, k, v, attn, cosine, sine, first, place, keys, w_qkv, w_out, gain, normed)
        ] + [
            dma((13,)),
            buf((8, rows, width), BF16), buf(q.shape, BF16), buf((tokens, cols), BF16), buf(k.shape, F32), buf(v.shape, F32),
            buf(w_out.shape, BF16), buf((8, NZ, share, cols), BF16),
            buf(by_owner, BF16), buf((NZ, 8, share, cols), BF16), buf((8, share, cols), BF16), buf((8, width), F32),
            dma((4,)), dma((4,)), dma((2, 4, 7)), dma((2, 4, 7)), dma((2, 4)), dma((2, 4)), dma((2, 4)), dma((3, 7)), dma((3, 7)), dma((4,)), dma((4,)),
            dma((32,)), dma((32,)), dma((9,)), dma((8,)), dma((8,)),
        ] + scatter_scratch(1, rows, width),
        compiler_params=pltpu.CompilerParams(collective_id=6, has_side_effects=True, vmem_limit_bytes=60 << 20),
        cost_estimate=takes(110),
        name="attention_back",
    )(g, err, q, k, v, attn, cosine, sine, first, place, keys, w_qkv, w_out, gain, normed, gate_g, up_g)


class Line:
    def __init__(self, c, z, slot, send, recv):
        self.c, self.z, self.slot, self.send, self.recv = c, z, slot, send, recv
        self.order = plane_order(z)

    def hop(self, up, t):
        zz = self.order[t]
        row = 0 if up else 1
        return remote(
            self.slot(zz), self.slot(zz), self.send.at[row, zz], self.recv.at[zz], (self.c, self.z + (1 if up else -1))
        )

    def hops(self, t, act):
        zz, z = self.order[t], self.z

        @pl.when((zz <= z) & (z < NZ - 1))
        def _():
            act(self.hop(True, t))

        @pl.when((zz >= z) & (z > 0))
        def _():
            act(self.hop(False, t))

    def step(self, t):
        if t > 0:
            self.hop(True, t).wait_recv()
        self.hops(t, lambda cp: cp.start())

    def end(self):
        for t in range(NZ):
            self.hops(t, lambda cp: cp.wait_send())


def front_kernel(
    x_ref, g_ref, mask_ref, wq_ref, wk_ref, wv_ref, wo_ref, wd_ref, wg_ref, cos_in, sin_in, first_in, place_in, keys_in,
    o_ref, go_ref, so_ref, norm_o, wqkv_o, outr_o, downr_o, gate_o, q_o, k_o, v_o, attn_o,
    wqkv, outr, downr, gatew, q_ref, k_ref, v_ref, attn_ref, cos_ref, sin_ref, first_ref, place_ref, keys_ref,
    normed, nall, acc, tmp_o, tmp_d, st_ref, isem, osem, wgsend, wgrecv, ssend, srecv,
    lsem, gsend, grecv, qzsend, qzrecv, ozsend, ozrecv, dsend, drecv, o2send, o2recv, d2send, d2recv, psend, precv, *scat
):
    here = place_on_plane()
    c, z, sib, xn, yn, diag = here
    rows, width = x_ref.shape
    tokens = 8 * rows
    wide = tmp_o.shape[2]
    mates = [lax.rem(c + s, 8) for s in range(1, 8)]
    others = [lax.rem(z + s, NZ) for s in (1, 2, 3)]
    flat, everyone = everyone_else(c, z)
    meet(everyone)
    sums = Scatter(here, [z], *scat)
    plane = Plane(here, lambda j: nall.at[j], psend, precv, rows // 2)
    line_q = Line(c, z, lambda zz: wqkv.at[zz], qzsend, qzrecv)
    line_o = Line(c, z, lambda zz: tmp_o.at[zz], ozsend, ozrecv)
    own_cols = pl.ds(pl.multiple_of(c * wide, wide), wide)

    def narrow(ref, n):
        return ref.at[:, pl.ds(pl.multiple_of(c * n, n), n)]

    q_keeps = [
        pltpu.make_async_copy(narrow(wq_ref, wide), wqkv.at[z, :, pl.ds(0, wide)], lsem.at[0]),
        pltpu.make_async_copy(narrow(wk_ref, HEAD_SIZE), wqkv.at[z, :, pl.ds(wide, HEAD_SIZE)], lsem.at[1]),
        pltpu.make_async_copy(narrow(wv_ref, HEAD_SIZE), wqkv.at[z, :, pl.ds(wide + HEAD_SIZE, HEAD_SIZE)], lsem.at[2]),
    ]
    o_keep = pltpu.make_async_copy(wo_ref.at[:, own_cols], tmp_o.at[z], lsem.at[3])
    d_keeps, downs = [], []
    for core in range(2):
        for hop in range(NZ):
            to = lax.rem(z + hop, NZ)
            src = wd_ref.at[pl.ds(pl.multiple_of((core * NZ + to) * wide, wide), wide), own_cols]
            if hop == 0:
                d_keeps.append(pltpu.make_async_copy(src, tmp_d.at[z, core], lsem.at[4 + core]))
            else:
                downs.append(remote(src, tmp_d.at[z, core], dsend.at[core, hop], drecv.at[core, hop], (c, to)))
    gate_cols = wg_ref.shape[1] // 32
    gates = []
    for hop in range(NZ):
        to = lax.rem(z + hop, NZ)
        src = wg_ref.at[:, pl.ds(pl.multiple_of((c * NZ + to) * gate_cols, gate_cols), gate_cols)]
        if hop == 0:
            g_keep = pltpu.make_async_copy(src, gatew.at[z], lsem.at[9])
        else:
            gates.append(remote(src, gatew.at[z], wgsend.at[hop], wgrecv.at[hop], (c, to)))
    for cp in [o_keep] + q_keeps + d_keeps + [g_keep]:
        cp.start()
    go_ref[z] = g_ref[...]
    gains = [remote(g_ref, go_ref.at[z], gsend.at[s], grecv.at[s], (c, t)) for s, t in enumerate(others)]
    for cp in gains:
        cp.start()
    o_keep.wait()
    line_o.step(0)
    got = fetches(
        [(cos_in, cos_ref), (sin_in, sin_ref), (first_in, first_ref), (place_in, place_ref), (keys_in, keys_ref)], isem
    )
    st_ref[...] = jnp.full(st_ref.shape, jnp.sum(mask_ref[...].astype(F32)), F32)
    so_ref[flat] = st_ref[...]

    def counts(act):
        def one(s, tc, tz):
            act(remote(st_ref, so_ref.at[flat], ssend.at[s], srecv.at[s], (tc, tz)))

        exchange_loop(c, z, one)

    x = x_ref[...].astype(F32)
    scaled = x * lax.rsqrt(jnp.mean(x * x, axis=-1, keepdims=True) + EPS)
    for cp in gains:
        cp.wait()
    piece = width // NZ
    for zz in range(NZ):
        normed[:, zz * piece : (zz + 1) * piece] = (
            scaled[:, zz * piece : (zz + 1) * piece] * go_ref[zz, 0:1, :]
        ).astype(BF16)
    for cp in plane.first(normed):
        cp.start()
    nall[c] = normed[...]
    counts(lambda cp: cp.start())
    line_o.step(1)
    for cp in q_keeps:
        cp.wait()
    line_q.step(0)
    line_o.step(2)
    for arrived, sends in zip(plane.arrive(), plane.second()):
        arrived.wait_recv()
        for cp in sends:
            cp.start()
    line_o.step(3)

    def regroup(buf, dst, send, recv, lrow):
        def block(j):
            return buf(j // 2, lax.rem(j, 2))

        out = [remote(block(m), dst.at[:, own_cols], send.at[s], recv.at[s], (m, z)) for s, m in enumerate(mates)]
        keep = pltpu.make_async_copy(block(c), dst.at[:, own_cols], lsem.at[lrow])
        for cp in out + [keep]:
            cp.start()
        return out + [keep]

    moved_o = regroup(lambda p, core: tmp_o.at[p, pl.ds(pl.multiple_of(core * wide, wide), wide)], outr, o2send, o2recv, 7)
    line_q.step(1)
    for cp in plane.diagonal():
        cp.wait_recv()
    plane.third().start()
    for cp in plane.across():
        cp.wait_recv()
    line_q.step(2)
    norm_keep = pltpu.make_async_copy(nall, norm_o, lsem.at[6])
    norm_keep.start()

    def project(t):
        zz = line_q.order[t]
        at = pl.ds(pl.multiple_of(zz * piece, piece), piece)
        term = jnp.dot(nall[:, :, at].reshape(tokens, piece), wqkv[zz], preferred_element_type=F32)
        acc[...] = term if t == 0 else acc[...] + term

    for t in range(3):
        project(t)
    line_q.step(3)
    for cp in downs:
        cp.start()
    project(3)
    for cp in got:
        cp.wait()

    def heads(i, _):
        at = pl.ds(pl.multiple_of(i * ROWS_AT_ONCE, ROWS_AT_ONCE), ROWS_AT_ONCE)
        cosine, sine = cos_ref[at, :], sin_ref[at, :]
        for h in range(wide // HEAD_SIZE):
            lanes = slice(h * HEAD_SIZE, (h + 1) * HEAD_SIZE)
            q_ref[at, lanes] = turn(acc[at, lanes], cosine, sine).astype(BF16)
        k_ref[at, :] = turn(acc[at, wide : wide + HEAD_SIZE], cosine, sine).astype(BF16)
        v_ref[at, :] = acc[at, wide + HEAD_SIZE :].astype(BF16)
        return 0

    lax.fori_loop(0, tokens // ROWS_AT_ONCE, heads, 0)

    saved = fetches([(wqkv, wqkv_o), (q_ref, q_o), (k_ref, k_o), (v_ref, v_o)], osem)

    def attend(b):
        at = pl.ds(pl.multiple_of(chip_at(c, b) * ROWS_AT_ONCE, ROWS_AT_ONCE), ROWS_AT_ONCE)
        k, v = k_ref[...], v_ref[...]
        first, place, keys = first_ref[at, :], place_ref[at, :], keys_ref[...]
        for h in range(wide // HEAD_SIZE):
            lanes = slice(h * HEAD_SIZE, (h + 1) * HEAD_SIZE)
            probs = block_probs(q_ref[at, lanes], k, first, place, keys)
            attn_ref[at, lanes] = jnp.dot(probs.astype(BF16), v, preferred_element_type=F32).astype(BF16)
        p = jnp.dot(attn_ref[at, :], outr[...], preferred_element_type=F32).astype(BF16)
        sums.part[0, b] = p.reshape(2, rows, width)
        sums.cross(0, b).start()

    for cp in moved_o:
        cp.wait()
    attend(3)
    attend(1)
    sums.one(0)
    attend(2)
    attend(0)
    saved += fetches([(outr, outr_o), (attn_ref, attn_o)], osem.at[pl.ds(4, 2)])
    sums.two(0)
    for cp in d_keeps + downs:
        cp.wait()
    moved_d = regroup(lambda p, core: tmp_d.at[p, core], downr, d2send, d2recv, 8)
    for cp in gates:
        cp.start()
    sums.three(0, o_ref)
    sums.end(o_ref)
    for cp in moved_d:
        cp.wait()
    saved += fetches([(downr, downr_o)], osem.at[pl.ds(6, 1)])
    for cp in gates + [g_keep]:
        cp.wait()
    saved += fetches([(gatew, gate_o)], osem.at[pl.ds(7, 1)])
    for cp in plane.first(normed) + plane.second()[0] + plane.second()[1] + [plane.third()]:
        cp.wait_send()
    line_q.end()
    line_o.end()
    counts(lambda cp: cp.wait())
    for cp in saved + [norm_keep]:
        cp.wait()


def attention_front(x, gains, mask, w_query, w_key, value_weight, w_output, w_down, w_gate, cosine, sine, first, place, keys):
    rows, width = x.shape
    tokens = 8 * rows
    depth = w_query.shape[0]
    wide = width // 8
    any_ = pl.BlockSpec(memory_space=pl.ANY)
    vmem = pl.BlockSpec(memory_space=pltpu.VMEM)
    dma, buf, out = pltpu.SemaphoreType.DMA, pltpu.VMEM, jax.ShapeDtypeStruct
    results = (
        out((NZ, depth, 2 * wide), BF16),
        out((wide, width), BF16),
        out((wide, width), BF16),
        out((NZ, depth, w_gate.shape[1] // 32), BF16),
        out((tokens, wide), BF16),
        out((tokens, HEAD_SIZE), BF16),
        out((tokens, HEAD_SIZE), BF16),
        out((tokens, wide), BF16),
    )
    return pl.pallas_call(
        front_kernel,
        out_shape=(
            out((rows, width), F32), out((NZ,) + gains.shape, F32), out((32, 8, 128), F32), out((8, rows, width), BF16)
        ) + results,
        in_specs=[vmem] * 3 + [any_] * 11,
        out_specs=(vmem,) * 3 + (any_,) * 9,
        scratch_shapes=[buf(r.shape, r.dtype) for r in results]
        + [buf(a.shape, a.dtype) for a in (cosine, sine, first, place, keys)]
        + [
            buf((rows, width), BF16), buf((8, rows, width), BF16), buf((tokens, 2 * wide), F32), buf((NZ, depth, wide), BF16),
            buf((NZ, 2, wide, wide), BF16), buf((8, 128), F32), dma((5,)), dma((8,)), dma((NZ,)), dma((NZ,)),
            dma((32,)), dma((32,)),
            dma((10,)), dma((3,)), dma((3,)), dma((2, 4)), dma((4,)), dma((2, 4)), dma((4,)), dma((2, 4)), dma((2, 4)),
            dma((7,)), dma((7,)), dma((7,)), dma((7,)), dma((8,)), dma((8,)),
        ] + scatter_scratch(1, rows, width),
        compiler_params=pltpu.CompilerParams(collective_id=8, has_side_effects=True, vmem_limit_bytes=60 << 20),
        cost_estimate=takes(95),
        name="attention_front",
    )(x, gains, mask, w_query, w_key, value_weight, w_output, w_down, w_gate, cosine, sine, first, place, keys)


def heads_and_columns(
    hidden_in,
    cotangent,
    teacher,
    valid_mask,
    doc_starts,
    attn_gain,
    w_query,
    w_key,
    value_weight,
    w_output,
    mlp_gain,
    w_gate,
    w_up,
    w_down,
):
    rows, width = hidden_in.shape[1:]
    c = lax.axis_index("ctx")
    z = lax.axis_index("fsdp")
    devices = lax.axis_size("ctx")
    tokens = rows * devices
    group = QUERY_HEADS // KEY_VALUE_HEADS
    qcols = group * HEAD_SIZE
    ffcols = FF // (devices * NZ)

    layer_input = hidden_in[0].astype(F32)
    gains = jnp.concatenate(
        [attn_gain.astype(F32)[None], mlp_gain.astype(F32)[None], jnp.zeros((6, attn_gain.shape[0]), F32)]
    )
    place, segment, offset = stream_places(tokens, rows, devices, doc_starts[0])
    freq = ROPE_BASE ** (-(jnp.arange(HEAD_SIZE // 2, dtype=F32) * 2.0 / HEAD_SIZE))
    angle = offset.astype(F32)[:, None] * freq[None, :]
    cosine = jnp.concatenate([jnp.cos(angle)] * 2, axis=1)
    sine = jnp.concatenate([-jnp.sin(angle), jnp.sin(angle)], axis=1)
    columns = ((place - offset)[:, None], place[:, None], place[None, :])
    branch, gains_all, counts, normed_all, w_qkv, out_rows, down_rows, gate_cols, q, k, v, attn = attention_front(
        hidden_in[0], gains, valid_mask, w_query, w_key, value_weight, w_output, w_down, w_gate, cosine, sine, *columns
    )
    attn_scale = gains_all[:, 0, :].reshape(1, width)
    mlp_scale = gains_all[:, 1, :].reshape(1, width)
    residual = layer_input + branch

    r2 = rms_norm_scale(residual)
    hat2 = residual * r2
    normed2 = (hat2 * mlp_scale).astype(BF16)
    maskf = valid_mask[0].astype(F32)
    mlp_out, normed2_all, gate_up, w_mlp = feed_forward(normed2, gate_cols, w_up, down_rows)
    count = jnp.sum(counts[:, 0, 0])
    outf = residual + mlp_out

    diff = outf - teacher[0].astype(F32)
    error_here = jnp.sum(maskf * jnp.mean(diff * diff, axis=-1))
    g_out = cotangent[0].astype(F32) + maskf[:, None] * diff * (2.0 / (count * width))
    g_norm2, _, gate_grads, up_grads, down_grads = feed_back(g_out.astype(BF16), w_mlp, down_rows, normed2_all, gate_up)

    g_hat2 = g_norm2 * mlp_scale
    g_residual = g_out + r2 * (g_hat2 - hat2 * jnp.mean(g_hat2 * hat2, axis=-1, keepdims=True))
    mlp_gain_term = jnp.sum(g_norm2 * hat2, axis=0, keepdims=True)
    g_norm1, got_gate, got_up, got_q, got_k, got_v, got_out, got_gains = attention_back(
        g_residual.astype(BF16), error_here.reshape(1, 1), q, k, v, attn, cosine, sine, *columns, w_qkv.reshape(width, -1), out_rows, mlp_gain_term,
        normed_all.reshape(tokens, width), gate_grads, up_grads,
    )

    r1 = rms_norm_scale(layer_input)
    hat1 = layer_input * r1
    g_hat1 = g_norm1 * attn_scale
    g_input = g_residual + r1 * (g_hat1 - hat1 * jnp.mean(g_hat1 * hat1, axis=-1, keepdims=True))

    parts = devices * NZ
    share = width // parts
    got_out = jnp.sum(got_out.astype(F32), axis=0)
    flat = c * NZ + z
    got_gains = jnp.sum(got_gains, axis=0)
    loss = got_gains[2, 0] / count
    got_gains = lax.dynamic_slice_in_dim(got_gains, flat % 2 * share, share, axis=1)
    own_scale = lax.dynamic_slice_in_dim(attn_scale[0], flat * share, share)

    return (
        loss,
        outf.astype(BF16)[None],
        g_input.astype(BF16)[None],
        got_gains[0] / own_scale,
        got_q.astype(F32),
        got_k.astype(F32),
        got_v.astype(F32),
        got_out,
        got_gains[1],
        got_gate.astype(F32),
        got_up.astype(F32),
        down_grads,
    )


def solution(mesh):
    small = dict(mesh.shape) == {"ctx": KEY_VALUE_HEADS, "fsdp": NZ}
    in_specs = (
        P("fsdp", "ctx", None),
        P("fsdp", "ctx", None),
        P("fsdp", "ctx", None),
        P("fsdp", "ctx"),
        P("fsdp", None),
        P("fsdp"),
        P("fsdp", None),
        P("fsdp", None),
        P("fsdp", None),
        P("fsdp", None),
        P("fsdp"),
        P("fsdp", None),
        P("fsdp", None),
        P("fsdp", None),
    )
    out_specs = (
        P(),
        P("fsdp", "ctx", None),
        P("fsdp", "ctx", None),
        P(("ctx", "fsdp")),
        P(("ctx", "fsdp"), None),
        P(("ctx", "fsdp"), None),
        P(("ctx", "fsdp"), None),
        P(("ctx", "fsdp"), None),
        P(("ctx", "fsdp")),
        P(("ctx", "fsdp"), None),
        P(("ctx", "fsdp"), None),
        P(("ctx", "fsdp"), None),
    )
    return jax.shard_map(
        heads_and_columns if small else per_device, mesh=mesh, in_specs=in_specs, out_specs=out_specs, check_vma=False
    )
```
